32 devices in a mesh: guide: 2 (over core), dp: 4 (over y, x), mp: 4 (over z).
Axes of the slice: x: 2, y: 2, z: 4, core: 2. Of those that a mesh axis runs over, the one named last changes fastest.
Arguments:
- states: bfloat16 [2, 32, 2048], P('guide', 'dp'), may hold values from -6 to 6
- lengths: int32 [2, 32], P('guide', 'dp'), may hold values from 1 to 32768, as said below
- sink_cache: bfloat16 [2, 32, 16, 2, 4, 128], P('guide', 'dp', 'mp'), may hold values from -48 to 48
- window_cache: bfloat16 [2, 32, 16, 2, 256, 128], P('guide', 'dp', 'mp'), may hold values from -360 to 360
- qkv_weight: bfloat16 [2048, 3, 16, 128], P(None, None, 'mp'), may hold values from -0.125 to 0.125
- out_weight: bfloat16 [16, 128, 2048], P('mp'), may hold values from -0.125 to 0.125
- expert_ids: int32 [2, 32, 8], replicated, may hold values from 0 to 63, all different within a row; in each aligned block of 8 rows (0 to 7, 8 to 15, ..., all dimensions but the last counted through in order) at most 2 rows name the same one
- route_weight: float32 [2, 32, 8], replicated, may hold values from 0.5 to 2
- expert_in: bfloat16 [2, 2048, 65536], P(None, None, ('guide', 'dp', 'mp')), may hold values from -0.125 to 0.125
- expert_out: bfloat16 [65536, 2048], P(('guide', 'dp', 'mp')), may hold values from -0.1875 to 0.1875
- vocab_weight: bfloat16 [2048, 26624], P(('guide', 'dp'), 'mp'), may hold values from -0.125 to 0.125
- guidance: float32 [32], P('dp'), may hold values from 1 to 5
Outputs:
- guided: float32 [32, 4, 2, 3328], P('dp', 'mp', 'guide')
The draws below stay inside these ranges and needn't reach their ends.
Inputs may be any that keep to these rules, and one draw needn't show every extreme that they name: `lengths`: one stream of one request has exactly 32768 cached positions. `expert_ids`: taking the tokens streams first, then requests, in aligned blocks of 8 tokens (the tokens of one device), no expert is named by more than 2 tokens of a block, a bound that some block reaches.
All inputs are finite; a program needn't handle non-finite values.
Results may differ from the reference program's by a relative error of at most 0.025.
Values may be sent and summed in bfloat16 or wider, within the bound.
No kernel may reach another device: no remote copies, remote signals or barrier semaphores. Data moves between devices by JAX's collectives and lax.ppermute only.
A program may use at most 128 MiB of HBM per device.

```python
import math
import jax
import jax.numpy as jnp
import numpy as np
from jax import lax

D = 2048
HEADS = 16
HD = 128
EXPERTS = 64
FFE = 1024
TOPK = 8
MOST = 2
VOCAB = 26624
SINKS = 4
WINDOW = 256
MAXLEN = 32768
R_DEV = 8
REQUESTS = 32
N_MP = 4


def draw_lengths(key, part):
    key_exp, key_extra, key_pick = jax.random.split(key, 3)
    exponent = jax.random.randint(key_exp, (2, REQUESTS), 0, 15)
    base_len = jnp.left_shift(jnp.ones_like(exponent), exponent)
    extra_len = jax.random.randint(key_extra, (2, REQUESTS), 0, 16384) % base_len
    drawn_len = (base_len + extra_len).reshape(-1)
    pick_index = jax.random.randint(key_pick, (), 0, 2 * REQUESTS)
    return drawn_len.at[pick_index].set(MAXLEN).reshape(2, REQUESTS).astype(jnp.int32)


def draw_sink_cache(key, part):
    sample = jnp.clip(jax.random.normal(key, (2, REQUESTS, HEADS, 2, SINKS, HD), jnp.float32), -6.0, 6.0)
    factor = jnp.array([2.5, 8.0], jnp.float32).reshape(1, 1, 1, 2, 1, 1)
    return (sample * factor).astype(jnp.bfloat16)


def draw_window_cache(key, part):
    key_main = jax.random.fold_in(key, 0)
    sample = jnp.clip(jax.random.normal(key_main, (2, REQUESTS, HEADS, 2, WINDOW, HD), jnp.float32), -6.0, 6.0)
    factor = jnp.array([1.0, 8.0], jnp.float32).reshape(1, 1, 1, 2, 1, 1)
    return (sample * factor).astype(jnp.bfloat16)


def steps_of(own_key, dims, cuts, least, largest):
    loudness = 1.0
    for dim, shards_of in cuts:
        heights = jax.random.uniform(jax.random.fold_in(jax.random.fold_in(own_key, 6), dim), (shards_of,), jnp.float32, least / len(cuts), largest / len(cuts))
        loudness = loudness * jnp.repeat(jnp.exp(heights), dims[dim] // shards_of).reshape((-1,) + (1,) * (len(dims) - 1 - dim))
    return loudness


def shared_out(rng, own, number, rows, amount, top, limit, skew):
    sequence = jax.random.permutation(rng, amount)
    crowded, common = portions_of(amount, rows * top, limit, skew, True), portions_of(amount, rows * top, limit, skew, False)
    places = jnp.arange(amount)

    def named(tallies, turn):
        used = int((tallies > 0).sum())
        fixed = max(1, used // 4)
        shifted = fixed + (places - fixed + turn * (used - fixed)) % max(1, amount - fixed)
        return jnp.zeros((amount,), jnp.int32).at[sequence[jnp.where(places < fixed, places, shifted)]].set(jnp.asarray(tallies, jnp.int32))

    tallies = jnp.where(number % 4 == 0, named(crowded, number // 4), named(common, number - number // 4 - 1))
    mixed = jax.random.permutation(jax.random.fold_in(own, 3), amount)
    donor, sink = mixed[0:amount // 2 * 2:2], mixed[1:amount // 2 * 2:2]
    room = jnp.minimum(tallies[donor] - 1, limit - tallies[sink]) // 2
    room = jnp.where((donor == sequence[0]) | (sink == sequence[0]) | (tallies[sink] == 0), 0, jnp.maximum(room, 0))
    shifted = jax.random.randint(jax.random.fold_in(own, 4), (amount // 2,), 0, 1 << 20) % (room + 1)
    tallies = tallies.at[donor].add(-shifted).at[sink].add(shifted)
    members = jnp.searchsorted(jnp.cumsum(tallies), jnp.arange(rows * top), side="right").astype(jnp.int32)
    grid = members.reshape(top, rows).T
    grid = grid[jax.random.permutation(jax.random.fold_in(own, 1), rows)]
    turn = jax.random.randint(jax.random.fold_in(own, 2), (rows, 1), 0, top)
    return jnp.take_along_axis(grid, (jnp.arange(top)[None, :] + turn) % top, axis=1)


def portions_of(count, total, limit, slope, full):
    loads = [(1 << 20) // math.isqrt(rank ** slope) + 1 for rank in range(1, count + 1)]
    largest = limit if full else min(limit, max(-(-total // count), total * loads[0] // sum(loads)))
    least = 1 if total - largest >= count - 1 else 0
    counts, spare = [largest] + [least] * (count - 1), total - largest - least * (count - 1)
    while spare > 0:
        candidates = [i for i in range(1, count) if counts[i] < largest] or [i for i in range(1, count) if counts[i] < limit]
        pool, remaining = sum([loads[i] for i in candidates]), spare
        for i in candidates:
            addition = min(limit - counts[i], max(1, remaining * loads[i] // pool), spare)
            counts[i] = counts[i] + addition
            spare = spare - addition
    return np.array(counts)


def scatter_about(rng, dims, width, most, pieces=(), kind=jnp.bfloat16):
    values = width * jax.random.normal(rng, dims, jnp.float32)
    if pieces:
        values = values * steps_of(rng, dims, pieces, -0.22, 0.18)
    return jnp.clip(values, -most, most).astype(kind)


def setup_inputs(seed: int = 0) -> dict:
    keys = jax.random.split(jax.random.key(seed), 13)
    states = scatter_about(keys[0], (2, REQUESTS, D), 1.0, 6.0, ((0, 2), (1, 4)))
    lengths = draw_lengths(jax.random.fold_in(keys[12], 71), 0)
    sink_cache = draw_sink_cache(jax.random.fold_in(keys[12], 71), 0)
    window_cache = draw_window_cache(jax.random.fold_in(keys[12], 71), 0)
    qkv_weight = scatter_about(keys[4], (D, 3, HEADS, HD), D ** -0.5, 0.125, ((2, 4),))
    out_weight = scatter_about(keys[5], (HEADS, HD, D), (HEADS * HD) ** -0.5, 0.125, ((0, 4),))
    expert_ids_keys = jax.random.split(jax.random.fold_in(keys[6], 1), 2 * REQUESTS // R_DEV)
    expert_ids_turns = jax.random.permutation(jax.random.fold_in(keys[6], 3), 2 * REQUESTS // R_DEV)
    expert_ids = jax.vmap(lambda own, number: shared_out(jax.random.fold_in(keys[6], 2), own, number, R_DEV, EXPERTS, TOPK, MOST, 2))(expert_ids_keys, expert_ids_turns).reshape((2, REQUESTS, TOPK))
    route_weight = jnp.clip(jax.random.uniform(keys[7], (2, REQUESTS, TOPK), jnp.float32, 0.5, 2.0), 0.5, 2.0)
    expert_in = scatter_about(keys[8], (2, D, EXPERTS * FFE), D ** -0.5, 0.125, ((2, 32),))
    expert_out = scatter_about(keys[9], (EXPERTS * FFE, D), FFE ** -0.5, 0.1875, ((0, 32),))
    vocab_weight = scatter_about(keys[10], (D, VOCAB), D ** -0.5, 0.125, ((0, 8), (1, 4)))
    guidance = jnp.clip(1.0 + 4.0 * jax.random.uniform(keys[11], (REQUESTS,), jnp.float32) ** steps_of(keys[11], (REQUESTS,), ((0, 4),), -0.2, 0.2), 1.0, 5.0)
    return dict(states=states, lengths=lengths, sink_cache=sink_cache, window_cache=window_cache, qkv_weight=qkv_weight, out_weight=out_weight, expert_ids=expert_ids, route_weight=route_weight, expert_in=expert_in, expert_out=expert_out, vocab_weight=vocab_weight, guidance=guidance)


EPSILON = 1e-05

def rms_norm(values):
    return values * lax.rsqrt(lax.optimization_barrier(jnp.mean(values * values, axis=-1, keepdims=True)) + EPSILON)

def rotate(vectors, positions):
    full_width = vectors.shape[-1]
    half_width = full_width // 2
    step_index = jnp.arange(half_width, dtype=jnp.float32)
    inverse = jnp.exp(step_index * (-2.0 * math.log(10000.0) / full_width))
    angles = positions.astype(jnp.float32)[:, None] * inverse[None, :]
    cosine = jnp.cos(angles)[:, None, :]
    sine_part = jnp.sin(angles)[:, None, :]
    first_half = vectors[..., :half_width]
    second = vectors[..., half_width:]
    return jnp.concatenate([first_half * cosine - second * sine_part, second * cosine + first_half * sine_part], axis=-1)

def attend(operands, qkv_weight, out_weight):
    hidden, stream_lengths, sink_rows, window = operands
    normed = rms_norm(hidden.astype(jnp.float32)).astype(jnp.bfloat16)
    projected = jnp.einsum('rd,dthe->rthe', normed.astype(jnp.float32), qkv_weight.astype(jnp.float32))
    query_rot = rotate(projected[:, 0], stream_lengths).astype(jnp.bfloat16)
    fresh_key = rotate(projected[:, 1], stream_lengths).astype(jnp.bfloat16)
    fresh_value = projected[:, 2].astype(jnp.bfloat16)
    key_rows = jnp.concatenate([sink_rows[:, :, 0], window[:, :, 0], fresh_key[:, :, None]], axis=2)
    value_rows = jnp.concatenate([sink_rows[:, :, 1], window[:, :, 1], fresh_value[:, :, None]], axis=2)
    sink_count = sink_rows.shape[3]
    window_count = window.shape[3]
    scores = jnp.einsum('rhe,rhne->rhn', query_rot.astype(jnp.float32), key_rows.astype(jnp.float32)) / math.sqrt(query_rot.shape[-1])
    slot_index = jnp.arange(sink_count + window_count + 1, dtype=jnp.int32)[None, None, :]
    length_limit = stream_lengths.astype(jnp.int32)[:, None, None]
    valid_slot = jnp.where(slot_index < sink_count, slot_index < length_limit, jnp.where(slot_index < sink_count + window_count, slot_index >= 2 * sink_count + window_count - length_limit, True))
    scores = jnp.where(valid_slot, scores, -1e+30)
    weights = jax.nn.softmax(scores, axis=-1).astype(jnp.bfloat16)
    mixture = jnp.einsum('rhn,rhne->rhe', weights.astype(jnp.float32), value_rows.astype(jnp.float32)).astype(jnp.bfloat16)
    output = jnp.einsum('rhe,hed->rd', mixture.astype(jnp.float32), out_weight.astype(jnp.float32))
    return (hidden.astype(jnp.float32) + output).astype(jnp.bfloat16)

def reference(states, lengths, sink_cache, window_cache, qkv_weight, out_weight, expert_ids, route_weight, expert_in, expert_out, vocab_weight, guidance):
    after_attention = lax.map(lambda operands: attend(operands, qkv_weight, out_weight), (states, lengths, sink_cache, window_cache))
    tokens_total = states.shape[0] * states.shape[1]
    model_width = states.shape[2]
    residual = after_attention.reshape(tokens_total, model_width)
    moe_in = rms_norm(residual.astype(jnp.float32)).astype(jnp.bfloat16)
    choice_rows = expert_ids.reshape(tokens_total, -1)
    route_rows = route_weight.reshape(tokens_total, -1)
    inputs_by_expert = expert_in.reshape(2, model_width, EXPERTS, FFE).transpose(2, 0, 1, 3)
    outputs_by_expert = expert_out.reshape(EXPERTS, FFE, model_width)

    def expert_step(running, operands):
        expert_index, weights_in, weights_out = operands
        coefficient = lax.optimization_barrier(jnp.sum(jnp.where(choice_rows == expert_index, route_rows, 0.0), axis=-1))
        gate = jnp.dot(moe_in, weights_in[0], preferred_element_type=jnp.float32)
        upward = jnp.dot(moe_in, weights_in[1], preferred_element_type=jnp.float32)
        activated = (jax.nn.silu(gate) * upward * coefficient[:, None]).astype(jnp.bfloat16)
        return (running + jnp.dot(activated, weights_out, preferred_element_type=jnp.float32), None)
    initial = jnp.zeros((tokens_total, model_width), jnp.float32)
    expert_sum, unused = lax.scan(expert_step, initial, (jnp.arange(EXPERTS, dtype=jnp.int32), inputs_by_expert, outputs_by_expert))
    final = rms_norm(residual.astype(jnp.float32) + expert_sum).astype(jnp.bfloat16)
    logits = jnp.dot(final, vocab_weight, preferred_element_type=jnp.float32).reshape(2, states.shape[1], -1)
    guided = logits[1] + guidance[:, None] * (logits[0] - logits[1])
    return guided.reshape(states.shape[1], N_MP, 2, VOCAB // (2 * N_MP))
```

```python
import math

import jax
import jax.numpy as jnp
from jax import lax
from jax.sharding import PartitionSpec as P

FFE = 1024

EPSILON = 1e-05

ROWS = ("guide", "dp")
DIRECT = 8


def swap(blocks, axis):
    count = lax.axis_size(axis)
    if count <= DIRECT:
        return [blocks[0]] + [
            lax.ppermute(blocks[j], axis, [(i, i ^ j) for i in range(count)]) for j in range(1, count)
        ]
    order = lax.axis_index(axis) ^ jnp.arange(count, dtype=jnp.int32)
    sent = jnp.take(jnp.stack(blocks), order, axis=0)
    received = lax.all_to_all(sent, axis, 0, 0, tiled=True)
    return list(jnp.take(received, order, axis=0))


def spread(block, axis):
    return swap([block] * lax.axis_size(axis), axis)


def rotate(vectors, positions):
    full_width = vectors.shape[-1]
    half_width = full_width // 2
    step_index = jnp.arange(half_width, dtype=jnp.float32)
    inverse = jnp.exp(step_index * (-2.0 * math.log(10000.0) / full_width))
    angles = positions.astype(jnp.float32)[:, None] * inverse[None, :]
    cosine = jnp.cos(angles)[:, None, :]
    sine_part = jnp.sin(angles)[:, None, :]
    first_half = vectors[..., :half_width]
    second = vectors[..., half_width:]
    return jnp.concatenate(
        [first_half * cosine - second * sine_part, second * cosine + first_half * sine_part],
        axis=-1,
    )


def rms_norm(values):
    return values * lax.rsqrt(jnp.mean(values * values, axis=-1, keepdims=True) + EPSILON)


def attend(hidden, own_lengths, sink_rows, window_rows, qkv_weight, out_weight):
    normed = rms_norm(hidden.astype(jnp.float32)).astype(jnp.bfloat16)
    projected = jnp.einsum("rd,dthe->rthe", normed, qkv_weight, preferred_element_type=jnp.float32)
    query_rot = rotate(projected[:, 0], own_lengths).astype(jnp.bfloat16)
    fresh_key = rotate(projected[:, 1], own_lengths).astype(jnp.bfloat16)
    fresh_value = projected[:, 2].astype(jnp.bfloat16)
    sink_count = sink_rows.shape[3]
    window_count = window_rows.shape[3]
    root_size = math.sqrt(query_rot.shape[-1])
    sink_scores = (
        jnp.einsum(
            "rhe,rhse->rhs", query_rot, sink_rows[:, :, 0], preferred_element_type=jnp.float32
        )
        / root_size
    )
    window_scores = (
        jnp.einsum(
            "rhe,rhwe->rhw", query_rot, window_rows[:, :, 0], preferred_element_type=jnp.float32
        )
        / root_size
    )
    self_scores = (
        jnp.einsum("rhe,rhe->rh", query_rot, fresh_key, preferred_element_type=jnp.float32)
        / root_size
    )
    length_limit = own_lengths[:, None, None]
    sink_valid = jnp.arange(sink_count, dtype=jnp.int32)[None, None, :] < length_limit
    window_valid = (
        jnp.arange(window_count, dtype=jnp.int32)[None, None, :]
        >= sink_count + window_count - length_limit
    )
    sink_scores = jnp.where(sink_valid, sink_scores, -1e30)
    window_scores = jnp.where(window_valid, window_scores, -1e30)
    highest = jnp.maximum(
        jnp.maximum(jnp.max(sink_scores, axis=-1), jnp.max(window_scores, axis=-1)), self_scores
    )
    sink_exp = jnp.exp(sink_scores - highest[..., None])
    window_exp = jnp.exp(window_scores - highest[..., None])
    self_exp = jnp.exp(self_scores - highest)
    totals = jnp.sum(sink_exp, axis=-1) + jnp.sum(window_exp, axis=-1) + self_exp
    sink_prob = (sink_exp / totals[..., None]).astype(jnp.bfloat16)
    window_prob = (window_exp / totals[..., None]).astype(jnp.bfloat16)
    self_prob = (self_exp / totals).astype(jnp.bfloat16)
    mixture = (
        jnp.einsum(
            "rhs,rhse->rhe", sink_prob, sink_rows[:, :, 1], preferred_element_type=jnp.float32
        )
        + jnp.einsum(
            "rhw,rhwe->rhe", window_prob, window_rows[:, :, 1], preferred_element_type=jnp.float32
        )
        + self_prob[..., None].astype(jnp.float32) * fresh_value.astype(jnp.float32)
    ).astype(jnp.bfloat16)
    return jnp.einsum("rhe,hed->rd", mixture, out_weight, preferred_element_type=jnp.float32)


def body(
    states,
    lengths,
    sink_cache,
    window_cache,
    qkv_weight,
    out_weight,
    expert_ids,
    route_weight,
    expert_in,
    expert_out,
    vocab_weight,
    guidance,
):
    hidden = states[0]
    request_count, width = hidden.shape
    group = lax.axis_size(ROWS)
    place = lax.axis_index(ROWS)
    streams_apart = group // lax.axis_size("guide")
    stream_index = lax.axis_index("guide")
    order = place ^ jnp.arange(group, dtype=jnp.int32)

    partial_out = attend(hidden, lengths[0], sink_cache[0], window_cache[0], qkv_weight, out_weight)
    partials = spread(partial_out.astype(jnp.bfloat16), "mp")
    attention_out = sum(block.astype(jnp.float32) for block in partials)
    own_residual = (hidden.astype(jnp.float32) + attention_out).astype(jnp.bfloat16)

    residual = jnp.concatenate(spread(own_residual, ROWS), axis=0)
    moe_in = rms_norm(residual.astype(jnp.float32)).astype(jnp.bfloat16)

    unit_count = expert_in.shape[2]
    unit_start = lax.axis_index(("guide", "dp", "mp")) * unit_count
    unit_expert = (unit_start + jnp.arange(unit_count, dtype=jnp.int32)) // FFE
    top = expert_ids.shape[-1]
    choice_rows = jnp.take(expert_ids.reshape(group, request_count, top), order, axis=0).reshape(-1, top)
    route_rows = jnp.take(route_weight.reshape(group, request_count, top), order, axis=0).reshape(-1, top)
    coefficient = jnp.sum(
        jnp.where(
            choice_rows[:, :, None] == unit_expert[None, None, :], route_rows[:, :, None], 0.0
        ),
        axis=1,
    )
    gate = jnp.dot(moe_in, expert_in[0], preferred_element_type=jnp.float32)
    upward = jnp.dot(moe_in, expert_in[1], preferred_element_type=jnp.float32)
    activated = (jax.nn.silu(gate) * upward * coefficient).astype(jnp.bfloat16)
    expert_terms = jnp.dot(activated, expert_out, preferred_element_type=jnp.float32).astype(jnp.bfloat16)

    share = vocab_weight.shape[0]
    sent = []
    for j in range(group):
        columns = lax.dynamic_slice_in_dim(expert_terms, (place ^ j) * share, share, 1)
        rows = columns.reshape(group, request_count, share)
        sent.append(jnp.concatenate([rows[i ^ j] for i in range(group)], axis=0))
    expert_part = sum(block.astype(jnp.float32) for block in swap(sent, ROWS))
    expert_total = sum(
        block.astype(jnp.float32) for block in spread(expert_part.astype(jnp.bfloat16), "mp")
    )
    own_columns = lax.dynamic_slice_in_dim(residual, place * share, share, 1)
    summed = own_columns.astype(jnp.float32) + expert_total

    squares = jnp.sum(summed * summed, axis=-1).reshape(group, request_count)
    note = jnp.concatenate([squares, guidance[None, :]], axis=0)
    notes = spread(note, ROWS)
    square_total = jnp.stack(
        [sum(notes[j][i ^ j] for j in range(group)) for i in range(group)]
    ).reshape(-1, 1)
    scale = lax.rsqrt(square_total / width + EPSILON)
    weight = jnp.stack([notes[i][group] for i in range(streams_apart)]).reshape(-1, 1)
    is_conditional = stream_index == 0
    own_factor = jnp.where(is_conditional, weight, 1.0 - weight)

    raw = jnp.dot(summed.astype(jnp.bfloat16), vocab_weight, preferred_element_type=jnp.float32)
    cut = streams_apart * request_count
    mixed = raw[:cut] * (scale[:cut] * own_factor) + raw[cut:] * (scale[cut:] * (1.0 - own_factor))
    half_width = mixed.shape[1] // 2
    mixed = mixed.astype(jnp.bfloat16).reshape(streams_apart, request_count, 2 * half_width)
    sent = [
        lax.dynamic_slice_in_dim(
            mixed[j % streams_apart], (stream_index ^ (j // streams_apart)) * half_width, half_width, 1
        )
        for j in range(group)
    ]
    guided = sum(block.astype(jnp.float32) for block in swap(sent, ROWS))
    return guided.reshape(request_count, 1, 1, half_width)


def solution(mesh):
    in_specs = (
        P("guide", "dp", None),
        P("guide", "dp"),
        P("guide", "dp", "mp", None, None, None),
        P("guide", "dp", "mp", None, None, None),
        P(None, None, "mp", None),
        P("mp", None, None),
        P(),
        P(),
        P(None, None, ("guide", "dp", "mp")),
        P(("guide", "dp", "mp"), None),
        P(("guide", "dp"), "mp"),
        P("dp"),
    )
    out_specs = P("dp", "mp", "guide", None)
    return jax.shard_map(body, mesh=mesh, in_specs=in_specs, out_specs=out_specs, check_vma=False)
```

```python
import math

import jax
import jax.numpy as jnp
from jax import lax
from jax.sharding import PartitionSpec as P

FFE = 1024

EPSILON = 1e-05

ROWS = ("guide", "dp")
ALL = ("guide", "dp", "mp")


def trade(blocks, axis):
    return lax.all_to_all(blocks, axis, 0, 0, tiled=True)


def spread(block, axis):
    return trade(jnp.broadcast_to(block[None], (lax.axis_size(axis),) + block.shape), axis)


def rotate(vectors, positions):
    full_width = vectors.shape[-1]
    half_width = full_width // 2
    step_index = jnp.arange(half_width, dtype=jnp.float32)
    inverse = jnp.exp(step_index * (-2.0 * math.log(10000.0) / full_width))
    angles = positions.astype(jnp.float32)[:, None] * inverse[None, :]
    cosine = jnp.cos(angles)[:, None, :]
    sine_part = jnp.sin(angles)[:, None, :]
    first_half = vectors[..., :half_width]
    second = vectors[..., half_width:]
    return jnp.concatenate(
        [first_half * cosine - second * sine_part, second * cosine + first_half * sine_part],
        axis=-1,
    )


def rms_norm(values):
    return values * lax.rsqrt(jnp.mean(values * values, axis=-1, keepdims=True) + EPSILON)


def attend(hidden, own_lengths, sink_rows, window_rows, qkv_weight, out_weight):
    normed = rms_norm(hidden.astype(jnp.float32)).astype(jnp.bfloat16)
    projected = jnp.einsum("rd,dthe->rthe", normed, qkv_weight, preferred_element_type=jnp.float32)
    query_rot = rotate(projected[:, 0], own_lengths).astype(jnp.bfloat16)
    fresh_key = rotate(projected[:, 1], own_lengths).astype(jnp.bfloat16)
    fresh_value = projected[:, 2].astype(jnp.bfloat16)
    sink_count = sink_rows.shape[3]
    window_count = window_rows.shape[3]
    root_size = math.sqrt(query_rot.shape[-1])
    sink_scores = (
        jnp.einsum(
            "rhe,rhse->rhs", query_rot, sink_rows[:, :, 0], preferred_element_type=jnp.float32
        )
        / root_size
    )
    window_scores = (
        jnp.einsum(
            "rhe,rhwe->rhw", query_rot, window_rows[:, :, 0], preferred_element_type=jnp.float32
        )
        / root_size
    )
    self_scores = (
        jnp.einsum("rhe,rhe->rh", query_rot, fresh_key, preferred_element_type=jnp.float32)
        / root_size
    )
    length_limit = own_lengths[:, None, None]
    sink_valid = jnp.arange(sink_count, dtype=jnp.int32)[None, None, :] < length_limit
    window_valid = (
        jnp.arange(window_count, dtype=jnp.int32)[None, None, :]
        >= sink_count + window_count - length_limit
    )
    sink_scores = jnp.where(sink_valid, sink_scores, -1e30)
    window_scores = jnp.where(window_valid, window_scores, -1e30)
    highest = jnp.maximum(
        jnp.maximum(jnp.max(sink_scores, axis=-1), jnp.max(window_scores, axis=-1)), self_scores
    )
    sink_exp = jnp.exp(sink_scores - highest[..., None])
    window_exp = jnp.exp(window_scores - highest[..., None])
    self_exp = jnp.exp(self_scores - highest)
    totals = jnp.sum(sink_exp, axis=-1) + jnp.sum(window_exp, axis=-1) + self_exp
    sink_prob = (sink_exp / totals[..., None]).astype(jnp.bfloat16)
    window_prob = (window_exp / totals[..., None]).astype(jnp.bfloat16)
    self_prob = (self_exp / totals).astype(jnp.bfloat16)
    mixture = (
        jnp.einsum(
            "rhs,rhse->rhe", sink_prob, sink_rows[:, :, 1], preferred_element_type=jnp.float32
        )
        + jnp.einsum(
            "rhw,rhwe->rhe", window_prob, window_rows[:, :, 1], preferred_element_type=jnp.float32
        )
        + self_prob[..., None].astype(jnp.float32) * fresh_value.astype(jnp.float32)
    ).astype(jnp.bfloat16)
    return jnp.einsum("rhe,hed->rd", mixture, out_weight, preferred_element_type=jnp.float32)


def body(
    states,
    lengths,
    sink_cache,
    window_cache,
    qkv_weight,
    out_weight,
    expert_ids,
    route_weight,
    expert_in,
    expert_out,
    vocab_weight,
    guidance,
):
    hidden = states[0]
    request_count, width = hidden.shape
    group = lax.axis_size(ROWS)
    mp = lax.axis_size("mp")
    tokens = group * request_count

    partial_out = attend(hidden, lengths[0], sink_cache[0], window_cache[0], qkv_weight, out_weight)
    first = lax.axis_index("mp") == 0
    partial_out = partial_out + jnp.where(first, hidden.astype(jnp.float32), 0.0)
    partials = spread(partial_out.astype(jnp.bfloat16), ALL).reshape(group, mp, request_count, width)
    residual = jnp.sum(partials.astype(jnp.float32), axis=1).reshape(tokens, width).astype(jnp.bfloat16)
    moe_in = rms_norm(residual.astype(jnp.float32)).astype(jnp.bfloat16)

    unit_count = expert_in.shape[2]
    unit_start = lax.axis_index(ALL) * unit_count
    unit_expert = (unit_start + jnp.arange(unit_count, dtype=jnp.int32)) // FFE
    choice_rows = expert_ids.reshape(-1, expert_ids.shape[-1])
    route_rows = route_weight.reshape(-1, route_weight.shape[-1])
    coefficient = jnp.sum(
        jnp.where(
            choice_rows[:, :, None] == unit_expert[None, None, :], route_rows[:, :, None], 0.0
        ),
        axis=1,
    )
    gate = jnp.dot(moe_in, expert_in[0], preferred_element_type=jnp.float32)
    upward = jnp.dot(moe_in, expert_in[1], preferred_element_type=jnp.float32)
    activated = (jax.nn.silu(gate) * upward * coefficient).astype(jnp.bfloat16)
    expert_terms = jnp.dot(activated, expert_out, preferred_element_type=jnp.float32).astype(jnp.bfloat16)

    share = vocab_weight.shape[0]
    sent = jnp.swapaxes(expert_terms.reshape(tokens, group, share), 0, 1)
    expert_part = jnp.sum(trade(sent, ROWS).astype(jnp.float32), axis=0)
    expert_total = jnp.sum(spread(expert_part.astype(jnp.bfloat16), "mp").astype(jnp.float32), axis=0)
    own_columns = lax.dynamic_slice_in_dim(residual, lax.axis_index(ROWS) * share, share, 1)
    summed = own_columns.astype(jnp.float32) + expert_total

    squares = jnp.sum(summed * summed, axis=-1)
    notes = spread(jnp.concatenate([squares, guidance]), ROWS)
    scale = lax.rsqrt(jnp.sum(notes[:, :tokens], axis=0) / width + EPSILON).reshape(2, -1, 1)
    weight = notes[: group // 2, tokens:].reshape(-1, 1)

    raw = jnp.dot(summed.astype(jnp.bfloat16), vocab_weight, preferred_element_type=jnp.float32)
    raw = raw.reshape(2, tokens // 2, -1)
    mixed = raw[0] * (scale[0] * weight) + raw[1] * (scale[1] * (1.0 - weight))
    half_width = mixed.shape[1] // 2
    mixed = mixed.astype(jnp.bfloat16).reshape(group // 2, request_count, 2, half_width)
    sent = jnp.transpose(mixed, (2, 0, 1, 3)).reshape(group, request_count, half_width)
    guided = jnp.sum(trade(sent, ROWS).astype(jnp.float32), axis=0)
    return guided.reshape(request_count, 1, 1, half_width)


def solution(mesh):
    in_specs = (
        P("guide", "dp", None),
        P("guide", "dp"),
        P("guide", "dp", "mp", None, None, None),
        P("guide", "dp", "mp", None, None, None),
        P(None, None, "mp", None),
        P("mp", None, None),
        P(),
        P(),
        P(None, None, ("guide", "dp", "mp")),
        P(("guide", "dp", "mp"), None),
        P(("guide", "dp"), "mp"),
        P("dp"),
    )
    out_specs = P("dp", "mp", "guide", None)
    return jax.shard_map(body, mesh=mesh, in_specs=in_specs, out_specs=out_specs, check_vma=False)
```

```python
import math

import jax
import jax.numpy as jnp
from jax import lax
from jax.experimental import pallas as pl
from jax.experimental.pallas import tpu as pltpu
from jax.sharding import PartitionSpec as P

FFE = 1024

EPSILON = 1e-05

ROWS = ("guide", "dp")
ALL = ("guide", "dp", "mp")


def trade(blocks, axis):
    return lax.all_to_all(blocks, axis, 0, 0, tiled=True)


def spread(block, axis):
    return trade(jnp.broadcast_to(block[None], (lax.axis_size(axis),) + block.shape), axis)


def step(block, axis, bit):
    count = lax.axis_size(axis)
    return lax.ppermute(block, axis, [(i, i ^ bit) for i in range(count)])


F32 = jnp.float32
BF16 = jnp.bfloat16
VMEM = pl.BlockSpec(memory_space=pltpu.VMEM)
SMEM = pl.BlockSpec(memory_space=pltpu.SMEM)
ANY = pl.BlockSpec(memory_space=pl.ANY)
MEGA = 1 << 20
NOTE = 128


def dot(left, right):
    return jnp.dot(left, right, preferred_element_type=F32)


def iota(shape, dim):
    return lax.broadcasted_iota(jnp.int32, shape, dim)


def attend_kernel(
    heads, sinks, states, cosine, sine, lengths, sink, qkv_hbm, window_hbm, out_hbm, result,
    qkv, window, out_weight, qkv_sems, window_sems, out_sem,
):
    requests, width = states.shape
    size = cosine.shape[1]
    parts = 3 * heads
    lanes = size * parts
    blocks = width // size
    chunks = qkv_sems.shape[0]
    chunk_rows = qkv.shape[0] // chunks
    slots = window.shape[3]
    rows = heads * requests
    qkv_copies = [
        pltpu.make_async_copy(
            qkv_hbm.at[pl.ds(c * chunk_rows, chunk_rows)], qkv.at[pl.ds(c * chunk_rows, chunk_rows)], qkv_sems.at[c]
        )
        for c in range(chunks)
    ]
    window_copies = [
        pltpu.make_async_copy(window_hbm.at[r], window.at[r], window_sems.at[r]) for r in range(requests)
    ]
    out_copy = pltpu.make_async_copy(out_hbm, out_weight, out_sem)
    for copy in qkv_copies + window_copies + [out_copy]:
        copy.start()

    hidden = states[...].astype(F32)
    normed = hidden * lax.rsqrt(jnp.mean(hidden * hidden, axis=-1, keepdims=True) + EPSILON)
    stacked = jnp.concatenate([normed[:, b * size : (b + 1) * size] for b in range(blocks)], axis=0)
    sub, lane = iota((size, lanes), 0) * parts, iota((size, lanes), 1)
    repeat = jnp.where((lane >= sub) & (lane < sub + parts), 1.0, 0.0).astype(BF16)
    repeated = dot(stacked.astype(BF16), repeat)
    kind = lax.rem(iota((requests, lanes), 1), parts)
    projected = jnp.zeros((parts * requests, size), F32)
    for b in range(blocks):
        if b % (blocks // chunks) == 0:
            qkv_copies[b // (blocks // chunks)].wait()
        piece = repeated[b * requests : (b + 1) * requests]
        spread_out = jnp.concatenate([jnp.where(kind == p, piece, 0.0) for p in range(parts)], axis=0)
        projected = projected + dot(spread_out.astype(BF16), qkv[b * lanes : (b + 1) * lanes, :])

    cos_rows = jnp.concatenate([cosine[...]] * heads, axis=0)
    sin_rows = jnp.concatenate([sine[...]] * heads, axis=0)
    limit = jnp.concatenate([lengths[...]] * heads, axis=0)

    def turn(values):
        return (values * cos_rows + pltpu.roll(values, size // 2, 1) * sin_rows).astype(BF16)

    query = turn(projected[:rows])
    fresh_key = turn(projected[rows : 2 * rows])
    fresh_value = projected[2 * rows :].astype(BF16).astype(F32)
    root_size = math.sqrt(size)
    across = (((1,), (1,)), ((), ()))

    self_scores = jnp.sum(query.astype(F32) * fresh_key.astype(F32), axis=-1, keepdims=True) / root_size
    sink_rows = sink[...]
    sink_total = sink_rows.shape[0]
    sink_scores = lax.dot_general(query, sink_rows, across, preferred_element_type=F32) / root_size
    row_id, column = iota((rows, sink_total), 0), iota((rows, sink_total), 1)
    slot = lax.rem(column, 2 * sinks)
    pair = lax.div(column, 2 * sinks)
    sink_valid = (
        (lax.rem(pair, heads) == lax.div(row_id, requests))
        & (lax.div(pair, heads) == lax.rem(row_id, requests))
        & (slot < sinks)
        & (slot < limit)
    )
    sink_scores = jnp.where(sink_valid, sink_scores, -1e30)

    mine = iota((requests, slots), 0)
    scores = [jnp.zeros((requests, slots), F32) for h in range(heads)]
    for r in range(requests):
        window_copies[r].wait()
        for h in range(heads):
            found = lax.dot_general(
                query[h * requests : (h + 1) * requests], window[r, h, 0], across, preferred_element_type=F32
            )
            scores[h] = jnp.where(mine == r, found, scores[h])
    scores = jnp.concatenate(scores, axis=0) / root_size
    valid = iota((rows, slots), 1) >= sinks + slots - limit
    scores = jnp.where(valid, scores, -1e30)

    highest = jnp.maximum(
        jnp.maximum(jnp.max(scores, axis=-1, keepdims=True), jnp.max(sink_scores, axis=-1, keepdims=True)),
        self_scores,
    )
    window_exp = jnp.exp(scores - highest)
    sink_exp = jnp.where(sink_valid, jnp.exp(sink_scores - highest), 0.0)
    self_exp = jnp.exp(self_scores - highest)
    total = jnp.sum(window_exp, axis=-1, keepdims=True) + jnp.sum(sink_exp, axis=-1, keepdims=True) + self_exp
    window_weight = (window_exp / total).astype(BF16).astype(F32)
    sink_weight = pltpu.roll(sink_exp / total, sinks, 1).astype(BF16)
    self_weight = (self_exp / total).astype(BF16).astype(F32)
    mixture = dot(sink_weight, sink_rows) + self_weight * fresh_value
    mixed = []
    for h in range(heads):
        own = window_weight[h * requests : (h + 1) * requests]
        found = mixture[h * requests : (h + 1) * requests]
        for r in range(requests):
            found = found + dot(jnp.where(mine == r, own, 0.0).astype(BF16), window[r, h, 1])
        mixed.append(found)
    out_copy.wait()
    result[...] = dot(jnp.concatenate(mixed, axis=1).astype(BF16), out_weight[...]).astype(result.dtype)


def attend_fast(hidden, own_lengths, sink_rows, window_rows, qkv_weight, out_weight):
    requests, width = hidden.shape
    heads, sinks, size = sink_rows.shape[1], sink_rows.shape[3], sink_rows.shape[4]
    half = size // 2
    inverse = jnp.exp(jnp.arange(half, dtype=F32) * (-2.0 * math.log(10000.0) / size))
    angles = own_lengths.astype(F32)[:, None] * inverse[None, :]
    cosine, sine = jnp.cos(angles), jnp.sin(angles)
    qkv = qkv_weight.reshape(-1, size)
    out = out_weight.reshape(-1, width)
    return pl.pallas_call(
        lambda *refs: attend_kernel(heads, sinks, *refs),
        out_shape=jax.ShapeDtypeStruct((requests, width), BF16),
        in_specs=[VMEM] * 5 + [ANY] * 3,
        out_specs=VMEM,
        scratch_shapes=[
            pltpu.VMEM(qkv.shape, BF16),
            pltpu.VMEM(window_rows.shape, BF16),
            pltpu.VMEM(out.shape, BF16),
            pltpu.SemaphoreType.DMA((4,)),
            pltpu.SemaphoreType.DMA((requests,)),
            pltpu.SemaphoreType.DMA,
        ],
        compiler_params=pltpu.CompilerParams(vmem_limit_bytes=24 * MEGA),
        name="attend",
    )(
        hidden,
        jnp.concatenate([cosine, cosine], axis=-1),
        jnp.concatenate([-sine, sine], axis=-1),
        own_lengths[:, None],
        sink_rows.reshape(-1, size),
        qkv,
        window_rows,
        out,
    )


def expert_kernel(
    chunk, place, near, far, ids, route, in_hbm, out_hbm, terms, own_columns,
    rows_scr, act, w_in, w_out, in_sems, out_sems,
):
    width = near.shape[1]
    group, tokens, share = terms.shape
    requests = tokens // group
    units = act.shape[1]
    chunks = units // chunk
    in_copies = [
        pltpu.make_async_copy(
            in_hbm.at[:, :, pl.ds(c * chunk, chunk)], w_in.at[:, :, pl.ds(c * chunk, chunk)], in_sems.at[c]
        )
        for c in range(chunks)
    ]
    out_copies = [
        pltpu.make_async_copy(
            out_hbm.at[:, pl.ds(j * share, share)], w_out.at[:, pl.ds(j * share, share)], out_sems.at[j]
        )
        for j in range(group)
    ]
    for copy in in_copies + out_copies:
        copy.start()
    own = place[0]
    half = group // 2
    for first, source in ((0, near), (half, far)):
        values = source[...].astype(F32)
        for i in range(half):
            start = pl.multiple_of((own ^ (first + i)) * requests, requests)
            rows_scr[pl.ds(start, requests), :] = values[i * requests : (i + 1) * requests]
    own_columns[...] = rows_scr[:, pl.ds(pl.multiple_of(own * share, share), share)]
    rows = rows_scr[...]
    moe_in = (rows * lax.rsqrt(jnp.mean(rows * rows, axis=-1, keepdims=True) + EPSILON)).astype(BF16)
    for c in range(chunks):
        expert = place[1] + c * chunk // FFE
        factor = jnp.sum(jnp.where(ids[...] == expert, route[...], 0.0), axis=-1, keepdims=True)
        in_copies[c].wait()
        columns = slice(c * chunk, (c + 1) * chunk)
        gate = dot(moe_in, w_in[0, :, columns])
        upward = dot(moe_in, w_in[1, :, columns])
        act[:, columns] = (gate / (1.0 + jnp.exp(-gate)) * upward * factor).astype(BF16)
    for j in range(group):
        out_copies[j].wait()
        terms[j] = dot(act[...], w_out[:, j * share : (j + 1) * share]).astype(BF16)


def experts_fast(near, far, expert_ids, route_weight, expert_in, expert_out, share):
    width = near.shape[1]
    group = lax.axis_size(ROWS)
    tokens = 2 * near.shape[0]
    units = expert_in.shape[2]
    chunk = min(512, units)
    top = expert_ids.shape[-1]
    place = jnp.stack([lax.axis_index(ROWS), lax.axis_index(ALL) * units // FFE]).astype(jnp.int32)
    return pl.pallas_call(
        lambda *refs: expert_kernel(chunk, *refs),
        out_shape=(
            jax.ShapeDtypeStruct((group, tokens, share), BF16),
            jax.ShapeDtypeStruct((tokens, share), F32),
        ),
        in_specs=[SMEM] + [VMEM] * 4 + [ANY] * 2,
        out_specs=(VMEM, VMEM),
        scratch_shapes=[
            pltpu.VMEM((tokens, width), F32),
            pltpu.VMEM((tokens, units), BF16),
            pltpu.VMEM(expert_in.shape, BF16),
            pltpu.VMEM(expert_out.shape, BF16),
            pltpu.SemaphoreType.DMA((units // chunk,)),
            pltpu.SemaphoreType.DMA((group,)),
        ],
        compiler_params=pltpu.CompilerParams(vmem_limit_bytes=36 * MEGA),
        name="experts",
    )(place, near, far, expert_ids.reshape(-1, top), route_weight.reshape(-1, top), expert_in, expert_out)


def sum_kernel(blocks, result):
    total = blocks[0].astype(F32)
    for j in range(1, blocks.shape[0]):
        total = total + blocks[j].astype(F32)
    result[...] = total.astype(result.dtype)


def sum_fast(blocks):
    return pl.pallas_call(
        sum_kernel,
        out_shape=jax.ShapeDtypeStruct(blocks.shape[1:], BF16),
        in_specs=[VMEM],
        out_specs=VMEM,
        name="add_up",
    )(blocks)


def head_kernel(chunk, own_columns, left, right, weight, sent):
    tokens = own_columns.shape[0]
    group, rows, _ = sent.shape
    requests = rows // 2
    half_width = weight.shape[1] // 2
    per_half = half_width // chunk
    summed = own_columns[...] + (left[...].astype(F32) + right[...].astype(F32))

    def hand_out(values, guide, start):
        for d in range(group // 2):
            sent[guide * (group // 2) + d, :, start : start + values.shape[1]] = jnp.concatenate(
                [values[d * requests : (d + 1) * requests], values[tokens // 2 + d * requests : tokens // 2 + (d + 1) * requests]],
                axis=0,
            ).astype(BF16)

    squares = jnp.broadcast_to(jnp.sum(summed * summed, axis=-1, keepdims=True), (tokens, NOTE))
    raw_in = summed.astype(BF16)
    for guide in range(2):
        hand_out(squares, guide, half_width)
        for c in range(per_half):
            first = (guide * per_half + c) * chunk
            hand_out(dot(raw_in, weight[:, first : first + chunk]), guide, c * chunk)


def head_fast(own_columns, left, right, weight, group):
    tokens = own_columns.shape[0]
    half_width = weight.shape[1] // 2
    return pl.pallas_call(
        lambda *refs: head_kernel(256, *refs),
        out_shape=jax.ShapeDtypeStruct((group, 2 * (tokens // group), half_width + NOTE), BF16),
        in_specs=[VMEM] * 4,
        out_specs=VMEM,
        compiler_params=pltpu.CompilerParams(vmem_limit_bytes=16 * MEGA),
        name="head",
    )(own_columns, left, right, weight)


def guide_kernel(width, blocks, weight, result):
    requests, half_width = result.shape
    total = blocks[0].astype(F32)
    for j in range(1, blocks.shape[0]):
        total = total + blocks[j].astype(F32)
    scale = lax.rsqrt(total[:, half_width : half_width + 1] / width + EPSILON)
    factor = weight[...]
    result[...] = total[:requests, :half_width] * (scale[:requests] * factor) + total[requests:, :half_width] * (
        scale[requests:] * (1.0 - factor)
    )


def guide_fast(blocks, guidance, width):
    return pl.pallas_call(
        lambda *refs: guide_kernel(width, *refs),
        out_shape=jax.ShapeDtypeStruct((blocks.shape[1] // 2, blocks.shape[2] - NOTE), F32),
        in_specs=[VMEM, VMEM],
        out_specs=VMEM,
        name="guide",
    )(blocks, guidance[:, None])


def fits(hidden, sink_rows, expert_in, vocab_weight):
    return (
        lax.axis_size(ROWS) == 8
        and lax.axis_size("mp") == 4
        and hidden.shape[0] == 8
        and sink_rows.shape[1] == 4
        and expert_in.shape[2] % 512 == 0
        and vocab_weight.shape[0] % 128 == 0
        and vocab_weight.shape[1] % 512 == 0
    )


def fast_body(
    states,
    lengths,
    sink_cache,
    window_cache,
    qkv_weight,
    out_weight,
    expert_ids,
    route_weight,
    expert_in,
    expert_out,
    vocab_weight,
    guidance,
):
    hidden = states[0]
    partial_out = attend_fast(hidden, lengths[0], sink_cache[0], window_cache[0], qkv_weight, out_weight)
    received = step(partial_out, "mp", 1)
    pair = (partial_out.astype(F32) + received.astype(F32)).astype(BF16)
    received = step(pair, "mp", 2)
    residual = (hidden.astype(F32) + (pair.astype(F32) + received.astype(F32))).astype(BF16)
    pair = jnp.concatenate([residual, step(residual, ROWS, 1)], axis=0)
    near = jnp.concatenate([pair, step(pair, ROWS, 2)], axis=0)
    far = step(near, ROWS, 4)
    terms, own_columns = experts_fast(
        near, far, expert_ids, route_weight, expert_in, expert_out, vocab_weight.shape[0]
    )
    part = sum_fast(trade(terms, ROWS))
    received = step(part, "mp", 1)
    pair = (part.astype(F32) + received.astype(F32)).astype(BF16)
    received = step(pair, "mp", 2)
    sent = head_fast(own_columns, pair, received, vocab_weight, lax.axis_size(ROWS))
    guided = guide_fast(trade(sent, ROWS), guidance, hidden.shape[1])
    return guided.reshape(guided.shape[0], 1, 1, guided.shape[1])


def rotate(vectors, positions):
    full_width = vectors.shape[-1]
    half_width = full_width // 2
    step_index = jnp.arange(half_width, dtype=jnp.float32)
    inverse = jnp.exp(step_index * (-2.0 * math.log(10000.0) / full_width))
    angles = positions.astype(jnp.float32)[:, None] * inverse[None, :]
    cosine = jnp.cos(angles)[:, None, :]
    sine_part = jnp.sin(angles)[:, None, :]
    first_half = vectors[..., :half_width]
    second = vectors[..., half_width:]
    return jnp.concatenate(
        [first_half * cosine - second * sine_part, second * cosine + first_half * sine_part],
        axis=-1,
    )


def rms_norm(values):
    return values * lax.rsqrt(jnp.mean(values * values, axis=-1, keepdims=True) + EPSILON)


def attend(hidden, own_lengths, sink_rows, window_rows, qkv_weight, out_weight):
    normed = rms_norm(hidden.astype(jnp.float32)).astype(jnp.bfloat16)
    projected = jnp.einsum("rd,dthe->rthe", normed, qkv_weight, preferred_element_type=jnp.float32)
    query_rot = rotate(projected[:, 0], own_lengths).astype(jnp.bfloat16)
    fresh_key = rotate(projected[:, 1], own_lengths).astype(jnp.bfloat16)
    fresh_value = projected[:, 2].astype(jnp.bfloat16)
    sink_count = sink_rows.shape[3]
    window_count = window_rows.shape[3]
    root_size = math.sqrt(query_rot.shape[-1])
    sink_scores = (
        jnp.einsum(
            "rhe,rhse->rhs", query_rot, sink_rows[:, :, 0], preferred_element_type=jnp.float32
        )
        / root_size
    )
    window_scores = (
        jnp.einsum(
            "rhe,rhwe->rhw", query_rot, window_rows[:, :, 0], preferred_element_type=jnp.float32
        )
        / root_size
    )
    self_scores = (
        jnp.einsum("rhe,rhe->rh", query_rot, fresh_key, preferred_element_type=jnp.float32)
        / root_size
    )
    length_limit = own_lengths[:, None, None]
    sink_valid = jnp.arange(sink_count, dtype=jnp.int32)[None, None, :] < length_limit
    window_valid = (
        jnp.arange(window_count, dtype=jnp.int32)[None, None, :]
        >= sink_count + window_count - length_limit
    )
    sink_scores = jnp.where(sink_valid, sink_scores, -1e30)
    window_scores = jnp.where(window_valid, window_scores, -1e30)
    highest = jnp.maximum(
        jnp.maximum(jnp.max(sink_scores, axis=-1), jnp.max(window_scores, axis=-1)), self_scores
    )
    sink_exp = jnp.exp(sink_scores - highest[..., None])
    window_exp = jnp.exp(window_scores - highest[..., None])
    self_exp = jnp.exp(self_scores - highest)
    totals = jnp.sum(sink_exp, axis=-1) + jnp.sum(window_exp, axis=-1) + self_exp
    sink_prob = (sink_exp / totals[..., None]).astype(jnp.bfloat16)
    window_prob = (window_exp / totals[..., None]).astype(jnp.bfloat16)
    self_prob = (self_exp / totals).astype(jnp.bfloat16)
    mixture = (
        jnp.einsum(
            "rhs,rhse->rhe", sink_prob, sink_rows[:, :, 1], preferred_element_type=jnp.float32
        )
        + jnp.einsum(
            "rhw,rhwe->rhe", window_prob, window_rows[:, :, 1], preferred_element_type=jnp.float32
        )
        + self_prob[..., None].astype(jnp.float32) * fresh_value.astype(jnp.float32)
    ).astype(jnp.bfloat16)
    return jnp.einsum("rhe,hed->rd", mixture, out_weight, preferred_element_type=jnp.float32)


def body(
    states,
    lengths,
    sink_cache,
    window_cache,
    qkv_weight,
    out_weight,
    expert_ids,
    route_weight,
    expert_in,
    expert_out,
    vocab_weight,
    guidance,
):
    hidden = states[0]
    if fits(hidden, sink_cache[0], expert_in, vocab_weight):
        return fast_body(
            states,
            lengths,
            sink_cache,
            window_cache,
            qkv_weight,
            out_weight,
            expert_ids,
            route_weight,
            expert_in,
            expert_out,
            vocab_weight,
            guidance,
        )
    request_count, width = hidden.shape
    group = lax.axis_size(ROWS)
    mp = lax.axis_size("mp")
    tokens = group * request_count

    partial_out = attend(hidden, lengths[0], sink_cache[0], window_cache[0], qkv_weight, out_weight)
    first = lax.axis_index("mp") == 0
    partial_out = partial_out + jnp.where(first, hidden.astype(jnp.float32), 0.0)
    partials = spread(partial_out.astype(jnp.bfloat16), ALL).reshape(group, mp, request_count, width)
    residual = jnp.sum(partials.astype(jnp.float32), axis=1).reshape(tokens, width).astype(jnp.bfloat16)
    moe_in = rms_norm(residual.astype(jnp.float32)).astype(jnp.bfloat16)

    unit_count = expert_in.shape[2]
    unit_start = lax.axis_index(ALL) * unit_count
    unit_expert = (unit_start + jnp.arange(unit_count, dtype=jnp.int32)) // FFE
    choice_rows = expert_ids.reshape(-1, expert_ids.shape[-1])
    route_rows = route_weight.reshape(-1, route_weight.shape[-1])
    coefficient = jnp.sum(
        jnp.where(
            choice_rows[:, :, None] == unit_expert[None, None, :], route_rows[:, :, None], 0.0
        ),
        axis=1,
    )
    gate = jnp.dot(moe_in, expert_in[0], preferred_element_type=jnp.float32)
    upward = jnp.dot(moe_in, expert_in[1], preferred_element_type=jnp.float32)
    activated = (jax.nn.silu(gate) * upward * coefficient).astype(jnp.bfloat16)
    expert_terms = jnp.dot(activated, expert_out, preferred_element_type=jnp.float32).astype(jnp.bfloat16)

    share = vocab_weight.shape[0]
    sent = jnp.swapaxes(expert_terms.reshape(tokens, group, share), 0, 1)
    expert_part = jnp.sum(trade(sent, ROWS).astype(jnp.float32), axis=0)
    expert_total = jnp.sum(spread(expert_part.astype(jnp.bfloat16), "mp").astype(jnp.float32), axis=0)
    own_columns = lax.dynamic_slice_in_dim(residual, lax.axis_index(ROWS) * share, share, 1)
    summed = own_columns.astype(jnp.float32) + expert_total

    squares = jnp.sum(summed * summed, axis=-1)
    notes = spread(jnp.concatenate([squares, guidance]), ROWS)
    scale = lax.rsqrt(jnp.sum(notes[:, :tokens], axis=0) / width + EPSILON).reshape(2, -1, 1)
    weight = notes[: group // 2, tokens:].reshape(-1, 1)

    raw = jnp.dot(summed.astype(jnp.bfloat16), vocab_weight, preferred_element_type=jnp.float32)
    raw = raw.reshape(2, tokens // 2, -1)
    mixed = raw[0] * (scale[0] * weight) + raw[1] * (scale[1] * (1.0 - weight))
    half_width = mixed.shape[1] // 2
    mixed = mixed.astype(jnp.bfloat16).reshape(group // 2, request_count, 2, half_width)
    sent = jnp.transpose(mixed, (2, 0, 1, 3)).reshape(group, request_count, half_width)
    guided = jnp.sum(trade(sent, ROWS).astype(jnp.float32), axis=0)
    return guided.reshape(request_count, 1, 1, half_width)


def solution(mesh):
    in_specs = (
        P("guide", "dp", None),
        P("guide", "dp"),
        P("guide", "dp", "mp", None, None, None),
        P("guide", "dp", "mp", None, None, None),
        P(None, None, "mp", None),
        P("mp", None, None),
        P(),
        P(),
        P(None, None, ("guide", "dp", "mp")),
        P(("guide", "dp", "mp"), None),
        P(("guide", "dp"), "mp"),
        P("dp"),
    )
    out_specs = P("dp", "mp", "guide", None)
    return jax.shard_map(body, mesh=mesh, in_specs=in_specs, out_specs=out_specs, check_vma=False)
```

```python
import math

import jax
import jax.numpy as jnp
from jax import lax
from jax.experimental import pallas as pl
from jax.experimental.pallas import tpu as pltpu
from jax.sharding import PartitionSpec as P

FFE = 1024

EPSILON = 1e-05

ROWS = ("guide", "dp")
ALL = ("guide", "dp", "mp")


def trade(blocks, axis):
    return lax.all_to_all(blocks, axis, 0, 0, tiled=True)


def spread(block, axis):
    return trade(jnp.broadcast_to(block[None], (lax.axis_size(axis),) + block.shape), axis)


def step(block, axis, bit):
    count = lax.axis_size(axis)
    return lax.ppermute(block, axis, [(i, i ^ bit) for i in range(count)])


F32 = jnp.float32
BF16 = jnp.bfloat16
VMEM = pl.BlockSpec(memory_space=pltpu.VMEM)
SMEM = pl.BlockSpec(memory_space=pltpu.SMEM)
HBM = pl.BlockSpec(memory_space=pltpu.HBM)
MEGA = 1 << 20
NOTE = 128


def dot(left, right):
    return jnp.dot(left, right, preferred_element_type=F32)


def iota(shape, dim):
    return lax.broadcasted_iota(jnp.int32, shape, dim)


def attend_kernel(
    heads, sinks, states_hbm, lengths_hbm, sink_hbm, qkv_hbm, window_hbm, out_hbm, result,
    states, lengths, sink, qkv, window, out_weight, first_sems, qkv_sems, window_sems, out_sem,
):
    requests, width = states.shape
    size = sink.shape[1]
    parts = 3 * heads
    lanes = size * parts
    blocks = width // size
    chunks = qkv_sems.shape[0]
    chunk_rows = qkv.shape[0] // chunks
    slots = window.shape[3]
    rows = heads * requests
    qkv_copies = [
        pltpu.make_async_copy(
            qkv_hbm.at[pl.ds(c * chunk_rows, chunk_rows)], qkv.at[pl.ds(c * chunk_rows, chunk_rows)], qkv_sems.at[c]
        )
        for c in range(chunks)
    ]
    window_copies = [
        pltpu.make_async_copy(window_hbm.at[r], window.at[r], window_sems.at[r]) for r in range(requests)
    ]
    out_copy = pltpu.make_async_copy(out_hbm, out_weight, out_sem)
    first_copies = [
        pltpu.make_async_copy(source, target, first_sems.at[i])
        for i, (source, target) in enumerate(((states_hbm, states), (lengths_hbm, lengths), (sink_hbm, sink)))
    ]
    for copy in first_copies + qkv_copies + window_copies + [out_copy]:
        copy.start()
    for copy in first_copies:
        copy.wait()

    length_row = jnp.broadcast_to(lengths[...], (requests, requests))
    diagonal = iota((requests, requests), 0) == iota((requests, requests), 1)
    length = jnp.sum(jnp.where(diagonal, length_row, 0), axis=-1, keepdims=True)
    lane_id = iota((requests, size), 1)
    low = lane_id < size // 2
    pair_index = jnp.where(low, lane_id, lane_id - size // 2).astype(F32)
    angles = length.astype(F32) * jnp.exp(pair_index * (-2.0 * math.log(10000.0) / size))
    cosine, sine = jnp.cos(angles), jnp.sin(angles)
    sine = jnp.where(low, -sine, sine)

    hidden = states[...].astype(F32)
    normed = hidden * lax.rsqrt(jnp.mean(hidden * hidden, axis=-1, keepdims=True) + EPSILON)
    stacked = jnp.concatenate([normed[:, b * size : (b + 1) * size] for b in range(blocks)], axis=0)
    sub, lane = iota((size, lanes), 0) * parts, iota((size, lanes), 1)
    repeat = jnp.where((lane >= sub) & (lane < sub + parts), 1.0, 0.0).astype(BF16)
    repeated = dot(stacked.astype(BF16), repeat)
    kind = lax.rem(iota((requests, lanes), 1), parts)
    projected = jnp.zeros((parts * requests, size), F32)
    for b in range(blocks):
        if b % (blocks // chunks) == 0:
            qkv_copies[b // (blocks // chunks)].wait()
        piece = repeated[b * requests : (b + 1) * requests]
        spread_out = jnp.concatenate([jnp.where(kind == p, piece, 0.0) for p in range(parts)], axis=0)
        projected = projected + dot(spread_out.astype(BF16), qkv[b * lanes : (b + 1) * lanes, :])

    cos_rows = jnp.concatenate([cosine] * heads, axis=0)
    sin_rows = jnp.concatenate([sine] * heads, axis=0)
    limit = jnp.concatenate([length] * heads, axis=0)

    def turn(values):
        return (values * cos_rows + pltpu.roll(values, size // 2, 1) * sin_rows).astype(BF16)

    query = turn(projected[:rows])
    fresh_key = turn(projected[rows : 2 * rows])
    fresh_value = projected[2 * rows :].astype(BF16).astype(F32)
    root_size = math.sqrt(size)
    across = (((1,), (1,)), ((), ()))

    self_scores = jnp.sum(query.astype(F32) * fresh_key.astype(F32), axis=-1, keepdims=True) / root_size
    sink_rows = sink[...]
    sink_total = sink_rows.shape[0]
    sink_scores = lax.dot_general(query, sink_rows, across, preferred_element_type=F32) / root_size
    row_id, column = iota((rows, sink_total), 0), iota((rows, sink_total), 1)
    slot = lax.rem(column, 2 * sinks)
    pair = lax.div(column, 2 * sinks)
    sink_valid = (
        (lax.rem(pair, heads) == lax.div(row_id, requests))
        & (lax.div(pair, heads) == lax.rem(row_id, requests))
        & (slot < sinks)
        & (slot < limit)
    )
    sink_scores = jnp.where(sink_valid, sink_scores, -1e30)

    mine = iota((requests, slots), 0)
    scores = [jnp.zeros((requests, slots), F32) for h in range(heads)]
    for r in range(requests):
        window_copies[r].wait()
        for h in range(heads):
            found = lax.dot_general(
                query[h * requests : (h + 1) * requests], window[r, h, 0], across, preferred_element_type=F32
            )
            scores[h] = jnp.where(mine == r, found, scores[h])
    scores = jnp.concatenate(scores, axis=0) / root_size
    valid = iota((rows, slots), 1) >= sinks + slots - limit
    scores = jnp.where(valid, scores, -1e30)

    highest = jnp.maximum(
        jnp.maximum(jnp.max(scores, axis=-1, keepdims=True), jnp.max(sink_scores, axis=-1, keepdims=True)),
        self_scores,
    )
    window_exp = jnp.exp(scores - highest)
    sink_exp = jnp.where(sink_valid, jnp.exp(sink_scores - highest), 0.0)
    self_exp = jnp.exp(self_scores - highest)
    total = jnp.sum(window_exp, axis=-1, keepdims=True) + jnp.sum(sink_exp, axis=-1, keepdims=True) + self_exp
    window_weight = (window_exp / total).astype(BF16).astype(F32)
    sink_weight = pltpu.roll(sink_exp / total, sinks, 1).astype(BF16)
    self_weight = (self_exp / total).astype(BF16).astype(F32)
    mixture = dot(sink_weight, sink_rows) + self_weight * fresh_value
    mixed = []
    for h in range(heads):
        own = window_weight[h * requests : (h + 1) * requests]
        found = mixture[h * requests : (h + 1) * requests]
        for r in range(requests):
            found = found + dot(jnp.where(mine == r, own, 0.0).astype(BF16), window[r, h, 1])
        mixed.append(found)
    out_copy.wait()
    result[...] = dot(jnp.concatenate(mixed, axis=1).astype(BF16), out_weight[...]).astype(result.dtype)


def attend_fast(hidden, own_lengths, sink_rows, window_rows, qkv_weight, out_weight):
    requests, width = hidden.shape
    heads, sinks, size = sink_rows.shape[1], sink_rows.shape[3], sink_rows.shape[4]
    qkv = qkv_weight.reshape(-1, size)
    out = out_weight.reshape(-1, width)
    return pl.pallas_call(
        lambda *refs: attend_kernel(heads, sinks, *refs),
        out_shape=jax.ShapeDtypeStruct((requests, width), BF16),
        in_specs=[HBM] * 6,
        out_specs=VMEM,
        scratch_shapes=[
            pltpu.VMEM(hidden.shape, BF16),
            pltpu.VMEM((1, requests), jnp.int32),
            pltpu.VMEM((sink_rows.size // size, size), BF16),
            pltpu.VMEM(qkv.shape, BF16),
            pltpu.VMEM(window_rows.shape, BF16),
            pltpu.VMEM(out.shape, BF16),
            pltpu.SemaphoreType.DMA((3,)),
            pltpu.SemaphoreType.DMA((4,)),
            pltpu.SemaphoreType.DMA((requests,)),
            pltpu.SemaphoreType.DMA,
        ],
        compiler_params=pltpu.CompilerParams(vmem_limit_bytes=24 * MEGA),
        name="attend",
    )(
        hidden,
        own_lengths[None, :],
        sink_rows.reshape(-1, size),
        qkv,
        window_rows,
        out,
    )


def expert_kernel(
    chunk, place, near, far, ids_hbm, route_hbm, in_hbm, out_hbm, terms, own_columns,
    rows_scr, act, ids, route, w_in, w_out, small_sems, in_sems, out_sems,
):
    width = near.shape[1]
    group, tokens, share = terms.shape
    requests = tokens // group
    units = act.shape[1]
    chunks = units // chunk
    in_copies = [
        pltpu.make_async_copy(
            in_hbm.at[:, :, pl.ds(c * chunk, chunk)], w_in.at[:, :, pl.ds(c * chunk, chunk)], in_sems.at[c]
        )
        for c in range(chunks)
    ]
    out_copies = [
        pltpu.make_async_copy(
            out_hbm.at[:, pl.ds(j * share, share)], w_out.at[:, pl.ds(j * share, share)], out_sems.at[j]
        )
        for j in range(group)
    ]
    small_copies = [
        pltpu.make_async_copy(ids_hbm, ids, small_sems.at[0]),
        pltpu.make_async_copy(route_hbm, route, small_sems.at[1]),
    ]
    for copy in small_copies + in_copies + out_copies:
        copy.start()
    own = place[0]
    half = group // 2
    for first, source in ((0, near), (half, far)):
        values = source[...].astype(F32)
        for i in range(half):
            start = pl.multiple_of((own ^ (first + i)) * requests, requests)
            rows_scr[pl.ds(start, requests), :] = values[i * requests : (i + 1) * requests]
    own_columns[...] = rows_scr[:, pl.ds(pl.multiple_of(own * share, share), share)]
    rows = rows_scr[...]
    moe_in = (rows * lax.rsqrt(jnp.mean(rows * rows, axis=-1, keepdims=True) + EPSILON)).astype(BF16)
    for copy in small_copies:
        copy.wait()
    per_stream = ids.shape[2]
    diagonal = iota((per_stream, per_stream), 0) == iota((per_stream, per_stream), 1)

    def factor_of(expert):
        columns = []
        for stream in range(2):
            row = jnp.sum(jnp.where(ids[stream] == expert, route[stream], 0.0), axis=0, keepdims=True)
            spread_out = jnp.broadcast_to(row, (per_stream, per_stream))
            columns.append(jnp.sum(jnp.where(diagonal, spread_out, 0.0), axis=-1, keepdims=True))
        return jnp.concatenate(columns, axis=0)

    for c in range(chunks):
        factor = factor_of(place[1] + c * chunk // FFE)
        in_copies[c].wait()
        columns = slice(c * chunk, (c + 1) * chunk)
        gate = dot(moe_in, w_in[0, :, columns])
        upward = dot(moe_in, w_in[1, :, columns])
        act[:, columns] = (gate / (1.0 + jnp.exp(-gate)) * upward * factor).astype(BF16)
    for j in range(group):
        out_copies[j].wait()
        terms[j] = dot(act[...], w_out[:, j * share : (j + 1) * share]).astype(BF16)


def experts_fast(near, far, expert_ids, route_weight, expert_in, expert_out, share):
    width = near.shape[1]
    group = lax.axis_size(ROWS)
    tokens = 2 * near.shape[0]
    units = expert_in.shape[2]
    chunk = min(512, units)
    top = expert_ids.shape[-1]
    place = jnp.stack([lax.axis_index(ROWS), lax.axis_index(ALL) * units // FFE]).astype(jnp.int32)
    return pl.pallas_call(
        lambda *refs: expert_kernel(chunk, *refs),
        out_shape=(
            jax.ShapeDtypeStruct((group, tokens, share), BF16),
            jax.ShapeDtypeStruct((tokens, share), F32),
        ),
        in_specs=[SMEM] + [VMEM] * 2 + [HBM] * 4,
        out_specs=(VMEM, VMEM),
        scratch_shapes=[
            pltpu.VMEM((tokens, width), F32),
            pltpu.VMEM((tokens, units), BF16),
            pltpu.VMEM((2, top, tokens // 2), jnp.int32),
            pltpu.VMEM((2, top, tokens // 2), F32),
            pltpu.VMEM(expert_in.shape, BF16),
            pltpu.VMEM(expert_out.shape, BF16),
            pltpu.SemaphoreType.DMA((2,)),
            pltpu.SemaphoreType.DMA((units // chunk,)),
            pltpu.SemaphoreType.DMA((group,)),
        ],
        compiler_params=pltpu.CompilerParams(vmem_limit_bytes=36 * MEGA),
        name="experts",
    )(place, near, far, jnp.swapaxes(expert_ids, 1, 2), jnp.swapaxes(route_weight, 1, 2), expert_in, expert_out)


def sum_kernel(blocks, result):
    total = blocks[0].astype(F32)
    for j in range(1, blocks.shape[0]):
        total = total + blocks[j].astype(F32)
    result[...] = total.astype(result.dtype)


def sum_fast(blocks):
    return pl.pallas_call(
        sum_kernel,
        out_shape=jax.ShapeDtypeStruct(blocks.shape[1:], BF16),
        in_specs=[VMEM],
        out_specs=VMEM,
        compiler_params=pltpu.CompilerParams(vmem_limit_bytes=8 * MEGA),
        name="add_up",
    )(blocks)


def head_kernel(chunk, own_columns, left, right, weight, sent):
    tokens = own_columns.shape[0]
    group, rows, _ = sent.shape
    requests = rows // 2
    half_width = weight.shape[1] // 2
    per_half = half_width // chunk
    summed = own_columns[...] + (left[...].astype(F32) + right[...].astype(F32))

    def hand_out(values, guide, start):
        for d in range(group // 2):
            sent[guide * (group // 2) + d, :, start : start + values.shape[1]] = jnp.concatenate(
                [values[d * requests : (d + 1) * requests], values[tokens // 2 + d * requests : tokens // 2 + (d + 1) * requests]],
                axis=0,
            ).astype(BF16)

    squares = jnp.broadcast_to(jnp.sum(summed * summed, axis=-1, keepdims=True), (tokens, NOTE))
    raw_in = summed.astype(BF16)
    for guide in range(2):
        hand_out(squares, guide, half_width)
        for c in range(per_half):
            first = (guide * per_half + c) * chunk
            hand_out(dot(raw_in, weight[:, first : first + chunk]), guide, c * chunk)


def head_fast(own_columns, left, right, weight, group):
    tokens = own_columns.shape[0]
    half_width = weight.shape[1] // 2
    return pl.pallas_call(
        lambda *refs: head_kernel(256, *refs),
        out_shape=jax.ShapeDtypeStruct((group, 2 * (tokens // group), half_width + NOTE), BF16),
        in_specs=[VMEM] * 4,
        out_specs=VMEM,
        compiler_params=pltpu.CompilerParams(vmem_limit_bytes=16 * MEGA),
        name="head",
    )(own_columns, left, right, weight)


def guide_kernel(width, blocks, weight, result):
    requests, half_width = result.shape[0], result.shape[3]
    total = blocks[0].astype(F32)
    for j in range(1, blocks.shape[0]):
        total = total + blocks[j].astype(F32)
    scale = lax.rsqrt(total[:, half_width : half_width + 1] / width + EPSILON)
    diagonal = iota((requests, requests), 0) == iota((requests, requests), 1)
    guidance = jnp.broadcast_to(weight[...], (requests, requests))
    factor = jnp.sum(jnp.where(diagonal, guidance, 0.0), axis=-1, keepdims=True)
    guided = total[:requests, :half_width] * (scale[:requests] * factor) + total[requests:, :half_width] * (
        scale[requests:] * (1.0 - factor)
    )
    for r in range(requests):
        result[r, 0] = guided[r : r + 1]


def guide_fast(blocks, guidance, width):
    return pl.pallas_call(
        lambda *refs: guide_kernel(width, *refs),
        out_shape=jax.ShapeDtypeStruct((blocks.shape[1] // 2, 1, 1, blocks.shape[2] - NOTE), F32),
        in_specs=[VMEM, VMEM],
        out_specs=VMEM,
        compiler_params=pltpu.CompilerParams(vmem_limit_bytes=12 * MEGA),
        name="guide",
    )(blocks, guidance[None, :])


def fits(hidden, sink_rows, expert_in, vocab_weight):
    return (
        lax.axis_size(ROWS) == 8
        and lax.axis_size("mp") == 4
        and hidden.shape[0] == 8
        and sink_rows.shape[1] == 4
        and expert_in.shape[2] % 512 == 0
        and vocab_weight.shape[0] % 128 == 0
        and vocab_weight.shape[1] % 512 == 0
    )


def fast_body(
    states,
    lengths,
    sink_cache,
    window_cache,
    qkv_weight,
    out_weight,
    expert_ids,
    route_weight,
    expert_in,
    expert_out,
    vocab_weight,
    guidance,
):
    hidden = states[0]
    partial_out = attend_fast(hidden, lengths[0], sink_cache[0], window_cache[0], qkv_weight, out_weight)
    received = step(partial_out, "mp", 1)
    pair = (partial_out.astype(F32) + received.astype(F32)).astype(BF16)
    received = step(pair, "mp", 2)
    residual = (hidden.astype(F32) + (pair.astype(F32) + received.astype(F32))).astype(BF16)
    pair = jnp.concatenate([residual, step(residual, ROWS, 1)], axis=0)
    near = jnp.concatenate([pair, step(pair, ROWS, 2)], axis=0)
    far = step(near, ROWS, 4)
    terms, own_columns = experts_fast(
        near, far, expert_ids, route_weight, expert_in, expert_out, vocab_weight.shape[0]
    )
    part = sum_fast(trade(terms, ROWS))
    received = step(part, "mp", 1)
    pair = (part.astype(F32) + received.astype(F32)).astype(BF16)
    received = step(pair, "mp", 2)
    sent = head_fast(own_columns, pair, received, vocab_weight, lax.axis_size(ROWS))
    return guide_fast(trade(sent, ROWS), guidance, hidden.shape[1])


def rotate(vectors, positions):
    full_width = vectors.shape[-1]
    half_width = full_width // 2
    step_index = jnp.arange(half_width, dtype=jnp.float32)
    inverse = jnp.exp(step_index * (-2.0 * math.log(10000.0) / full_width))
    angles = positions.astype(jnp.float32)[:, None] * inverse[None, :]
    cosine = jnp.cos(angles)[:, None, :]
    sine_part = jnp.sin(angles)[:, None, :]
    first_half = vectors[..., :half_width]
    second = vectors[..., half_width:]
    return jnp.concatenate(
        [first_half * cosine - second * sine_part, second * cosine + first_half * sine_part],
        axis=-1,
    )


def rms_norm(values):
    return values * lax.rsqrt(jnp.mean(values * values, axis=-1, keepdims=True) + EPSILON)


def attend(hidden, own_lengths, sink_rows, window_rows, qkv_weight, out_weight):
    normed = rms_norm(hidden.astype(jnp.float32)).astype(jnp.bfloat16)
    projected = jnp.einsum("rd,dthe->rthe", normed, qkv_weight, preferred_element_type=jnp.float32)
    query_rot = rotate(projected[:, 0], own_lengths).astype(jnp.bfloat16)
    fresh_key = rotate(projected[:, 1], own_lengths).astype(jnp.bfloat16)
    fresh_value = projected[:, 2].astype(jnp.bfloat16)
    sink_count = sink_rows.shape[3]
    window_count = window_rows.shape[3]
    root_size = math.sqrt(query_rot.shape[-1])
    sink_scores = (
        jnp.einsum(
            "rhe,rhse->rhs", query_rot, sink_rows[:, :, 0], preferred_element_type=jnp.float32
        )
        / root_size
    )
    window_scores = (
        jnp.einsum(
            "rhe,rhwe->rhw", query_rot, window_rows[:, :, 0], preferred_element_type=jnp.float32
        )
        / root_size
    )
    self_scores = (
        jnp.einsum("rhe,rhe->rh", query_rot, fresh_key, preferred_element_type=jnp.float32)
        / root_size
    )
    length_limit = own_lengths[:, None, None]
    sink_valid = jnp.arange(sink_count, dtype=jnp.int32)[None, None, :] < length_limit
    window_valid = (
        jnp.arange(window_count, dtype=jnp.int32)[None, None, :]
        >= sink_count + window_count - length_limit
    )
    sink_scores = jnp.where(sink_valid, sink_scores, -1e30)
    window_scores = jnp.where(window_valid, window_scores, -1e30)
    highest = jnp.maximum(
        jnp.maximum(jnp.max(sink_scores, axis=-1), jnp.max(window_scores, axis=-1)), self_scores
    )
    sink_exp = jnp.exp(sink_scores - highest[..., None])
    window_exp = jnp.exp(window_scores - highest[..., None])
    self_exp = jnp.exp(self_scores - highest)
    totals = jnp.sum(sink_exp, axis=-1) + jnp.sum(window_exp, axis=-1) + self_exp
    sink_prob = (sink_exp / totals[..., None]).astype(jnp.bfloat16)
    window_prob = (window_exp / totals[..., None]).astype(jnp.bfloat16)
    self_prob = (self_exp / totals).astype(jnp.bfloat16)
    mixture = (
        jnp.einsum(
            "rhs,rhse->rhe", sink_prob, sink_rows[:, :, 1], preferred_element_type=jnp.float32
        )
        + jnp.einsum(
            "rhw,rhwe->rhe", window_prob, window_rows[:, :, 1], preferred_element_type=jnp.float32
        )
        + self_prob[..., None].astype(jnp.float32) * fresh_value.astype(jnp.float32)
    ).astype(jnp.bfloat16)
    return jnp.einsum("rhe,hed->rd", mixture, out_weight, preferred_element_type=jnp.float32)


def body(
    states,
    lengths,
    sink_cache,
    window_cache,
    qkv_weight,
    out_weight,
    expert_ids,
    route_weight,
    expert_in,
    expert_out,
    vocab_weight,
    guidance,
):
    hidden = states[0]
    if fits(hidden, sink_cache[0], expert_in, vocab_weight):
        return fast_body(
            states,
            lengths,
            sink_cache,
            window_cache,
            qkv_weight,
            out_weight,
            expert_ids,
            route_weight,
            expert_in,
            expert_out,
            vocab_weight,
            guidance,
        )
    request_count, width = hidden.shape
    group = lax.axis_size(ROWS)
    mp = lax.axis_size("mp")
    tokens = group * request_count

    partial_out = attend(hidden, lengths[0], sink_cache[0], window_cache[0], qkv_weight, out_weight)
    first = lax.axis_index("mp") == 0
    partial_out = partial_out + jnp.where(first, hidden.astype(jnp.float32), 0.0)
    partials = spread(partial_out.astype(jnp.bfloat16), ALL).reshape(group, mp, request_count, width)
    residual = jnp.sum(partials.astype(jnp.float32), axis=1).reshape(tokens, width).astype(jnp.bfloat16)
    moe_in = rms_norm(residual.astype(jnp.float32)).astype(jnp.bfloat16)

    unit_count = expert_in.shape[2]
    unit_start = lax.axis_index(ALL) * unit_count
    unit_expert = (unit_start + jnp.arange(unit_count, dtype=jnp.int32)) // FFE
    choice_rows = expert_ids.reshape(-1, expert_ids.shape[-1])
    route_rows = route_weight.reshape(-1, route_weight.shape[-1])
    coefficient = jnp.sum(
        jnp.where(
            choice_rows[:, :, None] == unit_expert[None, None, :], route_rows[:, :, None], 0.0
        ),
        axis=1,
    )
    gate = jnp.dot(moe_in, expert_in[0], preferred_element_type=jnp.float32)
    upward = jnp.dot(moe_in, expert_in[1], preferred_element_type=jnp.float32)
    activated = (jax.nn.silu(gate) * upward * coefficient).astype(jnp.bfloat16)
    expert_terms = jnp.dot(activated, expert_out, preferred_element_type=jnp.float32).astype(jnp.bfloat16)

    share = vocab_weight.shape[0]
    sent = jnp.swapaxes(expert_terms.reshape(tokens, group, share), 0, 1)
    expert_part = jnp.sum(trade(sent, ROWS).astype(jnp.float32), axis=0)
    expert_total = jnp.sum(spread(expert_part.astype(jnp.bfloat16), "mp").astype(jnp.float32), axis=0)
    own_columns = lax.dynamic_slice_in_dim(residual, lax.axis_index(ROWS) * share, share, 1)
    summed = own_columns.astype(jnp.float32) + expert_total

    squares = jnp.sum(summed * summed, axis=-1)
    notes = spread(jnp.concatenate([squares, guidance]), ROWS)
    scale = lax.rsqrt(jnp.sum(notes[:, :tokens], axis=0) / width + EPSILON).reshape(2, -1, 1)
    weight = notes[: group // 2, tokens:].reshape(-1, 1)

    raw = jnp.dot(summed.astype(jnp.bfloat16), vocab_weight, preferred_element_type=jnp.float32)
    raw = raw.reshape(2, tokens // 2, -1)
    mixed = raw[0] * (scale[0] * weight) + raw[1] * (scale[1] * (1.0 - weight))
    half_width = mixed.shape[1] // 2
    mixed = mixed.astype(jnp.bfloat16).reshape(group // 2, request_count, 2, half_width)
    sent = jnp.transpose(mixed, (2, 0, 1, 3)).reshape(group, request_count, half_width)
    guided = jnp.sum(trade(sent, ROWS).astype(jnp.float32), axis=0)
    return guided.reshape(request_count, 1, 1, half_width)


def solution(mesh):
    in_specs = (
        P("guide", "dp", None),
        P("guide", "dp"),
        P("guide", "dp", "mp", None, None, None),
        P("guide", "dp", "mp", None, None, None),
        P(None, None, "mp", None),
        P("mp", None, None),
        P(),
        P(),
        P(None, None, ("guide", "dp", "mp")),
        P(("guide", "dp", "mp"), None),
        P(("guide", "dp"), "mp"),
        P("dp"),
    )
    out_specs = P("dp", "mp", "guide", None)
    return jax.shard_map(body, mesh=mesh, in_specs=in_specs, out_specs=out_specs, check_vma=False)
```

```python
import math

import jax
import jax.numpy as jnp
from jax import lax
from jax.experimental import pallas as pl
from jax.experimental.pallas import tpu as pltpu
from jax.sharding import PartitionSpec as P

FFE = 1024

EPSILON = 1e-05

ROWS = ("guide", "dp")
ALL = ("guide", "dp", "mp")


def trade(blocks, axis):
    return lax.all_to_all(blocks, axis, 0, 0, tiled=True)


def spread(block, axis):
    return trade(jnp.broadcast_to(block[None], (lax.axis_size(axis),) + block.shape), axis)


def step(block, axis, bit):
    count = lax.axis_size(axis)
    return lax.ppermute(block, axis, [(i, i ^ bit) for i in range(count)])


def swap(blocks, axis):
    return [blocks[0]] + [step(blocks[j], axis, j) for j in range(1, lax.axis_size(axis))]


F32 = jnp.float32
BF16 = jnp.bfloat16
VMEM = pl.BlockSpec(memory_space=pltpu.VMEM)
SMEM = pl.BlockSpec(memory_space=pltpu.SMEM)
HBM = pl.BlockSpec(memory_space=pltpu.HBM)
MEGA = 1 << 20
NOTE = 128


def dot(left, right):
    return jnp.dot(left, right, preferred_element_type=F32)


def iota(shape, dim):
    return lax.broadcasted_iota(jnp.int32, shape, dim)


def attend_kernel(
    heads, sinks, states_hbm, lengths_hbm, sink_hbm, qkv_hbm, window_hbm, out_hbm, result,
    states, lengths, sink, qkv, window, out_weight, first_sems, qkv_sems, window_sems, out_sem,
):
    requests, width = states.shape
    size = sink.shape[1]
    parts = 3 * heads
    lanes = size * parts
    blocks = width // size
    chunks = qkv_sems.shape[0]
    chunk_rows = qkv.shape[0] // chunks
    slots = window.shape[3]
    rows = heads * requests
    qkv_copies = [
        pltpu.make_async_copy(
            qkv_hbm.at[pl.ds(c * chunk_rows, chunk_rows)], qkv.at[pl.ds(c * chunk_rows, chunk_rows)], qkv_sems.at[c]
        )
        for c in range(chunks)
    ]
    window_copies = [
        pltpu.make_async_copy(window_hbm.at[r], window.at[r], window_sems.at[r]) for r in range(requests)
    ]
    out_copy = pltpu.make_async_copy(out_hbm, out_weight, out_sem)
    first_copies = [
        pltpu.make_async_copy(source, target, first_sems.at[i])
        for i, (source, target) in enumerate(((states_hbm, states), (lengths_hbm, lengths), (sink_hbm, sink)))
    ]
    for copy in first_copies + qkv_copies + window_copies + [out_copy]:
        copy.start()
    for copy in first_copies:
        copy.wait()

    length_row = jnp.broadcast_to(lengths[...], (requests, requests))
    diagonal = iota((requests, requests), 0) == iota((requests, requests), 1)
    length = jnp.sum(jnp.where(diagonal, length_row, 0), axis=-1, keepdims=True)
    lane_id = iota((requests, size), 1)
    low = lane_id < size // 2
    pair_index = jnp.where(low, lane_id, lane_id - size // 2).astype(F32)
    angles = length.astype(F32) * jnp.exp(pair_index * (-2.0 * math.log(10000.0) / size))
    cosine, sine = jnp.cos(angles), jnp.sin(angles)
    sine = jnp.where(low, -sine, sine)

    hidden = states[...].astype(F32)
    normed = hidden * lax.rsqrt(jnp.mean(hidden * hidden, axis=-1, keepdims=True) + EPSILON)
    stacked = jnp.concatenate([normed[:, b * size : (b + 1) * size] for b in range(blocks)], axis=0)
    sub, lane = iota((size, lanes), 0) * parts, iota((size, lanes), 1)
    repeat = jnp.where((lane >= sub) & (lane < sub + parts), 1.0, 0.0).astype(BF16)
    repeated = dot(stacked.astype(BF16), repeat)
    kind = lax.rem(iota((requests, lanes), 1), parts)
    projected = jnp.zeros((parts * requests, size), F32)
    for b in range(blocks):
        if b % (blocks // chunks) == 0:
            qkv_copies[b // (blocks // chunks)].wait()
        piece = repeated[b * requests : (b + 1) * requests]
        spread_out = jnp.concatenate([jnp.where(kind == p, piece, 0.0) for p in range(parts)], axis=0)
        projected = projected + dot(spread_out.astype(BF16), qkv[b * lanes : (b + 1) * lanes, :])

    cos_rows = jnp.concatenate([cosine] * heads, axis=0)
    sin_rows = jnp.concatenate([sine] * heads, axis=0)
    limit = jnp.concatenate([length] * heads, axis=0)

    def turn(values):
        return (values * cos_rows + pltpu.roll(values, size // 2, 1) * sin_rows).astype(BF16)

    query = turn(projected[:rows])
    fresh_key = turn(projected[rows : 2 * rows])
    fresh_value = projected[2 * rows :].astype(BF16).astype(F32)
    root_size = math.sqrt(size)
    across = (((1,), (1,)), ((), ()))

    self_scores = jnp.sum(query.astype(F32) * fresh_key.astype(F32), axis=-1, keepdims=True) / root_size
    sink_rows = sink[...]
    sink_total = sink_rows.shape[0]
    sink_scores = lax.dot_general(query, sink_rows, across, preferred_element_type=F32) / root_size
    row_id, column = iota((rows, sink_total), 0), iota((rows, sink_total), 1)
    slot = lax.rem(column, 2 * sinks)
    pair = lax.div(column, 2 * sinks)
    sink_valid = (
        (lax.rem(pair, heads) == lax.div(row_id, requests))
        & (lax.div(pair, heads) == lax.rem(row_id, requests))
        & (slot < sinks)
        & (slot < limit)
    )
    sink_scores = jnp.where(sink_valid, sink_scores, -1e30)

    mine = iota((requests, slots), 0)
    scores = [jnp.zeros((requests, slots), F32) for h in range(heads)]
    for r in range(requests):
        window_copies[r].wait()
        for h in range(heads):
            found = lax.dot_general(
                query[h * requests : (h + 1) * requests], window[r, h, 0], across, preferred_element_type=F32
            )
            scores[h] = jnp.where(mine == r, found, scores[h])
    scores = jnp.concatenate(scores, axis=0) / root_size
    valid = iota((rows, slots), 1) >= sinks + slots - limit
    scores = jnp.where(valid, scores, -1e30)

    highest = jnp.maximum(
        jnp.maximum(jnp.max(scores, axis=-1, keepdims=True), jnp.max(sink_scores, axis=-1, keepdims=True)),
        self_scores,
    )
    window_exp = jnp.exp(scores - highest)
    sink_exp = jnp.where(sink_valid, jnp.exp(sink_scores - highest), 0.0)
    self_exp = jnp.exp(self_scores - highest)
    total = jnp.sum(window_exp, axis=-1, keepdims=True) + jnp.sum(sink_exp, axis=-1, keepdims=True) + self_exp
    window_weight = (window_exp / total).astype(BF16).astype(F32)
    sink_weight = pltpu.roll(sink_exp / total, sinks, 1).astype(BF16)
    self_weight = (self_exp / total).astype(BF16).astype(F32)
    mixture = dot(sink_weight, sink_rows) + self_weight * fresh_value
    mixed = []
    for h in range(heads):
        own = window_weight[h * requests : (h + 1) * requests]
        found = mixture[h * requests : (h + 1) * requests]
        for r in range(requests):
            found = found + dot(jnp.where(mine == r, own, 0.0).astype(BF16), window[r, h, 1])
        mixed.append(found)
    out_copy.wait()
    result[...] = dot(jnp.concatenate(mixed, axis=1).astype(BF16), out_weight[...]).astype(result.dtype)


def attend_fast(hidden, own_lengths, sink_rows, window_rows, qkv_weight, out_weight):
    requests, width = hidden.shape
    heads, sinks, size = sink_rows.shape[1], sink_rows.shape[3], sink_rows.shape[4]
    qkv = qkv_weight.reshape(-1, size)
    out = out_weight.reshape(-1, width)
    return pl.pallas_call(
        lambda *refs: attend_kernel(heads, sinks, *refs),
        out_shape=jax.ShapeDtypeStruct((requests, width), BF16),
        in_specs=[HBM] * 6,
        out_specs=VMEM,
        scratch_shapes=[
            pltpu.VMEM(hidden.shape, BF16),
            pltpu.VMEM((1, requests), jnp.int32),
            pltpu.VMEM((sink_rows.size // size, size), BF16),
            pltpu.VMEM(qkv.shape, BF16),
            pltpu.VMEM(window_rows.shape, BF16),
            pltpu.VMEM(out.shape, BF16),
            pltpu.SemaphoreType.DMA((3,)),
            pltpu.SemaphoreType.DMA((4,)),
            pltpu.SemaphoreType.DMA((requests,)),
            pltpu.SemaphoreType.DMA,
        ],
        compiler_params=pltpu.CompilerParams(vmem_limit_bytes=60 * MEGA),
        name="attend",
    )(
        hidden,
        own_lengths[None, :],
        sink_rows.reshape(-1, size),
        qkv,
        window_rows,
        out,
    )


def expert_kernel(
    group, chunk, place, *refs
):
    blocks, refs = refs[:group], refs[group:]
    ids_hbm, route_hbm, in_hbm, out_hbm = refs[:4]
    terms, refs = refs[4 : 4 + group], refs[4 + group :]
    own_columns, rows_scr, act, ids, route, w_in, w_out, small_sems, in_sems, out_sems = refs
    requests = blocks[0].shape[0]
    tokens, share = terms[0].shape
    units = act.shape[1]
    chunks = units // chunk
    in_copies = [
        pltpu.make_async_copy(
            in_hbm.at[:, :, pl.ds(c * chunk, chunk)], w_in.at[:, :, pl.ds(c * chunk, chunk)], in_sems.at[c]
        )
        for c in range(chunks)
    ]
    out_copies = [
        pltpu.make_async_copy(
            out_hbm.at[:, pl.ds(pl.multiple_of((place[0] ^ j) * share, share), share)],
            w_out.at[:, pl.ds(j * share, share)],
            out_sems.at[j],
        )
        for j in range(group)
    ]
    small_copies = [
        pltpu.make_async_copy(ids_hbm, ids, small_sems.at[0]),
        pltpu.make_async_copy(route_hbm, route, small_sems.at[1]),
    ]
    for copy in small_copies + in_copies + out_copies:
        copy.start()
    own = place[0]
    for j in range(group):
        start = pl.multiple_of((own ^ j) * requests, requests)
        rows_scr[pl.ds(start, requests), :] = blocks[j][...].astype(F32)
    own_columns[...] = rows_scr[:, pl.ds(pl.multiple_of(own * share, share), share)]
    rows = rows_scr[...]
    moe_in = (rows * lax.rsqrt(jnp.mean(rows * rows, axis=-1, keepdims=True) + EPSILON)).astype(BF16)
    for copy in small_copies:
        copy.wait()
    per_stream = ids.shape[2]
    diagonal = iota((per_stream, per_stream), 0) == iota((per_stream, per_stream), 1)

    def factor_of(expert):
        columns = []
        for stream in range(2):
            row = jnp.sum(jnp.where(ids[stream] == expert, route[stream], 0.0), axis=0, keepdims=True)
            spread_out = jnp.broadcast_to(row, (per_stream, per_stream))
            columns.append(jnp.sum(jnp.where(diagonal, spread_out, 0.0), axis=-1, keepdims=True))
        return jnp.concatenate(columns, axis=0)

    for c in range(chunks):
        factor = factor_of(place[1] + c * chunk // FFE)
        in_copies[c].wait()
        columns = slice(c * chunk, (c + 1) * chunk)
        gate = dot(moe_in, w_in[0, :, columns])
        upward = dot(moe_in, w_in[1, :, columns])
        act[:, columns] = (gate / (1.0 + jnp.exp(-gate)) * upward * factor).astype(BF16)
    for j in range(group):
        out_copies[j].wait()
        terms[j][...] = dot(act[...], w_out[:, j * share : (j + 1) * share]).astype(BF16)


def experts_fast(blocks, expert_ids, route_weight, expert_in, expert_out, share):
    requests, width = blocks[0].shape
    group = len(blocks)
    tokens = group * requests
    units = expert_in.shape[2]
    chunk = min(512, units)
    top = expert_ids.shape[-1]
    place = jnp.stack([lax.axis_index(ROWS), lax.axis_index(ALL) * units // FFE]).astype(jnp.int32)
    *terms, own_columns = pl.pallas_call(
        lambda *refs: expert_kernel(group, chunk, *refs),
        out_shape=[jax.ShapeDtypeStruct((tokens, share), BF16)] * group
        + [jax.ShapeDtypeStruct((tokens, share), F32)],
        in_specs=[SMEM] + [VMEM] * group + [HBM] * 4,
        out_specs=[VMEM] * (group + 1),
        scratch_shapes=[
            pltpu.VMEM((tokens, width), F32),
            pltpu.VMEM((tokens, units), BF16),
            pltpu.VMEM((2, top, tokens // 2), jnp.int32),
            pltpu.VMEM((2, top, tokens // 2), F32),
            pltpu.VMEM(expert_in.shape, BF16),
            pltpu.VMEM(expert_out.shape, BF16),
            pltpu.SemaphoreType.DMA((2,)),
            pltpu.SemaphoreType.DMA((units // chunk,)),
            pltpu.SemaphoreType.DMA((group,)),
        ],
        compiler_params=pltpu.CompilerParams(vmem_limit_bytes=50 * MEGA),
        name="experts",
    )(place, *blocks, jnp.swapaxes(expert_ids, 1, 2), jnp.swapaxes(route_weight, 1, 2), expert_in, expert_out)
    return terms, own_columns


def add_up(blocks):
    total = blocks[0][...].astype(F32)
    for block in blocks[1:]:
        total = total + block[...].astype(F32)
    return total


def sum_kernel(*refs):
    refs[-1][...] = add_up(refs[:-1]).astype(BF16)


def sum_fast(blocks):
    return pl.pallas_call(
        sum_kernel,
        out_shape=jax.ShapeDtypeStruct(blocks[0].shape, BF16),
        in_specs=[VMEM] * len(blocks),
        out_specs=VMEM,
        compiler_params=pltpu.CompilerParams(vmem_limit_bytes=8 * MEGA),
        name="add_up",
    )(*blocks)


def head_kernel(chunk, place, own_columns, left, right, weight, near, far):
    tokens = own_columns.shape[0]
    count, rows, _ = near.shape
    requests = rows // 2
    half_width = weight.shape[1] // 2
    per_half = half_width // chunk
    guide, own = place[0], place[1]
    summed = own_columns[...] + (left[...].astype(F32) + right[...].astype(F32))

    def hand_out(values, target, start):
        for d in range(count):
            target[own ^ d, :, start : start + values.shape[1]] = jnp.concatenate(
                [values[d * requests : (d + 1) * requests], values[tokens // 2 + d * requests : tokens // 2 + (d + 1) * requests]],
                axis=0,
            ).astype(BF16)

    squares = jnp.broadcast_to(jnp.sum(summed * summed, axis=-1, keepdims=True), (tokens, NOTE))
    raw_in = summed.astype(BF16)
    for target, half in ((far, 1 - guide), (near, guide)):
        hand_out(squares, target, half_width)
        for c in range(per_half):
            first = pl.multiple_of(half * half_width + c * chunk, 128)
            hand_out(dot(raw_in, weight[:, pl.ds(first, chunk)]), target, c * chunk)


def head_fast(own_columns, left, right, weight):
    count = lax.axis_size("dp")
    tokens = own_columns.shape[0]
    half_width = weight.shape[1] // 2
    place = jnp.stack([lax.axis_index("guide"), lax.axis_index("dp")]).astype(jnp.int32)
    shape = jax.ShapeDtypeStruct((count, tokens // count, half_width + NOTE), BF16)
    return pl.pallas_call(
        lambda *refs: head_kernel(256, *refs),
        out_shape=[shape, shape],
        in_specs=[SMEM] + [VMEM] * 4,
        out_specs=[VMEM, VMEM],
        compiler_params=pltpu.CompilerParams(vmem_limit_bytes=16 * MEGA),
        name="head",
    )(place, own_columns, left, right, weight)


def pair_kernel(near, received, *results):
    for k, result in enumerate(results):
        result[...] = (near[k].astype(F32) + received[k].astype(F32)).astype(BF16)


def pair_fast(near, received):
    count = near.shape[0]
    return pl.pallas_call(
        pair_kernel,
        out_shape=[jax.ShapeDtypeStruct(near.shape[1:], BF16)] * count,
        in_specs=[VMEM, VMEM],
        out_specs=[VMEM] * count,
        compiler_params=pltpu.CompilerParams(vmem_limit_bytes=8 * MEGA),
        name="pair",
    )(near, received)


def guide_kernel(width, weight, *refs):
    result = refs[-1]
    requests, half_width = result.shape[0], result.shape[3]
    total = add_up(refs[:-1])
    scale = lax.rsqrt(total[:, half_width : half_width + 1] / width + EPSILON)
    diagonal = iota((requests, requests), 0) == iota((requests, requests), 1)
    guidance = jnp.broadcast_to(weight[...], (requests, requests))
    factor = jnp.sum(jnp.where(diagonal, guidance, 0.0), axis=-1, keepdims=True)
    guided = total[:requests, :half_width] * (scale[:requests] * factor) + total[requests:, :half_width] * (
        scale[requests:] * (1.0 - factor)
    )
    for r in range(requests):
        result[r, 0] = guided[r : r + 1]


def guide_fast(blocks, guidance, width):
    rows, columns = blocks[0].shape
    return pl.pallas_call(
        lambda *refs: guide_kernel(width, *refs),
        out_shape=jax.ShapeDtypeStruct((rows // 2, 1, 1, columns - NOTE), F32),
        in_specs=[VMEM] * (1 + len(blocks)),
        out_specs=VMEM,
        compiler_params=pltpu.CompilerParams(vmem_limit_bytes=12 * MEGA),
        name="guide",
    )(guidance[None, :], *blocks)


def fits(hidden, sink_rows, expert_in, vocab_weight):
    return (
        lax.axis_size(ROWS) == 8
        and lax.axis_size("mp") == 4
        and hidden.shape[0] == 8
        and sink_rows.shape[1] == 4
        and expert_in.shape[2] % 512 == 0
        and vocab_weight.shape[0] % 128 == 0
        and vocab_weight.shape[1] % 512 == 0
    )


def fast_body(
    states,
    lengths,
    sink_cache,
    window_cache,
    qkv_weight,
    out_weight,
    expert_ids,
    route_weight,
    expert_in,
    expert_out,
    vocab_weight,
    guidance,
):
    hidden = states[0]
    partial_out = attend_fast(hidden, lengths[0], sink_cache[0], window_cache[0], qkv_weight, out_weight)
    received = step(partial_out, "mp", 1)
    pair = (partial_out.astype(F32) + received.astype(F32)).astype(BF16)
    received = step(pair, "mp", 2)
    residual = (hidden.astype(F32) + (pair.astype(F32) + received.astype(F32))).astype(BF16)
    terms, own_columns = experts_fast(
        swap([residual] * lax.axis_size(ROWS), ROWS),
        expert_ids,
        route_weight,
        expert_in,
        expert_out,
        vocab_weight.shape[0],
    )
    part = sum_fast(swap(terms, ROWS))
    received = step(part, "mp", 1)
    pair = (part.astype(F32) + received.astype(F32)).astype(BF16)
    received = step(pair, "mp", 2)
    near, far = head_fast(own_columns, pair, received, vocab_weight)
    logits = swap(pair_fast(near, step(far, "guide", 1)), "dp")
    return guide_fast(logits, guidance, hidden.shape[1])


def rotate(vectors, positions):
    full_width = vectors.shape[-1]
    half_width = full_width // 2
    step_index = jnp.arange(half_width, dtype=jnp.float32)
    inverse = jnp.exp(step_index * (-2.0 * math.log(10000.0) / full_width))
    angles = positions.astype(jnp.float32)[:, None] * inverse[None, :]
    cosine = jnp.cos(angles)[:, None, :]
    sine_part = jnp.sin(angles)[:, None, :]
    first_half = vectors[..., :half_width]
    second = vectors[..., half_width:]
    return jnp.concatenate(
        [first_half * cosine - second * sine_part, second * cosine + first_half * sine_part],
        axis=-1,
    )


def rms_norm(values):
    return values * lax.rsqrt(jnp.mean(values * values, axis=-1, keepdims=True) + EPSILON)


def attend(hidden, own_lengths, sink_rows, window_rows, qkv_weight, out_weight):
    normed = rms_norm(hidden.astype(jnp.float32)).astype(jnp.bfloat16)
    projected = jnp.einsum("rd,dthe->rthe", normed, qkv_weight, preferred_element_type=jnp.float32)
    query_rot = rotate(projected[:, 0], own_lengths).astype(jnp.bfloat16)
    fresh_key = rotate(projected[:, 1], own_lengths).astype(jnp.bfloat16)
    fresh_value = projected[:, 2].astype(jnp.bfloat16)
    sink_count = sink_rows.shape[3]
    window_count = window_rows.shape[3]
    root_size = math.sqrt(query_rot.shape[-1])
    sink_scores = (
        jnp.einsum(
            "rhe,rhse->rhs", query_rot, sink_rows[:, :, 0], preferred_element_type=jnp.float32
        )
        / root_size
    )
    window_scores = (
        jnp.einsum(
            "rhe,rhwe->rhw", query_rot, window_rows[:, :, 0], preferred_element_type=jnp.float32
        )
        / root_size
    )
    self_scores = (
        jnp.einsum("rhe,rhe->rh", query_rot, fresh_key, preferred_element_type=jnp.float32)
        / root_size
    )
    length_limit = own_lengths[:, None, None]
    sink_valid = jnp.arange(sink_count, dtype=jnp.int32)[None, None, :] < length_limit
    window_valid = (
        jnp.arange(window_count, dtype=jnp.int32)[None, None, :]
        >= sink_count + window_count - length_limit
    )
    sink_scores = jnp.where(sink_valid, sink_scores, -1e30)
    window_scores = jnp.where(window_valid, window_scores, -1e30)
    highest = jnp.maximum(
        jnp.maximum(jnp.max(sink_scores, axis=-1), jnp.max(window_scores, axis=-1)), self_scores
    )
    sink_exp = jnp.exp(sink_scores - highest[..., None])
    window_exp = jnp.exp(window_scores - highest[..., None])
    self_exp = jnp.exp(self_scores - highest)
    totals = jnp.sum(sink_exp, axis=-1) + jnp.sum(window_exp, axis=-1) + self_exp
    sink_prob = (sink_exp / totals[..., None]).astype(jnp.bfloat16)
    window_prob = (window_exp / totals[..., None]).astype(jnp.bfloat16)
    self_prob = (self_exp / totals).astype(jnp.bfloat16)
    mixture = (
        jnp.einsum(
            "rhs,rhse->rhe", sink_prob, sink_rows[:, :, 1], preferred_element_type=jnp.float32
        )
        + jnp.einsum(
            "rhw,rhwe->rhe", window_prob, window_rows[:, :, 1], preferred_element_type=jnp.float32
        )
        + self_prob[..., None].astype(jnp.float32) * fresh_value.astype(jnp.float32)
    ).astype(jnp.bfloat16)
    return jnp.einsum("rhe,hed->rd", mixture, out_weight, preferred_element_type=jnp.float32)


def body(
    states,
    lengths,
    sink_cache,
    window_cache,
    qkv_weight,
    out_weight,
    expert_ids,
    route_weight,
    expert_in,
    expert_out,
    vocab_weight,
    guidance,
):
    hidden = states[0]
    if fits(hidden, sink_cache[0], expert_in, vocab_weight):
        return fast_body(
            states,
            lengths,
            sink_cache,
            window_cache,
            qkv_weight,
            out_weight,
            expert_ids,
            route_weight,
            expert_in,
            expert_out,
            vocab_weight,
            guidance,
        )
    request_count, width = hidden.shape
    group = lax.axis_size(ROWS)
    mp = lax.axis_size("mp")
    tokens = group * request_count

    partial_out = attend(hidden, lengths[0], sink_cache[0], window_cache[0], qkv_weight, out_weight)
    first = lax.axis_index("mp") == 0
    partial_out = partial_out + jnp.where(first, hidden.astype(jnp.float32), 0.0)
    partials = spread(partial_out.astype(jnp.bfloat16), ALL).reshape(group, mp, request_count, width)
    residual = jnp.sum(partials.astype(jnp.float32), axis=1).reshape(tokens, width).astype(jnp.bfloat16)
    moe_in = rms_norm(residual.astype(jnp.float32)).astype(jnp.bfloat16)

    unit_count = expert_in.shape[2]
    unit_start = lax.axis_index(ALL) * unit_count
    unit_expert = (unit_start + jnp.arange(unit_count, dtype=jnp.int32)) // FFE
    choice_rows = expert_ids.reshape(-1, expert_ids.shape[-1])
    route_rows = route_weight.reshape(-1, route_weight.shape[-1])
    coefficient = jnp.sum(
        jnp.where(
            choice_rows[:, :, None] == unit_expert[None, None, :], route_rows[:, :, None], 0.0
        ),
        axis=1,
    )
    gate = jnp.dot(moe_in, expert_in[0], preferred_element_type=jnp.float32)
    upward = jnp.dot(moe_in, expert_in[1], preferred_element_type=jnp.float32)
    activated = (jax.nn.silu(gate) * upward * coefficient).astype(jnp.bfloat16)
    expert_terms = jnp.dot(activated, expert_out, preferred_element_type=jnp.float32).astype(jnp.bfloat16)

    share = vocab_weight.shape[0]
    sent = jnp.swapaxes(expert_terms.reshape(tokens, group, share), 0, 1)
    expert_part = jnp.sum(trade(sent, ROWS).astype(jnp.float32), axis=0)
    expert_total = jnp.sum(spread(expert_part.astype(jnp.bfloat16), "mp").astype(jnp.float32), axis=0)
    own_columns = lax.dynamic_slice_in_dim(residual, lax.axis_index(ROWS) * share, share, 1)
    summed = own_columns.astype(jnp.float32) + expert_total

    squares = jnp.sum(summed * summed, axis=-1)
    notes = spread(jnp.concatenate([squares, guidance]), ROWS)
    scale = lax.rsqrt(jnp.sum(notes[:, :tokens], axis=0) / width + EPSILON).reshape(2, -1, 1)
    weight = notes[: group // 2, tokens:].reshape(-1, 1)

    raw = jnp.dot(summed.astype(jnp.bfloat16), vocab_weight, preferred_element_type=jnp.float32)
    raw = raw.reshape(2, tokens // 2, -1)
    mixed = raw[0] * (scale[0] * weight) + raw[1] * (scale[1] * (1.0 - weight))
    half_width = mixed.shape[1] // 2
    mixed = mixed.astype(jnp.bfloat16).reshape(group // 2, request_count, 2, half_width)
    sent = jnp.transpose(mixed, (2, 0, 1, 3)).reshape(group, request_count, half_width)
    guided = jnp.sum(trade(sent, ROWS).astype(jnp.float32), axis=0)
    return guided.reshape(request_count, 1, 1, half_width)


def solution(mesh):
    in_specs = (
        P("guide", "dp", None),
        P("guide", "dp"),
        P("guide", "dp", "mp", None, None, None),
        P("guide", "dp", "mp", None, None, None),
        P(None, None, "mp", None),
        P("mp", None, None),
        P(),
        P(),
        P(None, None, ("guide", "dp", "mp")),
        P(("guide", "dp", "mp"), None),
        P(("guide", "dp"), "mp"),
        P("dp"),
    )
    out_specs = P("dp", "mp", "guide", None)
    return jax.shard_map(body, mesh=mesh, in_specs=in_specs, out_specs=out_specs, check_vma=False)
```

```python
import math

import jax
import jax.numpy as jnp
from jax import lax
from jax.experimental import pallas as pl
from jax.experimental.pallas import tpu as pltpu
from jax.sharding import PartitionSpec as P

FFE = 1024

EPSILON = 1e-05

ROWS = ("guide", "dp")
ALL = ("guide", "dp", "mp")


def trade(blocks, axis):
    return lax.all_to_all(blocks, axis, 0, 0, tiled=True)


def spread(block, axis):
    return trade(jnp.broadcast_to(block[None], (lax.axis_size(axis),) + block.shape), axis)


def step(block, axis, bit):
    count = lax.axis_size(axis)
    return lax.ppermute(block, axis, [(i, i ^ bit) for i in range(count)])


def swap(blocks, axis):
    return [blocks[0]] + [step(blocks[j], axis, j) for j in range(1, lax.axis_size(axis))]


F32 = jnp.float32
BF16 = jnp.bfloat16
VMEM = pl.BlockSpec(memory_space=pltpu.VMEM)
SMEM = pl.BlockSpec(memory_space=pltpu.SMEM)
ANY = pl.BlockSpec(memory_space=pl.ANY)
HBM = pl.BlockSpec(memory_space=pltpu.HBM)
MEGA = 1 << 20
NOTE = 128


def dot(left, right):
    return jnp.dot(left, right, preferred_element_type=F32)


def iota(shape, dim):
    return lax.broadcasted_iota(jnp.int32, shape, dim)


def in_order(copies, ahead):
    state = [0, 0]

    def fill():
        while state[0] < min(len(copies), state[1] + ahead):
            copies[state[0]].start()
            state[0] += 1

    def wait():
        copies[state[1]].wait()
        state[1] += 1
        fill()

    fill()
    return wait


def load_kernel(chunk, index, hbm, after, result, sems):
    rows = hbm.shape[1] // sems.shape[1]
    copies = [
        pltpu.make_async_copy(
            hbm.at[k, pl.ds(i * rows, rows), pl.ds(index * chunk, chunk)],
            result.at[k, pl.ds(i * rows, rows), :],
            sems.at[k, i],
        )
        for k in range(hbm.shape[0])
        for i in range(sems.shape[1])
    ]
    for copy in copies:
        copy.start()
    for copy in copies:
        copy.wait()


def load_fast(weight, chunk, index, after):
    kinds, width, _ = weight.shape
    return pl.pallas_call(
        lambda *refs: load_kernel(chunk, index, *refs),
        out_shape=jax.ShapeDtypeStruct((kinds, width, chunk), BF16),
        in_specs=[HBM, ANY],
        out_specs=VMEM,
        scratch_shapes=[pltpu.SemaphoreType.DMA((kinds, 4))],
        compiler_params=pltpu.CompilerParams(vmem_limit_bytes=(47 - 4 * index) * MEGA),
        cost_estimate=pl.CostEstimate(flops=0, bytes_accessed=4 * kinds * width * chunk, transcendentals=0),
        name="load",
    )(weight, after)


def join_kernel(total, count, *refs):
    values = [ref[...].astype(F32) for ref in refs[:count]]
    joined = sum(values[1:], values[0]) if total else jnp.concatenate(values, axis=0)
    refs[-1][...] = joined.astype(BF16)


def join_fast(total, blocks, after):
    rows, columns = blocks[0].shape
    return pl.pallas_call(
        lambda *refs: join_kernel(total, len(blocks), *refs),
        out_shape=jax.ShapeDtypeStruct((rows if total else rows * len(blocks), columns), BF16),
        in_specs=[VMEM] * len(blocks) + [ANY],
        out_specs=VMEM,
        compiler_params=pltpu.CompilerParams(vmem_limit_bytes=4 * MEGA),
        name="join",
    )(*blocks, after)


def attend_kernel(
    heads, sinks, states_hbm, lengths_hbm, sink_hbm, qkv_hbm, window_hbm, out_hbm, result,
    states, lengths, sink, qkv, window, out_weight, first_sems, qkv_sems, window_sems, out_sem,
):
    requests, width = states.shape
    size = sink.shape[1]
    parts = 3 * heads
    lanes = size * parts
    blocks = width // size
    chunks = qkv_sems.shape[0]
    chunk_rows = qkv.shape[0] // chunks
    slots = window.shape[3]
    rows = heads * requests
    qkv_copies = [
        pltpu.make_async_copy(
            qkv_hbm.at[pl.ds(c * chunk_rows, chunk_rows)], qkv.at[pl.ds(c * chunk_rows, chunk_rows)], qkv_sems.at[c]
        )
        for c in range(chunks)
    ]
    key_copies, value_copies = [
        [
            pltpu.make_async_copy(window_hbm.at[r, :, k], window.at[r, :, k], window_sems.at[k, r])
            for r in range(requests)
        ]
        for k in range(2)
    ]
    out_copy = pltpu.make_async_copy(out_hbm, out_weight, out_sem)
    first_copies = [
        pltpu.make_async_copy(source, target, first_sems.at[i])
        for i, (source, target) in enumerate(((states_hbm, states), (lengths_hbm, lengths), (sink_hbm, sink)))
    ]
    wait = in_order(first_copies + qkv_copies + key_copies + value_copies + [out_copy], 6)
    for copy in first_copies:
        wait()

    length_row = jnp.broadcast_to(lengths[...], (requests, requests))
    diagonal = iota((requests, requests), 0) == iota((requests, requests), 1)
    length = jnp.sum(jnp.where(diagonal, length_row, 0), axis=-1, keepdims=True)
    lane_id = iota((requests, size), 1)
    low = lane_id < size // 2
    pair_index = jnp.where(low, lane_id, lane_id - size // 2).astype(F32)
    angles = length.astype(F32) * jnp.exp(pair_index * (-2.0 * math.log(10000.0) / size))
    cosine, sine = jnp.cos(angles), jnp.sin(angles)
    sine = jnp.where(low, -sine, sine)

    hidden = states[...].astype(F32)
    normed = hidden * lax.rsqrt(jnp.mean(hidden * hidden, axis=-1, keepdims=True) + EPSILON)
    stacked = jnp.concatenate([normed[:, b * size : (b + 1) * size] for b in range(blocks)], axis=0)
    sub, lane = iota((size, lanes), 0) * parts, iota((size, lanes), 1)
    repeat = jnp.where((lane >= sub) & (lane < sub + parts), 1.0, 0.0).astype(BF16)
    repeated = dot(stacked.astype(BF16), repeat)
    kind = lax.rem(iota((requests, lanes), 1), parts)
    projected = jnp.zeros((parts * requests, size), F32)
    for b in range(blocks):
        if b % (blocks // chunks) == 0:
            wait()
        piece = repeated[b * requests : (b + 1) * requests]
        spread_out = jnp.concatenate([jnp.where(kind == p, piece, 0.0) for p in range(parts)], axis=0)
        projected = projected + dot(spread_out.astype(BF16), qkv[b * lanes : (b + 1) * lanes, :])

    cos_rows = jnp.concatenate([cosine] * heads, axis=0)
    sin_rows = jnp.concatenate([sine] * heads, axis=0)
    limit = jnp.concatenate([length] * heads, axis=0)

    def turn(values):
        return (values * cos_rows + pltpu.roll(values, size // 2, 1) * sin_rows).astype(BF16)

    query = turn(projected[:rows])
    fresh_key = turn(projected[rows : 2 * rows])
    fresh_value = projected[2 * rows :].astype(BF16).astype(F32)
    root_size = math.sqrt(size)
    across = (((1,), (1,)), ((), ()))

    self_scores = jnp.sum(query.astype(F32) * fresh_key.astype(F32), axis=-1, keepdims=True) / root_size
    sink_rows = sink[...]
    sink_total = sink_rows.shape[0]
    sink_scores = lax.dot_general(query, sink_rows, across, preferred_element_type=F32) / root_size
    row_id, column = iota((rows, sink_total), 0), iota((rows, sink_total), 1)
    slot = lax.rem(column, 2 * sinks)
    pair = lax.div(column, 2 * sinks)
    sink_valid = (
        (lax.rem(pair, heads) == lax.div(row_id, requests))
        & (lax.div(pair, heads) == lax.rem(row_id, requests))
        & (slot < sinks)
        & (slot < limit)
    )
    sink_scores = jnp.where(sink_valid, sink_scores, -1e30)

    mine = iota((requests, slots), 0)
    scores = [jnp.zeros((requests, slots), F32) for h in range(heads)]
    for r in range(requests):
        wait()
        for h in range(heads):
            found = lax.dot_general(
                query[h * requests : (h + 1) * requests], window[r, h, 0], across, preferred_element_type=F32
            )
            scores[h] = jnp.where(mine == r, found, scores[h])
    scores = jnp.concatenate(scores, axis=0) / root_size
    valid = iota((rows, slots), 1) >= sinks + slots - limit
    scores = jnp.where(valid, scores, -1e30)

    highest = jnp.maximum(
        jnp.maximum(jnp.max(scores, axis=-1, keepdims=True), jnp.max(sink_scores, axis=-1, keepdims=True)),
        self_scores,
    )
    window_exp = jnp.exp(scores - highest)
    sink_exp = jnp.where(sink_valid, jnp.exp(sink_scores - highest), 0.0)
    self_exp = jnp.exp(self_scores - highest)
    total = jnp.sum(window_exp, axis=-1, keepdims=True) + jnp.sum(sink_exp, axis=-1, keepdims=True) + self_exp
    window_weight = (window_exp / total).astype(BF16).astype(F32)
    sink_weight = pltpu.roll(sink_exp / total, sinks, 1).astype(BF16)
    self_weight = (self_exp / total).astype(BF16).astype(F32)
    mixture = dot(sink_weight, sink_rows) + self_weight * fresh_value
    mixed = [mixture[h * requests : (h + 1) * requests] for h in range(heads)]
    for r in range(requests):
        wait()
        for h in range(heads):
            own = jnp.where(mine == r, window_weight[h * requests : (h + 1) * requests], 0.0)
            mixed[h] = mixed[h] + dot(own.astype(BF16), window[r, h, 1])
    wait()
    result[...] = dot(jnp.concatenate(mixed, axis=1).astype(BF16), out_weight[...]).astype(result.dtype)


def attend_fast(hidden, own_lengths, sink_rows, window_rows, qkv_weight, out_weight):
    requests, width = hidden.shape
    heads, sinks, size = sink_rows.shape[1], sink_rows.shape[3], sink_rows.shape[4]
    qkv = qkv_weight.reshape(-1, size)
    out = out_weight.reshape(-1, width)
    return pl.pallas_call(
        lambda *refs: attend_kernel(heads, sinks, *refs),
        out_shape=jax.ShapeDtypeStruct((requests, width), BF16),
        in_specs=[HBM] * 6,
        out_specs=VMEM,
        scratch_shapes=[
            pltpu.VMEM(hidden.shape, BF16),
            pltpu.VMEM((1, requests), jnp.int32),
            pltpu.VMEM((sink_rows.size // size, size), BF16),
            pltpu.VMEM(qkv.shape, BF16),
            pltpu.VMEM(window_rows.shape, BF16),
            pltpu.VMEM(out.shape, BF16),
            pltpu.SemaphoreType.DMA((3,)),
            pltpu.SemaphoreType.DMA((8,)),
            pltpu.SemaphoreType.DMA((2, requests)),
            pltpu.SemaphoreType.DMA,
        ],
        compiler_params=pltpu.CompilerParams(vmem_limit_bytes=60 * MEGA),
        name="attend",
    )(
        hidden,
        own_lengths[None, :],
        sink_rows.reshape(-1, size),
        qkv,
        window_rows,
        out,
    )


def expert_kernel(
    group, chunks, place, near, far, *refs
):
    w_in, refs = refs[:chunks], refs[chunks:]
    ids_hbm, route_hbm, out_hbm = refs[:3]
    terms, refs = refs[3 : 3 + group], refs[3 + group :]
    own_columns, rows_scr, act, ids, route, w_out, small_sems, out_sems = refs
    tokens, share = terms[0].shape
    requests = tokens // group
    chunk = act.shape[1] // chunks
    out_copies = [
        pltpu.make_async_copy(
            out_hbm.at[:, pl.ds(pl.multiple_of((place[0] ^ j) * share, share), share)],
            w_out.at[:, pl.ds(j * share, share)],
            out_sems.at[j],
        )
        for j in range(group)
    ]
    small_copies = [
        pltpu.make_async_copy(ids_hbm, ids, small_sems.at[0]),
        pltpu.make_async_copy(route_hbm, route, small_sems.at[1]),
    ]
    wait = in_order(small_copies + out_copies, 5)
    own = place[0]
    half = group // 2
    for first, source in ((0, near), (half, far)):
        values = source[...].astype(F32)
        for i in range(half):
            start = pl.multiple_of((own ^ (first + i)) * requests, requests)
            rows_scr[pl.ds(start, requests), :] = values[i * requests : (i + 1) * requests]
    own_columns[...] = rows_scr[:, pl.ds(pl.multiple_of(own * share, share), share)]
    rows = rows_scr[...]
    moe_in = (rows * lax.rsqrt(jnp.mean(rows * rows, axis=-1, keepdims=True) + EPSILON)).astype(BF16)
    for copy in small_copies:
        wait()
    per_stream = ids.shape[2]
    diagonal = iota((per_stream, per_stream), 0) == iota((per_stream, per_stream), 1)

    def factor_of(expert):
        columns = []
        for stream in range(2):
            row = jnp.sum(jnp.where(ids[stream] == expert, route[stream], 0.0), axis=0, keepdims=True)
            spread_out = jnp.broadcast_to(row, (per_stream, per_stream))
            columns.append(jnp.sum(jnp.where(diagonal, spread_out, 0.0), axis=-1, keepdims=True))
        return jnp.concatenate(columns, axis=0)

    for c in range(chunks):
        factor = factor_of(place[1] + c * chunk // FFE)
        gate = dot(moe_in, w_in[c][0])
        upward = dot(moe_in, w_in[c][1])
        act[:, c * chunk : (c + 1) * chunk] = (gate / (1.0 + jnp.exp(-gate)) * upward * factor).astype(BF16)
    for j in range(group):
        wait()
        terms[j][...] = dot(act[...], w_out[:, j * share : (j + 1) * share]).astype(BF16)


def experts_fast(near, far, expert_ids, route_weight, w_in, expert_out, share):
    width = near.shape[1]
    group = lax.axis_size(ROWS)
    tokens = 2 * near.shape[0]
    units = expert_out.shape[0]
    top = expert_ids.shape[-1]
    place = jnp.stack([lax.axis_index(ROWS), lax.axis_index(ALL) * units // FFE]).astype(jnp.int32)
    *terms, own_columns = pl.pallas_call(
        lambda *refs: expert_kernel(group, len(w_in), *refs),
        out_shape=[jax.ShapeDtypeStruct((tokens, share), BF16)] * group
        + [jax.ShapeDtypeStruct((tokens, share), F32)],
        in_specs=[SMEM] + [VMEM] * (2 + len(w_in)) + [HBM] * 3,
        out_specs=[VMEM] * (group + 1),
        scratch_shapes=[
            pltpu.VMEM((tokens, width), F32),
            pltpu.VMEM((tokens, units), BF16),
            pltpu.VMEM((2, top, tokens // 2), jnp.int32),
            pltpu.VMEM((2, top, tokens // 2), F32),
            pltpu.VMEM(expert_out.shape, BF16),
            pltpu.SemaphoreType.DMA((2,)),
            pltpu.SemaphoreType.DMA((group,)),
        ],
        compiler_params=pltpu.CompilerParams(vmem_limit_bytes=33 * MEGA),
        name="experts",
    )(place, near, far, *w_in, jnp.swapaxes(expert_ids, 1, 2), jnp.swapaxes(route_weight, 1, 2), expert_out)
    return terms, own_columns


def add_up(blocks):
    total = blocks[0][...].astype(F32)
    for block in blocks[1:]:
        total = total + block[...].astype(F32)
    return total


def sum_kernel(*refs):
    refs[-1][...] = add_up(refs[:-1]).astype(BF16)


def sum_fast(blocks):
    return pl.pallas_call(
        sum_kernel,
        out_shape=jax.ShapeDtypeStruct(blocks[0].shape, BF16),
        in_specs=[VMEM] * len(blocks),
        out_specs=VMEM,
        compiler_params=pltpu.CompilerParams(vmem_limit_bytes=8 * MEGA),
        name="add_up",
    )(*blocks)


def head_kernel(chunk, place, own_columns, left, right, weight, near, far):
    tokens = own_columns.shape[0]
    count, rows, _ = near.shape
    requests = rows // 2
    half_width = weight.shape[1] // 2
    per_half = half_width // chunk
    guide, own = place[0], place[1]
    summed = own_columns[...] + (left[...].astype(F32) + right[...].astype(F32))

    def hand_out(values, target, start):
        for d in range(count):
            target[own ^ d, :, start : start + values.shape[1]] = jnp.concatenate(
                [values[d * requests : (d + 1) * requests], values[tokens // 2 + d * requests : tokens // 2 + (d + 1) * requests]],
                axis=0,
            ).astype(BF16)

    squares = jnp.broadcast_to(jnp.sum(summed * summed, axis=-1, keepdims=True), (tokens, NOTE))
    raw_in = summed.astype(BF16)
    for target, half in ((far, 1 - guide), (near, guide)):
        hand_out(squares, target, half_width)
        for c in range(per_half):
            first = pl.multiple_of(half * half_width + c * chunk, 128)
            hand_out(dot(raw_in, weight[:, pl.ds(first, chunk)]), target, c * chunk)


def head_fast(own_columns, left, right, weight):
    count = lax.axis_size("dp")
    tokens = own_columns.shape[0]
    half_width = weight.shape[1] // 2
    place = jnp.stack([lax.axis_index("guide"), lax.axis_index("dp")]).astype(jnp.int32)
    shape = jax.ShapeDtypeStruct((count, tokens // count, half_width + NOTE), BF16)
    return pl.pallas_call(
        lambda *refs: head_kernel(256, *refs),
        out_shape=[shape, shape],
        in_specs=[SMEM] + [VMEM] * 4,
        out_specs=[VMEM, VMEM],
        compiler_params=pltpu.CompilerParams(vmem_limit_bytes=16 * MEGA),
        name="head",
    )(place, own_columns, left, right, weight)


def pair_kernel(near, received, *results):
    for k, result in enumerate(results):
        result[...] = (near[k].astype(F32) + received[k].astype(F32)).astype(BF16)


def pair_fast(near, received):
    count = near.shape[0]
    return pl.pallas_call(
        pair_kernel,
        out_shape=[jax.ShapeDtypeStruct(near.shape[1:], BF16)] * count,
        in_specs=[VMEM, VMEM],
        out_specs=[VMEM] * count,
        compiler_params=pltpu.CompilerParams(vmem_limit_bytes=8 * MEGA),
        name="pair",
    )(near, received)


def guide_kernel(width, weight, *refs):
    result = refs[-1]
    requests, half_width = result.shape[0], result.shape[3]
    total = add_up(refs[:-1])
    scale = lax.rsqrt(total[:, half_width : half_width + 1] / width + EPSILON)
    diagonal = iota((requests, requests), 0) == iota((requests, requests), 1)
    guidance = jnp.broadcast_to(weight[...], (requests, requests))
    factor = jnp.sum(jnp.where(diagonal, guidance, 0.0), axis=-1, keepdims=True)
    guided = total[:requests, :half_width] * (scale[:requests] * factor) + total[requests:, :half_width] * (
        scale[requests:] * (1.0 - factor)
    )
    for r in range(requests):
        result[r, 0] = guided[r : r + 1]


def guide_fast(blocks, guidance, width):
    rows, columns = blocks[0].shape
    return pl.pallas_call(
        lambda *refs: guide_kernel(width, *refs),
        out_shape=jax.ShapeDtypeStruct((rows // 2, 1, 1, columns - NOTE), F32),
        in_specs=[VMEM] * (1 + len(blocks)),
        out_specs=VMEM,
        compiler_params=pltpu.CompilerParams(vmem_limit_bytes=12 * MEGA),
        name="guide",
    )(guidance[None, :], *blocks)


def fits(hidden, sink_rows, expert_in, vocab_weight):
    return (
        lax.axis_size(ROWS) == 8
        and lax.axis_size("mp") == 4
        and hidden.shape[0] == 8
        and sink_rows.shape[1] == 4
        and expert_in.shape[2] % 512 == 0
        and vocab_weight.shape[0] % 128 == 0
        and vocab_weight.shape[1] % 512 == 0
    )


def fast_body(
    states,
    lengths,
    sink_cache,
    window_cache,
    qkv_weight,
    out_weight,
    expert_ids,
    route_weight,
    expert_in,
    expert_out,
    vocab_weight,
    guidance,
):
    hidden = states[0]
    partial_out = attend_fast(hidden, lengths[0], sink_cache[0], window_cache[0], qkv_weight, out_weight)
    chunk = expert_in.shape[2] // 4
    received = step(partial_out, "mp", 1)
    w0 = load_fast(expert_in, chunk, 0, lengths)
    pair = join_fast(True, [partial_out, received], w0)
    received = step(pair, "mp", 2)
    w1 = load_fast(expert_in, chunk, 1, pair)
    residual = join_fast(True, [hidden, pair, received], w1)
    received = step(residual, ROWS, 1)
    w2 = load_fast(expert_in, chunk, 2, residual)
    pair = join_fast(False, [residual, received], w2)
    received = step(pair, ROWS, 2)
    w3 = load_fast(expert_in, chunk, 3, pair)
    near = join_fast(False, [pair, received], w3)
    far = step(near, ROWS, 4)
    terms, own_columns = experts_fast(
        near, far, expert_ids, route_weight, [w0, w1, w2, w3], expert_out, vocab_weight.shape[0]
    )
    part = sum_fast(swap(terms, ROWS))
    received = step(part, "mp", 1)
    pair = (part.astype(F32) + received.astype(F32)).astype(BF16)
    received = step(pair, "mp", 2)
    near, far = head_fast(own_columns, pair, received, vocab_weight)
    logits = swap(pair_fast(near, step(far, "guide", 1)), "dp")
    return guide_fast(logits, guidance, hidden.shape[1])


def rotate(vectors, positions):
    full_width = vectors.shape[-1]
    half_width = full_width // 2
    step_index = jnp.arange(half_width, dtype=jnp.float32)
    inverse = jnp.exp(step_index * (-2.0 * math.log(10000.0) / full_width))
    angles = positions.astype(jnp.float32)[:, None] * inverse[None, :]
    cosine = jnp.cos(angles)[:, None, :]
    sine_part = jnp.sin(angles)[:, None, :]
    first_half = vectors[..., :half_width]
    second = vectors[..., half_width:]
    return jnp.concatenate(
        [first_half * cosine - second * sine_part, second * cosine + first_half * sine_part],
        axis=-1,
    )


def rms_norm(values):
    return values * lax.rsqrt(jnp.mean(values * values, axis=-1, keepdims=True) + EPSILON)


def attend(hidden, own_lengths, sink_rows, window_rows, qkv_weight, out_weight):
    normed = rms_norm(hidden.astype(jnp.float32)).astype(jnp.bfloat16)
    projected = jnp.einsum("rd,dthe->rthe", normed, qkv_weight, preferred_element_type=jnp.float32)
    query_rot = rotate(projected[:, 0], own_lengths).astype(jnp.bfloat16)
    fresh_key = rotate(projected[:, 1], own_lengths).astype(jnp.bfloat16)
    fresh_value = projected[:, 2].astype(jnp.bfloat16)
    sink_count = sink_rows.shape[3]
    window_count = window_rows.shape[3]
    root_size = math.sqrt(query_rot.shape[-1])
    sink_scores = (
        jnp.einsum(
            "rhe,rhse->rhs", query_rot, sink_rows[:, :, 0], preferred_element_type=jnp.float32
        )
        / root_size
    )
    window_scores = (
        jnp.einsum(
            "rhe,rhwe->rhw", query_rot, window_rows[:, :, 0], preferred_element_type=jnp.float32
        )
        / root_size
    )
    self_scores = (
        jnp.einsum("rhe,rhe->rh", query_rot, fresh_key, preferred_element_type=jnp.float32)
        / root_size
    )
    length_limit = own_lengths[:, None, None]
    sink_valid = jnp.arange(sink_count, dtype=jnp.int32)[None, None, :] < length_limit
    window_valid = (
        jnp.arange(window_count, dtype=jnp.int32)[None, None, :]
        >= sink_count + window_count - length_limit
    )
    sink_scores = jnp.where(sink_valid, sink_scores, -1e30)
    window_scores = jnp.where(window_valid, window_scores, -1e30)
    highest = jnp.maximum(
        jnp.maximum(jnp.max(sink_scores, axis=-1), jnp.max(window_scores, axis=-1)), self_scores
    )
    sink_exp = jnp.exp(sink_scores - highest[..., None])
    window_exp = jnp.exp(window_scores - highest[..., None])
    self_exp = jnp.exp(self_scores - highest)
    totals = jnp.sum(sink_exp, axis=-1) + jnp.sum(window_exp, axis=-1) + self_exp
    sink_prob = (sink_exp / totals[..., None]).astype(jnp.bfloat16)
    window_prob = (window_exp / totals[..., None]).astype(jnp.bfloat16)
    self_prob = (self_exp / totals).astype(jnp.bfloat16)
    mixture = (
        jnp.einsum(
            "rhs,rhse->rhe", sink_prob, sink_rows[:, :, 1], preferred_element_type=jnp.float32
        )
        + jnp.einsum(
            "rhw,rhwe->rhe", window_prob, window_rows[:, :, 1], preferred_element_type=jnp.float32
        )
        + self_prob[..., None].astype(jnp.float32) * fresh_value.astype(jnp.float32)
    ).astype(jnp.bfloat16)
    return jnp.einsum("rhe,hed->rd", mixture, out_weight, preferred_element_type=jnp.float32)


def body(
    states,
    lengths,
    sink_cache,
    window_cache,
    qkv_weight,
    out_weight,
    expert_ids,
    route_weight,
    expert_in,
    expert_out,
    vocab_weight,
    guidance,
):
    hidden = states[0]
    if fits(hidden, sink_cache[0], expert_in, vocab_weight):
        return fast_body(
            states,
            lengths,
            sink_cache,
            window_cache,
            qkv_weight,
            out_weight,
            expert_ids,
            route_weight,
            expert_in,
            expert_out,
            vocab_weight,
            guidance,
        )
    request_count, width = hidden.shape
    group = lax.axis_size(ROWS)
    mp = lax.axis_size("mp")
    tokens = group * request_count

    partial_out = attend(hidden, lengths[0], sink_cache[0], window_cache[0], qkv_weight, out_weight)
    first = lax.axis_index("mp") == 0
    partial_out = partial_out + jnp.where(first, hidden.astype(jnp.float32), 0.0)
    partials = spread(partial_out.astype(jnp.bfloat16), ALL).reshape(group, mp, request_count, width)
    residual = jnp.sum(partials.astype(jnp.float32), axis=1).reshape(tokens, width).astype(jnp.bfloat16)
    moe_in = rms_norm(residual.astype(jnp.float32)).astype(jnp.bfloat16)

    unit_count = expert_in.shape[2]
    unit_start = lax.axis_index(ALL) * unit_count
    unit_expert = (unit_start + jnp.arange(unit_count, dtype=jnp.int32)) // FFE
    choice_rows = expert_ids.reshape(-1, expert_ids.shape[-1])
    route_rows = route_weight.reshape(-1, route_weight.shape[-1])
    coefficient = jnp.sum(
        jnp.where(
            choice_rows[:, :, None] == unit_expert[None, None, :], route_rows[:, :, None], 0.0
        ),
        axis=1,
    )
    gate = jnp.dot(moe_in, expert_in[0], preferred_element_type=jnp.float32)
    upward = jnp.dot(moe_in, expert_in[1], preferred_element_type=jnp.float32)
    activated = (jax.nn.silu(gate) * upward * coefficient).astype(jnp.bfloat16)
    expert_terms = jnp.dot(activated, expert_out, preferred_element_type=jnp.float32).astype(jnp.bfloat16)

    share = vocab_weight.shape[0]
    sent = jnp.swapaxes(expert_terms.reshape(tokens, group, share), 0, 1)
    expert_part = jnp.sum(trade(sent, ROWS).astype(jnp.float32), axis=0)
    expert_total = jnp.sum(spread(expert_part.astype(jnp.bfloat16), "mp").astype(jnp.float32), axis=0)
    own_columns = lax.dynamic_slice_in_dim(residual, lax.axis_index(ROWS) * share, share, 1)
    summed = own_columns.astype(jnp.float32) + expert_total

    squares = jnp.sum(summed * summed, axis=-1)
    notes = spread(jnp.concatenate([squares, guidance]), ROWS)
    scale = lax.rsqrt(jnp.sum(notes[:, :tokens], axis=0) / width + EPSILON).reshape(2, -1, 1)
    weight = notes[: group // 2, tokens:].reshape(-1, 1)

    raw = jnp.dot(summed.astype(jnp.bfloat16), vocab_weight, preferred_element_type=jnp.float32)
    raw = raw.reshape(2, tokens // 2, -1)
    mixed = raw[0] * (scale[0] * weight) + raw[1] * (scale[1] * (1.0 - weight))
    half_width = mixed.shape[1] // 2
    mixed = mixed.astype(jnp.bfloat16).reshape(group // 2, request_count, 2, half_width)
    sent = jnp.transpose(mixed, (2, 0, 1, 3)).reshape(group, request_count, half_width)
    guided = jnp.sum(trade(sent, ROWS).astype(jnp.float32), axis=0)
    return guided.reshape(request_count, 1, 1, half_width)


def solution(mesh):
    in_specs = (
        P("guide", "dp", None),
        P("guide", "dp"),
        P("guide", "dp", "mp", None, None, None),
        P("guide", "dp", "mp", None, None, None),
        P(None, None, "mp", None),
        P("mp", None, None),
        P(),
        P(),
        P(None, None, ("guide", "dp", "mp")),
        P(("guide", "dp", "mp"), None),
        P(("guide", "dp"), "mp"),
        P("dp"),
    )
    out_specs = P("dp", "mp", "guide", None)
    return jax.shard_map(body, mesh=mesh, in_specs=in_specs, out_specs=out_specs, check_vma=False)
```

```python
import math

import jax
import jax.numpy as jnp
from jax import lax
from jax.experimental import pallas as pl
from jax.experimental.pallas import tpu as pltpu
from jax.sharding import PartitionSpec as P

FFE = 1024

EPSILON = 1e-05

ROWS = ("guide", "dp")
ALL = ("guide", "dp", "mp")


def trade(blocks, axis):
    return lax.all_to_all(blocks, axis, 0, 0, tiled=True)


def spread(block, axis):
    return trade(jnp.broadcast_to(block[None], (lax.axis_size(axis),) + block.shape), axis)


def step(block, axis, bit):
    count = lax.axis_size(axis)
    return lax.ppermute(block, axis, [(i, i ^ bit) for i in range(count)])


def swap(blocks, axis):
    return [blocks[0]] + [step(blocks[j], axis, j) for j in range(1, lax.axis_size(axis))]


F32 = jnp.float32
BF16 = jnp.bfloat16
VMEM = pl.BlockSpec(memory_space=pltpu.VMEM)
ANY = pl.BlockSpec(memory_space=pl.ANY)
HBM = pl.BlockSpec(memory_space=pltpu.HBM)
MEGA = 1 << 20
NOTE = 128


def dot(left, right):
    return jnp.dot(left, right, preferred_element_type=F32)


def iota(shape, dim):
    return lax.broadcasted_iota(jnp.int32, shape, dim)


def in_order(copies, ahead):
    state = [0, 0]

    def fill():
        while state[0] < min(len(copies), state[1] + ahead):
            copies[state[0]].start()
            state[0] += 1

    def wait():
        copies[state[1]].wait()
        state[1] += 1
        fill()

    fill()
    return wait


def load_kernel(chunk, index, hbm, after, result, sems):
    rows = hbm.shape[1] // sems.shape[1]
    copies = [
        pltpu.make_async_copy(
            hbm.at[k, pl.ds(i * rows, rows), pl.ds(index * chunk, chunk)],
            result.at[k, pl.ds(i * rows, rows), :],
            sems.at[k, i],
        )
        for k in range(hbm.shape[0])
        for i in range(sems.shape[1])
    ]
    for copy in copies:
        copy.start()
    for copy in copies:
        copy.wait()


def load_fast(weight, chunk, index, after):
    kinds, width, _ = weight.shape
    return pl.pallas_call(
        lambda *refs: load_kernel(chunk, index, *refs),
        out_shape=jax.ShapeDtypeStruct((kinds, width, chunk), BF16),
        in_specs=[HBM, ANY],
        out_specs=VMEM,
        scratch_shapes=[pltpu.SemaphoreType.DMA((kinds, 4))],
        compiler_params=pltpu.CompilerParams(vmem_limit_bytes=(47 - 4 * index) * MEGA),
        cost_estimate=pl.CostEstimate(flops=0, bytes_accessed=4 * kinds * width * chunk, transcendentals=0),
        name="load",
    )(weight, after)


def join_kernel(total, count, *refs):
    values = [ref[...].astype(F32) for ref in refs[:count]]
    joined = sum(values[1:], values[0]) if total else jnp.concatenate(values, axis=0)
    refs[-1][...] = joined.astype(BF16)


def join_fast(total, blocks, after):
    rows, columns = blocks[0].shape
    return pl.pallas_call(
        lambda *refs: join_kernel(total, len(blocks), *refs),
        out_shape=jax.ShapeDtypeStruct((rows if total else rows * len(blocks), columns), BF16),
        in_specs=[VMEM] * len(blocks) + [ANY],
        out_specs=VMEM,
        compiler_params=pltpu.CompilerParams(vmem_limit_bytes=4 * MEGA),
        name="join",
    )(*blocks, after)


def attend_kernel(
    heads, sinks, states_hbm, lengths_hbm, sink_hbm, qkv_hbm, window_hbm, out_hbm, result,
    states, lengths, sink, qkv, window, out_weight, first_sems, qkv_sems, window_sems, out_sem,
):
    requests, width = states.shape
    size = sink.shape[1]
    parts = 3 * heads
    lanes = size * parts
    blocks = width // size
    chunks = qkv_sems.shape[0]
    chunk_rows = qkv.shape[0] // chunks
    slots = window.shape[3]
    rows = heads * requests
    qkv_copies = [
        pltpu.make_async_copy(
            qkv_hbm.at[pl.ds(c * chunk_rows, chunk_rows)], qkv.at[pl.ds(c * chunk_rows, chunk_rows)], qkv_sems.at[c]
        )
        for c in range(chunks)
    ]
    key_copies, value_copies = [
        [
            pltpu.make_async_copy(window_hbm.at[r, :, k], window.at[r, :, k], window_sems.at[k, r])
            for r in range(requests)
        ]
        for k in range(2)
    ]
    out_copy = pltpu.make_async_copy(out_hbm, out_weight, out_sem)
    first_copies = [
        pltpu.make_async_copy(source, target, first_sems.at[i])
        for i, (source, target) in enumerate(((states_hbm, states), (lengths_hbm, lengths), (sink_hbm, sink)))
    ]
    wait = in_order(first_copies + qkv_copies + key_copies + value_copies + [out_copy], 6)
    for copy in first_copies:
        wait()

    length_row = jnp.broadcast_to(lengths[...], (requests, requests))
    diagonal = iota((requests, requests), 0) == iota((requests, requests), 1)
    length = jnp.sum(jnp.where(diagonal, length_row, 0), axis=-1, keepdims=True)
    lane_id = iota((requests, size), 1)
    low = lane_id < size // 2
    pair_index = jnp.where(low, lane_id, lane_id - size // 2).astype(F32)
    angles = length.astype(F32) * jnp.exp(pair_index * (-2.0 * math.log(10000.0) / size))
    cosine, sine = jnp.cos(angles), jnp.sin(angles)
    sine = jnp.where(low, -sine, sine)

    hidden = states[...].astype(F32)
    normed = hidden * lax.rsqrt(jnp.mean(hidden * hidden, axis=-1, keepdims=True) + EPSILON)
    stacked = jnp.concatenate([normed[:, b * size : (b + 1) * size] for b in range(blocks)], axis=0)
    sub, lane = iota((size, lanes), 0) * parts, iota((size, lanes), 1)
    repeat = jnp.where((lane >= sub) & (lane < sub + parts), 1.0, 0.0).astype(BF16)
    repeated = dot(stacked.astype(BF16), repeat)
    kind = lax.rem(iota((requests, lanes), 1), parts)
    projected = jnp.zeros((parts * requests, size), F32)
    for b in range(blocks):
        if b % (blocks // chunks) == 0:
            wait()
        piece = repeated[b * requests : (b + 1) * requests]
        spread_out = jnp.concatenate([jnp.where(kind == p, piece, 0.0) for p in range(parts)], axis=0)
        projected = projected + dot(spread_out.astype(BF16), qkv[b * lanes : (b + 1) * lanes, :])

    cos_rows = jnp.concatenate([cosine] * heads, axis=0)
    sin_rows = jnp.concatenate([sine] * heads, axis=0)
    limit = jnp.concatenate([length] * heads, axis=0)

    def turn(values):
        return (values * cos_rows + pltpu.roll(values, size // 2, 1) * sin_rows).astype(BF16)

    query = turn(projected[:rows])
    fresh_key = turn(projected[rows : 2 * rows])
    fresh_value = projected[2 * rows :].astype(BF16).astype(F32)
    root_size = math.sqrt(size)
    across = (((1,), (1,)), ((), ()))

    self_scores = jnp.sum(query.astype(F32) * fresh_key.astype(F32), axis=-1, keepdims=True) / root_size
    sink_rows = sink[...]
    sink_total = sink_rows.shape[0]
    sink_scores = lax.dot_general(query, sink_rows, across, preferred_element_type=F32) / root_size
    row_id, column = iota((rows, sink_total), 0), iota((rows, sink_total), 1)
    slot = lax.rem(column, 2 * sinks)
    pair = lax.div(column, 2 * sinks)
    sink_valid = (
        (lax.rem(pair, heads) == lax.div(row_id, requests))
        & (lax.div(pair, heads) == lax.rem(row_id, requests))
        & (slot < sinks)
        & (slot < limit)
    )
    sink_scores = jnp.where(sink_valid, sink_scores, -1e30)

    mine = iota((requests, slots), 0)
    scores = [jnp.zeros((requests, slots), F32) for h in range(heads)]
    for r in range(requests):
        wait()
        for h in range(heads):
            found = lax.dot_general(
                query[h * requests : (h + 1) * requests], window[r, h, 0], across, preferred_element_type=F32
            )
            scores[h] = jnp.where(mine == r, found, scores[h])
    scores = jnp.concatenate(scores, axis=0) / root_size
    valid = iota((rows, slots), 1) >= sinks + slots - limit
    scores = jnp.where(valid, scores, -1e30)

    highest = jnp.maximum(
        jnp.maximum(jnp.max(scores, axis=-1, keepdims=True), jnp.max(sink_scores, axis=-1, keepdims=True)),
        self_scores,
    )
    window_exp = jnp.exp(scores - highest)
    sink_exp = jnp.where(sink_valid, jnp.exp(sink_scores - highest), 0.0)
    self_exp = jnp.exp(self_scores - highest)
    total = jnp.sum(window_exp, axis=-1, keepdims=True) + jnp.sum(sink_exp, axis=-1, keepdims=True) + self_exp
    window_weight = (window_exp / total).astype(BF16).astype(F32)
    sink_weight = pltpu.roll(sink_exp / total, sinks, 1).astype(BF16)
    self_weight = (self_exp / total).astype(BF16).astype(F32)
    mixture = dot(sink_weight, sink_rows) + self_weight * fresh_value
    mixed = [mixture[h * requests : (h + 1) * requests] for h in range(heads)]
    for r in range(requests):
        wait()
        for h in range(heads):
            own = jnp.where(mine == r, window_weight[h * requests : (h + 1) * requests], 0.0)
            mixed[h] = mixed[h] + dot(own.astype(BF16), window[r, h, 1])
    wait()
    result[...] = dot(jnp.concatenate(mixed, axis=1).astype(BF16), out_weight[...]).astype(result.dtype)


def attend_fast(hidden, own_lengths, sink_rows, window_rows, qkv_weight, out_weight):
    requests, width = hidden.shape
    heads, sinks, size = sink_rows.shape[1], sink_rows.shape[3], sink_rows.shape[4]
    qkv = qkv_weight.reshape(-1, size)
    out = out_weight.reshape(-1, width)
    return pl.pallas_call(
        lambda *refs: attend_kernel(heads, sinks, *refs),
        out_shape=jax.ShapeDtypeStruct((requests, width), BF16),
        in_specs=[HBM] * 6,
        out_specs=VMEM,
        scratch_shapes=[
            pltpu.VMEM(hidden.shape, BF16),
            pltpu.VMEM((1, requests), jnp.int32),
            pltpu.VMEM((sink_rows.size // size, size), BF16),
            pltpu.VMEM(qkv.shape, BF16),
            pltpu.VMEM(window_rows.shape, BF16),
            pltpu.VMEM(out.shape, BF16),
            pltpu.SemaphoreType.DMA((3,)),
            pltpu.SemaphoreType.DMA((8,)),
            pltpu.SemaphoreType.DMA((2, requests)),
            pltpu.SemaphoreType.DMA,
        ],
        compiler_params=pltpu.CompilerParams(vmem_limit_bytes=60 * MEGA),
        name="attend",
    )(
        hidden,
        own_lengths[None, :],
        sink_rows.reshape(-1, size),
        qkv,
        window_rows,
        out,
    )


def expert_kernel(
    group, chunks, near, far, *refs
):
    w_in, refs = refs[:chunks], refs[chunks:]
    ids_hbm, route_hbm, out_hbm = refs[:3]
    terms, refs = refs[3 : 3 + group], refs[3 + group :]
    own_columns, rows_scr, act, ids, route, w_out, small_sems, out_sems = refs
    tokens, share = terms[0].shape
    requests = tokens // group
    units = act.shape[1]
    chunk = units // chunks
    own = lax.axis_index("guide") * (group // 2) + lax.axis_index("dp")
    first_expert = (own * lax.axis_size("mp") + lax.axis_index("mp")) * (units // FFE)
    out_copies = [
        pltpu.make_async_copy(
            out_hbm.at[:, pl.ds(pl.multiple_of((own ^ j) * share, share), share)],
            w_out.at[:, pl.ds(j * share, share)],
            out_sems.at[j],
        )
        for j in range(group)
    ]
    small_copies = [
        pltpu.make_async_copy(ids_hbm, ids, small_sems.at[0]),
        pltpu.make_async_copy(route_hbm, route, small_sems.at[1]),
    ]
    wait = in_order(small_copies + out_copies, 5)
    half = group // 2
    for first, source in ((0, near), (half, far)):
        values = source[...].astype(F32)
        for i in range(half):
            start = pl.multiple_of((own ^ (first + i)) * requests, requests)
            rows_scr[pl.ds(start, requests), :] = values[i * requests : (i + 1) * requests]
    own_columns[...] = rows_scr[:, pl.ds(pl.multiple_of(own * share, share), share)]
    rows = rows_scr[...]
    moe_in = (rows * lax.rsqrt(jnp.mean(rows * rows, axis=-1, keepdims=True) + EPSILON)).astype(BF16)
    for copy in small_copies:
        wait()
    per_stream = ids.shape[2]
    diagonal = iota((per_stream, per_stream), 0) == iota((per_stream, per_stream), 1)

    def factor_of(expert):
        columns = []
        for stream in range(2):
            row = jnp.sum(jnp.where(ids[stream] == expert, route[stream], 0.0), axis=0, keepdims=True)
            spread_out = jnp.broadcast_to(row, (per_stream, per_stream))
            columns.append(jnp.sum(jnp.where(diagonal, spread_out, 0.0), axis=-1, keepdims=True))
        return jnp.concatenate(columns, axis=0)

    for c in range(chunks):
        factor = factor_of(first_expert + c * chunk // FFE)
        gate = dot(moe_in, w_in[c][0])
        upward = dot(moe_in, w_in[c][1])
        act[:, c * chunk : (c + 1) * chunk] = (gate / (1.0 + jnp.exp(-gate)) * upward * factor).astype(BF16)
    for j in range(group):
        wait()
        terms[j][...] = dot(act[...], w_out[:, j * share : (j + 1) * share]).astype(BF16)


def experts_fast(near, far, expert_ids, route_weight, w_in, expert_out, share):
    width = near.shape[1]
    group = lax.axis_size(ROWS)
    tokens = 2 * near.shape[0]
    units = expert_out.shape[0]
    top = expert_ids.shape[-1]
    *terms, own_columns = pl.pallas_call(
        lambda *refs: expert_kernel(group, len(w_in), *refs),
        out_shape=[jax.ShapeDtypeStruct((tokens, share), BF16)] * group
        + [jax.ShapeDtypeStruct((tokens, share), F32)],
        in_specs=[VMEM] * (2 + len(w_in)) + [HBM] * 3,
        out_specs=[VMEM] * (group + 1),
        scratch_shapes=[
            pltpu.VMEM((tokens, width), F32),
            pltpu.VMEM((tokens, units), BF16),
            pltpu.VMEM((2, top, tokens // 2), jnp.int32),
            pltpu.VMEM((2, top, tokens // 2), F32),
            pltpu.VMEM(expert_out.shape, BF16),
            pltpu.SemaphoreType.DMA((2,)),
            pltpu.SemaphoreType.DMA((group,)),
        ],
        compiler_params=pltpu.CompilerParams(vmem_limit_bytes=33 * MEGA),
        name="experts",
    )(near, far, *w_in, jnp.swapaxes(expert_ids, 1, 2), jnp.swapaxes(route_weight, 1, 2), expert_out)
    return terms, own_columns


def add_up(blocks):
    total = blocks[0][...].astype(F32)
    for block in blocks[1:]:
        total = total + block[...].astype(F32)
    return total


def sum_kernel(*refs):
    refs[-1][...] = add_up(refs[:-1]).astype(BF16)


def sum_fast(blocks):
    return pl.pallas_call(
        sum_kernel,
        out_shape=jax.ShapeDtypeStruct(blocks[0].shape, BF16),
        in_specs=[VMEM] * len(blocks),
        out_specs=VMEM,
        compiler_params=pltpu.CompilerParams(vmem_limit_bytes=8 * MEGA),
        name="add_up",
    )(*blocks)


def head_kernel(chunk, own_columns, left, right, weight, near, far):
    tokens = own_columns.shape[0]
    count, rows, _ = near.shape
    requests = rows // 2
    half_width = weight.shape[1] // 2
    per_half = half_width // chunk
    guide, own = lax.axis_index("guide"), lax.axis_index("dp")
    summed = own_columns[...] + (left[...].astype(F32) + right[...].astype(F32))

    def hand_out(values, target, start):
        for d in range(count):
            target[own ^ d, :, start : start + values.shape[1]] = jnp.concatenate(
                [values[d * requests : (d + 1) * requests], values[tokens // 2 + d * requests : tokens // 2 + (d + 1) * requests]],
                axis=0,
            ).astype(BF16)

    squares = jnp.broadcast_to(jnp.sum(summed * summed, axis=-1, keepdims=True), (tokens, NOTE))
    raw_in = summed.astype(BF16)
    for target, half in ((far, 1 - guide), (near, guide)):
        hand_out(squares, target, half_width)
        for c in range(per_half):
            first = pl.multiple_of(half * half_width + c * chunk, 128)
            hand_out(dot(raw_in, weight[:, pl.ds(first, chunk)]), target, c * chunk)


def head_fast(own_columns, left, right, weight):
    count = lax.axis_size("dp")
    tokens = own_columns.shape[0]
    half_width = weight.shape[1] // 2
    shape = jax.ShapeDtypeStruct((count, tokens // count, half_width + NOTE), BF16)
    return pl.pallas_call(
        lambda *refs: head_kernel(256, *refs),
        out_shape=[shape, shape],
        in_specs=[VMEM] * 4,
        out_specs=[VMEM, VMEM],
        compiler_params=pltpu.CompilerParams(vmem_limit_bytes=16 * MEGA),
        name="head",
    )(own_columns, left, right, weight)


def pair_kernel(near, received, *results):
    for k, result in enumerate(results):
        result[...] = (near[k].astype(F32) + received[k].astype(F32)).astype(BF16)


def pair_fast(near, received):
    count = near.shape[0]
    return pl.pallas_call(
        pair_kernel,
        out_shape=[jax.ShapeDtypeStruct(near.shape[1:], BF16)] * count,
        in_specs=[VMEM, VMEM],
        out_specs=[VMEM] * count,
        compiler_params=pltpu.CompilerParams(vmem_limit_bytes=8 * MEGA),
        name="pair",
    )(near, received)


def guide_kernel(width, weight, *refs):
    result = refs[-1]
    requests, half_width = result.shape[0], result.shape[3]
    total = add_up(refs[:-1])
    scale = lax.rsqrt(total[:, half_width : half_width + 1] / width + EPSILON)
    diagonal = iota((requests, requests), 0) == iota((requests, requests), 1)
    guidance = jnp.broadcast_to(weight[...], (requests, requests))
    factor = jnp.sum(jnp.where(diagonal, guidance, 0.0), axis=-1, keepdims=True)
    guided = total[:requests, :half_width] * (scale[:requests] * factor) + total[requests:, :half_width] * (
        scale[requests:] * (1.0 - factor)
    )
    for r in range(requests):
        result[r, 0] = guided[r : r + 1]


def guide_fast(blocks, guidance, width):
    rows, columns = blocks[0].shape
    return pl.pallas_call(
        lambda *refs: guide_kernel(width, *refs),
        out_shape=jax.ShapeDtypeStruct((rows // 2, 1, 1, columns - NOTE), F32),
        in_specs=[VMEM] * (1 + len(blocks)),
        out_specs=VMEM,
        compiler_params=pltpu.CompilerParams(vmem_limit_bytes=12 * MEGA),
        name="guide",
    )(guidance[None, :], *blocks)


def fits(hidden, sink_rows, expert_in, vocab_weight):
    return (
        lax.axis_size(ROWS) == 8
        and lax.axis_size("mp") == 4
        and hidden.shape[0] == 8
        and sink_rows.shape[1] == 4
        and expert_in.shape[2] % (2 * FFE) == 0
        and vocab_weight.shape[0] % 128 == 0
        and vocab_weight.shape[1] % 512 == 0
    )


def fast_body(
    states,
    lengths,
    sink_cache,
    window_cache,
    qkv_weight,
    out_weight,
    expert_ids,
    route_weight,
    expert_in,
    expert_out,
    vocab_weight,
    guidance,
):
    hidden = states[0]
    partial_out = attend_fast(hidden, lengths[0], sink_cache[0], window_cache[0], qkv_weight, out_weight)
    chunk = expert_in.shape[2] // 4
    received = step(partial_out, "mp", 1)
    w0 = load_fast(expert_in, chunk, 0, lengths)
    pair = join_fast(True, [partial_out, received], w0)
    received = step(pair, "mp", 2)
    w1 = load_fast(expert_in, chunk, 1, pair)
    residual = join_fast(True, [hidden, pair, received], w1)
    received = step(residual, ROWS, 1)
    w2 = load_fast(expert_in, chunk, 2, residual)
    pair = join_fast(False, [residual, received], w2)
    received = step(pair, ROWS, 2)
    w3 = load_fast(expert_in, chunk, 3, pair)
    near = join_fast(False, [pair, received], w3)
    far = step(near, ROWS, 4)
    terms, own_columns = experts_fast(
        near, far, expert_ids, route_weight, [w0, w1, w2, w3], expert_out, vocab_weight.shape[0]
    )
    part = sum_fast(swap(terms, ROWS))
    received = step(part, "mp", 1)
    pair = (part.astype(F32) + received.astype(F32)).astype(BF16)
    received = step(pair, "mp", 2)
    near, far = head_fast(own_columns, pair, received, vocab_weight)
    logits = swap(pair_fast(near, step(far, "guide", 1)), "dp")
    return guide_fast(logits, guidance, hidden.shape[1])


def rotate(vectors, positions):
    full_width = vectors.shape[-1]
    half_width = full_width // 2
    step_index = jnp.arange(half_width, dtype=jnp.float32)
    inverse = jnp.exp(step_index * (-2.0 * math.log(10000.0) / full_width))
    angles = positions.astype(jnp.float32)[:, None] * inverse[None, :]
    cosine = jnp.cos(angles)[:, None, :]
    sine_part = jnp.sin(angles)[:, None, :]
    first_half = vectors[..., :half_width]
    second = vectors[..., half_width:]
    return jnp.concatenate(
        [first_half * cosine - second * sine_part, second * cosine + first_half * sine_part],
        axis=-1,
    )


def rms_norm(values):
    return values * lax.rsqrt(jnp.mean(values * values, axis=-1, keepdims=True) + EPSILON)


def attend(hidden, own_lengths, sink_rows, window_rows, qkv_weight, out_weight):
    normed = rms_norm(hidden.astype(jnp.float32)).astype(jnp.bfloat16)
    projected = jnp.einsum("rd,dthe->rthe", normed, qkv_weight, preferred_element_type=jnp.float32)
    query_rot = rotate(projected[:, 0], own_lengths).astype(jnp.bfloat16)
    fresh_key = rotate(projected[:, 1], own_lengths).astype(jnp.bfloat16)
    fresh_value = projected[:, 2].astype(jnp.bfloat16)
    sink_count = sink_rows.shape[3]
    window_count = window_rows.shape[3]
    root_size = math.sqrt(query_rot.shape[-1])
    sink_scores = (
        jnp.einsum(
            "rhe,rhse->rhs", query_rot, sink_rows[:, :, 0], preferred_element_type=jnp.float32
        )
        / root_size
    )
    window_scores = (
        jnp.einsum(
            "rhe,rhwe->rhw", query_rot, window_rows[:, :, 0], preferred_element_type=jnp.float32
        )
        / root_size
    )
    self_scores = (
        jnp.einsum("rhe,rhe->rh", query_rot, fresh_key, preferred_element_type=jnp.float32)
        / root_size
    )
    length_limit = own_lengths[:, None, None]
    sink_valid = jnp.arange(sink_count, dtype=jnp.int32)[None, None, :] < length_limit
    window_valid = (
        jnp.arange(window_count, dtype=jnp.int32)[None, None, :]
        >= sink_count + window_count - length_limit
    )
    sink_scores = jnp.where(sink_valid, sink_scores, -1e30)
    window_scores = jnp.where(window_valid, window_scores, -1e30)
    highest = jnp.maximum(
        jnp.maximum(jnp.max(sink_scores, axis=-1), jnp.max(window_scores, axis=-1)), self_scores
    )
    sink_exp = jnp.exp(sink_scores - highest[..., None])
    window_exp = jnp.exp(window_scores - highest[..., None])
    self_exp = jnp.exp(self_scores - highest)
    totals = jnp.sum(sink_exp, axis=-1) + jnp.sum(window_exp, axis=-1) + self_exp
    sink_prob = (sink_exp / totals[..., None]).astype(jnp.bfloat16)
    window_prob = (window_exp / totals[..., None]).astype(jnp.bfloat16)
    self_prob = (self_exp / totals).astype(jnp.bfloat16)
    mixture = (
        jnp.einsum(
            "rhs,rhse->rhe", sink_prob, sink_rows[:, :, 1], preferred_element_type=jnp.float32
        )
        + jnp.einsum(
            "rhw,rhwe->rhe", window_prob, window_rows[:, :, 1], preferred_element_type=jnp.float32
        )
        + self_prob[..., None].astype(jnp.float32) * fresh_value.astype(jnp.float32)
    ).astype(jnp.bfloat16)
    return jnp.einsum("rhe,hed->rd", mixture, out_weight, preferred_element_type=jnp.float32)


def body(
    states,
    lengths,
    sink_cache,
    window_cache,
    qkv_weight,
    out_weight,
    expert_ids,
    route_weight,
    expert_in,
    expert_out,
    vocab_weight,
    guidance,
):
    hidden = states[0]
    if fits(hidden, sink_cache[0], expert_in, vocab_weight):
        return fast_body(
            states,
            lengths,
            sink_cache,
            window_cache,
            qkv_weight,
            out_weight,
            expert_ids,
            route_weight,
            expert_in,
            expert_out,
            vocab_weight,
            guidance,
        )
    request_count, width = hidden.shape
    group = lax.axis_size(ROWS)
    mp = lax.axis_size("mp")
    tokens = group * request_count

    partial_out = attend(hidden, lengths[0], sink_cache[0], window_cache[0], qkv_weight, out_weight)
    first = lax.axis_index("mp") == 0
    partial_out = partial_out + jnp.where(first, hidden.astype(jnp.float32), 0.0)
    partials = spread(partial_out.astype(jnp.bfloat16), ALL).reshape(group, mp, request_count, width)
    residual = jnp.sum(partials.astype(jnp.float32), axis=1).reshape(tokens, width).astype(jnp.bfloat16)
    moe_in = rms_norm(residual.astype(jnp.float32)).astype(jnp.bfloat16)

    unit_count = expert_in.shape[2]
    unit_start = lax.axis_index(ALL) * unit_count
    unit_expert = (unit_start + jnp.arange(unit_count, dtype=jnp.int32)) // FFE
    choice_rows = expert_ids.reshape(-1, expert_ids.shape[-1])
    route_rows = route_weight.reshape(-1, route_weight.shape[-1])
    coefficient = jnp.sum(
        jnp.where(
            choice_rows[:, :, None] == unit_expert[None, None, :], route_rows[:, :, None], 0.0
        ),
        axis=1,
    )
    gate = jnp.dot(moe_in, expert_in[0], preferred_element_type=jnp.float32)
    upward = jnp.dot(moe_in, expert_in[1], preferred_element_type=jnp.float32)
    activated = (jax.nn.silu(gate) * upward * coefficient).astype(jnp.bfloat16)
    expert_terms = jnp.dot(activated, expert_out, preferred_element_type=jnp.float32).astype(jnp.bfloat16)

    share = vocab_weight.shape[0]
    sent = jnp.swapaxes(expert_terms.reshape(tokens, group, share), 0, 1)
    expert_part = jnp.sum(trade(sent, ROWS).astype(jnp.float32), axis=0)
    expert_total = jnp.sum(spread(expert_part.astype(jnp.bfloat16), "mp").astype(jnp.float32), axis=0)
    own_columns = lax.dynamic_slice_in_dim(residual, lax.axis_index(ROWS) * share, share, 1)
    summed = own_columns.astype(jnp.float32) + expert_total

    squares = jnp.sum(summed * summed, axis=-1)
    notes = spread(jnp.concatenate([squares, guidance]), ROWS)
    scale = lax.rsqrt(jnp.sum(notes[:, :tokens], axis=0) / width + EPSILON).reshape(2, -1, 1)
    weight = notes[: group // 2, tokens:].reshape(-1, 1)

    raw = jnp.dot(summed.astype(jnp.bfloat16), vocab_weight, preferred_element_type=jnp.float32)
    raw = raw.reshape(2, tokens // 2, -1)
    mixed = raw[0] * (scale[0] * weight) + raw[1] * (scale[1] * (1.0 - weight))
    half_width = mixed.shape[1] // 2
    mixed = mixed.astype(jnp.bfloat16).reshape(group // 2, request_count, 2, half_width)
    sent = jnp.transpose(mixed, (2, 0, 1, 3)).reshape(group, request_count, half_width)
    guided = jnp.sum(trade(sent, ROWS).astype(jnp.float32), axis=0)
    return guided.reshape(request_count, 1, 1, half_width)


def solution(mesh):
    in_specs = (
        P("guide", "dp", None),
        P("guide", "dp"),
        P("guide", "dp", "mp", None, None, None),
        P("guide", "dp", "mp", None, None, None),
        P(None, None, "mp", None),
        P("mp", None, None),
        P(),
        P(),
        P(None, None, ("guide", "dp", "mp")),
        P(("guide", "dp", "mp"), None),
        P(("guide", "dp"), "mp"),
        P("dp"),
    )
    out_specs = P("dp", "mp", "guide", None)
    return jax.shard_map(body, mesh=mesh, in_specs=in_specs, out_specs=out_specs, check_vma=False)
```

```python
import math

import jax
import jax.numpy as jnp
from jax import lax
from jax.experimental import pallas as pl
from jax.experimental.pallas import tpu as pltpu
from jax.sharding import PartitionSpec as P

FFE = 1024

EPSILON = 1e-05

ROWS = ("guide", "dp")
ALL = ("guide", "dp", "mp")


def trade(blocks, axis):
    return lax.all_to_all(blocks, axis, 0, 0, tiled=True)


def spread(block, axis):
    return trade(jnp.broadcast_to(block[None], (lax.axis_size(axis),) + block.shape), axis)


def step(block, axis, bit):
    count = lax.axis_size(axis)
    return lax.ppermute(block, axis, [(i, i ^ bit) for i in range(count)])


def swap(blocks, axis):
    return [blocks[0]] + [step(blocks[j], axis, j) for j in range(1, lax.axis_size(axis))]


F32 = jnp.float32
BF16 = jnp.bfloat16
VMEM = pl.BlockSpec(memory_space=pltpu.VMEM)
ANY = pl.BlockSpec(memory_space=pl.ANY)
HBM = pl.BlockSpec(memory_space=pltpu.HBM)
MEGA = 1 << 20
NOTE = 128


def dot(left, right):
    return jnp.dot(left, right, preferred_element_type=F32)


def iota(shape, dim):
    return lax.broadcasted_iota(jnp.int32, shape, dim)


def in_order(copies, ahead):
    state = [0, 0]

    def fill():
        while state[0] < min(len(copies), state[1] + ahead):
            copies[state[0]].start()
            state[0] += 1

    def wait():
        copies[state[1]].wait()
        state[1] += 1
        fill()

    fill()
    return wait


def load_kernel(chunk, index, hbm, after, result, sems):
    rows = hbm.shape[1] // sems.shape[1]
    copies = [
        pltpu.make_async_copy(
            hbm.at[k, pl.ds(i * rows, rows), pl.ds(index * chunk, chunk)],
            result.at[k, pl.ds(i * rows, rows), :],
            sems.at[k, i],
        )
        for k in range(hbm.shape[0])
        for i in range(sems.shape[1])
    ]
    for copy in copies:
        copy.start()
    for copy in copies:
        copy.wait()


def load_fast(weight, chunk, index, after):
    kinds, width, _ = weight.shape
    return pl.pallas_call(
        lambda *refs: load_kernel(chunk, index, *refs),
        out_shape=jax.ShapeDtypeStruct((kinds, width, chunk), BF16),
        in_specs=[HBM, ANY],
        out_specs=VMEM,
        scratch_shapes=[pltpu.SemaphoreType.DMA((kinds, 4))],
        compiler_params=pltpu.CompilerParams(vmem_limit_bytes=(47 - 4 * index) * MEGA),
        cost_estimate=pl.CostEstimate(flops=0, bytes_accessed=4 * kinds * width * chunk, transcendentals=0),
        name="load",
    )(weight, after)


def join_kernel(total, count, *refs):
    values = [ref[...].astype(F32) for ref in refs[:count]]
    joined = sum(values[1:], values[0]) if total else jnp.concatenate(values, axis=0)
    refs[-1][...] = joined.astype(BF16)


def join_fast(total, blocks, after):
    rows, columns = blocks[0].shape
    return pl.pallas_call(
        lambda *refs: join_kernel(total, len(blocks), *refs),
        out_shape=jax.ShapeDtypeStruct((rows if total else rows * len(blocks), columns), BF16),
        in_specs=[VMEM] * len(blocks) + [ANY],
        out_specs=VMEM,
        compiler_params=pltpu.CompilerParams(vmem_limit_bytes=4 * MEGA),
        name="join",
    )(*blocks, after)


def attend_kernel(
    heads, sinks, states_hbm, lengths_hbm, sink_hbm, qkv_hbm, window_hbm, out_hbm, result,
    states, lengths, sink, qkv, window, out_weight, first_sems, qkv_sems, window_sems, out_sem,
):
    requests, width = states.shape
    size = sink.shape[1]
    parts = 3 * heads
    lanes = size * parts
    blocks = width // size
    chunks = qkv_sems.shape[0]
    chunk_rows = qkv.shape[0] // chunks
    slots = window.shape[3]
    rows = heads * requests
    qkv_copies = [
        pltpu.make_async_copy(
            qkv_hbm.at[pl.ds(c * chunk_rows, chunk_rows)], qkv.at[pl.ds(c * chunk_rows, chunk_rows)], qkv_sems.at[c]
        )
        for c in range(chunks)
    ]
    key_copies, value_copies = [
        [
            pltpu.make_async_copy(window_hbm.at[r, :, k], window.at[r, :, k], window_sems.at[k, r])
            for r in range(requests)
        ]
        for k in range(2)
    ]
    out_copy = pltpu.make_async_copy(out_hbm, out_weight, out_sem)
    first_copies = [
        pltpu.make_async_copy(source, target, first_sems.at[i])
        for i, (source, target) in enumerate(((states_hbm, states), (lengths_hbm, lengths), (sink_hbm, sink)))
    ]
    wait = in_order(first_copies + qkv_copies + key_copies + value_copies + [out_copy], 6)
    for copy in first_copies:
        wait()

    length_row = jnp.broadcast_to(lengths[...], (requests, requests))
    diagonal = iota((requests, requests), 0) == iota((requests, requests), 1)
    length = jnp.sum(jnp.where(diagonal, length_row, 0), axis=-1, keepdims=True)
    lane_id = iota((requests, size), 1)
    low = lane_id < size // 2
    pair_index = jnp.where(low, lane_id, lane_id - size // 2).astype(F32)
    angles = length.astype(F32) * jnp.exp(pair_index * (-2.0 * math.log(10000.0) / size))
    cosine, sine = jnp.cos(angles), jnp.sin(angles)
    sine = jnp.where(low, -sine, sine)

    hidden = states[...].astype(F32)
    normed = hidden * lax.rsqrt(jnp.mean(hidden * hidden, axis=-1, keepdims=True) + EPSILON)
    stacked = jnp.concatenate([normed[:, b * size : (b + 1) * size] for b in range(blocks)], axis=0)
    sub, lane = iota((size, lanes), 0) * parts, iota((size, lanes), 1)
    repeat = jnp.where((lane >= sub) & (lane < sub + parts), 1.0, 0.0).astype(BF16)
    repeated = dot(stacked.astype(BF16), repeat)
    kind = lax.rem(iota((requests, lanes), 1), parts)
    projected = jnp.zeros((parts * requests, size), F32)
    for b in range(blocks):
        if b % (blocks // chunks) == 0:
            wait()
        piece = repeated[b * requests : (b + 1) * requests]
        spread_out = jnp.concatenate([jnp.where(kind == p, piece, 0.0) for p in range(parts)], axis=0)
        projected = projected + dot(spread_out.astype(BF16), qkv[b * lanes : (b + 1) * lanes, :])

    cos_rows = jnp.concatenate([cosine] * heads, axis=0)
    sin_rows = jnp.concatenate([sine] * heads, axis=0)
    limit = jnp.concatenate([length] * heads, axis=0)

    def turn(values):
        return (values * cos_rows + pltpu.roll(values, size // 2, 1) * sin_rows).astype(BF16)

    query = turn(projected[:rows])
    fresh_key = turn(projected[rows : 2 * rows])
    fresh_value = projected[2 * rows :].astype(BF16).astype(F32)
    root_size = math.sqrt(size)
    across = (((1,), (1,)), ((), ()))

    self_scores = jnp.sum(query.astype(F32) * fresh_key.astype(F32), axis=-1, keepdims=True) / root_size
    sink_rows = sink[...]
    sink_total = sink_rows.shape[0]
    sink_scores = lax.dot_general(query, sink_rows, across, preferred_element_type=F32) / root_size
    row_id, column = iota((rows, sink_total), 0), iota((rows, sink_total), 1)
    slot = lax.rem(column, 2 * sinks)
    pair = lax.div(column, 2 * sinks)
    sink_valid = (
        (lax.rem(pair, heads) == lax.div(row_id, requests))
        & (lax.div(pair, heads) == lax.rem(row_id, requests))
        & (slot < sinks)
        & (slot < limit)
    )
    sink_scores = jnp.where(sink_valid, sink_scores, -1e30)

    mine = iota((requests, slots), 0)
    scores = [jnp.zeros((requests, slots), F32) for h in range(heads)]
    for r in range(requests):
        wait()
        for h in range(heads):
            found = lax.dot_general(
                query[h * requests : (h + 1) * requests], window[r, h, 0], across, preferred_element_type=F32
            )
            scores[h] = jnp.where(mine == r, found, scores[h])
    scores = jnp.concatenate(scores, axis=0) / root_size
    valid = iota((rows, slots), 1) >= sinks + slots - limit
    scores = jnp.where(valid, scores, -1e30)

    highest = jnp.maximum(
        jnp.maximum(jnp.max(scores, axis=-1, keepdims=True), jnp.max(sink_scores, axis=-1, keepdims=True)),
        self_scores,
    )
    window_exp = jnp.exp(scores - highest)
    sink_exp = jnp.where(sink_valid, jnp.exp(sink_scores - highest), 0.0)
    self_exp = jnp.exp(self_scores - highest)
    total = jnp.sum(window_exp, axis=-1, keepdims=True) + jnp.sum(sink_exp, axis=-1, keepdims=True) + self_exp
    window_weight = (window_exp / total).astype(BF16).astype(F32)
    sink_weight = pltpu.roll(sink_exp / total, sinks, 1).astype(BF16)
    self_weight = (self_exp / total).astype(BF16).astype(F32)
    mixture = dot(sink_weight, sink_rows) + self_weight * fresh_value
    mixed = [mixture[h * requests : (h + 1) * requests] for h in range(heads)]
    for r in range(requests):
        wait()
        for h in range(heads):
            own = jnp.where(mine == r, window_weight[h * requests : (h + 1) * requests], 0.0)
            mixed[h] = mixed[h] + dot(own.astype(BF16), window[r, h, 1])
    wait()
    result[...] = dot(jnp.concatenate(mixed, axis=1).astype(BF16), out_weight[...]).astype(result.dtype)


def attend_fast(hidden, own_lengths, sink_rows, window_rows, qkv_weight, out_weight):
    requests, width = hidden.shape
    heads, sinks, size = sink_rows.shape[1], sink_rows.shape[3], sink_rows.shape[4]
    qkv = qkv_weight.reshape(-1, size)
    out = out_weight.reshape(-1, width)
    return pl.pallas_call(
        lambda *refs: attend_kernel(heads, sinks, *refs),
        out_shape=jax.ShapeDtypeStruct((requests, width), BF16),
        in_specs=[HBM] * 6,
        out_specs=VMEM,
        scratch_shapes=[
            pltpu.VMEM(hidden.shape, BF16),
            pltpu.VMEM((1, requests), jnp.int32),
            pltpu.VMEM((sink_rows.size // size, size), BF16),
            pltpu.VMEM(qkv.shape, BF16),
            pltpu.VMEM(window_rows.shape, BF16),
            pltpu.VMEM(out.shape, BF16),
            pltpu.SemaphoreType.DMA((3,)),
            pltpu.SemaphoreType.DMA((8,)),
            pltpu.SemaphoreType.DMA((2, requests)),
            pltpu.SemaphoreType.DMA,
        ],
        compiler_params=pltpu.CompilerParams(vmem_limit_bytes=60 * MEGA),
        name="attend",
    )(
        hidden,
        own_lengths[None, :],
        sink_rows.reshape(-1, size),
        qkv,
        window_rows,
        out,
    )


def expert_kernel(chunks, near, far, *refs):
    w_in, refs = refs[:chunks], refs[chunks:]
    ids_hbm, route_hbm, out_hbm, terms, act, w_near, own_columns, rows_scr, ids, route, w_far, small_sems, out_sems = refs
    count, tokens, share = terms.shape
    group = 2 * count
    requests = tokens // group
    units = act.shape[1]
    chunk = units // chunks
    own = lax.axis_index("guide") * count + lax.axis_index("dp")
    first_expert = (own * lax.axis_size("mp") + lax.axis_index("mp")) * (units // FFE)
    out_copies = [
        pltpu.make_async_copy(
            out_hbm.at[:, pl.ds(pl.multiple_of((own ^ (first + j)) * share, share), share)],
            target.at[:, pl.ds(j * share, share)],
            out_sems.at[first + j],
        )
        for first, target in ((count, w_far), (0, w_near))
        for j in range(count)
    ]
    small_copies = [
        pltpu.make_async_copy(ids_hbm, ids, small_sems.at[0]),
        pltpu.make_async_copy(route_hbm, route, small_sems.at[1]),
    ]
    for copy in small_copies + out_copies:
        copy.start()
    for first, source in ((0, near), (count, far)):
        values = source[...].astype(F32)
        for i in range(count):
            start = pl.multiple_of((own ^ (first + i)) * requests, requests)
            rows_scr[pl.ds(start, requests), :] = values[i * requests : (i + 1) * requests]
    own_columns[...] = rows_scr[:, pl.ds(pl.multiple_of(own * share, share), share)]
    rows = rows_scr[...]
    moe_in = (rows * lax.rsqrt(jnp.mean(rows * rows, axis=-1, keepdims=True) + EPSILON)).astype(BF16)
    for copy in small_copies:
        copy.wait()
    per_stream = ids.shape[2]
    diagonal = iota((per_stream, per_stream), 0) == iota((per_stream, per_stream), 1)

    def factor_of(expert):
        columns = []
        for stream in range(2):
            row = jnp.sum(jnp.where(ids[stream] == expert, route[stream], 0.0), axis=0, keepdims=True)
            spread_out = jnp.broadcast_to(row, (per_stream, per_stream))
            columns.append(jnp.sum(jnp.where(diagonal, spread_out, 0.0), axis=-1, keepdims=True))
        return jnp.concatenate(columns, axis=0)

    for c in range(chunks):
        factor = factor_of(first_expert + c * chunk // FFE)
        gate = dot(moe_in, w_in[c][0])
        upward = dot(moe_in, w_in[c][1])
        act[:, c * chunk : (c + 1) * chunk] = (gate / (1.0 + jnp.exp(-gate)) * upward * factor).astype(BF16)
    for j in range(count):
        out_copies[j].wait()
        terms[j] = dot(act[...], w_far[:, j * share : (j + 1) * share]).astype(BF16)
    for copy in out_copies[count:]:
        copy.wait()


def experts_fast(near, far, expert_ids, route_weight, w_in, expert_out, share):
    width = near.shape[1]
    count = lax.axis_size("dp")
    tokens = 2 * near.shape[0]
    units = expert_out.shape[0]
    top = expert_ids.shape[-1]
    return pl.pallas_call(
        lambda *refs: expert_kernel(len(w_in), *refs),
        out_shape=[
            jax.ShapeDtypeStruct((count, tokens, share), BF16),
            jax.ShapeDtypeStruct((tokens, units), BF16),
            jax.ShapeDtypeStruct((units, count * share), BF16),
            jax.ShapeDtypeStruct((tokens, share), F32),
        ],
        in_specs=[VMEM] * (2 + len(w_in)) + [HBM] * 3,
        out_specs=[VMEM] * 4,
        scratch_shapes=[
            pltpu.VMEM((tokens, width), F32),
            pltpu.VMEM((2, top, tokens // 2), jnp.int32),
            pltpu.VMEM((2, top, tokens // 2), F32),
            pltpu.VMEM((units, count * share), BF16),
            pltpu.SemaphoreType.DMA((2,)),
            pltpu.SemaphoreType.DMA((2 * count,)),
        ],
        compiler_params=pltpu.CompilerParams(vmem_limit_bytes=29 * MEGA),
        name="experts",
    )(near, far, *w_in, jnp.swapaxes(expert_ids, 1, 2), jnp.swapaxes(route_weight, 1, 2), expert_out)


def down_kernel(act, weight, terms):
    count, _, share = terms.shape
    for j in range(count):
        terms[j] = dot(act[...], weight[:, j * share : (j + 1) * share]).astype(BF16)


def down_fast(act, weight, share):
    tokens, units = act.shape
    count = weight.shape[1] // share
    return pl.pallas_call(
        down_kernel,
        out_shape=jax.ShapeDtypeStruct((count, tokens, share), BF16),
        in_specs=[VMEM] * 2,
        out_specs=VMEM,
        compiler_params=pltpu.CompilerParams(vmem_limit_bytes=8 * MEGA),
        cost_estimate=pl.CostEstimate(
            flops=2 * tokens * units * count * share, bytes_accessed=2 * units * count * share, transcendentals=0
        ),
        name="down",
    )(act, weight)


def add_up(blocks):
    total = blocks[0][...].astype(F32)
    for block in blocks[1:]:
        total = total + block[...].astype(F32)
    return total


def sum_kernel(*refs):
    refs[-1][...] = add_up(refs[:-1]).astype(BF16)


def sum_fast(blocks):
    return pl.pallas_call(
        sum_kernel,
        out_shape=jax.ShapeDtypeStruct(blocks[0].shape, BF16),
        in_specs=[VMEM] * len(blocks),
        out_specs=VMEM,
        compiler_params=pltpu.CompilerParams(vmem_limit_bytes=8 * MEGA),
        name="add_up",
    )(*blocks)


def head_kernel(chunk, other, own_columns, left, right, weight, target):
    tokens = own_columns.shape[0]
    count, rows, _ = target.shape
    requests = rows // 2
    half_width = weight.shape[1] // 2
    per_half = half_width // chunk
    guide, own = lax.axis_index("guide"), lax.axis_index("dp")
    summed = own_columns[...] + (left[...].astype(F32) + right[...].astype(F32))

    def hand_out(values, start):
        for d in range(count):
            target[own ^ d, :, start : start + values.shape[1]] = jnp.concatenate(
                [values[d * requests : (d + 1) * requests], values[tokens // 2 + d * requests : tokens // 2 + (d + 1) * requests]],
                axis=0,
            ).astype(BF16)

    squares = jnp.broadcast_to(jnp.sum(summed * summed, axis=-1, keepdims=True), (tokens, NOTE))
    raw_in = summed.astype(BF16)
    half = 1 - guide if other else guide
    hand_out(squares, half_width)
    for c in range(per_half):
        first = pl.multiple_of(half * half_width + c * chunk, 128)
        hand_out(dot(raw_in, weight[:, pl.ds(first, chunk)]), c * chunk)


def head_fast(other, own_columns, left, right, weight):
    count = lax.axis_size("dp")
    tokens = own_columns.shape[0]
    half_width = weight.shape[1] // 2
    return pl.pallas_call(
        lambda *refs: head_kernel(256, other, *refs),
        out_shape=jax.ShapeDtypeStruct((count, tokens // count, half_width + NOTE), BF16),
        in_specs=[VMEM] * 4,
        out_specs=VMEM,
        compiler_params=pltpu.CompilerParams(vmem_limit_bytes=12 * MEGA),
        cost_estimate=pl.CostEstimate(
            flops=tokens * weight.size, bytes_accessed=weight.size, transcendentals=0
        ),
        name="head",
    )(own_columns, left, right, weight)


def pair_kernel(near, received, *results):
    for k, result in enumerate(results):
        result[...] = (near[k].astype(F32) + received[k].astype(F32)).astype(BF16)


def pair_fast(near, received):
    count = near.shape[0]
    return pl.pallas_call(
        pair_kernel,
        out_shape=[jax.ShapeDtypeStruct(near.shape[1:], BF16)] * count,
        in_specs=[VMEM, VMEM],
        out_specs=[VMEM] * count,
        compiler_params=pltpu.CompilerParams(vmem_limit_bytes=8 * MEGA),
        name="pair",
    )(near, received)


def guide_kernel(width, weight, *refs):
    result = refs[-1]
    requests, half_width = result.shape[0], result.shape[3]
    total = add_up(refs[:-1])
    scale = lax.rsqrt(total[:, half_width : half_width + 1] / width + EPSILON)
    diagonal = iota((requests, requests), 0) == iota((requests, requests), 1)
    guidance = jnp.broadcast_to(weight[...], (requests, requests))
    factor = jnp.sum(jnp.where(diagonal, guidance, 0.0), axis=-1, keepdims=True)
    guided = total[:requests, :half_width] * (scale[:requests] * factor) + total[requests:, :half_width] * (
        scale[requests:] * (1.0 - factor)
    )
    for r in range(requests):
        result[r, 0] = guided[r : r + 1]


def guide_fast(blocks, guidance, width):
    rows, columns = blocks[0].shape
    return pl.pallas_call(
        lambda *refs: guide_kernel(width, *refs),
        out_shape=jax.ShapeDtypeStruct((rows // 2, 1, 1, columns - NOTE), F32),
        in_specs=[VMEM] * (1 + len(blocks)),
        out_specs=VMEM,
        compiler_params=pltpu.CompilerParams(vmem_limit_bytes=12 * MEGA),
        name="guide",
    )(guidance[None, :], *blocks)


def fits(hidden, sink_rows, expert_in, vocab_weight):
    return (
        lax.axis_size(ROWS) == 8
        and lax.axis_size("mp") == 4
        and hidden.shape[0] == 8
        and sink_rows.shape[1] == 4
        and expert_in.shape[2] % (2 * FFE) == 0
        and vocab_weight.shape[0] % 128 == 0
        and vocab_weight.shape[1] % 512 == 0
    )


def fast_body(
    states,
    lengths,
    sink_cache,
    window_cache,
    qkv_weight,
    out_weight,
    expert_ids,
    route_weight,
    expert_in,
    expert_out,
    vocab_weight,
    guidance,
):
    hidden = states[0]
    partial_out = attend_fast(hidden, lengths[0], sink_cache[0], window_cache[0], qkv_weight, out_weight)
    chunk = expert_in.shape[2] // 4
    received = step(partial_out, "mp", 1)
    w0 = load_fast(expert_in, chunk, 0, lengths)
    pair = join_fast(True, [partial_out, received], w0)
    received = step(pair, "mp", 2)
    w1 = load_fast(expert_in, chunk, 1, pair)
    residual = join_fast(True, [hidden, pair, received], w1)
    blocks = swap([residual] * lax.axis_size("dp"), "dp")
    w2 = load_fast(expert_in, chunk, 2, residual)
    near = join_fast(False, blocks, w2)
    far = step(near, "guide", 1)
    w3 = load_fast(expert_in, chunk, 3, near)
    share = vocab_weight.shape[0]
    terms, act, w_near, own_columns = experts_fast(
        near, far, expert_ids, route_weight, [w0, w1, w2, w3], expert_out, share
    )
    received = step(terms, "guide", 1)
    part = sum_fast(swap(pair_fast(down_fast(act, w_near, share), received), "dp"))
    received = step(part, "mp", 1)
    pair = (part.astype(F32) + received.astype(F32)).astype(BF16)
    received = step(pair, "mp", 2)
    far = step(head_fast(True, own_columns, pair, received, vocab_weight), "guide", 1)
    near = head_fast(False, own_columns, pair, received, vocab_weight)
    logits = swap(pair_fast(near, far), "dp")
    return guide_fast(logits, guidance, hidden.shape[1])


def rotate(vectors, positions):
    full_width = vectors.shape[-1]
    half_width = full_width // 2
    step_index = jnp.arange(half_width, dtype=jnp.float32)
    inverse = jnp.exp(step_index * (-2.0 * math.log(10000.0) / full_width))
    angles = positions.astype(jnp.float32)[:, None] * inverse[None, :]
    cosine = jnp.cos(angles)[:, None, :]
    sine_part = jnp.sin(angles)[:, None, :]
    first_half = vectors[..., :half_width]
    second = vectors[..., half_width:]
    return jnp.concatenate(
        [first_half * cosine - second * sine_part, second * cosine + first_half * sine_part],
        axis=-1,
    )


def rms_norm(values):
    return values * lax.rsqrt(jnp.mean(values * values, axis=-1, keepdims=True) + EPSILON)


def attend(hidden, own_lengths, sink_rows, window_rows, qkv_weight, out_weight):
    normed = rms_norm(hidden.astype(jnp.float32)).astype(jnp.bfloat16)
    projected = jnp.einsum("rd,dthe->rthe", normed, qkv_weight, preferred_element_type=jnp.float32)
    query_rot = rotate(projected[:, 0], own_lengths).astype(jnp.bfloat16)
    fresh_key = rotate(projected[:, 1], own_lengths).astype(jnp.bfloat16)
    fresh_value = projected[:, 2].astype(jnp.bfloat16)
    sink_count = sink_rows.shape[3]
    window_count = window_rows.shape[3]
    root_size = math.sqrt(query_rot.shape[-1])
    sink_scores = (
        jnp.einsum(
            "rhe,rhse->rhs", query_rot, sink_rows[:, :, 0], preferred_element_type=jnp.float32
        )
        / root_size
    )
    window_scores = (
        jnp.einsum(
            "rhe,rhwe->rhw", query_rot, window_rows[:, :, 0], preferred_element_type=jnp.float32
        )
        / root_size
    )
    self_scores = (
        jnp.einsum("rhe,rhe->rh", query_rot, fresh_key, preferred_element_type=jnp.float32)
        / root_size
    )
    length_limit = own_lengths[:, None, None]
    sink_valid = jnp.arange(sink_count, dtype=jnp.int32)[None, None, :] < length_limit
    window_valid = (
        jnp.arange(window_count, dtype=jnp.int32)[None, None, :]
        >= sink_count + window_count - length_limit
    )
    sink_scores = jnp.where(sink_valid, sink_scores, -1e30)
    window_scores = jnp.where(window_valid, window_scores, -1e30)
    highest = jnp.maximum(
        jnp.maximum(jnp.max(sink_scores, axis=-1), jnp.max(window_scores, axis=-1)), self_scores
    )
    sink_exp = jnp.exp(sink_scores - highest[..., None])
    window_exp = jnp.exp(window_scores - highest[..., None])
    self_exp = jnp.exp(self_scores - highest)
    totals = jnp.sum(sink_exp, axis=-1) + jnp.sum(window_exp, axis=-1) + self_exp
    sink_prob = (sink_exp / totals[..., None]).astype(jnp.bfloat16)
    window_prob = (window_exp / totals[..., None]).astype(jnp.bfloat16)
    self_prob = (self_exp / totals).astype(jnp.bfloat16)
    mixture = (
        jnp.einsum(
            "rhs,rhse->rhe", sink_prob, sink_rows[:, :, 1], preferred_element_type=jnp.float32
        )
        + jnp.einsum(
            "rhw,rhwe->rhe", window_prob, window_rows[:, :, 1], preferred_element_type=jnp.float32
        )
        + self_prob[..., None].astype(jnp.float32) * fresh_value.astype(jnp.float32)
    ).astype(jnp.bfloat16)
    return jnp.einsum("rhe,hed->rd", mixture, out_weight, preferred_element_type=jnp.float32)


def body(
    states,
    lengths,
    sink_cache,
    window_cache,
    qkv_weight,
    out_weight,
    expert_ids,
    route_weight,
    expert_in,
    expert_out,
    vocab_weight,
    guidance,
):
    hidden = states[0]
    if fits(hidden, sink_cache[0], expert_in, vocab_weight):
        return fast_body(
            states,
            lengths,
            sink_cache,
            window_cache,
            qkv_weight,
            out_weight,
            expert_ids,
            route_weight,
            expert_in,
            expert_out,
            vocab_weight,
            guidance,
        )
    request_count, width = hidden.shape
    group = lax.axis_size(ROWS)
    mp = lax.axis_size("mp")
    tokens = group * request_count

    partial_out = attend(hidden, lengths[0], sink_cache[0], window_cache[0], qkv_weight, out_weight)
    first = lax.axis_index("mp") == 0
    partial_out = partial_out + jnp.where(first, hidden.astype(jnp.float32), 0.0)
    partials = spread(partial_out.astype(jnp.bfloat16), ALL).reshape(group, mp, request_count, width)
    residual = jnp.sum(partials.astype(jnp.float32), axis=1).reshape(tokens, width).astype(jnp.bfloat16)
    moe_in = rms_norm(residual.astype(jnp.float32)).astype(jnp.bfloat16)

    unit_count = expert_in.shape[2]
    unit_start = lax.axis_index(ALL) * unit_count
    unit_expert = (unit_start + jnp.arange(unit_count, dtype=jnp.int32)) // FFE
    choice_rows = expert_ids.reshape(-1, expert_ids.shape[-1])
    route_rows = route_weight.reshape(-1, route_weight.shape[-1])
    coefficient = jnp.sum(
        jnp.where(
            choice_rows[:, :, None] == unit_expert[None, None, :], route_rows[:, :, None], 0.0
        ),
        axis=1,
    )
    gate = jnp.dot(moe_in, expert_in[0], preferred_element_type=jnp.float32)
    upward = jnp.dot(moe_in, expert_in[1], preferred_element_type=jnp.float32)
    activated = (jax.nn.silu(gate) * upward * coefficient).astype(jnp.bfloat16)
    expert_terms = jnp.dot(activated, expert_out, preferred_element_type=jnp.float32).astype(jnp.bfloat16)

    share = vocab_weight.shape[0]
    sent = jnp.swapaxes(expert_terms.reshape(tokens, group, share), 0, 1)
    expert_part = jnp.sum(trade(sent, ROWS).astype(jnp.float32), axis=0)
    expert_total = jnp.sum(spread(expert_part.astype(jnp.bfloat16), "mp").astype(jnp.float32), axis=0)
    own_columns = lax.dynamic_slice_in_dim(residual, lax.axis_index(ROWS) * share, share, 1)
    summed = own_columns.astype(jnp.float32) + expert_total

    squares = jnp.sum(summed * summed, axis=-1)
    notes = spread(jnp.concatenate([squares, guidance]), ROWS)
    scale = lax.rsqrt(jnp.sum(notes[:, :tokens], axis=0) / width + EPSILON).reshape(2, -1, 1)
    weight = notes[: group // 2, tokens:].reshape(-1, 1)

    raw = jnp.dot(summed.astype(jnp.bfloat16), vocab_weight, preferred_element_type=jnp.float32)
    raw = raw.reshape(2, tokens // 2, -1)
    mixed = raw[0] * (scale[0] * weight) + raw[1] * (scale[1] * (1.0 - weight))
    half_width = mixed.shape[1] // 2
    mixed = mixed.astype(jnp.bfloat16).reshape(group // 2, request_count, 2, half_width)
    sent = jnp.transpose(mixed, (2, 0, 1, 3)).reshape(group, request_count, half_width)
    guided = jnp.sum(trade(sent, ROWS).astype(jnp.float32), axis=0)
    return guided.reshape(request_count, 1, 1, half_width)


def solution(mesh):
    in_specs = (
        P("guide", "dp", None),
        P("guide", "dp"),
        P("guide", "dp", "mp", None, None, None),
        P("guide", "dp", "mp", None, None, None),
        P(None, None, "mp", None),
        P("mp", None, None),
        P(),
        P(),
        P(None, None, ("guide", "dp", "mp")),
        P(("guide", "dp", "mp"), None),
        P(("guide", "dp"), "mp"),
        P("dp"),
    )
    out_specs = P("dp", "mp", "guide", None)
    return jax.shard_map(body, mesh=mesh, in_specs=in_specs, out_specs=out_specs, check_vma=False)
```

```python
import math

import jax
import jax.numpy as jnp
from jax import lax
from jax.experimental import pallas as pl
from jax.experimental.pallas import tpu as pltpu
from jax.sharding import PartitionSpec as P

FFE = 1024

EPSILON = 1e-05

ROWS = ("guide", "dp")
ALL = ("guide", "dp", "mp")


def trade(blocks, axis):
    return lax.all_to_all(blocks, axis, 0, 0, tiled=True)


def spread(block, axis):
    return trade(jnp.broadcast_to(block[None], (lax.axis_size(axis),) + block.shape), axis)


def step(block, axis, bit):
    count = lax.axis_size(axis)
    return lax.ppermute(block, axis, [(i, i ^ bit) for i in range(count)])


def swap(blocks, axis):
    return [blocks[0]] + [step(blocks[j], axis, j) for j in range(1, lax.axis_size(axis))]


F32 = jnp.float32
BF16 = jnp.bfloat16
VMEM = pl.BlockSpec(memory_space=pltpu.VMEM)
ANY = pl.BlockSpec(memory_space=pl.ANY)
HBM = pl.BlockSpec(memory_space=pltpu.HBM)
MEGA = 1 << 20
NOTE = 128


def dot(left, right):
    return jnp.dot(left, right, preferred_element_type=F32)


def iota(shape, dim):
    return lax.broadcasted_iota(jnp.int32, shape, dim)


def load_kernel(first, chunk, hbm, after, result, sems):
    rows = hbm.shape[1] // sems.shape[1]
    copies = [
        pltpu.make_async_copy(
            hbm.at[k, pl.ds(i * rows, rows), pl.ds(first, chunk)],
            result.at[k, pl.ds(i * rows, rows), :],
            sems.at[k, i],
        )
        for k in range(hbm.shape[0])
        for i in range(sems.shape[1])
    ]
    for copy in copies:
        copy.start()
    for copy in copies:
        copy.wait()


def load_fast(weight, first, chunk, room, after):
    kinds, width, _ = weight.shape
    return pl.pallas_call(
        lambda *refs: load_kernel(first, chunk, *refs),
        out_shape=jax.ShapeDtypeStruct((kinds, width, chunk), BF16),
        in_specs=[HBM, ANY],
        out_specs=VMEM,
        scratch_shapes=[pltpu.SemaphoreType.DMA((kinds, 4))],
        compiler_params=pltpu.CompilerParams(vmem_limit_bytes=room * MEGA),
        cost_estimate=pl.CostEstimate(flops=0, bytes_accessed=4 * kinds * width * chunk, transcendentals=0),
        name="load",
    )(weight, after)


def join_kernel(total, count, *refs):
    values = [ref[...].astype(F32) for ref in refs[:count]]
    joined = sum(values[1:], values[0]) if total else jnp.concatenate(values, axis=0)
    refs[-1][...] = joined.astype(BF16)


def join_fast(total, blocks, after):
    rows, columns = blocks[0].shape
    return pl.pallas_call(
        lambda *refs: join_kernel(total, len(blocks), *refs),
        out_shape=jax.ShapeDtypeStruct((rows if total else rows * len(blocks), columns), BF16),
        in_specs=[VMEM] * len(blocks) + [ANY],
        out_specs=VMEM,
        compiler_params=pltpu.CompilerParams(vmem_limit_bytes=4 * MEGA),
        name="join",
    )(*blocks, after)


def attend_kernel(
    heads, sinks, states_hbm, lengths_hbm, sink_hbm, qkv_hbm, window_hbm, out_hbm, result,
    states, lengths, sink, qkv, window, out_weight, spread_out, first_sems, qkv_sems, window_sems, out_sem,
):
    requests, width = states.shape
    size = sink.shape[1]
    parts = 3 * heads
    lanes = size * parts
    blocks = width // size
    chunks = qkv_sems.shape[0]
    chunk_rows = qkv.shape[0] // chunks
    slots = window.shape[3]
    rows = heads * requests
    qkv_copies = [
        pltpu.make_async_copy(
            qkv_hbm.at[pl.ds(c * chunk_rows, chunk_rows)], qkv.at[pl.ds(c * chunk_rows, chunk_rows)], qkv_sems.at[c]
        )
        for c in range(chunks)
    ]
    key_copies, value_copies = [
        [
            pltpu.make_async_copy(window_hbm.at[r, :, k], window.at[r, :, k], window_sems.at[k, r])
            for r in range(requests)
        ]
        for k in range(2)
    ]
    out_copy = pltpu.make_async_copy(out_hbm, out_weight, out_sem)
    first_copies = [
        pltpu.make_async_copy(source, target, first_sems.at[i])
        for i, (source, target) in enumerate(((states_hbm, states), (lengths_hbm, lengths), (sink_hbm, sink)))
    ]
    for copy in first_copies + qkv_copies:
        copy.start()
    sub, lane = iota((size, lanes), 0) * parts, iota((size, lanes), 1)
    repeat = jnp.where((lane >= sub) & (lane < sub + parts), 1.0, 0.0).astype(BF16)
    kind = lax.rem(iota((requests, lanes), 1), parts)
    for copy in first_copies:
        copy.wait()
    hidden = states[...].astype(F32)
    normed = hidden * lax.rsqrt(jnp.mean(hidden * hidden, axis=-1, keepdims=True) + EPSILON)
    stacked = jnp.concatenate([normed[:, b * size : (b + 1) * size] for b in range(blocks)], axis=0)
    repeated = dot(stacked.astype(BF16), repeat)
    for b in range(blocks):
        piece = repeated[b * requests : (b + 1) * requests]
        spread_out[:, b * lanes : (b + 1) * lanes] = jnp.concatenate(
            [jnp.where(kind == p, piece, 0.0) for p in range(parts)], axis=0
        ).astype(BF16)

    length_row = jnp.broadcast_to(lengths[...], (requests, requests))
    diagonal = iota((requests, requests), 0) == iota((requests, requests), 1)
    length = jnp.sum(jnp.where(diagonal, length_row, 0), axis=-1, keepdims=True)
    lane_id = iota((requests, size), 1)
    low = lane_id < size // 2
    pair_index = jnp.where(low, lane_id, lane_id - size // 2).astype(F32)
    angles = length.astype(F32) * jnp.exp(pair_index * (-2.0 * math.log(10000.0) / size))
    cosine, sine = jnp.cos(angles), jnp.sin(angles)
    sine = jnp.where(low, -sine, sine)

    projected = jnp.zeros((parts * requests, size), F32)
    later = [key_copies, value_copies, [out_copy]]
    for c in range(chunks):
        qkv_copies[c].wait()
        for copy in later[c] if c < len(later) else []:
            copy.start()
        part = slice(c * chunk_rows, (c + 1) * chunk_rows)
        projected = projected + dot(spread_out[:, part], qkv[part, :])

    cos_rows = jnp.concatenate([cosine] * heads, axis=0)
    sin_rows = jnp.concatenate([sine] * heads, axis=0)
    limit = jnp.concatenate([length] * heads, axis=0)

    def turn(values):
        return (values * cos_rows + pltpu.roll(values, size // 2, 1) * sin_rows).astype(BF16)

    query = turn(projected[:rows])
    fresh_key = turn(projected[rows : 2 * rows])
    fresh_value = projected[2 * rows :].astype(BF16).astype(F32)
    root_size = math.sqrt(size)
    across = (((1,), (1,)), ((), ()))

    self_scores = jnp.sum(query.astype(F32) * fresh_key.astype(F32), axis=-1, keepdims=True) / root_size
    sink_rows = sink[...]
    sink_total = sink_rows.shape[0]
    sink_scores = lax.dot_general(query, sink_rows, across, preferred_element_type=F32) / root_size
    row_id, column = iota((rows, sink_total), 0), iota((rows, sink_total), 1)
    slot = lax.rem(column, 2 * sinks)
    pair = lax.div(column, 2 * sinks)
    sink_valid = (
        (lax.rem(pair, heads) == lax.div(row_id, requests))
        & (lax.div(pair, heads) == lax.rem(row_id, requests))
        & (slot < sinks)
        & (slot < limit)
    )
    sink_scores = jnp.where(sink_valid, sink_scores, -1e30)

    mine = iota((requests, slots), 0)
    for copy in key_copies:
        copy.wait()
    scores = []
    for h in range(heads):
        keys = window[:, h, 0].reshape(requests * slots, size)
        found = lax.dot_general(query[h * requests : (h + 1) * requests], keys, across, preferred_element_type=F32)
        own = jnp.where(mine == 0, found[:, :slots], 0.0)
        for r in range(1, requests):
            own = jnp.where(mine == r, found[:, r * slots : (r + 1) * slots], own)
        scores.append(own)
    scores = jnp.concatenate(scores, axis=0) / root_size
    valid = iota((rows, slots), 1) >= sinks + slots - limit
    scores = jnp.where(valid, scores, -1e30)

    highest = jnp.maximum(
        jnp.maximum(jnp.max(scores, axis=-1, keepdims=True), jnp.max(sink_scores, axis=-1, keepdims=True)),
        self_scores,
    )
    window_exp = jnp.exp(scores - highest)
    sink_exp = jnp.where(sink_valid, jnp.exp(sink_scores - highest), 0.0)
    self_exp = jnp.exp(self_scores - highest)
    total = jnp.sum(window_exp, axis=-1, keepdims=True) + jnp.sum(sink_exp, axis=-1, keepdims=True) + self_exp
    window_weight = (window_exp / total).astype(BF16).astype(F32)
    sink_weight = pltpu.roll(sink_exp / total, sinks, 1).astype(BF16)
    self_weight = (self_exp / total).astype(BF16).astype(F32)
    mixture = dot(sink_weight, sink_rows) + self_weight * fresh_value
    for copy in value_copies:
        copy.wait()
    mixed = []
    for h in range(heads):
        own = window_weight[h * requests : (h + 1) * requests]
        wide = jnp.concatenate([jnp.where(mine == r, own, 0.0) for r in range(requests)], axis=1).astype(BF16)
        values = window[:, h, 1].reshape(requests * slots, size)
        mixed.append(mixture[h * requests : (h + 1) * requests] + dot(wide, values))
    out_copy.wait()
    result[...] = dot(jnp.concatenate(mixed, axis=1).astype(BF16), out_weight[...]).astype(result.dtype)


def attend_fast(hidden, own_lengths, sink_rows, window_rows, qkv_weight, out_weight):
    requests, width = hidden.shape
    heads, sinks, size = sink_rows.shape[1], sink_rows.shape[3], sink_rows.shape[4]
    qkv = qkv_weight.reshape(-1, size)
    out = out_weight.reshape(-1, width)
    return pl.pallas_call(
        lambda *refs: attend_kernel(heads, sinks, *refs),
        out_shape=jax.ShapeDtypeStruct((requests, width), BF16),
        in_specs=[HBM] * 6,
        out_specs=VMEM,
        scratch_shapes=[
            pltpu.VMEM(hidden.shape, BF16),
            pltpu.VMEM((1, requests), jnp.int32),
            pltpu.VMEM((sink_rows.size // size, size), BF16),
            pltpu.VMEM(qkv.shape, BF16),
            pltpu.VMEM(window_rows.shape, BF16),
            pltpu.VMEM(out.shape, BF16),
            pltpu.VMEM((3 * heads * requests, qkv.shape[0]), BF16),
            pltpu.SemaphoreType.DMA((3,)),
            pltpu.SemaphoreType.DMA((4,)),
            pltpu.SemaphoreType.DMA((2, requests)),
            pltpu.SemaphoreType.DMA,
        ],
        compiler_params=pltpu.CompilerParams(vmem_limit_bytes=60 * MEGA),
        name="attend",
    )(
        hidden,
        own_lengths[None, :],
        sink_rows.reshape(-1, size),
        qkv,
        window_rows,
        out,
    )


def expert_kernel(chunks, near, far, *refs):
    w_in, refs = refs[:chunks], refs[chunks:]
    ids_hbm, route_hbm, out_hbm, terms, act, w_near, own_columns, rows_scr, ids, route, w_far, small_sems, out_sems = refs
    count, tokens, share = terms.shape
    group = 2 * count
    requests = tokens // group
    units = act.shape[1]
    own = lax.axis_index("guide") * count + lax.axis_index("dp")
    first_expert = (own * lax.axis_size("mp") + lax.axis_index("mp")) * (units // FFE)
    out_copies = [
        pltpu.make_async_copy(
            out_hbm.at[:, pl.ds(pl.multiple_of((own ^ (first + j)) * share, share), share)],
            target.at[:, pl.ds(j * share, share)],
            out_sems.at[first + j],
        )
        for first, target in ((count, w_far), (0, w_near))
        for j in range(count)
    ]
    small_copies = [
        pltpu.make_async_copy(ids_hbm, ids, small_sems.at[0]),
        pltpu.make_async_copy(route_hbm, route, small_sems.at[1]),
    ]
    for copy in small_copies + out_copies:
        copy.start()
    for first, source in ((0, near), (count, far)):
        values = source[...].astype(F32)
        for i in range(count):
            start = pl.multiple_of((own ^ (first + i)) * requests, requests)
            rows_scr[pl.ds(start, requests), :] = values[i * requests : (i + 1) * requests]
    own_columns[...] = rows_scr[:, pl.ds(pl.multiple_of(own * share, share), share)]
    rows = rows_scr[...]
    moe_in = (rows * lax.rsqrt(jnp.mean(rows * rows, axis=-1, keepdims=True) + EPSILON)).astype(BF16)
    for copy in small_copies:
        copy.wait()
    per_stream = ids.shape[2]
    diagonal = iota((per_stream, per_stream), 0) == iota((per_stream, per_stream), 1)

    def factor_of(expert):
        columns = []
        for stream in range(2):
            row = jnp.sum(jnp.where(ids[stream] == expert, route[stream], 0.0), axis=0, keepdims=True)
            spread_out = jnp.broadcast_to(row, (per_stream, per_stream))
            columns.append(jnp.sum(jnp.where(diagonal, spread_out, 0.0), axis=-1, keepdims=True))
        return jnp.concatenate(columns, axis=0)

    start = 0
    for weight in w_in:
        unit, start = start, start + weight.shape[2]
        factor = factor_of(first_expert + unit // FFE)
        gate = dot(moe_in, weight[0])
        upward = dot(moe_in, weight[1])
        act[:, unit:start] = (gate / (1.0 + jnp.exp(-gate)) * upward * factor).astype(BF16)
    for j in range(count):
        out_copies[j].wait()
        terms[j] = dot(act[...], w_far[:, j * share : (j + 1) * share]).astype(BF16)
    for copy in out_copies[count:]:
        copy.wait()


def experts_fast(near, far, expert_ids, route_weight, w_in, expert_out, share):
    width = near.shape[1]
    count = lax.axis_size("dp")
    tokens = 2 * near.shape[0]
    units = expert_out.shape[0]
    top = expert_ids.shape[-1]
    return pl.pallas_call(
        lambda *refs: expert_kernel(len(w_in), *refs),
        out_shape=[
            jax.ShapeDtypeStruct((count, tokens, share), BF16),
            jax.ShapeDtypeStruct((tokens, units), BF16),
            jax.ShapeDtypeStruct((units, count * share), BF16),
            jax.ShapeDtypeStruct((tokens, share), F32),
        ],
        in_specs=[VMEM] * (2 + len(w_in)) + [HBM] * 3,
        out_specs=[VMEM] * 4,
        scratch_shapes=[
            pltpu.VMEM((tokens, width), F32),
            pltpu.VMEM((2, top, tokens // 2), jnp.int32),
            pltpu.VMEM((2, top, tokens // 2), F32),
            pltpu.VMEM((units, count * share), BF16),
            pltpu.SemaphoreType.DMA((2,)),
            pltpu.SemaphoreType.DMA((2 * count,)),
        ],
        compiler_params=pltpu.CompilerParams(vmem_limit_bytes=29 * MEGA),
        name="experts",
    )(near, far, *w_in, jnp.swapaxes(expert_ids, 1, 2), jnp.swapaxes(route_weight, 1, 2), expert_out)


def down_kernel(act, weight, terms):
    count, _, share = terms.shape
    for j in range(count):
        terms[j] = dot(act[...], weight[:, j * share : (j + 1) * share]).astype(BF16)


def down_fast(act, weight, share):
    tokens, units = act.shape
    count = weight.shape[1] // share
    return pl.pallas_call(
        down_kernel,
        out_shape=jax.ShapeDtypeStruct((count, tokens, share), BF16),
        in_specs=[VMEM] * 2,
        out_specs=VMEM,
        compiler_params=pltpu.CompilerParams(vmem_limit_bytes=8 * MEGA),
        cost_estimate=pl.CostEstimate(
            flops=2 * tokens * units * count * share, bytes_accessed=2 * units * count * share, transcendentals=0
        ),
        name="down",
    )(act, weight)


def add_up(blocks):
    total = blocks[0][...].astype(F32)
    for block in blocks[1:]:
        total = total + block[...].astype(F32)
    return total


def sum_kernel(*refs):
    refs[-1][...] = add_up(refs[:-1]).astype(BF16)


def sum_fast(blocks):
    return pl.pallas_call(
        sum_kernel,
        out_shape=jax.ShapeDtypeStruct(blocks[0].shape, BF16),
        in_specs=[VMEM] * len(blocks),
        out_specs=VMEM,
        compiler_params=pltpu.CompilerParams(vmem_limit_bytes=8 * MEGA),
        name="add_up",
    )(*blocks)


def head_kernel(chunk, other, own_columns, left, right, weight, target):
    tokens = own_columns.shape[0]
    count, rows, _ = target.shape
    requests = rows // 2
    half_width = weight.shape[1] // 2
    per_half = half_width // chunk
    guide, own = lax.axis_index("guide"), lax.axis_index("dp")
    summed = own_columns[...] + (left[...].astype(F32) + right[...].astype(F32))

    def hand_out(values, start):
        for d in range(count):
            target[own ^ d, :, start : start + values.shape[1]] = jnp.concatenate(
                [values[d * requests : (d + 1) * requests], values[tokens // 2 + d * requests : tokens // 2 + (d + 1) * requests]],
                axis=0,
            ).astype(BF16)

    squares = jnp.broadcast_to(jnp.sum(summed * summed, axis=-1, keepdims=True), (tokens, NOTE))
    raw_in = summed.astype(BF16)
    half = 1 - guide if other else guide
    hand_out(squares, half_width)
    for c in range(per_half):
        first = pl.multiple_of(half * half_width + c * chunk, 128)
        hand_out(dot(raw_in, weight[:, pl.ds(first, chunk)]), c * chunk)


def head_fast(other, own_columns, left, right, weight):
    count = lax.axis_size("dp")
    tokens = own_columns.shape[0]
    half_width = weight.shape[1] // 2
    return pl.pallas_call(
        lambda *refs: head_kernel(256, other, *refs),
        out_shape=jax.ShapeDtypeStruct((count, tokens // count, half_width + NOTE), BF16),
        in_specs=[VMEM] * 4,
        out_specs=VMEM,
        compiler_params=pltpu.CompilerParams(vmem_limit_bytes=12 * MEGA),
        cost_estimate=pl.CostEstimate(
            flops=tokens * weight.size, bytes_accessed=weight.size, transcendentals=0
        ),
        name="head",
    )(own_columns, left, right, weight)


def pair_kernel(near, received, *results):
    for k, result in enumerate(results):
        result[...] = (near[k].astype(F32) + received[k].astype(F32)).astype(BF16)


def pair_fast(near, received):
    count = near.shape[0]
    return pl.pallas_call(
        pair_kernel,
        out_shape=[jax.ShapeDtypeStruct(near.shape[1:], BF16)] * count,
        in_specs=[VMEM, VMEM],
        out_specs=[VMEM] * count,
        compiler_params=pltpu.CompilerParams(vmem_limit_bytes=8 * MEGA),
        name="pair",
    )(near, received)


def guide_kernel(width, weight, *refs):
    result = refs[-1]
    requests, half_width = result.shape[0], result.shape[3]
    total = add_up(refs[:-1])
    scale = lax.rsqrt(total[:, half_width : half_width + 1] / width + EPSILON)
    diagonal = iota((requests, requests), 0) == iota((requests, requests), 1)
    guidance = jnp.broadcast_to(weight[...], (requests, requests))
    factor = jnp.sum(jnp.where(diagonal, guidance, 0.0), axis=-1, keepdims=True)
    guided = total[:requests, :half_width] * (scale[:requests] * factor) + total[requests:, :half_width] * (
        scale[requests:] * (1.0 - factor)
    )
    for r in range(requests):
        result[r, 0] = guided[r : r + 1]


def guide_fast(blocks, guidance, width):
    rows, columns = blocks[0].shape
    return pl.pallas_call(
        lambda *refs: guide_kernel(width, *refs),
        out_shape=jax.ShapeDtypeStruct((rows // 2, 1, 1, columns - NOTE), F32),
        in_specs=[VMEM] * (1 + len(blocks)),
        out_specs=VMEM,
        compiler_params=pltpu.CompilerParams(vmem_limit_bytes=12 * MEGA),
        name="guide",
    )(guidance[None, :], *blocks)


def fits(hidden, sink_rows, expert_in, vocab_weight):
    return (
        lax.axis_size(ROWS) == 8
        and lax.axis_size("mp") == 4
        and hidden.shape[0] == 8
        and sink_rows.shape[1] == 4
        and expert_in.shape[2] % (2 * FFE) == 0
        and vocab_weight.shape[0] % 128 == 0
        and vocab_weight.shape[1] % 512 == 0
    )


def fast_body(
    states,
    lengths,
    sink_cache,
    window_cache,
    qkv_weight,
    out_weight,
    expert_ids,
    route_weight,
    expert_in,
    expert_out,
    vocab_weight,
    guidance,
):
    hidden = states[0]
    partial_out = attend_fast(hidden, lengths[0], sink_cache[0], window_cache[0], qkv_weight, out_weight)
    chunk = expert_in.shape[2] // 4
    received = step(partial_out, "mp", 1)
    w0 = load_fast(expert_in, 0, chunk, 47, lengths)
    pair = join_fast(True, [partial_out, received], w0)
    received = step(pair, "mp", 2)
    w1 = load_fast(expert_in, chunk, chunk, 43, pair)
    residual = join_fast(True, [hidden, pair, received], w1)
    blocks = swap([residual] * lax.axis_size("dp"), "dp")
    w2 = load_fast(expert_in, 2 * chunk, chunk, 39, residual)
    near = join_fast(False, blocks, w2)
    far = step(near, "guide", 1)
    w3 = load_fast(expert_in, 3 * chunk, chunk, 35, near)
    share = vocab_weight.shape[0]
    terms, act, w_near, own_columns = experts_fast(
        near, far, expert_ids, route_weight, [w0, w1, w2, w3], expert_out, share
    )
    received = step(terms, "guide", 1)
    part = sum_fast(swap(pair_fast(down_fast(act, w_near, share), received), "dp"))
    received = step(part, "mp", 1)
    pair = (part.astype(F32) + received.astype(F32)).astype(BF16)
    received = step(pair, "mp", 2)
    far = step(head_fast(True, own_columns, pair, received, vocab_weight), "guide", 1)
    near = head_fast(False, own_columns, pair, received, vocab_weight)
    logits = swap(pair_fast(near, far), "dp")
    return guide_fast(logits, guidance, hidden.shape[1])


def rotate(vectors, positions):
    full_width = vectors.shape[-1]
    half_width = full_width // 2
    step_index = jnp.arange(half_width, dtype=jnp.float32)
    inverse = jnp.exp(step_index * (-2.0 * math.log(10000.0) / full_width))
    angles = positions.astype(jnp.float32)[:, None] * inverse[None, :]
    cosine = jnp.cos(angles)[:, None, :]
    sine_part = jnp.sin(angles)[:, None, :]
    first_half = vectors[..., :half_width]
    second = vectors[..., half_width:]
    return jnp.concatenate(
        [first_half * cosine - second * sine_part, second * cosine + first_half * sine_part],
        axis=-1,
    )


def rms_norm(values):
    return values * lax.rsqrt(jnp.mean(values * values, axis=-1, keepdims=True) + EPSILON)


def attend(hidden, own_lengths, sink_rows, window_rows, qkv_weight, out_weight):
    normed = rms_norm(hidden.astype(jnp.float32)).astype(jnp.bfloat16)
    projected = jnp.einsum("rd,dthe->rthe", normed, qkv_weight, preferred_element_type=jnp.float32)
    query_rot = rotate(projected[:, 0], own_lengths).astype(jnp.bfloat16)
    fresh_key = rotate(projected[:, 1], own_lengths).astype(jnp.bfloat16)
    fresh_value = projected[:, 2].astype(jnp.bfloat16)
    sink_count = sink_rows.shape[3]
    window_count = window_rows.shape[3]
    root_size = math.sqrt(query_rot.shape[-1])
    sink_scores = (
        jnp.einsum(
            "rhe,rhse->rhs", query_rot, sink_rows[:, :, 0], preferred_element_type=jnp.float32
        )
        / root_size
    )
    window_scores = (
        jnp.einsum(
            "rhe,rhwe->rhw", query_rot, window_rows[:, :, 0], preferred_element_type=jnp.float32
        )
        / root_size
    )
    self_scores = (
        jnp.einsum("rhe,rhe->rh", query_rot, fresh_key, preferred_element_type=jnp.float32)
        / root_size
    )
    length_limit = own_lengths[:, None, None]
    sink_valid = jnp.arange(sink_count, dtype=jnp.int32)[None, None, :] < length_limit
    window_valid = (
        jnp.arange(window_count, dtype=jnp.int32)[None, None, :]
        >= sink_count + window_count - length_limit
    )
    sink_scores = jnp.where(sink_valid, sink_scores, -1e30)
    window_scores = jnp.where(window_valid, window_scores, -1e30)
    highest = jnp.maximum(
        jnp.maximum(jnp.max(sink_scores, axis=-1), jnp.max(window_scores, axis=-1)), self_scores
    )
    sink_exp = jnp.exp(sink_scores - highest[..., None])
    window_exp = jnp.exp(window_scores - highest[..., None])
    self_exp = jnp.exp(self_scores - highest)
    totals = jnp.sum(sink_exp, axis=-1) + jnp.sum(window_exp, axis=-1) + self_exp
    sink_prob = (sink_exp / totals[..., None]).astype(jnp.bfloat16)
    window_prob = (window_exp / totals[..., None]).astype(jnp.bfloat16)
    self_prob = (self_exp / totals).astype(jnp.bfloat16)
    mixture = (
        jnp.einsum(
            "rhs,rhse->rhe", sink_prob, sink_rows[:, :, 1], preferred_element_type=jnp.float32
        )
        + jnp.einsum(
            "rhw,rhwe->rhe", window_prob, window_rows[:, :, 1], preferred_element_type=jnp.float32
        )
        + self_prob[..., None].astype(jnp.float32) * fresh_value.astype(jnp.float32)
    ).astype(jnp.bfloat16)
    return jnp.einsum("rhe,hed->rd", mixture, out_weight, preferred_element_type=jnp.float32)


def body(
    states,
    lengths,
    sink_cache,
    window_cache,
    qkv_weight,
    out_weight,
    expert_ids,
    route_weight,
    expert_in,
    expert_out,
    vocab_weight,
    guidance,
):
    hidden = states[0]
    if fits(hidden, sink_cache[0], expert_in, vocab_weight):
        return fast_body(
            states,
            lengths,
            sink_cache,
            window_cache,
            qkv_weight,
            out_weight,
            expert_ids,
            route_weight,
            expert_in,
            expert_out,
            vocab_weight,
            guidance,
        )
    request_count, width = hidden.shape
    group = lax.axis_size(ROWS)
    mp = lax.axis_size("mp")
    tokens = group * request_count

    partial_out = attend(hidden, lengths[0], sink_cache[0], window_cache[0], qkv_weight, out_weight)
    first = lax.axis_index("mp") == 0
    partial_out = partial_out + jnp.where(first, hidden.astype(jnp.float32), 0.0)
    partials = spread(partial_out.astype(jnp.bfloat16), ALL).reshape(group, mp, request_count, width)
    residual = jnp.sum(partials.astype(jnp.float32), axis=1).reshape(tokens, width).astype(jnp.bfloat16)
    moe_in = rms_norm(residual.astype(jnp.float32)).astype(jnp.bfloat16)

    unit_count = expert_in.shape[2]
    unit_start = lax.axis_index(ALL) * unit_count
    unit_expert = (unit_start + jnp.arange(unit_count, dtype=jnp.int32)) // FFE
    choice_rows = expert_ids.reshape(-1, expert_ids.shape[-1])
    route_rows = route_weight.reshape(-1, route_weight.shape[-1])
    coefficient = jnp.sum(
        jnp.where(
            choice_rows[:, :, None] == unit_expert[None, None, :], route_rows[:, :, None], 0.0
        ),
        axis=1,
    )
    gate = jnp.dot(moe_in, expert_in[0], preferred_element_type=jnp.float32)
    upward = jnp.dot(moe_in, expert_in[1], preferred_element_type=jnp.float32)
    activated = (jax.nn.silu(gate) * upward * coefficient).astype(jnp.bfloat16)
    expert_terms = jnp.dot(activated, expert_out, preferred_element_type=jnp.float32).astype(jnp.bfloat16)

    share = vocab_weight.shape[0]
    sent = jnp.swapaxes(expert_terms.reshape(tokens, group, share), 0, 1)
    expert_part = jnp.sum(trade(sent, ROWS).astype(jnp.float32), axis=0)
    expert_total = jnp.sum(spread(expert_part.astype(jnp.bfloat16), "mp").astype(jnp.float32), axis=0)
    own_columns = lax.dynamic_slice_in_dim(residual, lax.axis_index(ROWS) * share, share, 1)
    summed = own_columns.astype(jnp.float32) + expert_total

    squares = jnp.sum(summed * summed, axis=-1)
    notes = spread(jnp.concatenate([squares, guidance]), ROWS)
    scale = lax.rsqrt(jnp.sum(notes[:, :tokens], axis=0) / width + EPSILON).reshape(2, -1, 1)
    weight = notes[: group // 2, tokens:].reshape(-1, 1)

    raw = jnp.dot(summed.astype(jnp.bfloat16), vocab_weight, preferred_element_type=jnp.float32)
    raw = raw.reshape(2, tokens // 2, -1)
    mixed = raw[0] * (scale[0] * weight) + raw[1] * (scale[1] * (1.0 - weight))
    half_width = mixed.shape[1] // 2
    mixed = mixed.astype(jnp.bfloat16).reshape(group // 2, request_count, 2, half_width)
    sent = jnp.transpose(mixed, (2, 0, 1, 3)).reshape(group, request_count, half_width)
    guided = jnp.sum(trade(sent, ROWS).astype(jnp.float32), axis=0)
    return guided.reshape(request_count, 1, 1, half_width)


def solution(mesh):
    in_specs = (
        P("guide", "dp", None),
        P("guide", "dp"),
        P("guide", "dp", "mp", None, None, None),
        P("guide", "dp", "mp", None, None, None),
        P(None, None, "mp", None),
        P("mp", None, None),
        P(),
        P(),
        P(None, None, ("guide", "dp", "mp")),
        P(("guide", "dp", "mp"), None),
        P(("guide", "dp"), "mp"),
        P("dp"),
    )
    out_specs = P("dp", "mp", "guide", None)
    return jax.shard_map(body, mesh=mesh, in_specs=in_specs, out_specs=out_specs, check_vma=False)
```

```python
import math

import jax
import jax.numpy as jnp
from jax import lax
from jax.experimental import pallas as pl
from jax.experimental.pallas import tpu as pltpu
from jax.sharding import PartitionSpec as P

FFE = 1024

EPSILON = 1e-05

ROWS = ("guide", "dp")
ALL = ("guide", "dp", "mp")


def trade(blocks, axis):
    return lax.all_to_all(blocks, axis, 0, 0, tiled=True)


def spread(block, axis):
    return trade(jnp.broadcast_to(block[None], (lax.axis_size(axis),) + block.shape), axis)


def step(block, axis, bit):
    count = lax.axis_size(axis)
    return lax.ppermute(block, axis, [(i, i ^ bit) for i in range(count)])


def swap(blocks, axis):
    return [blocks[0]] + [step(blocks[j], axis, j) for j in range(1, lax.axis_size(axis))]


F32 = jnp.float32
BF16 = jnp.bfloat16
VMEM = pl.BlockSpec(memory_space=pltpu.VMEM)
ANY = pl.BlockSpec(memory_space=pl.ANY)
HBM = pl.BlockSpec(memory_space=pltpu.HBM)
MEGA = 1 << 20
NOTE = 128


def dot(left, right):
    return jnp.dot(left, right, preferred_element_type=F32)


def iota(shape, dim):
    return lax.broadcasted_iota(jnp.int32, shape, dim)


def load_kernel(first, chunk, hbm, after, result, sems):
    rows = hbm.shape[1] // sems.shape[1]
    copies = [
        pltpu.make_async_copy(
            hbm.at[k, pl.ds(i * rows, rows), pl.ds(first, chunk)],
            result.at[k, pl.ds(i * rows, rows), :],
            sems.at[k, i],
        )
        for k in range(hbm.shape[0])
        for i in range(sems.shape[1])
    ]
    for copy in copies:
        copy.start()
    for copy in copies:
        copy.wait()


def load_fast(weight, first, chunk, room, after):
    kinds, width, _ = weight.shape
    return pl.pallas_call(
        lambda *refs: load_kernel(first, chunk, *refs),
        out_shape=jax.ShapeDtypeStruct((kinds, width, chunk), BF16),
        in_specs=[HBM, ANY],
        out_specs=VMEM,
        scratch_shapes=[pltpu.SemaphoreType.DMA((kinds, 4))],
        compiler_params=pltpu.CompilerParams(vmem_limit_bytes=room * MEGA),
        cost_estimate=pl.CostEstimate(flops=0, bytes_accessed=4 * kinds * width * chunk, transcendentals=0),
        name="load",
    )(weight, after)


def join_kernel(total, count, *refs):
    values = [ref[...].astype(F32) for ref in refs[:count]]
    joined = sum(values[1:], values[0]) if total else jnp.concatenate(values, axis=0)
    refs[-1][...] = joined.astype(BF16)


def join_fast(total, blocks, after):
    rows, columns = blocks[0].shape
    return pl.pallas_call(
        lambda *refs: join_kernel(total, len(blocks), *refs),
        out_shape=jax.ShapeDtypeStruct((rows if total else rows * len(blocks), columns), BF16),
        in_specs=[VMEM] * len(blocks) + [ANY],
        out_specs=VMEM,
        compiler_params=pltpu.CompilerParams(vmem_limit_bytes=4 * MEGA),
        name="join",
    )(*blocks, after)


def attend_kernel(
    heads, sinks, states_hbm, lengths_hbm, sink_hbm, qkv_hbm, window_hbm, out_hbm, result,
    states, lengths, sink, qkv, keys, values, out_weight, spread_out, first_sems, qkv_sems, key_sems, value_sems, out_sem,
):
    requests, width = states.shape
    size = sink.shape[1]
    parts = 3 * heads
    lanes = size * parts
    blocks = width // size
    chunks = qkv_sems.shape[0]
    chunk_rows = qkv.shape[0] // chunks
    slots = keys.shape[2]
    rows = heads * requests
    qkv_copies = [
        [
            pltpu.make_async_copy(
                qkv_hbm.at[pl.ds((2 * c + i) * chunk_rows, chunk_rows)],
                qkv.at[pl.ds(c * chunk_rows, chunk_rows), pl.ds(i * size, size)],
                qkv_sems.at[c, i],
            )
            for i in range(2)
        ]
        for c in range(chunks)
    ]
    key_copies = [
        pltpu.make_async_copy(window_hbm.at[r, :, 0], keys.at[r], key_sems.at[r]) for r in range(requests)
    ]
    value_copies = [
        pltpu.make_async_copy(
            window_hbm.at[:, h, 1], values.at[h // 2, :, :, pl.ds((h % 2) * size, size)], value_sems.at[h]
        )
        for h in range(heads)
    ]
    out_copy = pltpu.make_async_copy(out_hbm, out_weight, out_sem)
    first_copies = [
        pltpu.make_async_copy(source, target, first_sems.at[i])
        for i, (source, target) in enumerate(((states_hbm, states), (lengths_hbm, lengths), (sink_hbm, sink)))
    ]
    for copy in first_copies + sum(qkv_copies, []):
        copy.start()
    sub, lane = iota((size, lanes), 0) * parts, iota((size, lanes), 1)
    repeat = jnp.where((lane >= sub) & (lane < sub + parts), 1.0, 0.0).astype(BF16)
    kind = lax.rem(iota((requests, lanes), 1), parts)
    for copy in first_copies:
        copy.wait()
    hidden = states[...].astype(F32)
    normed = hidden * lax.rsqrt(jnp.mean(hidden * hidden, axis=-1, keepdims=True) + EPSILON)
    stacked = jnp.concatenate([normed[:, b * size : (b + 1) * size] for b in range(blocks)], axis=0)
    repeated = dot(stacked.astype(BF16), repeat)
    run = blocks // (2 * chunks)
    high = parts * requests
    for b in range(blocks):
        piece = repeated[b * requests : (b + 1) * requests]
        side, place = b // run % 2, b // (2 * run) * run + b % run
        spread_out[side * high : (side + 1) * high, place * lanes : (place + 1) * lanes] = jnp.concatenate(
            [jnp.where(kind == p, piece, 0.0) for p in range(parts)], axis=0
        ).astype(BF16)

    length_row = jnp.broadcast_to(lengths[...], (requests, requests))
    diagonal = iota((requests, requests), 0) == iota((requests, requests), 1)
    length = jnp.sum(jnp.where(diagonal, length_row, 0), axis=-1, keepdims=True)
    lane_id = iota((requests, size), 1)
    low = lane_id < size // 2
    pair_index = jnp.where(low, lane_id, lane_id - size // 2).astype(F32)
    angles = length.astype(F32) * jnp.exp(pair_index * (-2.0 * math.log(10000.0) / size))
    cosine, sine = jnp.cos(angles), jnp.sin(angles)
    sine = jnp.where(low, -sine, sine)

    projected = jnp.zeros((high, size), F32)
    later = [key_copies, value_copies, [out_copy]]
    for c in range(chunks):
        for copy in qkv_copies[c]:
            copy.wait()
        for copy in later[c] if c < len(later) else []:
            copy.start()
        part = slice(c * chunk_rows, (c + 1) * chunk_rows)
        both = dot(spread_out[:, part], qkv[part, :])
        projected = projected + (both[:high, :size] + both[high:, size:])

    cos_rows = jnp.concatenate([cosine] * heads, axis=0)
    sin_rows = jnp.concatenate([sine] * heads, axis=0)
    limit = jnp.concatenate([length] * heads, axis=0)

    def turn(values):
        return (values * cos_rows + pltpu.roll(values, size // 2, 1) * sin_rows).astype(BF16)

    query = turn(projected[:rows])
    fresh_key = turn(projected[rows : 2 * rows])
    fresh_value = projected[2 * rows :].astype(BF16).astype(F32)
    root_size = math.sqrt(size)
    across = (((1,), (1,)), ((), ()))

    self_scores = jnp.sum(query.astype(F32) * fresh_key.astype(F32), axis=-1, keepdims=True) / root_size
    sink_rows = sink[...]
    sink_total = sink_rows.shape[0]
    sink_scores = lax.dot_general(query, sink_rows, across, preferred_element_type=F32) / root_size
    row_id, column = iota((rows, sink_total), 0), iota((rows, sink_total), 1)
    slot = lax.rem(column, 2 * sinks)
    pair = lax.div(column, 2 * sinks)
    sink_valid = (
        (lax.rem(pair, heads) == lax.div(row_id, requests))
        & (lax.div(pair, heads) == lax.rem(row_id, requests))
        & (slot < sinks)
        & (slot < limit)
    )
    sink_scores = jnp.where(sink_valid, sink_scores, -1e30)

    mine = iota((requests, slots), 0)
    for copy in key_copies:
        copy.wait()
    scores = []
    for h in range(heads):
        own_keys = keys[:, h].reshape(requests * slots, size)
        found = lax.dot_general(query[h * requests : (h + 1) * requests], own_keys, across, preferred_element_type=F32)
        own = jnp.where(mine == 0, found[:, :slots], 0.0)
        for r in range(1, requests):
            own = jnp.where(mine == r, found[:, r * slots : (r + 1) * slots], own)
        scores.append(own)
    scores = jnp.concatenate(scores, axis=0) / root_size
    valid = iota((rows, slots), 1) >= sinks + slots - limit
    scores = jnp.where(valid, scores, -1e30)

    highest = jnp.maximum(
        jnp.maximum(jnp.max(scores, axis=-1, keepdims=True), jnp.max(sink_scores, axis=-1, keepdims=True)),
        self_scores,
    )
    window_exp = jnp.exp(scores - highest)
    sink_exp = jnp.where(sink_valid, jnp.exp(sink_scores - highest), 0.0)
    self_exp = jnp.exp(self_scores - highest)
    total = jnp.sum(window_exp, axis=-1, keepdims=True) + jnp.sum(sink_exp, axis=-1, keepdims=True) + self_exp
    window_weight = (window_exp / total).astype(BF16).astype(F32)
    sink_weight = pltpu.roll(sink_exp / total, sinks, 1).astype(BF16)
    self_weight = (self_exp / total).astype(BF16).astype(F32)
    mixture = dot(sink_weight, sink_rows) + self_weight * fresh_value
    for copy in value_copies:
        copy.wait()
    mixed = []
    for h in range(0, heads, 2):
        own = window_weight[h * requests : (h + 2) * requests]
        request = lax.rem(iota((2 * requests, slots), 0), requests)
        wide = jnp.concatenate([jnp.where(request == r, own, 0.0) for r in range(requests)], axis=1).astype(BF16)
        both = dot(wide, values[h // 2].reshape(requests * slots, 2 * size))
        for i in range(2):
            found = both[i * requests : (i + 1) * requests, i * size : (i + 1) * size]
            mixed.append(mixture[(h + i) * requests : (h + i + 1) * requests] + found)
    out_copy.wait()
    result[...] = dot(jnp.concatenate(mixed, axis=1).astype(BF16), out_weight[...]).astype(result.dtype)


def attend_fast(hidden, own_lengths, sink_rows, window_rows, qkv_weight, out_weight):
    requests, width = hidden.shape
    heads, sinks, size = sink_rows.shape[1], sink_rows.shape[3], sink_rows.shape[4]
    slots = window_rows.shape[3]
    qkv = qkv_weight.reshape(-1, size)
    out = out_weight.reshape(-1, width)
    return pl.pallas_call(
        lambda *refs: attend_kernel(heads, sinks, *refs),
        out_shape=jax.ShapeDtypeStruct((requests, width), BF16),
        in_specs=[HBM] * 6,
        out_specs=VMEM,
        scratch_shapes=[
            pltpu.VMEM(hidden.shape, BF16),
            pltpu.VMEM((1, requests), jnp.int32),
            pltpu.VMEM((sink_rows.size // size, size), BF16),
            pltpu.VMEM((qkv.shape[0] // 2, 2 * size), BF16),
            pltpu.VMEM((requests, heads, slots, size), BF16),
            pltpu.VMEM((heads // 2, requests, slots, 2 * size), BF16),
            pltpu.VMEM(out.shape, BF16),
            pltpu.VMEM((6 * heads * requests, qkv.shape[0] // 2), BF16),
            pltpu.SemaphoreType.DMA((3,)),
            pltpu.SemaphoreType.DMA((4, 2)),
            pltpu.SemaphoreType.DMA((requests,)),
            pltpu.SemaphoreType.DMA((heads,)),
            pltpu.SemaphoreType.DMA,
        ],
        compiler_params=pltpu.CompilerParams(vmem_limit_bytes=60 * MEGA),
        name="attend",
    )(
        hidden,
        own_lengths[None, :],
        sink_rows.reshape(-1, size),
        qkv,
        window_rows,
        out,
    )


def expert_kernel(chunks, near, far, *refs):
    w_in, refs = refs[:chunks], refs[chunks:]
    ids_hbm, route_hbm, in_hbm, out_hbm, terms, act, w_near, own_columns, *refs = refs
    rows_scr, ids, route, w_last, w_far, small_sems, last_sems, out_sems = refs
    count, tokens, share = terms.shape
    group = 2 * count
    requests = tokens // group
    units = act.shape[1]
    own = lax.axis_index("guide") * count + lax.axis_index("dp")
    first_expert = (own * lax.axis_size("mp") + lax.axis_index("mp")) * (units // FFE)
    out_copies = [
        pltpu.make_async_copy(
            out_hbm.at[:, pl.ds(pl.multiple_of((own ^ (first + j)) * share, share), share)],
            target.at[:, pl.ds(j * share, share)],
            out_sems.at[first + j],
        )
        for first, target in ((count, w_far), (0, w_near))
        for j in range(count)
    ]
    small_copies = [
        pltpu.make_async_copy(ids_hbm, ids, small_sems.at[0]),
        pltpu.make_async_copy(route_hbm, route, small_sems.at[1]),
    ]
    last = w_last.shape[2]
    last_copies = [
        pltpu.make_async_copy(in_hbm.at[k, :, pl.ds(units - last, last)], w_last.at[k], last_sems.at[k])
        for k in range(2)
    ]
    for copy in small_copies + last_copies + out_copies:
        copy.start()
    for first, source in ((0, near), (count, far)):
        values = source[...].astype(F32)
        for i in range(count):
            start = pl.multiple_of((own ^ (first + i)) * requests, requests)
            rows_scr[pl.ds(start, requests), :] = values[i * requests : (i + 1) * requests]
    own_columns[...] = rows_scr[:, pl.ds(pl.multiple_of(own * share, share), share)]
    rows = rows_scr[...]
    moe_in = (rows * lax.rsqrt(jnp.mean(rows * rows, axis=-1, keepdims=True) + EPSILON)).astype(BF16)
    for copy in small_copies:
        copy.wait()
    per_stream = ids.shape[2]
    diagonal = iota((per_stream, per_stream), 0) == iota((per_stream, per_stream), 1)

    def factor_of(expert):
        columns = []
        for stream in range(2):
            row = jnp.sum(jnp.where(ids[stream] == expert, route[stream], 0.0), axis=0, keepdims=True)
            spread_out = jnp.broadcast_to(row, (per_stream, per_stream))
            columns.append(jnp.sum(jnp.where(diagonal, spread_out, 0.0), axis=-1, keepdims=True))
        return jnp.concatenate(columns, axis=0)

    start = 0
    for weight in (*w_in, w_last):
        if weight is w_last:
            for copy in last_copies:
                copy.wait()
        unit, start = start, start + weight.shape[2]
        factor = factor_of(first_expert + unit // FFE)
        gate = dot(moe_in, weight[0])
        upward = dot(moe_in, weight[1])
        act[:, unit:start] = (gate / (1.0 + jnp.exp(-gate)) * upward * factor).astype(BF16)
    for j in range(count):
        out_copies[j].wait()
        terms[j] = dot(act[...], w_far[:, j * share : (j + 1) * share]).astype(BF16)
    for copy in out_copies[count:]:
        copy.wait()


def experts_fast(near, far, expert_ids, route_weight, w_in, expert_in, expert_out, share):
    width = near.shape[1]
    count = lax.axis_size("dp")
    tokens = 2 * near.shape[0]
    units = expert_out.shape[0]
    last = units - sum(weight.shape[2] for weight in w_in)
    top = expert_ids.shape[-1]
    return pl.pallas_call(
        lambda *refs: expert_kernel(len(w_in), *refs),
        out_shape=[
            jax.ShapeDtypeStruct((count, tokens, share), BF16),
            jax.ShapeDtypeStruct((tokens, units), BF16),
            jax.ShapeDtypeStruct((units, count * share), BF16),
            jax.ShapeDtypeStruct((tokens, share), F32),
        ],
        in_specs=[VMEM] * (2 + len(w_in)) + [HBM] * 4,
        out_specs=[VMEM] * 4,
        scratch_shapes=[
            pltpu.VMEM((tokens, width), F32),
            pltpu.VMEM((2, top, tokens // 2), jnp.int32),
            pltpu.VMEM((2, top, tokens // 2), F32),
            pltpu.VMEM((2, width, last), BF16),
            pltpu.VMEM((units, count * share), BF16),
            pltpu.SemaphoreType.DMA((2,)),
            pltpu.SemaphoreType.DMA((2,)),
            pltpu.SemaphoreType.DMA((2 * count,)),
        ],
        compiler_params=pltpu.CompilerParams(vmem_limit_bytes=29 * MEGA),
        name="experts",
    )(near, far, *w_in, jnp.swapaxes(expert_ids, 1, 2), jnp.swapaxes(route_weight, 1, 2), expert_in, expert_out)


def down_kernel(act, weight, terms):
    count, _, share = terms.shape
    for j in range(count):
        terms[j] = dot(act[...], weight[:, j * share : (j + 1) * share]).astype(BF16)


def down_fast(act, weight, share):
    tokens, units = act.shape
    count = weight.shape[1] // share
    return pl.pallas_call(
        down_kernel,
        out_shape=jax.ShapeDtypeStruct((count, tokens, share), BF16),
        in_specs=[VMEM] * 2,
        out_specs=VMEM,
        compiler_params=pltpu.CompilerParams(vmem_limit_bytes=8 * MEGA),
        cost_estimate=pl.CostEstimate(
            flops=2 * tokens * units * count * share, bytes_accessed=2 * units * count * share, transcendentals=0
        ),
        name="down",
    )(act, weight)


def add_up(blocks):
    total = blocks[0][...].astype(F32)
    for block in blocks[1:]:
        total = total + block[...].astype(F32)
    return total


def sum_kernel(*refs):
    refs[-1][...] = add_up(refs[:-1]).astype(BF16)


def sum_fast(blocks):
    return pl.pallas_call(
        sum_kernel,
        out_shape=jax.ShapeDtypeStruct(blocks[0].shape, BF16),
        in_specs=[VMEM] * len(blocks),
        out_specs=VMEM,
        compiler_params=pltpu.CompilerParams(vmem_limit_bytes=8 * MEGA),
        name="add_up",
    )(*blocks)


def head_kernel(chunk, other, own_columns, left, right, weight, target):
    tokens = own_columns.shape[0]
    count, rows, _ = target.shape
    requests = rows // 2
    half_width = weight.shape[1] // 2
    per_half = half_width // chunk
    guide, own = lax.axis_index("guide"), lax.axis_index("dp")
    summed = own_columns[...] + (left[...].astype(F32) + right[...].astype(F32))

    def hand_out(values, start):
        for d in range(count):
            target[own ^ d, :, start : start + values.shape[1]] = jnp.concatenate(
                [values[d * requests : (d + 1) * requests], values[tokens // 2 + d * requests : tokens // 2 + (d + 1) * requests]],
                axis=0,
            ).astype(BF16)

    squares = jnp.broadcast_to(jnp.sum(summed * summed, axis=-1, keepdims=True), (tokens, NOTE))
    raw_in = summed.astype(BF16)
    half = 1 - guide if other else guide
    hand_out(squares, half_width)
    for c in range(per_half):
        first = pl.multiple_of(half * half_width + c * chunk, 128)
        hand_out(dot(raw_in, weight[:, pl.ds(first, chunk)]), c * chunk)


def head_fast(other, own_columns, left, right, weight):
    count = lax.axis_size("dp")
    tokens = own_columns.shape[0]
    half_width = weight.shape[1] // 2
    return pl.pallas_call(
        lambda *refs: head_kernel(256, other, *refs),
        out_shape=jax.ShapeDtypeStruct((count, tokens // count, half_width + NOTE), BF16),
        in_specs=[VMEM] * 4,
        out_specs=VMEM,
        compiler_params=pltpu.CompilerParams(vmem_limit_bytes=12 * MEGA),
        cost_estimate=pl.CostEstimate(
            flops=tokens * weight.size, bytes_accessed=weight.size, transcendentals=0
        ),
        name="head",
    )(own_columns, left, right, weight)


def pair_kernel(near, received, *results):
    for k, result in enumerate(results):
        result[...] = (near[k].astype(F32) + received[k].astype(F32)).astype(BF16)


def pair_fast(near, received):
    count = near.shape[0]
    return pl.pallas_call(
        pair_kernel,
        out_shape=[jax.ShapeDtypeStruct(near.shape[1:], BF16)] * count,
        in_specs=[VMEM, VMEM],
        out_specs=[VMEM] * count,
        compiler_params=pltpu.CompilerParams(vmem_limit_bytes=8 * MEGA),
        name="pair",
    )(near, received)


def guide_kernel(width, weight, *refs):
    result = refs[-1]
    requests, half_width = result.shape[0], result.shape[3]
    total = add_up(refs[:-1])
    scale = lax.rsqrt(total[:, half_width : half_width + 1] / width + EPSILON)
    diagonal = iota((requests, requests), 0) == iota((requests, requests), 1)
    guidance = jnp.broadcast_to(weight[...], (requests, requests))
    factor = jnp.sum(jnp.where(diagonal, guidance, 0.0), axis=-1, keepdims=True)
    guided = total[:requests, :half_width] * (scale[:requests] * factor) + total[requests:, :half_width] * (
        scale[requests:] * (1.0 - factor)
    )
    for r in range(requests):
        result[r, 0] = guided[r : r + 1]


def guide_fast(blocks, guidance, width):
    rows, columns = blocks[0].shape
    return pl.pallas_call(
        lambda *refs: guide_kernel(width, *refs),
        out_shape=jax.ShapeDtypeStruct((rows // 2, 1, 1, columns - NOTE), F32),
        in_specs=[VMEM] * (1 + len(blocks)),
        out_specs=VMEM,
        compiler_params=pltpu.CompilerParams(vmem_limit_bytes=12 * MEGA),
        name="guide",
    )(guidance[None, :], *blocks)


def fits(hidden, sink_rows, expert_in, vocab_weight):
    return (
        lax.axis_size(ROWS) == 8
        and lax.axis_size("mp") == 4
        and hidden.shape[0] == 8
        and sink_rows.shape[1] == 4
        and expert_in.shape[2] % (2 * FFE) == 0
        and vocab_weight.shape[0] % 128 == 0
        and vocab_weight.shape[1] % 512 == 0
    )


def fast_body(
    states,
    lengths,
    sink_cache,
    window_cache,
    qkv_weight,
    out_weight,
    expert_ids,
    route_weight,
    expert_in,
    expert_out,
    vocab_weight,
    guidance,
):
    hidden = states[0]
    partial_out = attend_fast(hidden, lengths[0], sink_cache[0], window_cache[0], qkv_weight, out_weight)
    chunk = expert_in.shape[2] // 4
    received = step(partial_out, "mp", 1)
    w0 = load_fast(expert_in, 0, chunk, 47, lengths)
    pair = join_fast(True, [partial_out, received], w0)
    received = step(pair, "mp", 2)
    w1 = load_fast(expert_in, chunk, chunk, 43, pair)
    residual = join_fast(True, [hidden, pair, received], w1)
    blocks = swap([residual] * lax.axis_size("dp"), "dp")
    w2 = load_fast(expert_in, 2 * chunk, chunk, 39, residual)
    near = join_fast(False, blocks, w2)
    far = step(near, "guide", 1)
    w3 = load_fast(expert_in, 3 * chunk, chunk // 2, 37, near)
    share = vocab_weight.shape[0]
    terms, act, w_near, own_columns = experts_fast(
        near, far, expert_ids, route_weight, [w0, w1, w2, w3], expert_in, expert_out, share
    )
    received = step(terms, "guide", 1)
    part = sum_fast(swap(pair_fast(down_fast(act, w_near, share), received), "dp"))
    received = step(part, "mp", 1)
    pair = (part.astype(F32) + received.astype(F32)).astype(BF16)
    received = step(pair, "mp", 2)
    far = step(head_fast(True, own_columns, pair, received, vocab_weight), "guide", 1)
    near = head_fast(False, own_columns, pair, received, vocab_weight)
    logits = swap(pair_fast(near, far), "dp")
    return guide_fast(logits, guidance, hidden.shape[1])


def rotate(vectors, positions):
    full_width = vectors.shape[-1]
    half_width = full_width // 2
    step_index = jnp.arange(half_width, dtype=jnp.float32)
    inverse = jnp.exp(step_index * (-2.0 * math.log(10000.0) / full_width))
    angles = positions.astype(jnp.float32)[:, None] * inverse[None, :]
    cosine = jnp.cos(angles)[:, None, :]
    sine_part = jnp.sin(angles)[:, None, :]
    first_half = vectors[..., :half_width]
    second = vectors[..., half_width:]
    return jnp.concatenate(
        [first_half * cosine - second * sine_part, second * cosine + first_half * sine_part],
        axis=-1,
    )


def rms_norm(values):
    return values * lax.rsqrt(jnp.mean(values * values, axis=-1, keepdims=True) + EPSILON)


def attend(hidden, own_lengths, sink_rows, window_rows, qkv_weight, out_weight):
    normed = rms_norm(hidden.astype(jnp.float32)).astype(jnp.bfloat16)
    projected = jnp.einsum("rd,dthe->rthe", normed, qkv_weight, preferred_element_type=jnp.float32)
    query_rot = rotate(projected[:, 0], own_lengths).astype(jnp.bfloat16)
    fresh_key = rotate(projected[:, 1], own_lengths).astype(jnp.bfloat16)
    fresh_value = projected[:, 2].astype(jnp.bfloat16)
    sink_count = sink_rows.shape[3]
    window_count = window_rows.shape[3]
    root_size = math.sqrt(query_rot.shape[-1])
    sink_scores = (
        jnp.einsum(
            "rhe,rhse->rhs", query_rot, sink_rows[:, :, 0], preferred_element_type=jnp.float32
        )
        / root_size
    )
    window_scores = (
        jnp.einsum(
            "rhe,rhwe->rhw", query_rot, window_rows[:, :, 0], preferred_element_type=jnp.float32
        )
        / root_size
    )
    self_scores = (
        jnp.einsum("rhe,rhe->rh", query_rot, fresh_key, preferred_element_type=jnp.float32)
        / root_size
    )
    length_limit = own_lengths[:, None, None]
    sink_valid = jnp.arange(sink_count, dtype=jnp.int32)[None, None, :] < length_limit
    window_valid = (
        jnp.arange(window_count, dtype=jnp.int32)[None, None, :]
        >= sink_count + window_count - length_limit
    )
    sink_scores = jnp.where(sink_valid, sink_scores, -1e30)
    window_scores = jnp.where(window_valid, window_scores, -1e30)
    highest = jnp.maximum(
        jnp.maximum(jnp.max(sink_scores, axis=-1), jnp.max(window_scores, axis=-1)), self_scores
    )
    sink_exp = jnp.exp(sink_scores - highest[..., None])
    window_exp = jnp.exp(window_scores - highest[..., None])
    self_exp = jnp.exp(self_scores - highest)
    totals = jnp.sum(sink_exp, axis=-1) + jnp.sum(window_exp, axis=-1) + self_exp
    sink_prob = (sink_exp / totals[..., None]).astype(jnp.bfloat16)
    window_prob = (window_exp / totals[..., None]).astype(jnp.bfloat16)
    self_prob = (self_exp / totals).astype(jnp.bfloat16)
    mixture = (
        jnp.einsum(
            "rhs,rhse->rhe", sink_prob, sink_rows[:, :, 1], preferred_element_type=jnp.float32
        )
        + jnp.einsum(
            "rhw,rhwe->rhe", window_prob, window_rows[:, :, 1], preferred_element_type=jnp.float32
        )
        + self_prob[..., None].astype(jnp.float32) * fresh_value.astype(jnp.float32)
    ).astype(jnp.bfloat16)
    return jnp.einsum("rhe,hed->rd", mixture, out_weight, preferred_element_type=jnp.float32)


def body(
    states,
    lengths,
    sink_cache,
    window_cache,
    qkv_weight,
    out_weight,
    expert_ids,
    route_weight,
    expert_in,
    expert_out,
    vocab_weight,
    guidance,
):
    hidden = states[0]
    if fits(hidden, sink_cache[0], expert_in, vocab_weight):
        return fast_body(
            states,
            lengths,
            sink_cache,
            window_cache,
            qkv_weight,
            out_weight,
            expert_ids,
            route_weight,
            expert_in,
            expert_out,
            vocab_weight,
            guidance,
        )
    request_count, width = hidden.shape
    group = lax.axis_size(ROWS)
    mp = lax.axis_size("mp")
    tokens = group * request_count

    partial_out = attend(hidden, lengths[0], sink_cache[0], window_cache[0], qkv_weight, out_weight)
    first = lax.axis_index("mp") == 0
    partial_out = partial_out + jnp.where(first, hidden.astype(jnp.float32), 0.0)
    partials = spread(partial_out.astype(jnp.bfloat16), ALL).reshape(group, mp, request_count, width)
    residual = jnp.sum(partials.astype(jnp.float32), axis=1).reshape(tokens, width).astype(jnp.bfloat16)
    moe_in = rms_norm(residual.astype(jnp.float32)).astype(jnp.bfloat16)

    unit_count = expert_in.shape[2]
    unit_start = lax.axis_index(ALL) * unit_count
    unit_expert = (unit_start + jnp.arange(unit_count, dtype=jnp.int32)) // FFE
    choice_rows = expert_ids.reshape(-1, expert_ids.shape[-1])
    route_rows = route_weight.reshape(-1, route_weight.shape[-1])
    coefficient = jnp.sum(
        jnp.where(
            choice_rows[:, :, None] == unit_expert[None, None, :], route_rows[:, :, None], 0.0
        ),
        axis=1,
    )
    gate = jnp.dot(moe_in, expert_in[0], preferred_element_type=jnp.float32)
    upward = jnp.dot(moe_in, expert_in[1], preferred_element_type=jnp.float32)
    activated = (jax.nn.silu(gate) * upward * coefficient).astype(jnp.bfloat16)
    expert_terms = jnp.dot(activated, expert_out, preferred_element_type=jnp.float32).astype(jnp.bfloat16)

    share = vocab_weight.shape[0]
    sent = jnp.swapaxes(expert_terms.reshape(tokens, group, share), 0, 1)
    expert_part = jnp.sum(trade(sent, ROWS).astype(jnp.float32), axis=0)
    expert_total = jnp.sum(spread(expert_part.astype(jnp.bfloat16), "mp").astype(jnp.float32), axis=0)
    own_columns = lax.dynamic_slice_in_dim(residual, lax.axis_index(ROWS) * share, share, 1)
    summed = own_columns.astype(jnp.float32) + expert_total

    squares = jnp.sum(summed * summed, axis=-1)
    notes = spread(jnp.concatenate([squares, guidance]), ROWS)
    scale = lax.rsqrt(jnp.sum(notes[:, :tokens], axis=0) / width + EPSILON).reshape(2, -1, 1)
    weight = notes[: group // 2, tokens:].reshape(-1, 1)

    raw = jnp.dot(summed.astype(jnp.bfloat16), vocab_weight, preferred_element_type=jnp.float32)
    raw = raw.reshape(2, tokens // 2, -1)
    mixed = raw[0] * (scale[0] * weight) + raw[1] * (scale[1] * (1.0 - weight))
    half_width = mixed.shape[1] // 2
    mixed = mixed.astype(jnp.bfloat16).reshape(group // 2, request_count, 2, half_width)
    sent = jnp.transpose(mixed, (2, 0, 1, 3)).reshape(group, request_count, half_width)
    guided = jnp.sum(trade(sent, ROWS).astype(jnp.float32), axis=0)
    return guided.reshape(request_count, 1, 1, half_width)


def solution(mesh):
    in_specs = (
        P("guide", "dp", None),
        P("guide", "dp"),
        P("guide", "dp", "mp", None, None, None),
        P("guide", "dp", "mp", None, None, None),
        P(None, None, "mp", None),
        P("mp", None, None),
        P(),
        P(),
        P(None, None, ("guide", "dp", "mp")),
        P(("guide", "dp", "mp"), None),
        P(("guide", "dp"), "mp"),
        P("dp"),
    )
    out_specs = P("dp", "mp", "guide", None)
    return jax.shard_map(body, mesh=mesh, in_specs=in_specs, out_specs=out_specs, check_vma=False)
```

```python
import math

import jax
import jax.numpy as jnp
from jax import lax
from jax.experimental import pallas as pl
from jax.experimental.pallas import tpu as pltpu
from jax.sharding import PartitionSpec as P

FFE = 1024

EPSILON = 1e-05

ROWS = ("guide", "dp")
ALL = ("guide", "dp", "mp")


def trade(blocks, axis):
    return lax.all_to_all(blocks, axis, 0, 0, tiled=True)


def spread(block, axis):
    return trade(jnp.broadcast_to(block[None], (lax.axis_size(axis),) + block.shape), axis)


def step(block, axis, bit):
    count = lax.axis_size(axis)
    return lax.ppermute(block, axis, [(i, i ^ bit) for i in range(count)])


def swap(blocks, axis):
    return [blocks[0]] + [step(blocks[j], axis, j) for j in range(1, lax.axis_size(axis))]


F32 = jnp.float32
BF16 = jnp.bfloat16
VMEM = pl.BlockSpec(memory_space=pltpu.VMEM)
ANY = pl.BlockSpec(memory_space=pl.ANY)
HBM = pl.BlockSpec(memory_space=pltpu.HBM)
MEGA = 1 << 20
NOTE = 128


def dot(left, right):
    return jnp.dot(left, right, preferred_element_type=F32)


def iota(shape, dim):
    return lax.broadcasted_iota(jnp.int32, shape, dim)


def load_kernel(first, chunk, hbm, after, result, sems):
    rows = hbm.shape[1] // sems.shape[1]
    copies = [
        pltpu.make_async_copy(
            hbm.at[k, pl.ds(i * rows, rows), pl.ds(first, chunk)],
            result.at[k, pl.ds(i * rows, rows), :],
            sems.at[k, i],
        )
        for k in range(hbm.shape[0])
        for i in range(sems.shape[1])
    ]
    for copy in copies:
        copy.start()
    for copy in copies:
        copy.wait()


def load_fast(weight, first, chunk, room, after):
    kinds, width, _ = weight.shape
    return pl.pallas_call(
        lambda *refs: load_kernel(first, chunk, *refs),
        out_shape=jax.ShapeDtypeStruct((kinds, width, chunk), BF16),
        in_specs=[HBM, ANY],
        out_specs=VMEM,
        scratch_shapes=[pltpu.SemaphoreType.DMA((kinds, 4))],
        compiler_params=pltpu.CompilerParams(vmem_limit_bytes=room * MEGA),
        cost_estimate=pl.CostEstimate(flops=0, bytes_accessed=4 * kinds * width * chunk, transcendentals=0),
        name="load",
    )(weight, after)


def join_kernel(total, count, *refs):
    values = [ref[...].astype(F32) for ref in refs[:count]]
    joined = sum(values[1:], values[0]) if total else jnp.concatenate(values, axis=0)
    refs[-1][...] = joined.astype(BF16)


def join_fast(total, blocks, after):
    rows, columns = blocks[0].shape
    return pl.pallas_call(
        lambda *refs: join_kernel(total, len(blocks), *refs),
        out_shape=jax.ShapeDtypeStruct((rows if total else rows * len(blocks), columns), BF16),
        in_specs=[VMEM] * len(blocks) + [ANY],
        out_specs=VMEM,
        compiler_params=pltpu.CompilerParams(vmem_limit_bytes=4 * MEGA),
        name="join",
    )(*blocks, after)


def attend_kernel(
    heads, sinks, states_hbm, lengths_hbm, sink_hbm, qkv_hbm, window_hbm, out_hbm, result,
    states, lengths, sink, qkv, window, out_weight, spread_out, first_sems, qkv_sems, window_sems, out_sem,
):
    requests, width = states.shape
    size = sink.shape[1]
    parts = 3 * heads
    lanes = size * parts
    blocks = width // size
    chunks = qkv_sems.shape[0]
    chunk_rows = qkv.shape[0] // chunks
    slots = window.shape[3]
    rows = heads * requests
    qkv_copies = [
        pltpu.make_async_copy(
            qkv_hbm.at[pl.ds(c * chunk_rows, chunk_rows)], qkv.at[pl.ds(c * chunk_rows, chunk_rows)], qkv_sems.at[c]
        )
        for c in range(chunks)
    ]
    key_copies, value_copies = [
        [
            pltpu.make_async_copy(window_hbm.at[r, :, k], window.at[r, :, k], window_sems.at[k, r])
            for r in range(requests)
        ]
        for k in range(2)
    ]
    out_copy = pltpu.make_async_copy(out_hbm, out_weight, out_sem)
    first_copies = [
        pltpu.make_async_copy(source, target, first_sems.at[i])
        for i, (source, target) in enumerate(((states_hbm, states), (lengths_hbm, lengths), (sink_hbm, sink)))
    ]
    for copy in first_copies + qkv_copies:
        copy.start()
    sub, lane = iota((size, lanes), 0) * parts, iota((size, lanes), 1)
    repeat = jnp.where((lane >= sub) & (lane < sub + parts), 1.0, 0.0).astype(BF16)
    kind = lax.rem(iota((requests, lanes), 1), parts)
    for copy in first_copies:
        copy.wait()
    hidden = states[...].astype(F32)
    normed = hidden * lax.rsqrt(jnp.mean(hidden * hidden, axis=-1, keepdims=True) + EPSILON)
    stacked = jnp.concatenate([normed[:, b * size : (b + 1) * size] for b in range(blocks)], axis=0)
    repeated = dot(stacked.astype(BF16), repeat)
    run = blocks // chunks

    def lay_out(c):
        for b in range(c * run, (c + 1) * run):
            piece = repeated[b * requests : (b + 1) * requests]
            spread_out[:, b * lanes : (b + 1) * lanes] = jnp.concatenate(
                [jnp.where(kind == p, piece, 0.0) for p in range(parts)], axis=0
            ).astype(BF16)

    lay_out(0)
    projected = jnp.zeros((parts * requests, size), F32)
    later = [key_copies, value_copies, [out_copy]]
    for c in range(chunks):
        qkv_copies[c].wait()
        for copy in later[c] if c < len(later) else []:
            copy.start()
        part = slice(c * chunk_rows, (c + 1) * chunk_rows)
        if c + 1 < chunks:
            lay_out(c + 1)
        if c == chunks - 1:
            length_row = jnp.broadcast_to(lengths[...], (requests, requests))
            diagonal = iota((requests, requests), 0) == iota((requests, requests), 1)
            length = jnp.sum(jnp.where(diagonal, length_row, 0), axis=-1, keepdims=True)
            lane_id = iota((requests, size), 1)
            low = lane_id < size // 2
            pair_index = jnp.where(low, lane_id, lane_id - size // 2).astype(F32)
            angles = length.astype(F32) * jnp.exp(pair_index * (-2.0 * math.log(10000.0) / size))
            cosine, sine = jnp.cos(angles), jnp.sin(angles)
            sine = jnp.where(low, -sine, sine)
        projected = projected + dot(spread_out[:, part], qkv[part, :])

    cos_rows = jnp.concatenate([cosine] * heads, axis=0)
    sin_rows = jnp.concatenate([sine] * heads, axis=0)
    limit = jnp.concatenate([length] * heads, axis=0)

    def turn(values):
        return (values * cos_rows + pltpu.roll(values, size // 2, 1) * sin_rows).astype(BF16)

    query = turn(projected[:rows])
    fresh_key = turn(projected[rows : 2 * rows])
    fresh_value = projected[2 * rows :].astype(BF16).astype(F32)
    root_size = math.sqrt(size)
    across = (((1,), (1,)), ((), ()))

    self_scores = jnp.sum(query.astype(F32) * fresh_key.astype(F32), axis=-1, keepdims=True) / root_size
    sink_rows = sink[...]
    sink_total = sink_rows.shape[0]
    sink_scores = lax.dot_general(query, sink_rows, across, preferred_element_type=F32) / root_size
    row_id, column = iota((rows, sink_total), 0), iota((rows, sink_total), 1)
    slot = lax.rem(column, 2 * sinks)
    pair = lax.div(column, 2 * sinks)
    sink_valid = (
        (lax.rem(pair, heads) == lax.div(row_id, requests))
        & (lax.div(pair, heads) == lax.rem(row_id, requests))
        & (slot < sinks)
        & (slot < limit)
    )
    sink_scores = jnp.where(sink_valid, sink_scores, -1e30)

    mine = iota((requests, slots), 0)
    for copy in key_copies:
        copy.wait()
    scores = []
    for h in range(heads):
        keys = window[:, h, 0].reshape(requests * slots, size)
        found = lax.dot_general(query[h * requests : (h + 1) * requests], keys, across, preferred_element_type=F32)
        own = jnp.where(mine == 0, found[:, :slots], 0.0)
        for r in range(1, requests):
            own = jnp.where(mine == r, found[:, r * slots : (r + 1) * slots], own)
        scores.append(own)
    scores = jnp.concatenate(scores, axis=0) / root_size
    valid = iota((rows, slots), 1) >= sinks + slots - limit
    scores = jnp.where(valid, scores, -1e30)

    highest = jnp.maximum(
        jnp.maximum(jnp.max(scores, axis=-1, keepdims=True), jnp.max(sink_scores, axis=-1, keepdims=True)),
        self_scores,
    )
    window_exp = jnp.exp(scores - highest)
    sink_exp = jnp.where(sink_valid, jnp.exp(sink_scores - highest), 0.0)
    self_exp = jnp.exp(self_scores - highest)
    total = jnp.sum(window_exp, axis=-1, keepdims=True) + jnp.sum(sink_exp, axis=-1, keepdims=True) + self_exp
    window_weight = (window_exp / total).astype(BF16).astype(F32)
    sink_weight = pltpu.roll(sink_exp / total, sinks, 1).astype(BF16)
    self_weight = (self_exp / total).astype(BF16).astype(F32)
    mixture = dot(sink_weight, sink_rows) + self_weight * fresh_value
    for copy in value_copies:
        copy.wait()
    mixed = []
    for h in range(heads):
        own = window_weight[h * requests : (h + 1) * requests]
        wide = jnp.concatenate([jnp.where(mine == r, own, 0.0) for r in range(requests)], axis=1).astype(BF16)
        values = window[:, h, 1].reshape(requests * slots, size)
        mixed.append(mixture[h * requests : (h + 1) * requests] + dot(wide, values))
    out_copy.wait()
    result[...] = dot(jnp.concatenate(mixed, axis=1).astype(BF16), out_weight[...]).astype(result.dtype)


def attend_fast(hidden, own_lengths, sink_rows, window_rows, qkv_weight, out_weight):
    requests, width = hidden.shape
    heads, sinks, size = sink_rows.shape[1], sink_rows.shape[3], sink_rows.shape[4]
    qkv = qkv_weight.reshape(-1, size)
    out = out_weight.reshape(-1, width)
    return pl.pallas_call(
        lambda *refs: attend_kernel(heads, sinks, *refs),
        out_shape=jax.ShapeDtypeStruct((requests, width), BF16),
        in_specs=[HBM] * 6,
        out_specs=VMEM,
        scratch_shapes=[
            pltpu.VMEM(hidden.shape, BF16),
            pltpu.VMEM((1, requests), jnp.int32),
            pltpu.VMEM((sink_rows.size // size, size), BF16),
            pltpu.VMEM(qkv.shape, BF16),
            pltpu.VMEM(window_rows.shape, BF16),
            pltpu.VMEM(out.shape, BF16),
            pltpu.VMEM((3 * heads * requests, qkv.shape[0]), BF16),
            pltpu.SemaphoreType.DMA((3,)),
            pltpu.SemaphoreType.DMA((4,)),
            pltpu.SemaphoreType.DMA((2, requests)),
            pltpu.SemaphoreType.DMA,
        ],
        compiler_params=pltpu.CompilerParams(vmem_limit_bytes=60 * MEGA),
        name="attend",
    )(
        hidden,
        own_lengths[None, :],
        sink_rows.reshape(-1, size),
        qkv,
        window_rows,
        out,
    )


def expert_kernel(chunks, near, far, *refs):
    w_in, refs = refs[:chunks], refs[chunks:]
    ids_hbm, route_hbm, in_hbm, out_hbm, terms, act, w_near, own_columns, *refs = refs
    rows_scr, ids, route, w_last, w_far, small_sems, last_sems, out_sems = refs
    count, tokens, share = terms.shape
    group = 2 * count
    requests = tokens // group
    units = act.shape[1]
    own = lax.axis_index("guide") * count + lax.axis_index("dp")
    first_expert = (own * lax.axis_size("mp") + lax.axis_index("mp")) * (units // FFE)
    guide, place = lax.axis_index("guide"), lax.axis_index("dp")
    half_width = count * share
    runs = units // out_sems.shape[1]
    out_copies = [
        [
            pltpu.make_async_copy(
                out_hbm.at[pl.ds(i * runs, runs), pl.ds(pl.multiple_of(half * half_width, half_width), half_width)],
                target.at[pl.ds(i * runs, runs), :],
                out_sems.at[k, i],
            )
            for i in range(out_sems.shape[1])
        ]
        for k, (half, target) in enumerate(((1 - guide, w_far), (guide, w_near)))
    ]
    small_copies = [
        pltpu.make_async_copy(ids_hbm, ids, small_sems.at[0]),
        pltpu.make_async_copy(route_hbm, route, small_sems.at[1]),
    ]
    last = w_last.shape[2]
    last_copies = [
        pltpu.make_async_copy(in_hbm.at[k, :, pl.ds(units - last, last)], w_last.at[k], last_sems.at[k])
        for k in range(2)
    ]
    for copy in small_copies + last_copies + out_copies[0] + out_copies[1]:
        copy.start()
    for first, source in ((0, near), (count, far)):
        values = source[...].astype(F32)
        for i in range(count):
            start = pl.multiple_of((own ^ (first + i)) * requests, requests)
            rows_scr[pl.ds(start, requests), :] = values[i * requests : (i + 1) * requests]
    own_columns[...] = rows_scr[:, pl.ds(pl.multiple_of(own * share, share), share)]
    rows = rows_scr[...]
    moe_in = (rows * lax.rsqrt(jnp.mean(rows * rows, axis=-1, keepdims=True) + EPSILON)).astype(BF16)
    for copy in small_copies:
        copy.wait()
    per_stream = ids.shape[2]
    diagonal = iota((per_stream, per_stream), 0) == iota((per_stream, per_stream), 1)

    def factor_of(expert):
        columns = []
        for stream in range(2):
            row = jnp.sum(jnp.where(ids[stream] == expert, route[stream], 0.0), axis=0, keepdims=True)
            spread_out = jnp.broadcast_to(row, (per_stream, per_stream))
            columns.append(jnp.sum(jnp.where(diagonal, spread_out, 0.0), axis=-1, keepdims=True))
        return jnp.concatenate(columns, axis=0)

    start = 0
    for weight in (*w_in, w_last):
        if weight is w_last:
            for copy in last_copies:
                copy.wait()
        unit, start = start, start + weight.shape[2]
        factor = factor_of(first_expert + unit // FFE)
        gate = dot(moe_in, weight[0])
        upward = dot(moe_in, weight[1])
        act[:, unit:start] = (gate / (1.0 + jnp.exp(-gate)) * upward * factor).astype(BF16)
    for copy in out_copies[0]:
        copy.wait()
    for d in range(count):
        terms[place ^ d] = dot(act[...], w_far[:, d * share : (d + 1) * share]).astype(BF16)
    for copy in out_copies[1]:
        copy.wait()


def experts_fast(near, far, expert_ids, route_weight, w_in, expert_in, expert_out, share):
    width = near.shape[1]
    count = lax.axis_size("dp")
    tokens = 2 * near.shape[0]
    units = expert_out.shape[0]
    last = units - sum(weight.shape[2] for weight in w_in)
    top = expert_ids.shape[-1]
    return pl.pallas_call(
        lambda *refs: expert_kernel(len(w_in), *refs),
        out_shape=[
            jax.ShapeDtypeStruct((count, tokens, share), BF16),
            jax.ShapeDtypeStruct((tokens, units), BF16),
            jax.ShapeDtypeStruct((units, count * share), BF16),
            jax.ShapeDtypeStruct((tokens, share), F32),
        ],
        in_specs=[VMEM] * (2 + len(w_in)) + [HBM] * 4,
        out_specs=[VMEM] * 4,
        scratch_shapes=[
            pltpu.VMEM((tokens, width), F32),
            pltpu.VMEM((2, top, tokens // 2), jnp.int32),
            pltpu.VMEM((2, top, tokens // 2), F32),
            pltpu.VMEM((2, width, last), BF16),
            pltpu.VMEM((units, count * share), BF16),
            pltpu.SemaphoreType.DMA((2,)),
            pltpu.SemaphoreType.DMA((2,)),
            pltpu.SemaphoreType.DMA((2, 4)),
        ],
        compiler_params=pltpu.CompilerParams(vmem_limit_bytes=29 * MEGA),
        name="experts",
    )(near, far, *w_in, jnp.swapaxes(expert_ids, 1, 2), jnp.swapaxes(route_weight, 1, 2), expert_in, expert_out)


def down_kernel(act, weight, terms):
    count, _, share = terms.shape
    place = lax.axis_index("dp")
    for d in range(count):
        terms[place ^ d] = dot(act[...], weight[:, d * share : (d + 1) * share]).astype(BF16)


def down_fast(act, weight, share):
    tokens, units = act.shape
    count = weight.shape[1] // share
    return pl.pallas_call(
        down_kernel,
        out_shape=jax.ShapeDtypeStruct((count, tokens, share), BF16),
        in_specs=[VMEM] * 2,
        out_specs=VMEM,
        compiler_params=pltpu.CompilerParams(vmem_limit_bytes=8 * MEGA),
        cost_estimate=pl.CostEstimate(
            flops=2 * tokens * units * count * share, bytes_accessed=2 * units * count * share, transcendentals=0
        ),
        name="down",
    )(act, weight)


def add_up(blocks):
    total = blocks[0][...].astype(F32)
    for block in blocks[1:]:
        total = total + block[...].astype(F32)
    return total


def sum_kernel(*refs):
    refs[-1][...] = add_up(refs[:-1]).astype(BF16)


def sum_fast(blocks):
    return pl.pallas_call(
        sum_kernel,
        out_shape=jax.ShapeDtypeStruct(blocks[0].shape, BF16),
        in_specs=[VMEM] * len(blocks),
        out_specs=VMEM,
        compiler_params=pltpu.CompilerParams(vmem_limit_bytes=8 * MEGA),
        name="add_up",
    )(*blocks)


def head_kernel(chunk, other, own_columns, left, right, weight, target):
    tokens = own_columns.shape[0]
    count, rows, _ = target.shape
    requests = rows // 2
    half_width = weight.shape[1] // 2
    per_half = half_width // chunk
    guide, own = lax.axis_index("guide"), lax.axis_index("dp")
    summed = own_columns[...] + (left[...].astype(F32) + right[...].astype(F32))

    def hand_out(values, start):
        for d in range(count):
            target[own ^ d, :, start : start + values.shape[1]] = jnp.concatenate(
                [values[d * requests : (d + 1) * requests], values[tokens // 2 + d * requests : tokens // 2 + (d + 1) * requests]],
                axis=0,
            ).astype(BF16)

    squares = jnp.broadcast_to(jnp.sum(summed * summed, axis=-1, keepdims=True), (tokens, NOTE))
    raw_in = summed.astype(BF16)
    half = 1 - guide if other else guide
    hand_out(squares, half_width)
    for c in range(per_half):
        first = pl.multiple_of(half * half_width + c * chunk, 128)
        hand_out(dot(raw_in, weight[:, pl.ds(first, chunk)]), c * chunk)


def head_fast(other, own_columns, left, right, weight):
    count = lax.axis_size("dp")
    tokens = own_columns.shape[0]
    half_width = weight.shape[1] // 2
    return pl.pallas_call(
        lambda *refs: head_kernel(256, other, *refs),
        out_shape=jax.ShapeDtypeStruct((count, tokens // count, half_width + NOTE), BF16),
        in_specs=[VMEM] * 4,
        out_specs=VMEM,
        compiler_params=pltpu.CompilerParams(vmem_limit_bytes=12 * MEGA),
        cost_estimate=pl.CostEstimate(
            flops=tokens * weight.size, bytes_accessed=weight.size, transcendentals=0
        ),
        name="head",
    )(own_columns, left, right, weight)


def pair_kernel(near, received, *results):
    for k, result in enumerate(results):
        result[...] = (near[k].astype(F32) + received[k].astype(F32)).astype(BF16)


def pair_fast(near, received):
    count = near.shape[0]
    return pl.pallas_call(
        pair_kernel,
        out_shape=[jax.ShapeDtypeStruct(near.shape[1:], BF16)] * count,
        in_specs=[VMEM, VMEM],
        out_specs=[VMEM] * count,
        compiler_params=pltpu.CompilerParams(vmem_limit_bytes=8 * MEGA),
        name="pair",
    )(near, received)


def guide_kernel(width, weight, *refs):
    result = refs[-1]
    requests, half_width = result.shape[0], result.shape[3]
    total = add_up(refs[:-1])
    scale = lax.rsqrt(total[:, half_width : half_width + 1] / width + EPSILON)
    diagonal = iota((requests, requests), 0) == iota((requests, requests), 1)
    guidance = jnp.broadcast_to(weight[...], (requests, requests))
    factor = jnp.sum(jnp.where(diagonal, guidance, 0.0), axis=-1, keepdims=True)
    guided = total[:requests, :half_width] * (scale[:requests] * factor) + total[requests:, :half_width] * (
        scale[requests:] * (1.0 - factor)
    )
    for r in range(requests):
        result[r, 0] = guided[r : r + 1]


def guide_fast(blocks, guidance, width):
    rows, columns = blocks[0].shape
    return pl.pallas_call(
        lambda *refs: guide_kernel(width, *refs),
        out_shape=jax.ShapeDtypeStruct((rows // 2, 1, 1, columns - NOTE), F32),
        in_specs=[VMEM] * (1 + len(blocks)),
        out_specs=VMEM,
        compiler_params=pltpu.CompilerParams(vmem_limit_bytes=12 * MEGA),
        name="guide",
    )(guidance[None, :], *blocks)


def fits(hidden, sink_rows, expert_in, vocab_weight):
    return (
        lax.axis_size(ROWS) == 8
        and lax.axis_size("mp") == 4
        and hidden.shape[0] == 8
        and sink_rows.shape[1] == 4
        and expert_in.shape[2] % (2 * FFE) == 0
        and vocab_weight.shape[0] % 128 == 0
        and vocab_weight.shape[1] % 512 == 0
    )


def fast_body(
    states,
    lengths,
    sink_cache,
    window_cache,
    qkv_weight,
    out_weight,
    expert_ids,
    route_weight,
    expert_in,
    expert_out,
    vocab_weight,
    guidance,
):
    hidden = states[0]
    partial_out = attend_fast(hidden, lengths[0], sink_cache[0], window_cache[0], qkv_weight, out_weight)
    chunk = expert_in.shape[2] // 4
    received = step(partial_out, "mp", 1)
    w0 = load_fast(expert_in, 0, chunk, 47, lengths)
    pair = join_fast(True, [partial_out, received], w0)
    received = step(pair, "mp", 2)
    w1 = load_fast(expert_in, chunk, chunk, 43, pair)
    residual = join_fast(True, [hidden, pair, received], w1)
    blocks = swap([residual] * lax.axis_size("dp"), "dp")
    w2 = load_fast(expert_in, 2 * chunk, chunk, 39, residual)
    near = join_fast(False, blocks, w2)
    far = step(near, "guide", 1)
    w3 = load_fast(expert_in, 3 * chunk, chunk // 2, 37, near)
    share = vocab_weight.shape[0]
    terms, act, w_near, own_columns = experts_fast(
        near, far, expert_ids, route_weight, [w0, w1, w2, w3], expert_in, expert_out, share
    )
    received = step(terms, "guide", 1)
    part = sum_fast(swap(pair_fast(down_fast(act, w_near, share), received), "dp"))
    received = step(part, "mp", 1)
    pair = (part.astype(F32) + received.astype(F32)).astype(BF16)
    received = step(pair, "mp", 2)
    far = step(head_fast(True, own_columns, pair, received, vocab_weight), "guide", 1)
    near = head_fast(False, own_columns, pair, received, vocab_weight)
    logits = swap(pair_fast(near, far), "dp")
    return guide_fast(logits, guidance, hidden.shape[1])


def rotate(vectors, positions):
    full_width = vectors.shape[-1]
    half_width = full_width // 2
    step_index = jnp.arange(half_width, dtype=jnp.float32)
    inverse = jnp.exp(step_index * (-2.0 * math.log(10000.0) / full_width))
    angles = positions.astype(jnp.float32)[:, None] * inverse[None, :]
    cosine = jnp.cos(angles)[:, None, :]
    sine_part = jnp.sin(angles)[:, None, :]
    first_half = vectors[..., :half_width]
    second = vectors[..., half_width:]
    return jnp.concatenate(
        [first_half * cosine - second * sine_part, second * cosine + first_half * sine_part],
        axis=-1,
    )


def rms_norm(values):
    return values * lax.rsqrt(jnp.mean(values * values, axis=-1, keepdims=True) + EPSILON)


def attend(hidden, own_lengths, sink_rows, window_rows, qkv_weight, out_weight):
    normed = rms_norm(hidden.astype(jnp.float32)).astype(jnp.bfloat16)
    projected = jnp.einsum("rd,dthe->rthe", normed, qkv_weight, preferred_element_type=jnp.float32)
    query_rot = rotate(projected[:, 0], own_lengths).astype(jnp.bfloat16)
    fresh_key = rotate(projected[:, 1], own_lengths).astype(jnp.bfloat16)
    fresh_value = projected[:, 2].astype(jnp.bfloat16)
    sink_count = sink_rows.shape[3]
    window_count = window_rows.shape[3]
    root_size = math.sqrt(query_rot.shape[-1])
    sink_scores = (
        jnp.einsum(
            "rhe,rhse->rhs", query_rot, sink_rows[:, :, 0], preferred_element_type=jnp.float32
        )
        / root_size
    )
    window_scores = (
        jnp.einsum(
            "rhe,rhwe->rhw", query_rot, window_rows[:, :, 0], preferred_element_type=jnp.float32
        )
        / root_size
    )
    self_scores = (
        jnp.einsum("rhe,rhe->rh", query_rot, fresh_key, preferred_element_type=jnp.float32)
        / root_size
    )
    length_limit = own_lengths[:, None, None]
    sink_valid = jnp.arange(sink_count, dtype=jnp.int32)[None, None, :] < length_limit
    window_valid = (
        jnp.arange(window_count, dtype=jnp.int32)[None, None, :]
        >= sink_count + window_count - length_limit
    )
    sink_scores = jnp.where(sink_valid, sink_scores, -1e30)
    window_scores = jnp.where(window_valid, window_scores, -1e30)
    highest = jnp.maximum(
        jnp.maximum(jnp.max(sink_scores, axis=-1), jnp.max(window_scores, axis=-1)), self_scores
    )
    sink_exp = jnp.exp(sink_scores - highest[..., None])
    window_exp = jnp.exp(window_scores - highest[..., None])
    self_exp = jnp.exp(self_scores - highest)
    totals = jnp.sum(sink_exp, axis=-1) + jnp.sum(window_exp, axis=-1) + self_exp
    sink_prob = (sink_exp / totals[..., None]).astype(jnp.bfloat16)
    window_prob = (window_exp / totals[..., None]).astype(jnp.bfloat16)
    self_prob = (self_exp / totals).astype(jnp.bfloat16)
    mixture = (
        jnp.einsum(
            "rhs,rhse->rhe", sink_prob, sink_rows[:, :, 1], preferred_element_type=jnp.float32
        )
        + jnp.einsum(
            "rhw,rhwe->rhe", window_prob, window_rows[:, :, 1], preferred_element_type=jnp.float32
        )
        + self_prob[..., None].astype(jnp.float32) * fresh_value.astype(jnp.float32)
    ).astype(jnp.bfloat16)
    return jnp.einsum("rhe,hed->rd", mixture, out_weight, preferred_element_type=jnp.float32)


def body(
    states,
    lengths,
    sink_cache,
    window_cache,
    qkv_weight,
    out_weight,
    expert_ids,
    route_weight,
    expert_in,
    expert_out,
    vocab_weight,
    guidance,
):
    hidden = states[0]
    if fits(hidden, sink_cache[0], expert_in, vocab_weight):
        return fast_body(
            states,
            lengths,
            sink_cache,
            window_cache,
            qkv_weight,
            out_weight,
            expert_ids,
            route_weight,
            expert_in,
            expert_out,
            vocab_weight,
            guidance,
        )
    request_count, width = hidden.shape
    group = lax.axis_size(ROWS)
    mp = lax.axis_size("mp")
    tokens = group * request_count

    partial_out = attend(hidden, lengths[0], sink_cache[0], window_cache[0], qkv_weight, out_weight)
    first = lax.axis_index("mp") == 0
    partial_out = partial_out + jnp.where(first, hidden.astype(jnp.float32), 0.0)
    partials = spread(partial_out.astype(jnp.bfloat16), ALL).reshape(group, mp, request_count, width)
    residual = jnp.sum(partials.astype(jnp.float32), axis=1).reshape(tokens, width).astype(jnp.bfloat16)
    moe_in = rms_norm(residual.astype(jnp.float32)).astype(jnp.bfloat16)

    unit_count = expert_in.shape[2]
    unit_start = lax.axis_index(ALL) * unit_count
    unit_expert = (unit_start + jnp.arange(unit_count, dtype=jnp.int32)) // FFE
    choice_rows = expert_ids.reshape(-1, expert_ids.shape[-1])
    route_rows = route_weight.reshape(-1, route_weight.shape[-1])
    coefficient = jnp.sum(
        jnp.where(
            choice_rows[:, :, None] == unit_expert[None, None, :], route_rows[:, :, None], 0.0
        ),
        axis=1,
    )
    gate = jnp.dot(moe_in, expert_in[0], preferred_element_type=jnp.float32)
    upward = jnp.dot(moe_in, expert_in[1], preferred_element_type=jnp.float32)
    activated = (jax.nn.silu(gate) * upward * coefficient).astype(jnp.bfloat16)
    expert_terms = jnp.dot(activated, expert_out, preferred_element_type=jnp.float32).astype(jnp.bfloat16)

    share = vocab_weight.shape[0]
    sent = jnp.swapaxes(expert_terms.reshape(tokens, group, share), 0, 1)
    expert_part = jnp.sum(trade(sent, ROWS).astype(jnp.float32), axis=0)
    expert_total = jnp.sum(spread(expert_part.astype(jnp.bfloat16), "mp").astype(jnp.float32), axis=0)
    own_columns = lax.dynamic_slice_in_dim(residual, lax.axis_index(ROWS) * share, share, 1)
    summed = own_columns.astype(jnp.float32) + expert_total

    squares = jnp.sum(summed * summed, axis=-1)
    notes = spread(jnp.concatenate([squares, guidance]), ROWS)
    scale = lax.rsqrt(jnp.sum(notes[:, :tokens], axis=0) / width + EPSILON).reshape(2, -1, 1)
    weight = notes[: group // 2, tokens:].reshape(-1, 1)

    raw = jnp.dot(summed.astype(jnp.bfloat16), vocab_weight, preferred_element_type=jnp.float32)
    raw = raw.reshape(2, tokens // 2, -1)
    mixed = raw[0] * (scale[0] * weight) + raw[1] * (scale[1] * (1.0 - weight))
    half_width = mixed.shape[1] // 2
    mixed = mixed.astype(jnp.bfloat16).reshape(group // 2, request_count, 2, half_width)
    sent = jnp.transpose(mixed, (2, 0, 1, 3)).reshape(group, request_count, half_width)
    guided = jnp.sum(trade(sent, ROWS).astype(jnp.float32), axis=0)
    return guided.reshape(request_count, 1, 1, half_width)


def solution(mesh):
    in_specs = (
        P("guide", "dp", None),
        P("guide", "dp"),
        P("guide", "dp", "mp", None, None, None),
        P("guide", "dp", "mp", None, None, None),
        P(None, None, "mp", None),
        P("mp", None, None),
        P(),
        P(),
        P(None, None, ("guide", "dp", "mp")),
        P(("guide", "dp", "mp"), None),
        P(("guide", "dp"), "mp"),
        P("dp"),
    )
    out_specs = P("dp", "mp", "guide", None)
    return jax.shard_map(body, mesh=mesh, in_specs=in_specs, out_specs=out_specs, check_vma=False)
```

```python
import math

import jax
import jax.numpy as jnp
from jax import lax
from jax.experimental import pallas as pl
from jax.experimental.pallas import tpu as pltpu
from jax.sharding import PartitionSpec as P

FFE = 1024

EPSILON = 1e-05

ROWS = ("guide", "dp")
ALL = ("guide", "dp", "mp")


def trade(blocks, axis):
    return lax.all_to_all(blocks, axis, 0, 0, tiled=True)


def spread(block, axis):
    return trade(jnp.broadcast_to(block[None], (lax.axis_size(axis),) + block.shape), axis)


def step(block, axis, bit):
    count = lax.axis_size(axis)
    return lax.ppermute(block, axis, [(i, i ^ bit) for i in range(count)])


def swap(blocks, axis):
    return [blocks[0]] + [step(blocks[j], axis, j) for j in range(1, lax.axis_size(axis))]


F32 = jnp.float32
BF16 = jnp.bfloat16
VMEM = pl.BlockSpec(memory_space=pltpu.VMEM)
ANY = pl.BlockSpec(memory_space=pl.ANY)
HBM = pl.BlockSpec(memory_space=pltpu.HBM)
MEGA = 1 << 20
NOTE = 128


def dot(left, right):
    return jnp.dot(left, right, preferred_element_type=F32)


def iota(shape, dim):
    return lax.broadcasted_iota(jnp.int32, shape, dim)


def load_kernel(first, chunk, hbm, after, result, sems):
    rows = hbm.shape[1] // sems.shape[1]
    copies = [
        pltpu.make_async_copy(
            hbm.at[k, pl.ds(i * rows, rows), pl.ds(first, chunk)],
            result.at[k, pl.ds(i * rows, rows), :],
            sems.at[k, i],
        )
        for k in range(hbm.shape[0])
        for i in range(sems.shape[1])
    ]
    for copy in copies:
        copy.start()
    for copy in copies:
        copy.wait()


def load_fast(weight, first, chunk, room, after):
    kinds, width, _ = weight.shape
    return pl.pallas_call(
        lambda *refs: load_kernel(first, chunk, *refs),
        out_shape=jax.ShapeDtypeStruct((kinds, width, chunk), BF16),
        in_specs=[HBM, ANY],
        out_specs=VMEM,
        scratch_shapes=[pltpu.SemaphoreType.DMA((kinds, 4))],
        compiler_params=pltpu.CompilerParams(vmem_limit_bytes=room * MEGA),
        cost_estimate=pl.CostEstimate(flops=0, bytes_accessed=4 * kinds * width * chunk, transcendentals=0),
        name="load",
    )(weight, after)


def join_kernel(total, count, *refs):
    values = [ref[...].astype(F32) for ref in refs[:count]]
    joined = sum(values[1:], values[0]) if total else jnp.concatenate(values, axis=0)
    refs[-1][...] = joined.astype(BF16)


def join_fast(total, blocks, after):
    rows, columns = blocks[0].shape
    return pl.pallas_call(
        lambda *refs: join_kernel(total, len(blocks), *refs),
        out_shape=jax.ShapeDtypeStruct((rows if total else rows * len(blocks), columns), BF16),
        in_specs=[VMEM] * len(blocks) + [ANY],
        out_specs=VMEM,
        compiler_params=pltpu.CompilerParams(vmem_limit_bytes=4 * MEGA),
        name="join",
    )(*blocks, after)


def attend_kernel(
    heads, sinks, states_hbm, lengths_hbm, sink_hbm, qkv_hbm, window_hbm, out_hbm, result,
    states, lengths, sink, qkv, window, out_weight, spread_out, first_sems, qkv_sems, window_sems, out_sem,
):
    requests, width = states.shape
    size = sink.shape[1]
    parts = 3 * heads
    lanes = size * parts
    blocks = width // size
    chunks = qkv_sems.shape[0]
    chunk_rows = qkv.shape[0] // chunks
    slots = window.shape[3]
    rows = heads * requests
    qkv_copies = [
        pltpu.make_async_copy(
            qkv_hbm.at[pl.ds(c * chunk_rows, chunk_rows)], qkv.at[pl.ds(c * chunk_rows, chunk_rows)], qkv_sems.at[c]
        )
        for c in range(chunks)
    ]
    key_copies, value_copies = [
        [
            pltpu.make_async_copy(window_hbm.at[r, :, k], window.at[r, :, k], window_sems.at[k, r])
            for r in range(requests)
        ]
        for k in range(2)
    ]
    out_copy = pltpu.make_async_copy(out_hbm, out_weight, out_sem)
    first_copies = [
        pltpu.make_async_copy(source, target, first_sems.at[i])
        for i, (source, target) in enumerate(((states_hbm, states), (lengths_hbm, lengths), (sink_hbm, sink)))
    ]
    for copy in first_copies + qkv_copies + key_copies:
        copy.start()
    sub, lane = iota((size, lanes), 0) * parts, iota((size, lanes), 1)
    repeat = jnp.where((lane >= sub) & (lane < sub + parts), 1.0, 0.0).astype(BF16)
    kind = lax.rem(iota((requests, lanes), 1), parts)
    for copy in first_copies:
        copy.wait()
    hidden = states[...].astype(F32)
    normed = hidden * lax.rsqrt(jnp.mean(hidden * hidden, axis=-1, keepdims=True) + EPSILON)
    stacked = jnp.concatenate([normed[:, b * size : (b + 1) * size] for b in range(blocks)], axis=0)
    repeated = dot(stacked.astype(BF16), repeat)
    run = blocks // chunks
    high = parts * requests
    half_rows = chunk_rows // 2

    def lay_out(c):
        for b in range(c * run, (c + 1) * run):
            piece = repeated[b * requests : (b + 1) * requests]
            side, place = b % run // (run // 2), b // run * (run // 2) + b % (run // 2)
            spread_out[side * high : (side + 1) * high, place * lanes : (place + 1) * lanes] = jnp.concatenate(
                [jnp.where(kind == p, piece, 0.0) for p in range(parts)], axis=0
            ).astype(BF16)

    lay_out(0)
    projected = jnp.zeros((high, size), F32)
    later = [value_copies, [out_copy]]
    for c in range(chunks):
        qkv_copies[c].wait()
        for copy in later[c] if c < len(later) else []:
            copy.start()
        if c + 1 < chunks:
            lay_out(c + 1)
        if c == chunks - 1:
            length_row = jnp.broadcast_to(lengths[...], (requests, requests))
            diagonal = iota((requests, requests), 0) == iota((requests, requests), 1)
            length = jnp.sum(jnp.where(diagonal, length_row, 0), axis=-1, keepdims=True)
            lane_id = iota((requests, size), 1)
            low = lane_id < size // 2
            pair_index = jnp.where(low, lane_id, lane_id - size // 2).astype(F32)
            angles = length.astype(F32) * jnp.exp(pair_index * (-2.0 * math.log(10000.0) / size))
            cosine, sine = jnp.cos(angles), jnp.sin(angles)
            sine = jnp.where(low, -sine, sine)
        first = c * chunk_rows
        wide = jnp.concatenate([qkv[first : first + half_rows], qkv[first + half_rows : first + chunk_rows]], axis=1)
        both = dot(spread_out[:, c * half_rows : (c + 1) * half_rows], wide)
        projected = projected + (both[:high, :size] + both[high:, size:])

    cos_rows = jnp.concatenate([cosine] * heads, axis=0)
    sin_rows = jnp.concatenate([sine] * heads, axis=0)
    limit = jnp.concatenate([length] * heads, axis=0)

    def turn(values):
        return (values * cos_rows + pltpu.roll(values, size // 2, 1) * sin_rows).astype(BF16)

    query = turn(projected[:rows])
    fresh_key = turn(projected[rows : 2 * rows])
    fresh_value = projected[2 * rows :].astype(BF16).astype(F32)
    root_size = math.sqrt(size)
    across = (((1,), (1,)), ((), ()))

    self_scores = jnp.sum(query.astype(F32) * fresh_key.astype(F32), axis=-1, keepdims=True) / root_size
    sink_rows = sink[...]
    sink_total = sink_rows.shape[0]
    sink_scores = lax.dot_general(query, sink_rows, across, preferred_element_type=F32) / root_size
    row_id, column = iota((rows, sink_total), 0), iota((rows, sink_total), 1)
    slot = lax.rem(column, 2 * sinks)
    pair = lax.div(column, 2 * sinks)
    sink_valid = (
        (lax.rem(pair, heads) == lax.div(row_id, requests))
        & (lax.div(pair, heads) == lax.rem(row_id, requests))
        & (slot < sinks)
        & (slot < limit)
    )
    sink_scores = jnp.where(sink_valid, sink_scores, -1e30)

    mine = iota((requests, slots), 0)
    for copy in key_copies:
        copy.wait()
    scores = []
    for h in range(heads):
        keys = window[:, h, 0].reshape(requests * slots, size)
        found = lax.dot_general(query[h * requests : (h + 1) * requests], keys, across, preferred_element_type=F32)
        own = jnp.where(mine == 0, found[:, :slots], 0.0)
        for r in range(1, requests):
            own = jnp.where(mine == r, found[:, r * slots : (r + 1) * slots], own)
        scores.append(own)
    scores = jnp.concatenate(scores, axis=0) / root_size
    valid = iota((rows, slots), 1) >= sinks + slots - limit
    scores = jnp.where(valid, scores, -1e30)

    highest = jnp.maximum(
        jnp.maximum(jnp.max(scores, axis=-1, keepdims=True), jnp.max(sink_scores, axis=-1, keepdims=True)),
        self_scores,
    )
    window_exp = jnp.exp(scores - highest)
    sink_exp = jnp.where(sink_valid, jnp.exp(sink_scores - highest), 0.0)
    self_exp = jnp.exp(self_scores - highest)
    total = jnp.sum(window_exp, axis=-1, keepdims=True) + jnp.sum(sink_exp, axis=-1, keepdims=True) + self_exp
    window_weight = (window_exp / total).astype(BF16).astype(F32)
    sink_weight = pltpu.roll(sink_exp / total, sinks, 1).astype(BF16)
    self_weight = (self_exp / total).astype(BF16).astype(F32)
    mixture = dot(sink_weight, sink_rows) + self_weight * fresh_value
    for copy in value_copies:
        copy.wait()
    mixed = []
    request = lax.rem(iota((2 * requests, slots), 0), requests)
    for h in range(0, heads, 2):
        own = window_weight[h * requests : (h + 2) * requests]
        spread_weight = jnp.concatenate([jnp.where(request == r, own, 0.0) for r in range(requests)], axis=1)
        values = [window[:, h + i, 1].reshape(requests * slots, size) for i in range(2)]
        both = dot(spread_weight.astype(BF16), jnp.concatenate(values, axis=1))
        for i in range(2):
            found = both[i * requests : (i + 1) * requests, i * size : (i + 1) * size]
            mixed.append(mixture[(h + i) * requests : (h + i + 1) * requests] + found)
    out_copy.wait()
    result[...] = dot(jnp.concatenate(mixed, axis=1).astype(BF16), out_weight[...]).astype(result.dtype)


def attend_fast(hidden, own_lengths, sink_rows, window_rows, qkv_weight, out_weight):
    requests, width = hidden.shape
    heads, sinks, size = sink_rows.shape[1], sink_rows.shape[3], sink_rows.shape[4]
    qkv = qkv_weight.reshape(-1, size)
    out = out_weight.reshape(-1, width)
    return pl.pallas_call(
        lambda *refs: attend_kernel(heads, sinks, *refs),
        out_shape=jax.ShapeDtypeStruct((requests, width), BF16),
        in_specs=[HBM] * 6,
        out_specs=VMEM,
        scratch_shapes=[
            pltpu.VMEM(hidden.shape, BF16),
            pltpu.VMEM((1, requests), jnp.int32),
            pltpu.VMEM((sink_rows.size // size, size), BF16),
            pltpu.VMEM(qkv.shape, BF16),
            pltpu.VMEM(window_rows.shape, BF16),
            pltpu.VMEM(out.shape, BF16),
            pltpu.VMEM((6 * heads * requests, qkv.shape[0] // 2), BF16),
            pltpu.SemaphoreType.DMA((3,)),
            pltpu.SemaphoreType.DMA((4,)),
            pltpu.SemaphoreType.DMA((2, requests)),
            pltpu.SemaphoreType.DMA,
        ],
        compiler_params=pltpu.CompilerParams(vmem_limit_bytes=60 * MEGA),
        name="attend",
    )(
        hidden,
        own_lengths[None, :],
        sink_rows.reshape(-1, size),
        qkv,
        window_rows,
        out,
    )


def expert_kernel(chunks, near, far, *refs):
    w_in, refs = refs[:chunks], refs[chunks:]
    ids_hbm, route_hbm, in_hbm, out_hbm, terms, act, w_near, own_columns, *refs = refs
    rows_scr, ids, route, w_last, w_far, small_sems, last_sems, out_sems = refs
    count, tokens, share = terms.shape
    group = 2 * count
    requests = tokens // group
    units = act.shape[1]
    own = lax.axis_index("guide") * count + lax.axis_index("dp")
    first_expert = (own * lax.axis_size("mp") + lax.axis_index("mp")) * (units // FFE)
    guide, place = lax.axis_index("guide"), lax.axis_index("dp")
    half_width = count * share
    runs = units // out_sems.shape[1]
    out_copies = [
        [
            pltpu.make_async_copy(
                out_hbm.at[pl.ds(i * runs, runs), pl.ds(pl.multiple_of(half * half_width, half_width), half_width)],
                target.at[pl.ds(i * runs, runs), :],
                out_sems.at[k, i],
            )
            for i in range(out_sems.shape[1])
        ]
        for k, (half, target) in enumerate(((1 - guide, w_far), (guide, w_near)))
    ]
    small_copies = [
        pltpu.make_async_copy(ids_hbm, ids, small_sems.at[0]),
        pltpu.make_async_copy(route_hbm, route, small_sems.at[1]),
    ]
    last = w_last.shape[2]
    last_copies = [
        pltpu.make_async_copy(in_hbm.at[k, :, pl.ds(units - last, last)], w_last.at[k], last_sems.at[k])
        for k in range(2)
    ]
    for copy in small_copies + last_copies + out_copies[0] + out_copies[1]:
        copy.start()
    for first, source in ((0, near), (count, far)):
        values = source[...].astype(F32)
        for i in range(count):
            start = pl.multiple_of((own ^ (first + i)) * requests, requests)
            rows_scr[pl.ds(start, requests), :] = values[i * requests : (i + 1) * requests]
    own_columns[...] = rows_scr[:, pl.ds(pl.multiple_of(own * share, share), share)]
    rows = rows_scr[...]
    moe_in = (rows * lax.rsqrt(jnp.mean(rows * rows, axis=-1, keepdims=True) + EPSILON)).astype(BF16)
    for copy in small_copies:
        copy.wait()
    per_stream = ids.shape[2]
    diagonal = iota((per_stream, per_stream), 0) == iota((per_stream, per_stream), 1)

    def factor_of(expert):
        columns = []
        for stream in range(2):
            row = jnp.sum(jnp.where(ids[stream] == expert, route[stream], 0.0), axis=0, keepdims=True)
            spread_out = jnp.broadcast_to(row, (per_stream, per_stream))
            columns.append(jnp.sum(jnp.where(diagonal, spread_out, 0.0), axis=-1, keepdims=True))
        return jnp.concatenate(columns, axis=0)

    start = 0
    for weight in (*w_in, w_last):
        if weight is w_last:
            for copy in last_copies:
                copy.wait()
        unit, start = start, start + weight.shape[2]
        factor = factor_of(first_expert + unit // FFE)
        gate = dot(moe_in, weight[0])
        upward = dot(moe_in, weight[1])
        act[:, unit:start] = (gate / (1.0 + jnp.exp(-gate)) * upward * factor).astype(BF16)
    for copy in out_copies[0]:
        copy.wait()
    for d in range(count):
        terms[place ^ d] = dot(act[...], w_far[:, d * share : (d + 1) * share]).astype(BF16)
    for copy in out_copies[1]:
        copy.wait()


def experts_fast(near, far, expert_ids, route_weight, w_in, expert_in, expert_out, share):
    width = near.shape[1]
    count = lax.axis_size("dp")
    tokens = 2 * near.shape[0]
    units = expert_out.shape[0]
    last = units - sum(weight.shape[2] for weight in w_in)
    top = expert_ids.shape[-1]
    return pl.pallas_call(
        lambda *refs: expert_kernel(len(w_in), *refs),
        out_shape=[
            jax.ShapeDtypeStruct((count, tokens, share), BF16),
            jax.ShapeDtypeStruct((tokens, units), BF16),
            jax.ShapeDtypeStruct((units, count * share), BF16),
            jax.ShapeDtypeStruct((tokens, share), F32),
        ],
        in_specs=[VMEM] * (2 + len(w_in)) + [HBM] * 4,
        out_specs=[VMEM] * 4,
        scratch_shapes=[
            pltpu.VMEM((tokens, width), F32),
            pltpu.VMEM((2, top, tokens // 2), jnp.int32),
            pltpu.VMEM((2, top, tokens // 2), F32),
            pltpu.VMEM((2, width, last), BF16),
            pltpu.VMEM((units, count * share), BF16),
            pltpu.SemaphoreType.DMA((2,)),
            pltpu.SemaphoreType.DMA((2,)),
            pltpu.SemaphoreType.DMA((2, 4)),
        ],
        compiler_params=pltpu.CompilerParams(vmem_limit_bytes=29 * MEGA),
        name="experts",
    )(near, far, *w_in, jnp.swapaxes(expert_ids, 1, 2), jnp.swapaxes(route_weight, 1, 2), expert_in, expert_out)


def down_kernel(act, weight, terms):
    count, _, share = terms.shape
    place = lax.axis_index("dp")
    for d in range(count):
        terms[place ^ d] = dot(act[...], weight[:, d * share : (d + 1) * share]).astype(BF16)


def down_fast(act, weight, share):
    tokens, units = act.shape
    count = weight.shape[1] // share
    return pl.pallas_call(
        down_kernel,
        out_shape=jax.ShapeDtypeStruct((count, tokens, share), BF16),
        in_specs=[VMEM] * 2,
        out_specs=VMEM,
        compiler_params=pltpu.CompilerParams(vmem_limit_bytes=8 * MEGA),
        cost_estimate=pl.CostEstimate(
            flops=2 * tokens * units * count * share, bytes_accessed=2 * units * count * share, transcendentals=0
        ),
        name="down",
    )(act, weight)


def add_up(blocks):
    total = blocks[0][...].astype(F32)
    for block in blocks[1:]:
        total = total + block[...].astype(F32)
    return total


def sum_kernel(*refs):
    refs[-1][...] = add_up(refs[:-1]).astype(BF16)


def sum_fast(blocks):
    return pl.pallas_call(
        sum_kernel,
        out_shape=jax.ShapeDtypeStruct(blocks[0].shape, BF16),
        in_specs=[VMEM] * len(blocks),
        out_specs=VMEM,
        compiler_params=pltpu.CompilerParams(vmem_limit_bytes=8 * MEGA),
        name="add_up",
    )(*blocks)


def head_kernel(chunk, other, own_columns, left, right, weight, target):
    tokens = own_columns.shape[0]
    count, rows, _ = target.shape
    requests = rows // 2
    half_width = weight.shape[1] // 2
    per_half = half_width // chunk
    guide, own = lax.axis_index("guide"), lax.axis_index("dp")
    summed = own_columns[...] + (left[...].astype(F32) + right[...].astype(F32))

    def hand_out(values, start):
        for d in range(count):
            target[own ^ d, :, start : start + values.shape[1]] = jnp.concatenate(
                [values[d * requests : (d + 1) * requests], values[tokens // 2 + d * requests : tokens // 2 + (d + 1) * requests]],
                axis=0,
            ).astype(BF16)

    squares = jnp.broadcast_to(jnp.sum(summed * summed, axis=-1, keepdims=True), (tokens, NOTE))
    raw_in = summed.astype(BF16)
    half = 1 - guide if other else guide
    hand_out(squares, half_width)
    for c in range(per_half):
        first = pl.multiple_of(half * half_width + c * chunk, 128)
        hand_out(dot(raw_in, weight[:, pl.ds(first, chunk)]), c * chunk)


def head_fast(other, own_columns, left, right, weight):
    count = lax.axis_size("dp")
    tokens = own_columns.shape[0]
    half_width = weight.shape[1] // 2
    return pl.pallas_call(
        lambda *refs: head_kernel(256, other, *refs),
        out_shape=jax.ShapeDtypeStruct((count, tokens // count, half_width + NOTE), BF16),
        in_specs=[VMEM] * 4,
        out_specs=VMEM,
        compiler_params=pltpu.CompilerParams(vmem_limit_bytes=12 * MEGA),
        cost_estimate=pl.CostEstimate(
            flops=tokens * weight.size, bytes_accessed=weight.size, transcendentals=0
        ),
        name="head",
    )(own_columns, left, right, weight)


def pair_kernel(near, received, *results):
    for k, result in enumerate(results):
        result[...] = (near[k].astype(F32) + received[k].astype(F32)).astype(BF16)


def pair_fast(near, received):
    count = near.shape[0]
    return pl.pallas_call(
        pair_kernel,
        out_shape=[jax.ShapeDtypeStruct(near.shape[1:], BF16)] * count,
        in_specs=[VMEM, VMEM],
        out_specs=[VMEM] * count,
        compiler_params=pltpu.CompilerParams(vmem_limit_bytes=8 * MEGA),
        name="pair",
    )(near, received)


def guide_kernel(width, weight, *refs):
    result = refs[-1]
    requests, half_width = result.shape[0], result.shape[3]
    total = add_up(refs[:-1])
    scale = lax.rsqrt(total[:, half_width : half_width + 1] / width + EPSILON)
    diagonal = iota((requests, requests), 0) == iota((requests, requests), 1)
    guidance = jnp.broadcast_to(weight[...], (requests, requests))
    factor = jnp.sum(jnp.where(diagonal, guidance, 0.0), axis=-1, keepdims=True)
    guided = total[:requests, :half_width] * (scale[:requests] * factor) + total[requests:, :half_width] * (
        scale[requests:] * (1.0 - factor)
    )
    for r in range(requests):
        result[r, 0] = guided[r : r + 1]


def guide_fast(blocks, guidance, width):
    rows, columns = blocks[0].shape
    return pl.pallas_call(
        lambda *refs: guide_kernel(width, *refs),
        out_shape=jax.ShapeDtypeStruct((rows // 2, 1, 1, columns - NOTE), F32),
        in_specs=[VMEM] * (1 + len(blocks)),
        out_specs=VMEM,
        compiler_params=pltpu.CompilerParams(vmem_limit_bytes=12 * MEGA),
        name="guide",
    )(guidance[None, :], *blocks)


def fits(hidden, sink_rows, expert_in, vocab_weight):
    return (
        lax.axis_size(ROWS) == 8
        and lax.axis_size("mp") == 4
        and hidden.shape[0] == 8
        and sink_rows.shape[1] == 4
        and expert_in.shape[2] % (2 * FFE) == 0
        and vocab_weight.shape[0] % 128 == 0
        and vocab_weight.shape[1] % 512 == 0
    )


def fast_body(
    states,
    lengths,
    sink_cache,
    window_cache,
    qkv_weight,
    out_weight,
    expert_ids,
    route_weight,
    expert_in,
    expert_out,
    vocab_weight,
    guidance,
):
    hidden = states[0]
    partial_out = attend_fast(hidden, lengths[0], sink_cache[0], window_cache[0], qkv_weight, out_weight)
    chunk = expert_in.shape[2] // 4
    received = step(partial_out, "mp", 1)
    w0 = load_fast(expert_in, 0, chunk, 47, lengths)
    pair = join_fast(True, [partial_out, received], w0)
    received = step(pair, "mp", 2)
    w1 = load_fast(expert_in, chunk, chunk, 43, pair)
    residual = join_fast(True, [hidden, pair, received], w1)
    blocks = swap([residual] * lax.axis_size("dp"), "dp")
    w2 = load_fast(expert_in, 2 * chunk, chunk, 39, residual)
    near = join_fast(False, blocks, w2)
    far = step(near, "guide", 1)
    w3 = load_fast(expert_in, 3 * chunk, chunk // 2, 37, near)
    share = vocab_weight.shape[0]
    terms, act, w_near, own_columns = experts_fast(
        near, far, expert_ids, route_weight, [w0, w1, w2, w3], expert_in, expert_out, share
    )
    received = step(terms, "guide", 1)
    part = sum_fast(swap(pair_fast(down_fast(act, w_near, share), received), "dp"))
    received = step(part, "mp", 1)
    pair = (part.astype(F32) + received.astype(F32)).astype(BF16)
    received = step(pair, "mp", 2)
    far = step(head_fast(True, own_columns, pair, received, vocab_weight), "guide", 1)
    near = head_fast(False, own_columns, pair, received, vocab_weight)
    logits = swap(pair_fast(near, far), "dp")
    return guide_fast(logits, guidance, hidden.shape[1])


def rotate(vectors, positions):
    full_width = vectors.shape[-1]
    half_width = full_width // 2
    step_index = jnp.arange(half_width, dtype=jnp.float32)
    inverse = jnp.exp(step_index * (-2.0 * math.log(10000.0) / full_width))
    angles = positions.astype(jnp.float32)[:, None] * inverse[None, :]
    cosine = jnp.cos(angles)[:, None, :]
    sine_part = jnp.sin(angles)[:, None, :]
    first_half = vectors[..., :half_width]
    second = vectors[..., half_width:]
    return jnp.concatenate(
        [first_half * cosine - second * sine_part, second * cosine + first_half * sine_part],
        axis=-1,
    )


def rms_norm(values):
    return values * lax.rsqrt(jnp.mean(values * values, axis=-1, keepdims=True) + EPSILON)


def attend(hidden, own_lengths, sink_rows, window_rows, qkv_weight, out_weight):
    normed = rms_norm(hidden.astype(jnp.float32)).astype(jnp.bfloat16)
    projected = jnp.einsum("rd,dthe->rthe", normed, qkv_weight, preferred_element_type=jnp.float32)
    query_rot = rotate(projected[:, 0], own_lengths).astype(jnp.bfloat16)
    fresh_key = rotate(projected[:, 1], own_lengths).astype(jnp.bfloat16)
    fresh_value = projected[:, 2].astype(jnp.bfloat16)
    sink_count = sink_rows.shape[3]
    window_count = window_rows.shape[3]
    root_size = math.sqrt(query_rot.shape[-1])
    sink_scores = (
        jnp.einsum(
            "rhe,rhse->rhs", query_rot, sink_rows[:, :, 0], preferred_element_type=jnp.float32
        )
        / root_size
    )
    window_scores = (
        jnp.einsum(
            "rhe,rhwe->rhw", query_rot, window_rows[:, :, 0], preferred_element_type=jnp.float32
        )
        / root_size
    )
    self_scores = (
        jnp.einsum("rhe,rhe->rh", query_rot, fresh_key, preferred_element_type=jnp.float32)
        / root_size
    )
    length_limit = own_lengths[:, None, None]
    sink_valid = jnp.arange(sink_count, dtype=jnp.int32)[None, None, :] < length_limit
    window_valid = (
        jnp.arange(window_count, dtype=jnp.int32)[None, None, :]
        >= sink_count + window_count - length_limit
    )
    sink_scores = jnp.where(sink_valid, sink_scores, -1e30)
    window_scores = jnp.where(window_valid, window_scores, -1e30)
    highest = jnp.maximum(
        jnp.maximum(jnp.max(sink_scores, axis=-1), jnp.max(window_scores, axis=-1)), self_scores
    )
    sink_exp = jnp.exp(sink_scores - highest[..., None])
    window_exp = jnp.exp(window_scores - highest[..., None])
    self_exp = jnp.exp(self_scores - highest)
    totals = jnp.sum(sink_exp, axis=-1) + jnp.sum(window_exp, axis=-1) + self_exp
    sink_prob = (sink_exp / totals[..., None]).astype(jnp.bfloat16)
    window_prob = (window_exp / totals[..., None]).astype(jnp.bfloat16)
    self_prob = (self_exp / totals).astype(jnp.bfloat16)
    mixture = (
        jnp.einsum(
            "rhs,rhse->rhe", sink_prob, sink_rows[:, :, 1], preferred_element_type=jnp.float32
        )
        + jnp.einsum(
            "rhw,rhwe->rhe", window_prob, window_rows[:, :, 1], preferred_element_type=jnp.float32
        )
        + self_prob[..., None].astype(jnp.float32) * fresh_value.astype(jnp.float32)
    ).astype(jnp.bfloat16)
    return jnp.einsum("rhe,hed->rd", mixture, out_weight, preferred_element_type=jnp.float32)


def body(
    states,
    lengths,
    sink_cache,
    window_cache,
    qkv_weight,
    out_weight,
    expert_ids,
    route_weight,
    expert_in,
    expert_out,
    vocab_weight,
    guidance,
):
    hidden = states[0]
    if fits(hidden, sink_cache[0], expert_in, vocab_weight):
        return fast_body(
            states,
            lengths,
            sink_cache,
            window_cache,
            qkv_weight,
            out_weight,
            expert_ids,
            route_weight,
            expert_in,
            expert_out,
            vocab_weight,
            guidance,
        )
    request_count, width = hidden.shape
    group = lax.axis_size(ROWS)
    mp = lax.axis_size("mp")
    tokens = group * request_count

    partial_out = attend(hidden, lengths[0], sink_cache[0], window_cache[0], qkv_weight, out_weight)
    first = lax.axis_index("mp") == 0
    partial_out = partial_out + jnp.where(first, hidden.astype(jnp.float32), 0.0)
    partials = spread(partial_out.astype(jnp.bfloat16), ALL).reshape(group, mp, request_count, width)
    residual = jnp.sum(partials.astype(jnp.float32), axis=1).reshape(tokens, width).astype(jnp.bfloat16)
    moe_in = rms_norm(residual.astype(jnp.float32)).astype(jnp.bfloat16)

    unit_count = expert_in.shape[2]
    unit_start = lax.axis_index(ALL) * unit_count
    unit_expert = (unit_start + jnp.arange(unit_count, dtype=jnp.int32)) // FFE
    choice_rows = expert_ids.reshape(-1, expert_ids.shape[-1])
    route_rows = route_weight.reshape(-1, route_weight.shape[-1])
    coefficient = jnp.sum(
        jnp.where(
            choice_rows[:, :, None] == unit_expert[None, None, :], route_rows[:, :, None], 0.0
        ),
        axis=1,
    )
    gate = jnp.dot(moe_in, expert_in[0], preferred_element_type=jnp.float32)
    upward = jnp.dot(moe_in, expert_in[1], preferred_element_type=jnp.float32)
    activated = (jax.nn.silu(gate) * upward * coefficient).astype(jnp.bfloat16)
    expert_terms = jnp.dot(activated, expert_out, preferred_element_type=jnp.float32).astype(jnp.bfloat16)

    share = vocab_weight.shape[0]
    sent = jnp.swapaxes(expert_terms.reshape(tokens, group, share), 0, 1)
    expert_part = jnp.sum(trade(sent, ROWS).astype(jnp.float32), axis=0)
    expert_total = jnp.sum(spread(expert_part.astype(jnp.bfloat16), "mp").astype(jnp.float32), axis=0)
    own_columns = lax.dynamic_slice_in_dim(residual, lax.axis_index(ROWS) * share, share, 1)
    summed = own_columns.astype(jnp.float32) + expert_total

    squares = jnp.sum(summed * summed, axis=-1)
    notes = spread(jnp.concatenate([squares, guidance]), ROWS)
    scale = lax.rsqrt(jnp.sum(notes[:, :tokens], axis=0) / width + EPSILON).reshape(2, -1, 1)
    weight = notes[: group // 2, tokens:].reshape(-1, 1)

    raw = jnp.dot(summed.astype(jnp.bfloat16), vocab_weight, preferred_element_type=jnp.float32)
    raw = raw.reshape(2, tokens // 2, -1)
    mixed = raw[0] * (scale[0] * weight) + raw[1] * (scale[1] * (1.0 - weight))
    half_width = mixed.shape[1] // 2
    mixed = mixed.astype(jnp.bfloat16).reshape(group // 2, request_count, 2, half_width)
    sent = jnp.transpose(mixed, (2, 0, 1, 3)).reshape(group, request_count, half_width)
    guided = jnp.sum(trade(sent, ROWS).astype(jnp.float32), axis=0)
    return guided.reshape(request_count, 1, 1, half_width)


def solution(mesh):
    in_specs = (
        P("guide", "dp", None),
        P("guide", "dp"),
        P("guide", "dp", "mp", None, None, None),
        P("guide", "dp", "mp", None, None, None),
        P(None, None, "mp", None),
        P("mp", None, None),
        P(),
        P(),
        P(None, None, ("guide", "dp", "mp")),
        P(("guide", "dp", "mp"), None),
        P(("guide", "dp"), "mp"),
        P("dp"),
    )
    out_specs = P("dp", "mp", "guide", None)
    return jax.shard_map(body, mesh=mesh, in_specs=in_specs, out_specs=out_specs, check_vma=False)
```

```python
import math

import jax
import jax.numpy as jnp
from jax import lax
from jax.experimental import pallas as pl
from jax.experimental.pallas import tpu as pltpu
from jax.sharding import PartitionSpec as P

FFE = 1024

EPSILON = 1e-05

ROWS = ("guide", "dp")
ALL = ("guide", "dp", "mp")


def trade(blocks, axis):
    return lax.all_to_all(blocks, axis, 0, 0, tiled=True)


def spread(block, axis):
    return trade(jnp.broadcast_to(block[None], (lax.axis_size(axis),) + block.shape), axis)


def step(block, axis, bit):
    count = lax.axis_size(axis)
    return lax.ppermute(block, axis, [(i, i ^ bit) for i in range(count)])


def swap(blocks, axis):
    return [blocks[0]] + [step(blocks[j], axis, j) for j in range(1, lax.axis_size(axis))]


F32 = jnp.float32
BF16 = jnp.bfloat16
VMEM = pl.BlockSpec(memory_space=pltpu.VMEM)
ANY = pl.BlockSpec(memory_space=pl.ANY)
HBM = pl.BlockSpec(memory_space=pltpu.HBM)
MEGA = 1 << 20
NOTE = 128


def dot(left, right):
    return jnp.dot(left, right, preferred_element_type=F32)


def iota(shape, dim):
    return lax.broadcasted_iota(jnp.int32, shape, dim)


def load_kernel(first, chunk, hbm, after, result, sems):
    rows = hbm.shape[1] // sems.shape[1]
    copies = [
        pltpu.make_async_copy(
            hbm.at[k, pl.ds(i * rows, rows), pl.ds(first, chunk)],
            result.at[k, pl.ds(i * rows, rows), :],
            sems.at[k, i],
        )
        for k in range(hbm.shape[0])
        for i in range(sems.shape[1])
    ]
    for copy in copies:
        copy.start()
    for copy in copies:
        copy.wait()


def load_fast(weight, first, chunk, room, after):
    kinds, width, _ = weight.shape
    return pl.pallas_call(
        lambda *refs: load_kernel(first, chunk, *refs),
        out_shape=jax.ShapeDtypeStruct((kinds, width, chunk), BF16),
        in_specs=[HBM, ANY],
        out_specs=VMEM,
        scratch_shapes=[pltpu.SemaphoreType.DMA((kinds, 4))],
        compiler_params=pltpu.CompilerParams(vmem_limit_bytes=room * MEGA),
        cost_estimate=pl.CostEstimate(flops=0, bytes_accessed=4 * kinds * width * chunk, transcendentals=0),
        name="load",
    )(weight, after)


def join_kernel(total, count, *refs):
    values = [ref[...].astype(F32) for ref in refs[:count]]
    joined = sum(values[1:], values[0]) if total else jnp.concatenate(values, axis=0)
    refs[-1][...] = joined.astype(BF16)


def join_fast(total, blocks, after):
    rows, columns = blocks[0].shape
    return pl.pallas_call(
        lambda *refs: join_kernel(total, len(blocks), *refs),
        out_shape=jax.ShapeDtypeStruct((rows if total else rows * len(blocks), columns), BF16),
        in_specs=[VMEM] * len(blocks) + [ANY],
        out_specs=VMEM,
        compiler_params=pltpu.CompilerParams(vmem_limit_bytes=4 * MEGA),
        name="join",
    )(*blocks, after)


def attend_kernel(
    heads, sinks, states_hbm, lengths_hbm, sink_hbm, qkv_hbm, window_hbm, out_hbm, result,
    states, lengths, sink, qkv, window, out_weight, spread_out, first_sems, qkv_sems, window_sems, out_sem,
):
    requests, width = states.shape
    size = sink.shape[1]
    parts = 3 * heads
    lanes = size * parts
    blocks = width // size
    chunks = qkv_sems.shape[0]
    chunk_rows = qkv.shape[0] // chunks
    slots = window.shape[3]
    rows = heads * requests
    qkv_copies = [
        pltpu.make_async_copy(
            qkv_hbm.at[pl.ds(c * chunk_rows, chunk_rows)], qkv.at[pl.ds(c * chunk_rows, chunk_rows)], qkv_sems.at[c]
        )
        for c in range(chunks)
    ]
    key_copies, value_copies = [
        [
            pltpu.make_async_copy(window_hbm.at[r, :, k], window.at[r, :, k], window_sems.at[k, r])
            for r in range(requests)
        ]
        for k in range(2)
    ]
    out_copy = pltpu.make_async_copy(out_hbm, out_weight, out_sem)
    first_copies = [
        pltpu.make_async_copy(source, target, first_sems.at[i])
        for i, (source, target) in enumerate(((states_hbm, states), (lengths_hbm, lengths), (sink_hbm, sink)))
    ]
    for copy in first_copies + qkv_copies[: chunks // 2]:
        copy.start()
    sub, lane = iota((size, lanes), 0) * parts, iota((size, lanes), 1)
    repeat = jnp.where((lane >= sub) & (lane < sub + parts), 1.0, 0.0).astype(BF16)
    kind = lax.rem(iota((requests, lanes), 1), parts)
    for copy in first_copies:
        copy.wait()
    for copy in qkv_copies[chunks // 2 :]:
        copy.start()
    hidden = states[...].astype(F32)
    normed = hidden * lax.rsqrt(jnp.mean(hidden * hidden, axis=-1, keepdims=True) + EPSILON)
    stacked = jnp.concatenate([normed[:, b * size : (b + 1) * size] for b in range(blocks)], axis=0)
    repeated = dot(stacked.astype(BF16), repeat)
    run = blocks // chunks

    def lay_out(c):
        for b in range(c * run, (c + 1) * run):
            piece = repeated[b * requests : (b + 1) * requests]
            spread_out[:, b * lanes : (b + 1) * lanes] = jnp.concatenate(
                [jnp.where(kind == p, piece, 0.0) for p in range(parts)], axis=0
            ).astype(BF16)

    lay_out(0)
    projected = jnp.zeros((parts * requests, size), F32)
    for copy in key_copies:
        copy.start()
    later = {chunks // 4: value_copies, chunks // 2: [out_copy]}
    for c in range(chunks):
        qkv_copies[c].wait()
        for copy in later.get(c, []):
            copy.start()
        part = slice(c * chunk_rows, (c + 1) * chunk_rows)
        if c + 1 < chunks:
            lay_out(c + 1)
        if c == chunks - 1:
            length_row = jnp.broadcast_to(lengths[...], (requests, requests))
            diagonal = iota((requests, requests), 0) == iota((requests, requests), 1)
            length = jnp.sum(jnp.where(diagonal, length_row, 0), axis=-1, keepdims=True)
            lane_id = iota((requests, size), 1)
            low = lane_id < size // 2
            pair_index = jnp.where(low, lane_id, lane_id - size // 2).astype(F32)
            angles = length.astype(F32) * jnp.exp(pair_index * (-2.0 * math.log(10000.0) / size))
            cosine, sine = jnp.cos(angles), jnp.sin(angles)
            sine = jnp.where(low, -sine, sine)
        projected = projected + dot(spread_out[:, part], qkv[part, :])

    cos_rows = jnp.concatenate([cosine] * heads, axis=0)
    sin_rows = jnp.concatenate([sine] * heads, axis=0)
    limit = jnp.concatenate([length] * heads, axis=0)

    def turn(values):
        return (values * cos_rows + pltpu.roll(values, size // 2, 1) * sin_rows).astype(BF16)

    query = turn(projected[:rows])
    fresh_key = turn(projected[rows : 2 * rows])
    fresh_value = projected[2 * rows :].astype(BF16).astype(F32)
    root_size = math.sqrt(size)
    across = (((1,), (1,)), ((), ()))

    self_scores = jnp.sum(query.astype(F32) * fresh_key.astype(F32), axis=-1, keepdims=True) / root_size
    sink_rows = sink[...]
    sink_total = sink_rows.shape[0]
    sink_scores = lax.dot_general(query, sink_rows, across, preferred_element_type=F32) / root_size
    row_id, column = iota((rows, sink_total), 0), iota((rows, sink_total), 1)
    slot = lax.rem(column, 2 * sinks)
    pair = lax.div(column, 2 * sinks)
    sink_valid = (
        (lax.rem(pair, heads) == lax.div(row_id, requests))
        & (lax.div(pair, heads) == lax.rem(row_id, requests))
        & (slot < sinks)
        & (slot < limit)
    )
    sink_scores = jnp.where(sink_valid, sink_scores, -1e30)

    mine = iota((requests, slots), 0)
    for copy in key_copies:
        copy.wait()
    scores = []
    for h in range(heads):
        keys = window[:, h, 0].reshape(requests * slots, size)
        found = lax.dot_general(query[h * requests : (h + 1) * requests], keys, across, preferred_element_type=F32)
        own = jnp.where(mine == 0, found[:, :slots], 0.0)
        for r in range(1, requests):
            own = jnp.where(mine == r, found[:, r * slots : (r + 1) * slots], own)
        scores.append(own)
    scores = jnp.concatenate(scores, axis=0) / root_size
    valid = iota((rows, slots), 1) >= sinks + slots - limit
    scores = jnp.where(valid, scores, -1e30)

    highest = jnp.maximum(
        jnp.maximum(jnp.max(scores, axis=-1, keepdims=True), jnp.max(sink_scores, axis=-1, keepdims=True)),
        self_scores,
    )
    window_exp = jnp.exp(scores - highest)
    sink_exp = jnp.where(sink_valid, jnp.exp(sink_scores - highest), 0.0)
    self_exp = jnp.exp(self_scores - highest)
    total = jnp.sum(window_exp, axis=-1, keepdims=True) + jnp.sum(sink_exp, axis=-1, keepdims=True) + self_exp
    window_weight = (window_exp / total).astype(BF16).astype(F32)
    sink_weight = pltpu.roll(sink_exp / total, sinks, 1).astype(BF16)
    self_weight = (self_exp / total).astype(BF16).astype(F32)
    mixture = dot(sink_weight, sink_rows) + self_weight * fresh_value
    for copy in value_copies:
        copy.wait()
    mixed = []
    for h in range(heads):
        own = window_weight[h * requests : (h + 1) * requests]
        wide = jnp.concatenate([jnp.where(mine == r, own, 0.0) for r in range(requests)], axis=1).astype(BF16)
        values = window[:, h, 1].reshape(requests * slots, size)
        mixed.append(mixture[h * requests : (h + 1) * requests] + dot(wide, values))
    out_copy.wait()
    result[...] = dot(jnp.concatenate(mixed, axis=1).astype(BF16), out_weight[...]).astype(result.dtype)


def attend_fast(hidden, own_lengths, sink_rows, window_rows, qkv_weight, out_weight):
    requests, width = hidden.shape
    heads, sinks, size = sink_rows.shape[1], sink_rows.shape[3], sink_rows.shape[4]
    qkv = qkv_weight.reshape(-1, size)
    out = out_weight.reshape(-1, width)
    return pl.pallas_call(
        lambda *refs: attend_kernel(heads, sinks, *refs),
        out_shape=jax.ShapeDtypeStruct((requests, width), BF16),
        in_specs=[HBM] * 6,
        out_specs=VMEM,
        scratch_shapes=[
            pltpu.VMEM(hidden.shape, BF16),
            pltpu.VMEM((1, requests), jnp.int32),
            pltpu.VMEM((sink_rows.size // size, size), BF16),
            pltpu.VMEM(qkv.shape, BF16),
            pltpu.VMEM(window_rows.shape, BF16),
            pltpu.VMEM(out.shape, BF16),
            pltpu.VMEM((3 * heads * requests, qkv.shape[0]), BF16),
            pltpu.SemaphoreType.DMA((3,)),
            pltpu.SemaphoreType.DMA((8,)),
            pltpu.SemaphoreType.DMA((2, requests)),
            pltpu.SemaphoreType.DMA,
        ],
        compiler_params=pltpu.CompilerParams(vmem_limit_bytes=60 * MEGA),
        name="attend",
    )(
        hidden,
        own_lengths[None, :],
        sink_rows.reshape(-1, size),
        qkv,
        window_rows,
        out,
    )


def expert_kernel(chunks, near, far, *refs):
    w_in, refs = refs[:chunks], refs[chunks:]
    ids_hbm, route_hbm, in_hbm, out_hbm, terms, act, w_near, own_columns, *refs = refs
    rows_scr, ids, route, w_last, w_far, small_sems, last_sems, out_sems = refs
    count, tokens, share = terms.shape
    group = 2 * count
    requests = tokens // group
    units = act.shape[1]
    own = lax.axis_index("guide") * count + lax.axis_index("dp")
    first_expert = (own * lax.axis_size("mp") + lax.axis_index("mp")) * (units // FFE)
    guide, place = lax.axis_index("guide"), lax.axis_index("dp")
    half_width = count * share
    runs = units // out_sems.shape[1]
    out_copies = [
        [
            pltpu.make_async_copy(
                out_hbm.at[pl.ds(i * runs, runs), pl.ds(pl.multiple_of(half * half_width, half_width), half_width)],
                target.at[pl.ds(i * runs, runs), :],
                out_sems.at[k, i],
            )
            for i in range(out_sems.shape[1])
        ]
        for k, (half, target) in enumerate(((1 - guide, w_far), (guide, w_near)))
    ]
    small_copies = [
        pltpu.make_async_copy(ids_hbm, ids, small_sems.at[0]),
        pltpu.make_async_copy(route_hbm, route, small_sems.at[1]),
    ]
    last = w_last.shape[2]
    last_copies = [
        pltpu.make_async_copy(in_hbm.at[k, :, pl.ds(units - last, last)], w_last.at[k], last_sems.at[k])
        for k in range(2)
    ]
    for copy in small_copies + last_copies + out_copies[0] + out_copies[1]:
        copy.start()
    for first, source in ((0, near), (count, far)):
        values = source[...].astype(F32)
        for i in range(count):
            start = pl.multiple_of((own ^ (first + i)) * requests, requests)
            rows_scr[pl.ds(start, requests), :] = values[i * requests : (i + 1) * requests]
    own_columns[...] = rows_scr[:, pl.ds(pl.multiple_of(own * share, share), share)]
    rows = rows_scr[...]
    moe_in = (rows * lax.rsqrt(jnp.mean(rows * rows, axis=-1, keepdims=True) + EPSILON)).astype(BF16)
    for copy in small_copies:
        copy.wait()
    per_stream = ids.shape[2]
    diagonal = iota((per_stream, per_stream), 0) == iota((per_stream, per_stream), 1)

    def factor_of(expert):
        columns = []
        for stream in range(2):
            row = jnp.sum(jnp.where(ids[stream] == expert, route[stream], 0.0), axis=0, keepdims=True)
            spread_out = jnp.broadcast_to(row, (per_stream, per_stream))
            columns.append(jnp.sum(jnp.where(diagonal, spread_out, 0.0), axis=-1, keepdims=True))
        return jnp.concatenate(columns, axis=0)

    start = 0
    for weight in (*w_in, w_last):
        if weight is w_last:
            for copy in last_copies:
                copy.wait()
        unit, start = start, start + weight.shape[2]
        factor = factor_of(first_expert + unit // FFE)
        gate = dot(moe_in, weight[0])
        upward = dot(moe_in, weight[1])
        act[:, unit:start] = (gate / (1.0 + jnp.exp(-gate)) * upward * factor).astype(BF16)
    for copy in out_copies[0]:
        copy.wait()
    for d in range(count):
        terms[place ^ d] = dot(act[...], w_far[:, d * share : (d + 1) * share]).astype(BF16)
    for copy in out_copies[1]:
        copy.wait()


def experts_fast(near, far, expert_ids, route_weight, w_in, expert_in, expert_out, share):
    width = near.shape[1]
    count = lax.axis_size("dp")
    tokens = 2 * near.shape[0]
    units = expert_out.shape[0]
    last = units - sum(weight.shape[2] for weight in w_in)
    top = expert_ids.shape[-1]
    return pl.pallas_call(
        lambda *refs: expert_kernel(len(w_in), *refs),
        out_shape=[
            jax.ShapeDtypeStruct((count, tokens, share), BF16),
            jax.ShapeDtypeStruct((tokens, units), BF16),
            jax.ShapeDtypeStruct((units, count * share), BF16),
            jax.ShapeDtypeStruct((tokens, share), F32),
        ],
        in_specs=[VMEM] * (2 + len(w_in)) + [HBM] * 4,
        out_specs=[VMEM] * 4,
        scratch_shapes=[
            pltpu.VMEM((tokens, width), F32),
            pltpu.VMEM((2, top, tokens // 2), jnp.int32),
            pltpu.VMEM((2, top, tokens // 2), F32),
            pltpu.VMEM((2, width, last), BF16),
            pltpu.VMEM((units, count * share), BF16),
            pltpu.SemaphoreType.DMA((2,)),
            pltpu.SemaphoreType.DMA((2,)),
            pltpu.SemaphoreType.DMA((2, 4)),
        ],
        compiler_params=pltpu.CompilerParams(vmem_limit_bytes=29 * MEGA),
        name="experts",
    )(near, far, *w_in, jnp.swapaxes(expert_ids, 1, 2), jnp.swapaxes(route_weight, 1, 2), expert_in, expert_out)


def down_kernel(act, weight, terms):
    count, _, share = terms.shape
    place = lax.axis_index("dp")
    for d in range(count):
        terms[place ^ d] = dot(act[...], weight[:, d * share : (d + 1) * share]).astype(BF16)


def down_fast(act, weight, share):
    tokens, units = act.shape
    count = weight.shape[1] // share
    return pl.pallas_call(
        down_kernel,
        out_shape=jax.ShapeDtypeStruct((count, tokens, share), BF16),
        in_specs=[VMEM] * 2,
        out_specs=VMEM,
        compiler_params=pltpu.CompilerParams(vmem_limit_bytes=8 * MEGA),
        cost_estimate=pl.CostEstimate(
            flops=2 * tokens * units * count * share, bytes_accessed=2 * units * count * share, transcendentals=0
        ),
        name="down",
    )(act, weight)


def add_up(blocks):
    total = blocks[0][...].astype(F32)
    for block in blocks[1:]:
        total = total + block[...].astype(F32)
    return total


def sum_kernel(*refs):
    refs[-1][...] = add_up(refs[:-1]).astype(BF16)


def sum_fast(blocks):
    return pl.pallas_call(
        sum_kernel,
        out_shape=jax.ShapeDtypeStruct(blocks[0].shape, BF16),
        in_specs=[VMEM] * len(blocks),
        out_specs=VMEM,
        compiler_params=pltpu.CompilerParams(vmem_limit_bytes=8 * MEGA),
        name="add_up",
    )(*blocks)


def head_kernel(chunk, other, own_columns, left, right, weight, target):
    tokens = own_columns.shape[0]
    count, rows, _ = target.shape
    requests = rows // 2
    half_width = weight.shape[1] // 2
    per_half = half_width // chunk
    guide, own = lax.axis_index("guide"), lax.axis_index("dp")
    summed = own_columns[...] + (left[...].astype(F32) + right[...].astype(F32))

    def hand_out(values, start):
        for d in range(count):
            target[own ^ d, :, start : start + values.shape[1]] = jnp.concatenate(
                [values[d * requests : (d + 1) * requests], values[tokens // 2 + d * requests : tokens // 2 + (d + 1) * requests]],
                axis=0,
            ).astype(BF16)

    squares = jnp.broadcast_to(jnp.sum(summed * summed, axis=-1, keepdims=True), (tokens, NOTE))
    raw_in = summed.astype(BF16)
    half = 1 - guide if other else guide
    hand_out(squares, half_width)
    for c in range(per_half):
        first = pl.multiple_of(half * half_width + c * chunk, 128)
        hand_out(dot(raw_in, weight[:, pl.ds(first, chunk)]), c * chunk)


def head_fast(other, own_columns, left, right, weight):
    count = lax.axis_size("dp")
    tokens = own_columns.shape[0]
    half_width = weight.shape[1] // 2
    return pl.pallas_call(
        lambda *refs: head_kernel(256, other, *refs),
        out_shape=jax.ShapeDtypeStruct((count, tokens // count, half_width + NOTE), BF16),
        in_specs=[VMEM] * 4,
        out_specs=VMEM,
        compiler_params=pltpu.CompilerParams(vmem_limit_bytes=12 * MEGA),
        cost_estimate=pl.CostEstimate(
            flops=tokens * weight.size, bytes_accessed=weight.size, transcendentals=0
        ),
        name="head",
    )(own_columns, left, right, weight)


def pair_kernel(near, received, *results):
    for k, result in enumerate(results):
        result[...] = (near[k].astype(F32) + received[k].astype(F32)).astype(BF16)


def pair_fast(near, received):
    count = near.shape[0]
    return pl.pallas_call(
        pair_kernel,
        out_shape=[jax.ShapeDtypeStruct(near.shape[1:], BF16)] * count,
        in_specs=[VMEM, VMEM],
        out_specs=[VMEM] * count,
        compiler_params=pltpu.CompilerParams(vmem_limit_bytes=8 * MEGA),
        name="pair",
    )(near, received)


def guide_kernel(width, weight, *refs):
    result = refs[-1]
    requests, half_width = result.shape[0], result.shape[3]
    total = add_up(refs[:-1])
    scale = lax.rsqrt(total[:, half_width : half_width + 1] / width + EPSILON)
    diagonal = iota((requests, requests), 0) == iota((requests, requests), 1)
    guidance = jnp.broadcast_to(weight[...], (requests, requests))
    factor = jnp.sum(jnp.where(diagonal, guidance, 0.0), axis=-1, keepdims=True)
    guided = total[:requests, :half_width] * (scale[:requests] * factor) + total[requests:, :half_width] * (
        scale[requests:] * (1.0 - factor)
    )
    for r in range(requests):
        result[r, 0] = guided[r : r + 1]


def guide_fast(blocks, guidance, width):
    rows, columns = blocks[0].shape
    return pl.pallas_call(
        lambda *refs: guide_kernel(width, *refs),
        out_shape=jax.ShapeDtypeStruct((rows // 2, 1, 1, columns - NOTE), F32),
        in_specs=[VMEM] * (1 + len(blocks)),
        out_specs=VMEM,
        compiler_params=pltpu.CompilerParams(vmem_limit_bytes=12 * MEGA),
        name="guide",
    )(guidance[None, :], *blocks)


def fits(hidden, sink_rows, expert_in, vocab_weight):
    return (
        lax.axis_size(ROWS) == 8
        and lax.axis_size("mp") == 4
        and hidden.shape[0] == 8
        and sink_rows.shape[1] == 4
        and expert_in.shape[2] % (2 * FFE) == 0
        and vocab_weight.shape[0] % 128 == 0
        and vocab_weight.shape[1] % 512 == 0
    )


def fast_body(
    states,
    lengths,
    sink_cache,
    window_cache,
    qkv_weight,
    out_weight,
    expert_ids,
    route_weight,
    expert_in,
    expert_out,
    vocab_weight,
    guidance,
):
    hidden = states[0]
    partial_out = attend_fast(hidden, lengths[0], sink_cache[0], window_cache[0], qkv_weight, out_weight)
    chunk = expert_in.shape[2] // 4
    received = step(partial_out, "mp", 1)
    w0 = load_fast(expert_in, 0, chunk, 47, lengths)
    pair = join_fast(True, [partial_out, received], w0)
    received = step(pair, "mp", 2)
    w1 = load_fast(expert_in, chunk, chunk, 43, pair)
    residual = join_fast(True, [hidden, pair, received], w1)
    blocks = swap([residual] * lax.axis_size("dp"), "dp")
    w2 = load_fast(expert_in, 2 * chunk, chunk, 39, residual)
    near = join_fast(False, blocks, w2)
    far = step(near, "guide", 1)
    w3 = load_fast(expert_in, 3 * chunk, chunk // 2, 37, near)
    share = vocab_weight.shape[0]
    terms, act, w_near, own_columns = experts_fast(
        near, far, expert_ids, route_weight, [w0, w1, w2, w3], expert_in, expert_out, share
    )
    received = step(terms, "guide", 1)
    part = sum_fast(swap(pair_fast(down_fast(act, w_near, share), received), "dp"))
    received = step(part, "mp", 1)
    pair = (part.astype(F32) + received.astype(F32)).astype(BF16)
    received = step(pair, "mp", 2)
    far = step(head_fast(True, own_columns, pair, received, vocab_weight), "guide", 1)
    near = head_fast(False, own_columns, pair, received, vocab_weight)
    logits = swap(pair_fast(near, far), "dp")
    return guide_fast(logits, guidance, hidden.shape[1])


def rotate(vectors, positions):
    full_width = vectors.shape[-1]
    half_width = full_width // 2
    step_index = jnp.arange(half_width, dtype=jnp.float32)
    inverse = jnp.exp(step_index * (-2.0 * math.log(10000.0) / full_width))
    angles = positions.astype(jnp.float32)[:, None] * inverse[None, :]
    cosine = jnp.cos(angles)[:, None, :]
    sine_part = jnp.sin(angles)[:, None, :]
    first_half = vectors[..., :half_width]
    second = vectors[..., half_width:]
    return jnp.concatenate(
        [first_half * cosine - second * sine_part, second * cosine + first_half * sine_part],
        axis=-1,
    )


def rms_norm(values):
    return values * lax.rsqrt(jnp.mean(values * values, axis=-1, keepdims=True) + EPSILON)


def attend(hidden, own_lengths, sink_rows, window_rows, qkv_weight, out_weight):
    normed = rms_norm(hidden.astype(jnp.float32)).astype(jnp.bfloat16)
    projected = jnp.einsum("rd,dthe->rthe", normed, qkv_weight, preferred_element_type=jnp.float32)
    query_rot = rotate(projected[:, 0], own_lengths).astype(jnp.bfloat16)
    fresh_key = rotate(projected[:, 1], own_lengths).astype(jnp.bfloat16)
    fresh_value = projected[:, 2].astype(jnp.bfloat16)
    sink_count = sink_rows.shape[3]
    window_count = window_rows.shape[3]
    root_size = math.sqrt(query_rot.shape[-1])
    sink_scores = (
        jnp.einsum(
            "rhe,rhse->rhs", query_rot, sink_rows[:, :, 0], preferred_element_type=jnp.float32
        )
        / root_size
    )
    window_scores = (
        jnp.einsum(
            "rhe,rhwe->rhw", query_rot, window_rows[:, :, 0], preferred_element_type=jnp.float32
        )
        / root_size
    )
    self_scores = (
        jnp.einsum("rhe,rhe->rh", query_rot, fresh_key, preferred_element_type=jnp.float32)
        / root_size
    )
    length_limit = own_lengths[:, None, None]
    sink_valid = jnp.arange(sink_count, dtype=jnp.int32)[None, None, :] < length_limit
    window_valid = (
        jnp.arange(window_count, dtype=jnp.int32)[None, None, :]
        >= sink_count + window_count - length_limit
    )
    sink_scores = jnp.where(sink_valid, sink_scores, -1e30)
    window_scores = jnp.where(window_valid, window_scores, -1e30)
    highest = jnp.maximum(
        jnp.maximum(jnp.max(sink_scores, axis=-1), jnp.max(window_scores, axis=-1)), self_scores
    )
    sink_exp = jnp.exp(sink_scores - highest[..., None])
    window_exp = jnp.exp(window_scores - highest[..., None])
    self_exp = jnp.exp(self_scores - highest)
    totals = jnp.sum(sink_exp, axis=-1) + jnp.sum(window_exp, axis=-1) + self_exp
    sink_prob = (sink_exp / totals[..., None]).astype(jnp.bfloat16)
    window_prob = (window_exp / totals[..., None]).astype(jnp.bfloat16)
    self_prob = (self_exp / totals).astype(jnp.bfloat16)
    mixture = (
        jnp.einsum(
            "rhs,rhse->rhe", sink_prob, sink_rows[:, :, 1], preferred_element_type=jnp.float32
        )
        + jnp.einsum(
            "rhw,rhwe->rhe", window_prob, window_rows[:, :, 1], preferred_element_type=jnp.float32
        )
        + self_prob[..., None].astype(jnp.float32) * fresh_value.astype(jnp.float32)
    ).astype(jnp.bfloat16)
    return jnp.einsum("rhe,hed->rd", mixture, out_weight, preferred_element_type=jnp.float32)


def body(
    states,
    lengths,
    sink_cache,
    window_cache,
    qkv_weight,
    out_weight,
    expert_ids,
    route_weight,
    expert_in,
    expert_out,
    vocab_weight,
    guidance,
):
    hidden = states[0]
    if fits(hidden, sink_cache[0], expert_in, vocab_weight):
        return fast_body(
            states,
            lengths,
            sink_cache,
            window_cache,
            qkv_weight,
            out_weight,
            expert_ids,
            route_weight,
            expert_in,
            expert_out,
            vocab_weight,
            guidance,
        )
    request_count, width = hidden.shape
    group = lax.axis_size(ROWS)
    mp = lax.axis_size("mp")
    tokens = group * request_count

    partial_out = attend(hidden, lengths[0], sink_cache[0], window_cache[0], qkv_weight, out_weight)
    first = lax.axis_index("mp") == 0
    partial_out = partial_out + jnp.where(first, hidden.astype(jnp.float32), 0.0)
    partials = spread(partial_out.astype(jnp.bfloat16), ALL).reshape(group, mp, request_count, width)
    residual = jnp.sum(partials.astype(jnp.float32), axis=1).reshape(tokens, width).astype(jnp.bfloat16)
    moe_in = rms_norm(residual.astype(jnp.float32)).astype(jnp.bfloat16)

    unit_count = expert_in.shape[2]
    unit_start = lax.axis_index(ALL) * unit_count
    unit_expert = (unit_start + jnp.arange(unit_count, dtype=jnp.int32)) // FFE
    choice_rows = expert_ids.reshape(-1, expert_ids.shape[-1])
    route_rows = route_weight.reshape(-1, route_weight.shape[-1])
    coefficient = jnp.sum(
        jnp.where(
            choice_rows[:, :, None] == unit_expert[None, None, :], route_rows[:, :, None], 0.0
        ),
        axis=1,
    )
    gate = jnp.dot(moe_in, expert_in[0], preferred_element_type=jnp.float32)
    upward = jnp.dot(moe_in, expert_in[1], preferred_element_type=jnp.float32)
    activated = (jax.nn.silu(gate) * upward * coefficient).astype(jnp.bfloat16)
    expert_terms = jnp.dot(activated, expert_out, preferred_element_type=jnp.float32).astype(jnp.bfloat16)

    share = vocab_weight.shape[0]
    sent = jnp.swapaxes(expert_terms.reshape(tokens, group, share), 0, 1)
    expert_part = jnp.sum(trade(sent, ROWS).astype(jnp.float32), axis=0)
    expert_total = jnp.sum(spread(expert_part.astype(jnp.bfloat16), "mp").astype(jnp.float32), axis=0)
    own_columns = lax.dynamic_slice_in_dim(residual, lax.axis_index(ROWS) * share, share, 1)
    summed = own_columns.astype(jnp.float32) + expert_total

    squares = jnp.sum(summed * summed, axis=-1)
    notes = spread(jnp.concatenate([squares, guidance]), ROWS)
    scale = lax.rsqrt(jnp.sum(notes[:, :tokens], axis=0) / width + EPSILON).reshape(2, -1, 1)
    weight = notes[: group // 2, tokens:].reshape(-1, 1)

    raw = jnp.dot(summed.astype(jnp.bfloat16), vocab_weight, preferred_element_type=jnp.float32)
    raw = raw.reshape(2, tokens // 2, -1)
    mixed = raw[0] * (scale[0] * weight) + raw[1] * (scale[1] * (1.0 - weight))
    half_width = mixed.shape[1] // 2
    mixed = mixed.astype(jnp.bfloat16).reshape(group // 2, request_count, 2, half_width)
    sent = jnp.transpose(mixed, (2, 0, 1, 3)).reshape(group, request_count, half_width)
    guided = jnp.sum(trade(sent, ROWS).astype(jnp.float32), axis=0)
    return guided.reshape(request_count, 1, 1, half_width)


def solution(mesh):
    in_specs = (
        P("guide", "dp", None),
        P("guide", "dp"),
        P("guide", "dp", "mp", None, None, None),
        P("guide", "dp", "mp", None, None, None),
        P(None, None, "mp", None),
        P("mp", None, None),
        P(),
        P(),
        P(None, None, ("guide", "dp", "mp")),
        P(("guide", "dp", "mp"), None),
        P(("guide", "dp"), "mp"),
        P("dp"),
    )
    out_specs = P("dp", "mp", "guide", None)
    return jax.shard_map(body, mesh=mesh, in_specs=in_specs, out_specs=out_specs, check_vma=False)
```

```python
import math

import jax
import jax.numpy as jnp
from jax import lax
from jax.experimental import pallas as pl
from jax.experimental.pallas import tpu as pltpu
from jax.sharding import PartitionSpec as P

FFE = 1024

EPSILON = 1e-05

ROWS = ("guide", "dp")
ALL = ("guide", "dp", "mp")


def trade(blocks, axis):
    return lax.all_to_all(blocks, axis, 0, 0, tiled=True)


def spread(block, axis):
    return trade(jnp.broadcast_to(block[None], (lax.axis_size(axis),) + block.shape), axis)


def step(block, axis, bit):
    count = lax.axis_size(axis)
    return lax.ppermute(block, axis, [(i, i ^ bit) for i in range(count)])


def swap(blocks, axis):
    return [blocks[0]] + [step(blocks[j], axis, j) for j in range(1, lax.axis_size(axis))]


F32 = jnp.float32
BF16 = jnp.bfloat16
VMEM = pl.BlockSpec(memory_space=pltpu.VMEM)
ANY = pl.BlockSpec(memory_space=pl.ANY)
HBM = pl.BlockSpec(memory_space=pltpu.HBM)
MEGA = 1 << 20
NOTE = 128


def dot(left, right):
    return jnp.dot(left, right, preferred_element_type=F32)


def iota(shape, dim):
    return lax.broadcasted_iota(jnp.int32, shape, dim)


def load_kernel(first, chunk, hbm, after, result, sems):
    rows = hbm.shape[1] // sems.shape[1]
    copies = [
        pltpu.make_async_copy(
            hbm.at[k, pl.ds(i * rows, rows), pl.ds(first, chunk)],
            result.at[k, pl.ds(i * rows, rows), :],
            sems.at[k, i],
        )
        for k in range(hbm.shape[0])
        for i in range(sems.shape[1])
    ]
    for copy in copies:
        copy.start()
    for copy in copies:
        copy.wait()


def load_fast(weight, first, chunk, room, after):
    kinds, width, _ = weight.shape
    return pl.pallas_call(
        lambda *refs: load_kernel(first, chunk, *refs),
        out_shape=jax.ShapeDtypeStruct((kinds, width, chunk), BF16),
        in_specs=[HBM, ANY],
        out_specs=VMEM,
        scratch_shapes=[pltpu.SemaphoreType.DMA((kinds, 4))],
        compiler_params=pltpu.CompilerParams(vmem_limit_bytes=room * MEGA),
        cost_estimate=pl.CostEstimate(flops=0, bytes_accessed=4 * kinds * width * chunk, transcendentals=0),
        name="load",
    )(weight, after)


def join_kernel(total, count, *refs):
    values = [ref[...].astype(F32) for ref in refs[:count]]
    joined = sum(values[1:], values[0]) if total else jnp.concatenate(values, axis=0)
    refs[-1][...] = joined.astype(BF16)


def join_fast(total, blocks, after):
    rows, columns = blocks[0].shape
    return pl.pallas_call(
        lambda *refs: join_kernel(total, len(blocks), *refs),
        out_shape=jax.ShapeDtypeStruct((rows if total else rows * len(blocks), columns), BF16),
        in_specs=[VMEM] * len(blocks) + [ANY],
        out_specs=VMEM,
        compiler_params=pltpu.CompilerParams(vmem_limit_bytes=4 * MEGA),
        name="join",
    )(*blocks, after)


def attend_kernel(
    heads, sinks, states_hbm, lengths_hbm, sink_hbm, qkv_hbm, window_hbm, out_hbm, result,
    states, lengths, sink, qkv, window, out_weight, spread_out, first_sems, qkv_sems, window_sems, out_sem,
):
    requests, width = states.shape
    size = sink.shape[1]
    parts = 3 * heads
    lanes = size * parts
    blocks = width // size
    chunks = qkv_sems.shape[0]
    chunk_rows = qkv.shape[0] // chunks
    slots = window.shape[3]
    rows = heads * requests
    qkv_copies = [
        pltpu.make_async_copy(
            qkv_hbm.at[pl.ds(c * chunk_rows, chunk_rows)], qkv.at[pl.ds(c * chunk_rows, chunk_rows)], qkv_sems.at[c]
        )
        for c in range(chunks)
    ]
    key_copies, value_copies = [
        [
            pltpu.make_async_copy(window_hbm.at[r, :, k], window.at[r, :, k], window_sems.at[k, r])
            for r in range(requests)
        ]
        for k in range(2)
    ]
    out_copy = pltpu.make_async_copy(out_hbm, out_weight, out_sem)
    first_copies = [
        pltpu.make_async_copy(source, target, first_sems.at[i])
        for i, (source, target) in enumerate(((states_hbm, states), (lengths_hbm, lengths), (sink_hbm, sink)))
    ]
    for copy in first_copies + qkv_copies[: chunks // 2]:
        copy.start()
    sub, lane = iota((size, lanes), 0) * parts, iota((size, lanes), 1)
    repeat = jnp.where((lane >= sub) & (lane < sub + parts), 1.0, 0.0).astype(BF16)
    kind = lax.rem(iota((requests, lanes), 1), parts)
    for copy in first_copies:
        copy.wait()
    for copy in qkv_copies[chunks // 2 :]:
        copy.start()
    hidden = states[...].astype(F32)
    normed = hidden * lax.rsqrt(jnp.mean(hidden * hidden, axis=-1, keepdims=True) + EPSILON)
    stacked = jnp.concatenate([normed[:, b * size : (b + 1) * size] for b in range(blocks)], axis=0)
    repeated = dot(stacked.astype(BF16), repeat)
    run = blocks // chunks

    def lay_out(c):
        for b in range(c * run, (c + 1) * run):
            piece = repeated[b * requests : (b + 1) * requests]
            spread_out[:, b * lanes : (b + 1) * lanes] = jnp.concatenate(
                [jnp.where(kind == p, piece, 0.0) for p in range(parts)], axis=0
            ).astype(BF16)

    lay_out(0)
    projected = jnp.zeros((parts * requests, size), F32)
    for copy in key_copies:
        copy.start()
    later = {chunks // 4: value_copies, chunks // 2: [out_copy]}
    for c in range(chunks):
        qkv_copies[c].wait()
        for copy in later.get(c, []):
            copy.start()
        part = slice(c * chunk_rows, (c + 1) * chunk_rows)
        if c + 1 < chunks:
            lay_out(c + 1)
        if c == chunks - 1:
            length_row = jnp.broadcast_to(lengths[...], (requests, requests))
            diagonal = iota((requests, requests), 0) == iota((requests, requests), 1)
            length = jnp.sum(jnp.where(diagonal, length_row, 0), axis=-1, keepdims=True)
            lane_id = iota((requests, size), 1)
            low = lane_id < size // 2
            pair_index = jnp.where(low, lane_id, lane_id - size // 2).astype(F32)
            angles = length.astype(F32) * jnp.exp(pair_index * (-2.0 * math.log(10000.0) / size))
            cosine, sine = jnp.cos(angles), jnp.sin(angles)
            sine = jnp.where(low, -sine, sine)
        projected = projected + dot(spread_out[:, part], qkv[part, :])

    cos_rows = jnp.concatenate([cosine] * heads, axis=0)
    sin_rows = jnp.concatenate([sine] * heads, axis=0)
    limit = jnp.concatenate([length] * heads, axis=0)

    def turn(values):
        return (values * cos_rows + pltpu.roll(values, size // 2, 1) * sin_rows).astype(BF16)

    query = turn(projected[:rows])
    fresh_key = turn(projected[rows : 2 * rows])
    fresh_value = projected[2 * rows :].astype(BF16).astype(F32)
    root_size = math.sqrt(size)
    across = (((1,), (1,)), ((), ()))

    self_scores = jnp.sum(query.astype(F32) * fresh_key.astype(F32), axis=-1, keepdims=True) / root_size
    sink_rows = sink[...]
    sink_total = sink_rows.shape[0]
    sink_scores = lax.dot_general(query, sink_rows, across, preferred_element_type=F32) / root_size
    row_id, column = iota((rows, sink_total), 0), iota((rows, sink_total), 1)
    slot = lax.rem(column, 2 * sinks)
    pair = lax.div(column, 2 * sinks)
    sink_valid = (
        (lax.rem(pair, heads) == lax.div(row_id, requests))
        & (lax.div(pair, heads) == lax.rem(row_id, requests))
        & (slot < sinks)
        & (slot < limit)
    )
    sink_scores = jnp.where(sink_valid, sink_scores, -1e30)

    mine = iota((requests, slots), 0)
    for copy in key_copies:
        copy.wait()
    scores = []
    for h in range(heads):
        keys = window[:, h, 0].reshape(requests * slots, size)
        found = lax.dot_general(query[h * requests : (h + 1) * requests], keys, across, preferred_element_type=F32)
        own = jnp.where(mine == 0, found[:, :slots], 0.0)
        for r in range(1, requests):
            own = jnp.where(mine == r, found[:, r * slots : (r + 1) * slots], own)
        scores.append(own)
    scores = jnp.concatenate(scores, axis=0) / root_size
    valid = iota((rows, slots), 1) >= sinks + slots - limit
    scores = jnp.where(valid, scores, -1e30)

    highest = jnp.maximum(
        jnp.maximum(jnp.max(scores, axis=-1, keepdims=True), jnp.max(sink_scores, axis=-1, keepdims=True)),
        self_scores,
    )
    window_exp = jnp.exp(scores - highest)
    sink_exp = jnp.where(sink_valid, jnp.exp(sink_scores - highest), 0.0)
    self_exp = jnp.exp(self_scores - highest)
    total = jnp.sum(window_exp, axis=-1, keepdims=True) + jnp.sum(sink_exp, axis=-1, keepdims=True) + self_exp
    window_weight = (window_exp / total).astype(BF16).astype(F32)
    sink_weight = pltpu.roll(sink_exp / total, sinks, 1).astype(BF16)
    self_weight = (self_exp / total).astype(BF16).astype(F32)
    mixture = dot(sink_weight, sink_rows) + self_weight * fresh_value
    for copy in value_copies:
        copy.wait()
    mixed = []
    for h in range(heads):
        own = window_weight[h * requests : (h + 1) * requests]
        wide = jnp.concatenate([jnp.where(mine == r, own, 0.0) for r in range(requests)], axis=1).astype(BF16)
        values = window[:, h, 1].reshape(requests * slots, size)
        mixed.append(mixture[h * requests : (h + 1) * requests] + dot(wide, values))
    out_copy.wait()
    result[...] = dot(jnp.concatenate(mixed, axis=1).astype(BF16), out_weight[...]).astype(result.dtype)


def attend_fast(hidden, own_lengths, sink_rows, window_rows, qkv_weight, out_weight):
    requests, width = hidden.shape
    heads, sinks, size = sink_rows.shape[1], sink_rows.shape[3], sink_rows.shape[4]
    qkv = qkv_weight.reshape(-1, size)
    out = out_weight.reshape(-1, width)
    return pl.pallas_call(
        lambda *refs: attend_kernel(heads, sinks, *refs),
        out_shape=jax.ShapeDtypeStruct((requests, width), BF16),
        in_specs=[HBM] * 6,
        out_specs=VMEM,
        scratch_shapes=[
            pltpu.VMEM(hidden.shape, BF16),
            pltpu.VMEM((1, requests), jnp.int32),
            pltpu.VMEM((sink_rows.size // size, size), BF16),
            pltpu.VMEM(qkv.shape, BF16),
            pltpu.VMEM(window_rows.shape, BF16),
            pltpu.VMEM(out.shape, BF16),
            pltpu.VMEM((3 * heads * requests, qkv.shape[0]), BF16),
            pltpu.SemaphoreType.DMA((3,)),
            pltpu.SemaphoreType.DMA((8,)),
            pltpu.SemaphoreType.DMA((2, requests)),
            pltpu.SemaphoreType.DMA,
        ],
        compiler_params=pltpu.CompilerParams(vmem_limit_bytes=60 * MEGA),
        name="attend",
    )(
        hidden,
        own_lengths[None, :],
        sink_rows.reshape(-1, size),
        qkv,
        window_rows,
        out,
    )


def expert_kernel(chunks, near, far, *refs):
    w_in, refs = refs[:chunks], refs[chunks:]
    ids_hbm, route_hbm, in_hbm, out_hbm, terms, act, w_near, own_columns, *refs = refs
    rows_scr, ids, route, w_last, w_far, small_sems, last_sems, out_sems = refs
    count, tokens, share = terms.shape
    group = 2 * count
    requests = tokens // group
    units = act.shape[1]
    own = lax.axis_index("guide") * count + lax.axis_index("dp")
    first_expert = (own * lax.axis_size("mp") + lax.axis_index("mp")) * (units // FFE)
    guide, place = lax.axis_index("guide"), lax.axis_index("dp")
    half_width = count * share
    runs = units // out_sems.shape[1]
    out_copies = [
        [
            pltpu.make_async_copy(
                out_hbm.at[pl.ds(i * runs, runs), pl.ds(pl.multiple_of(half * half_width, half_width), half_width)],
                target.at[pl.ds(i * runs, runs), :],
                out_sems.at[k, i],
            )
            for i in range(out_sems.shape[1])
        ]
        for k, (half, target) in enumerate(((1 - guide, w_far), (guide, w_near)))
    ]
    small_copies = [
        pltpu.make_async_copy(ids_hbm, ids, small_sems.at[0]),
        pltpu.make_async_copy(route_hbm, route, small_sems.at[1]),
    ]
    last = w_last.shape[2]
    last_copies = [
        pltpu.make_async_copy(in_hbm.at[k, :, pl.ds(units - last, last)], w_last.at[k], last_sems.at[k])
        for k in range(2)
    ]
    for copy in small_copies + last_copies + out_copies[0] + out_copies[1]:
        copy.start()
    for first, source in ((0, near), (count, far)):
        values = source[...].astype(F32)
        for i in range(count):
            start = pl.multiple_of((own ^ (first + i)) * requests, requests)
            rows_scr[pl.ds(start, requests), :] = values[i * requests : (i + 1) * requests]
    own_columns[...] = rows_scr[:, pl.ds(pl.multiple_of(own * share, share), share)]
    rows = rows_scr[...]
    moe_in = (rows * lax.rsqrt(jnp.mean(rows * rows, axis=-1, keepdims=True) + EPSILON)).astype(BF16)
    for copy in small_copies:
        copy.wait()
    per_stream = ids.shape[2]
    diagonal = iota((per_stream, per_stream), 0) == iota((per_stream, per_stream), 1)

    def factor_of(expert):
        columns = []
        for stream in range(2):
            row = jnp.sum(jnp.where(ids[stream] == expert, route[stream], 0.0), axis=0, keepdims=True)
            spread_out = jnp.broadcast_to(row, (per_stream, per_stream))
            columns.append(jnp.sum(jnp.where(diagonal, spread_out, 0.0), axis=-1, keepdims=True))
        return jnp.concatenate(columns, axis=0)

    start = 0
    for weight in (*w_in, w_last):
        if weight is w_last:
            for copy in last_copies:
                copy.wait()
        unit, start = start, start + weight.shape[2]
        factor = factor_of(first_expert + unit // FFE)
        gate = dot(moe_in, weight[0])
        upward = dot(moe_in, weight[1])
        act[:, unit:start] = (gate / (1.0 + jnp.exp(-gate)) * upward * factor).astype(BF16)
    for copy in out_copies[0]:
        copy.wait()
    for d in range(count):
        terms[place ^ d] = dot(act[...], w_far[:, d * share : (d + 1) * share]).astype(BF16)
    for copy in out_copies[1]:
        copy.wait()


def experts_fast(near, far, expert_ids, route_weight, w_in, expert_in, expert_out, share):
    width = near.shape[1]
    count = lax.axis_size("dp")
    tokens = 2 * near.shape[0]
    units = expert_out.shape[0]
    last = units - sum(weight.shape[2] for weight in w_in)
    top = expert_ids.shape[-1]
    return pl.pallas_call(
        lambda *refs: expert_kernel(len(w_in), *refs),
        out_shape=[
            jax.ShapeDtypeStruct((count, tokens, share), BF16),
            jax.ShapeDtypeStruct((tokens, units), BF16),
            jax.ShapeDtypeStruct((units, count * share), BF16),
            jax.ShapeDtypeStruct((tokens, share), F32),
        ],
        in_specs=[VMEM] * (2 + len(w_in)) + [HBM] * 4,
        out_specs=[VMEM] * 4,
        scratch_shapes=[
            pltpu.VMEM((tokens, width), F32),
            pltpu.VMEM((2, top, tokens // 2), jnp.int32),
            pltpu.VMEM((2, top, tokens // 2), F32),
            pltpu.VMEM((2, width, last), BF16),
            pltpu.VMEM((units, count * share), BF16),
            pltpu.SemaphoreType.DMA((2,)),
            pltpu.SemaphoreType.DMA((2,)),
            pltpu.SemaphoreType.DMA((2, 4)),
        ],
        compiler_params=pltpu.CompilerParams(vmem_limit_bytes=29 * MEGA),
        name="experts",
    )(near, far, *w_in, jnp.swapaxes(expert_ids, 1, 2), jnp.swapaxes(route_weight, 1, 2), expert_in, expert_out)


def down_kernel(act, weight, terms):
    count, _, share = terms.shape
    place = lax.axis_index("dp")
    for d in range(count):
        terms[place ^ d] = dot(act[...], weight[:, d * share : (d + 1) * share]).astype(BF16)


def down_fast(act, weight, share):
    tokens, units = act.shape
    count = weight.shape[1] // share
    return pl.pallas_call(
        down_kernel,
        out_shape=jax.ShapeDtypeStruct((count, tokens, share), BF16),
        in_specs=[VMEM] * 2,
        out_specs=VMEM,
        compiler_params=pltpu.CompilerParams(vmem_limit_bytes=8 * MEGA),
        cost_estimate=pl.CostEstimate(
            flops=2 * tokens * units * count * share, bytes_accessed=2 * units * count * share, transcendentals=0
        ),
        name="down",
    )(act, weight)


def add_up(blocks):
    total = blocks[0][...].astype(F32)
    for block in blocks[1:]:
        total = total + block[...].astype(F32)
    return total


def sum_kernel(*refs):
    refs[-1][...] = add_up(refs[:-1]).astype(BF16)


def sum_fast(blocks):
    return pl.pallas_call(
        sum_kernel,
        out_shape=jax.ShapeDtypeStruct(blocks[0].shape, BF16),
        in_specs=[VMEM] * len(blocks),
        out_specs=VMEM,
        compiler_params=pltpu.CompilerParams(vmem_limit_bytes=8 * MEGA),
        name="add_up",
    )(*blocks)


def head_kernel(chunk, other, own_columns, left, right, weight, early, target, scratch):
    tokens = own_columns.shape[0]
    rows = early.shape[0]
    count = tokens // rows
    requests = rows // 2
    half_width = weight.shape[1] // 2
    per_half = half_width // chunk
    guide, own = lax.axis_index("guide"), lax.axis_index("dp")
    summed = own_columns[...] + (left[...].astype(F32) + right[...].astype(F32))

    def hand_out(values, start):
        width = values.shape[1]
        scratch[:, :width] = values
        for k in range(count):
            first = pl.multiple_of((own ^ k) * requests, requests)
            second = pl.multiple_of(tokens // 2 + (own ^ k) * requests, requests)
            block = jnp.concatenate(
                [scratch[pl.ds(first, requests), :width], scratch[pl.ds(second, requests), :width]], axis=0
            ).astype(BF16)
            if k == count - 1:
                early[:, start : start + width] = block
            else:
                target[k, :, start : start + width] = block

    squares = jnp.broadcast_to(jnp.sum(summed * summed, axis=-1, keepdims=True), (tokens, NOTE))
    raw_in = summed.astype(BF16)
    half = 1 - guide if other else guide
    hand_out(squares, half_width)
    for c in range(per_half):
        first = pl.multiple_of(half * half_width + c * chunk, 128)
        hand_out(dot(raw_in, weight[:, pl.ds(first, chunk)]), c * chunk)


def head_fast(other, own_columns, left, right, weight):
    count = lax.axis_size("dp")
    tokens = own_columns.shape[0]
    half_width = weight.shape[1] // 2
    return pl.pallas_call(
        lambda *refs: head_kernel(256, other, *refs),
        out_shape=[
            jax.ShapeDtypeStruct((tokens // count, half_width + NOTE), BF16),
            jax.ShapeDtypeStruct((count - 1, tokens // count, half_width + NOTE), BF16),
        ],
        in_specs=[VMEM] * 4,
        out_specs=[VMEM] * 2,
        scratch_shapes=[pltpu.VMEM((tokens, 256), F32)],
        compiler_params=pltpu.CompilerParams(vmem_limit_bytes=12 * MEGA),
        cost_estimate=pl.CostEstimate(
            flops=tokens * weight.size, bytes_accessed=weight.size, transcendentals=0
        ),
        name="head",
    )(own_columns, left, right, weight)


def early_kernel(near, received, waiting, total, passed):
    total[...] = add_up([near, received]).astype(BF16)
    passed[...] = waiting[...]


def early_fast(near, received, waiting):
    return pl.pallas_call(
        early_kernel,
        out_shape=[jax.ShapeDtypeStruct(near.shape, BF16), jax.ShapeDtypeStruct(waiting.shape, BF16)],
        in_specs=[VMEM] * 3,
        out_specs=[VMEM] * 2,
        compiler_params=pltpu.CompilerParams(vmem_limit_bytes=8 * MEGA),
        name="early",
    )(near, received, waiting)


def pair_kernel(near, received, *results):
    for k, result in enumerate(results):
        result[...] = (near[k].astype(F32) + received[k].astype(F32)).astype(BF16)


def pair_fast(near, received):
    count = near.shape[0]
    return pl.pallas_call(
        pair_kernel,
        out_shape=[jax.ShapeDtypeStruct(near.shape[1:], BF16)] * count,
        in_specs=[VMEM, VMEM],
        out_specs=[VMEM] * count,
        compiler_params=pltpu.CompilerParams(vmem_limit_bytes=8 * MEGA),
        name="pair",
    )(near, received)


def guide_kernel(width, weight, *refs):
    result = refs[-1]
    requests, half_width = result.shape[0], result.shape[3]
    total = add_up(refs[:-1])
    scale = lax.rsqrt(total[:, half_width : half_width + 1] / width + EPSILON)
    diagonal = iota((requests, requests), 0) == iota((requests, requests), 1)
    guidance = jnp.broadcast_to(weight[...], (requests, requests))
    factor = jnp.sum(jnp.where(diagonal, guidance, 0.0), axis=-1, keepdims=True)
    guided = total[:requests, :half_width] * (scale[:requests] * factor) + total[requests:, :half_width] * (
        scale[requests:] * (1.0 - factor)
    )
    for r in range(requests):
        result[r, 0] = guided[r : r + 1]


def guide_fast(blocks, guidance, width):
    rows, columns = blocks[0].shape
    return pl.pallas_call(
        lambda *refs: guide_kernel(width, *refs),
        out_shape=jax.ShapeDtypeStruct((rows // 2, 1, 1, columns - NOTE), F32),
        in_specs=[VMEM] * (1 + len(blocks)),
        out_specs=VMEM,
        compiler_params=pltpu.CompilerParams(vmem_limit_bytes=12 * MEGA),
        name="guide",
    )(guidance[None, :], *blocks)


def fits(hidden, sink_rows, expert_in, vocab_weight):
    return (
        lax.axis_size(ROWS) == 8
        and lax.axis_size("mp") == 4
        and hidden.shape[0] == 8
        and sink_rows.shape[1] == 4
        and expert_in.shape[2] % (2 * FFE) == 0
        and vocab_weight.shape[0] % 128 == 0
        and vocab_weight.shape[1] % 512 == 0
    )


def fast_body(
    states,
    lengths,
    sink_cache,
    window_cache,
    qkv_weight,
    out_weight,
    expert_ids,
    route_weight,
    expert_in,
    expert_out,
    vocab_weight,
    guidance,
):
    hidden = states[0]
    partial_out = attend_fast(hidden, lengths[0], sink_cache[0], window_cache[0], qkv_weight, out_weight)
    chunk = expert_in.shape[2] // 4
    received = step(partial_out, "mp", 1)
    w0 = load_fast(expert_in, 0, chunk, 47, lengths)
    pair = join_fast(True, [partial_out, received], w0)
    received = step(pair, "mp", 2)
    w1 = load_fast(expert_in, chunk, chunk, 43, pair)
    residual = join_fast(True, [hidden, pair, received], w1)
    blocks = swap([residual] * lax.axis_size("dp"), "dp")
    w2 = load_fast(expert_in, 2 * chunk, chunk, 39, residual)
    near = join_fast(False, blocks, w2)
    far = step(near, "guide", 1)
    w3 = load_fast(expert_in, 3 * chunk, chunk // 2, 37, near)
    share = vocab_weight.shape[0]
    terms, act, w_near, own_columns = experts_fast(
        near, far, expert_ids, route_weight, [w0, w1, w2, w3], expert_in, expert_out, share
    )
    received = step(terms, "guide", 1)
    part = sum_fast(swap(pair_fast(down_fast(act, w_near, share), received), "dp"))
    received = step(part, "mp", 1)
    pair = (part.astype(F32) + received.astype(F32)).astype(BF16)
    received = step(pair, "mp", 2)
    far_early, far = head_fast(True, own_columns, pair, received, vocab_weight)
    far_early = step(far_early, "guide", 1)
    near_early, near = head_fast(False, own_columns, pair, received, vocab_weight)
    last = lax.axis_size("dp") - 1
    early, far = early_fast(near_early, far_early, far)
    blocks = pair_fast(near, step(far, "guide", 1))
    logits = [step(early, "dp", last)]
    logits += [blocks[0]] + [step(blocks[k], "dp", k) for k in range(1, last)]
    return guide_fast(logits, guidance, hidden.shape[1])


def rotate(vectors, positions):
    full_width = vectors.shape[-1]
    half_width = full_width // 2
    step_index = jnp.arange(half_width, dtype=jnp.float32)
    inverse = jnp.exp(step_index * (-2.0 * math.log(10000.0) / full_width))
    angles = positions.astype(jnp.float32)[:, None] * inverse[None, :]
    cosine = jnp.cos(angles)[:, None, :]
    sine_part = jnp.sin(angles)[:, None, :]
    first_half = vectors[..., :half_width]
    second = vectors[..., half_width:]
    return jnp.concatenate(
        [first_half * cosine - second * sine_part, second * cosine + first_half * sine_part],
        axis=-1,
    )


def rms_norm(values):
    return values * lax.rsqrt(jnp.mean(values * values, axis=-1, keepdims=True) + EPSILON)


def attend(hidden, own_lengths, sink_rows, window_rows, qkv_weight, out_weight):
    normed = rms_norm(hidden.astype(jnp.float32)).astype(jnp.bfloat16)
    projected = jnp.einsum("rd,dthe->rthe", normed, qkv_weight, preferred_element_type=jnp.float32)
    query_rot = rotate(projected[:, 0], own_lengths).astype(jnp.bfloat16)
    fresh_key = rotate(projected[:, 1], own_lengths).astype(jnp.bfloat16)
    fresh_value = projected[:, 2].astype(jnp.bfloat16)
    sink_count = sink_rows.shape[3]
    window_count = window_rows.shape[3]
    root_size = math.sqrt(query_rot.shape[-1])
    sink_scores = (
        jnp.einsum(
            "rhe,rhse->rhs", query_rot, sink_rows[:, :, 0], preferred_element_type=jnp.float32
        )
        / root_size
    )
    window_scores = (
        jnp.einsum(
            "rhe,rhwe->rhw", query_rot, window_rows[:, :, 0], preferred_element_type=jnp.float32
        )
        / root_size
    )
    self_scores = (
        jnp.einsum("rhe,rhe->rh", query_rot, fresh_key, preferred_element_type=jnp.float32)
        / root_size
    )
    length_limit = own_lengths[:, None, None]
    sink_valid = jnp.arange(sink_count, dtype=jnp.int32)[None, None, :] < length_limit
    window_valid = (
        jnp.arange(window_count, dtype=jnp.int32)[None, None, :]
        >= sink_count + window_count - length_limit
    )
    sink_scores = jnp.where(sink_valid, sink_scores, -1e30)
    window_scores = jnp.where(window_valid, window_scores, -1e30)
    highest = jnp.maximum(
        jnp.maximum(jnp.max(sink_scores, axis=-1), jnp.max(window_scores, axis=-1)), self_scores
    )
    sink_exp = jnp.exp(sink_scores - highest[..., None])
    window_exp = jnp.exp(window_scores - highest[..., None])
    self_exp = jnp.exp(self_scores - highest)
    totals = jnp.sum(sink_exp, axis=-1) + jnp.sum(window_exp, axis=-1) + self_exp
    sink_prob = (sink_exp / totals[..., None]).astype(jnp.bfloat16)
    window_prob = (window_exp / totals[..., None]).astype(jnp.bfloat16)
    self_prob = (self_exp / totals).astype(jnp.bfloat16)
    mixture = (
        jnp.einsum(
            "rhs,rhse->rhe", sink_prob, sink_rows[:, :, 1], preferred_element_type=jnp.float32
        )
        + jnp.einsum(
            "rhw,rhwe->rhe", window_prob, window_rows[:, :, 1], preferred_element_type=jnp.float32
        )
        + self_prob[..., None].astype(jnp.float32) * fresh_value.astype(jnp.float32)
    ).astype(jnp.bfloat16)
    return jnp.einsum("rhe,hed->rd", mixture, out_weight, preferred_element_type=jnp.float32)


def body(
    states,
    lengths,
    sink_cache,
    window_cache,
    qkv_weight,
    out_weight,
    expert_ids,
    route_weight,
    expert_in,
    expert_out,
    vocab_weight,
    guidance,
):
    hidden = states[0]
    if fits(hidden, sink_cache[0], expert_in, vocab_weight):
        return fast_body(
            states,
            lengths,
            sink_cache,
            window_cache,
            qkv_weight,
            out_weight,
            expert_ids,
            route_weight,
            expert_in,
            expert_out,
            vocab_weight,
            guidance,
        )
    request_count, width = hidden.shape
    group = lax.axis_size(ROWS)
    mp = lax.axis_size("mp")
    tokens = group * request_count

    partial_out = attend(hidden, lengths[0], sink_cache[0], window_cache[0], qkv_weight, out_weight)
    first = lax.axis_index("mp") == 0
    partial_out = partial_out + jnp.where(first, hidden.astype(jnp.float32), 0.0)
    partials = spread(partial_out.astype(jnp.bfloat16), ALL).reshape(group, mp, request_count, width)
    residual = jnp.sum(partials.astype(jnp.float32), axis=1).reshape(tokens, width).astype(jnp.bfloat16)
    moe_in = rms_norm(residual.astype(jnp.float32)).astype(jnp.bfloat16)

    unit_count = expert_in.shape[2]
    unit_start = lax.axis_index(ALL) * unit_count
    unit_expert = (unit_start + jnp.arange(unit_count, dtype=jnp.int32)) // FFE
    choice_rows = expert_ids.reshape(-1, expert_ids.shape[-1])
    route_rows = route_weight.reshape(-1, route_weight.shape[-1])
    coefficient = jnp.sum(
        jnp.where(
            choice_rows[:, :, None] == unit_expert[None, None, :], route_rows[:, :, None], 0.0
        ),
        axis=1,
    )
    gate = jnp.dot(moe_in, expert_in[0], preferred_element_type=jnp.float32)
    upward = jnp.dot(moe_in, expert_in[1], preferred_element_type=jnp.float32)
    activated = (jax.nn.silu(gate) * upward * coefficient).astype(jnp.bfloat16)
    expert_terms = jnp.dot(activated, expert_out, preferred_element_type=jnp.float32).astype(jnp.bfloat16)

    share = vocab_weight.shape[0]
    sent = jnp.swapaxes(expert_terms.reshape(tokens, group, share), 0, 1)
    expert_part = jnp.sum(trade(sent, ROWS).astype(jnp.float32), axis=0)
    expert_total = jnp.sum(spread(expert_part.astype(jnp.bfloat16), "mp").astype(jnp.float32), axis=0)
    own_columns = lax.dynamic_slice_in_dim(residual, lax.axis_index(ROWS) * share, share, 1)
    summed = own_columns.astype(jnp.float32) + expert_total

    squares = jnp.sum(summed * summed, axis=-1)
    notes = spread(jnp.concatenate([squares, guidance]), ROWS)
    scale = lax.rsqrt(jnp.sum(notes[:, :tokens], axis=0) / width + EPSILON).reshape(2, -1, 1)
    weight = notes[: group // 2, tokens:].reshape(-1, 1)

    raw = jnp.dot(summed.astype(jnp.bfloat16), vocab_weight, preferred_element_type=jnp.float32)
    raw = raw.reshape(2, tokens // 2, -1)
    mixed = raw[0] * (scale[0] * weight) + raw[1] * (scale[1] * (1.0 - weight))
    half_width = mixed.shape[1] // 2
    mixed = mixed.astype(jnp.bfloat16).reshape(group // 2, request_count, 2, half_width)
    sent = jnp.transpose(mixed, (2, 0, 1, 3)).reshape(group, request_count, half_width)
    guided = jnp.sum(trade(sent, ROWS).astype(jnp.float32), axis=0)
    return guided.reshape(request_count, 1, 1, half_width)


def solution(mesh):
    in_specs = (
        P("guide", "dp", None),
        P("guide", "dp"),
        P("guide", "dp", "mp", None, None, None),
        P("guide", "dp", "mp", None, None, None),
        P(None, None, "mp", None),
        P("mp", None, None),
        P(),
        P(),
        P(None, None, ("guide", "dp", "mp")),
        P(("guide", "dp", "mp"), None),
        P(("guide", "dp"), "mp"),
        P("dp"),
    )
    out_specs = P("dp", "mp", "guide", None)
    return jax.shard_map(body, mesh=mesh, in_specs=in_specs, out_specs=out_specs, check_vma=False)
```

```python
import math

import jax
import jax.numpy as jnp
from jax import lax
from jax.experimental import pallas as pl
from jax.experimental.pallas import tpu as pltpu
from jax.sharding import PartitionSpec as P

FFE = 1024

EPSILON = 1e-05

ROWS = ("guide", "dp")
ALL = ("guide", "dp", "mp")


def trade(blocks, axis):
    return lax.all_to_all(blocks, axis, 0, 0, tiled=True)


def spread(block, axis):
    return trade(jnp.broadcast_to(block[None], (lax.axis_size(axis),) + block.shape), axis)


def step(block, axis, bit):
    count = lax.axis_size(axis)
    return lax.ppermute(block, axis, [(i, i ^ bit) for i in range(count)])


def swap(blocks, axis):
    return [blocks[0]] + [step(blocks[j], axis, j) for j in range(1, lax.axis_size(axis))]


F32 = jnp.float32
BF16 = jnp.bfloat16
VMEM = pl.BlockSpec(memory_space=pltpu.VMEM)
ANY = pl.BlockSpec(memory_space=pl.ANY)
HBM = pl.BlockSpec(memory_space=pltpu.HBM)
MEGA = 1 << 20
NOTE = 128


def dot(left, right):
    return jnp.dot(left, right, preferred_element_type=F32)


def iota(shape, dim):
    return lax.broadcasted_iota(jnp.int32, shape, dim)


def load_kernel(first, chunk, hbm, after, result, sems):
    rows = hbm.shape[1] // sems.shape[1]
    copies = [
        pltpu.make_async_copy(
            hbm.at[k, pl.ds(i * rows, rows), pl.ds(first, chunk)],
            result.at[k, pl.ds(i * rows, rows), :],
            sems.at[k, i],
        )
        for k in range(hbm.shape[0])
        for i in range(sems.shape[1])
    ]
    for copy in copies:
        copy.start()
    for copy in copies:
        copy.wait()


def load_fast(weight, first, chunk, room, after):
    kinds, width, _ = weight.shape
    return pl.pallas_call(
        lambda *refs: load_kernel(first, chunk, *refs),
        out_shape=jax.ShapeDtypeStruct((kinds, width, chunk), BF16),
        in_specs=[HBM, ANY],
        out_specs=VMEM,
        scratch_shapes=[pltpu.SemaphoreType.DMA((kinds, 4))],
        compiler_params=pltpu.CompilerParams(vmem_limit_bytes=room * MEGA),
        cost_estimate=pl.CostEstimate(flops=0, bytes_accessed=4 * kinds * width * chunk, transcendentals=0),
        name="load",
    )(weight, after)


def join_kernel(total, count, *refs):
    values = [ref[...].astype(F32) for ref in refs[:count]]
    joined = sum(values[1:], values[0]) if total else jnp.concatenate(values, axis=0)
    refs[-1][...] = joined.astype(BF16)


def join_fast(total, blocks, after):
    rows, columns = blocks[0].shape
    return pl.pallas_call(
        lambda *refs: join_kernel(total, len(blocks), *refs),
        out_shape=jax.ShapeDtypeStruct((rows if total else rows * len(blocks), columns), BF16),
        in_specs=[VMEM] * len(blocks) + [ANY],
        out_specs=VMEM,
        compiler_params=pltpu.CompilerParams(vmem_limit_bytes=4 * MEGA),
        name="join",
    )(*blocks, after)


def attend_kernel(
    heads, sinks, states_hbm, lengths_hbm, sink_hbm, qkv_hbm, window_hbm, out_hbm, result,
    states, lengths, sink, qkv, window, out_weight, spread_out, first_sems, qkv_sems, window_sems, out_sem,
):
    requests, width = states.shape
    size = sink.shape[1]
    parts = 3 * heads
    lanes = size * parts
    blocks = width // size
    chunks = qkv_sems.shape[0]
    chunk_rows = qkv.shape[0] // chunks
    slots = window.shape[3]
    rows = heads * requests
    qkv_copies = [
        pltpu.make_async_copy(
            qkv_hbm.at[pl.ds(c * chunk_rows, chunk_rows)], qkv.at[pl.ds(c * chunk_rows, chunk_rows)], qkv_sems.at[c]
        )
        for c in range(chunks)
    ]
    key_copies, value_copies = [
        [
            pltpu.make_async_copy(window_hbm.at[r, :, k], window.at[r, :, k], window_sems.at[k, r])
            for r in range(requests)
        ]
        for k in range(2)
    ]
    out_copy = pltpu.make_async_copy(out_hbm, out_weight, out_sem)
    first_copies = [
        pltpu.make_async_copy(source, target, first_sems.at[i])
        for i, (source, target) in enumerate(((states_hbm, states), (lengths_hbm, lengths), (sink_hbm, sink)))
    ]
    for copy in first_copies + qkv_copies[: chunks // 2]:
        copy.start()
    sub, lane = iota((size, lanes), 0) * parts, iota((size, lanes), 1)
    repeat = jnp.where((lane >= sub) & (lane < sub + parts), 1.0, 0.0).astype(BF16)
    kind = lax.rem(iota((requests, lanes), 1), parts)
    for copy in first_copies:
        copy.wait()
    for copy in qkv_copies[chunks // 2 :]:
        copy.start()
    hidden = states[...].astype(F32)
    normed = hidden * lax.rsqrt(jnp.mean(hidden * hidden, axis=-1, keepdims=True) + EPSILON)
    stacked = jnp.concatenate([normed[:, b * size : (b + 1) * size] for b in range(blocks)], axis=0)
    repeated = dot(stacked.astype(BF16), repeat)
    run = blocks // chunks

    def lay_out(c):
        for b in range(c * run, (c + 1) * run):
            piece = repeated[b * requests : (b + 1) * requests]
            spread_out[:, b * lanes : (b + 1) * lanes] = jnp.concatenate(
                [jnp.where(kind == p, piece, 0.0) for p in range(parts)], axis=0
            ).astype(BF16)

    lay_out(0)
    projected = jnp.zeros((parts * requests, size), F32)
    for copy in key_copies:
        copy.start()
    later = {0: value_copies, chunks // 4: [out_copy]}
    for c in range(chunks):
        qkv_copies[c].wait()
        for copy in later.get(c, []):
            copy.start()
        part = slice(c * chunk_rows, (c + 1) * chunk_rows)
        if c + 1 < chunks:
            lay_out(c + 1)
        if c == chunks - 1:
            length_row = jnp.broadcast_to(lengths[...], (requests, requests))
            diagonal = iota((requests, requests), 0) == iota((requests, requests), 1)
            length = jnp.sum(jnp.where(diagonal, length_row, 0), axis=-1, keepdims=True)
            lane_id = iota((requests, size), 1)
            low = lane_id < size // 2
            pair_index = jnp.where(low, lane_id, lane_id - size // 2).astype(F32)
            angles = length.astype(F32) * jnp.exp(pair_index * (-2.0 * math.log(10000.0) / size))
            cosine, sine = jnp.cos(angles), jnp.sin(angles)
            sine = jnp.where(low, -sine, sine)
        projected = projected + dot(spread_out[:, part], qkv[part, :])

    cos_rows = jnp.concatenate([cosine] * heads, axis=0)
    sin_rows = jnp.concatenate([sine] * heads, axis=0)
    limit = jnp.concatenate([length] * heads, axis=0)

    def turn(values):
        return (values * cos_rows + pltpu.roll(values, size // 2, 1) * sin_rows).astype(BF16)

    query = turn(projected[:rows])
    fresh_key = turn(projected[rows : 2 * rows])
    fresh_value = projected[2 * rows :].astype(BF16).astype(F32)
    root_size = math.sqrt(size)
    across = (((1,), (1,)), ((), ()))

    self_scores = jnp.sum(query.astype(F32) * fresh_key.astype(F32), axis=-1, keepdims=True) / root_size
    sink_rows = sink[...]
    sink_total = sink_rows.shape[0]
    sink_scores = lax.dot_general(query, sink_rows, across, preferred_element_type=F32) / root_size
    row_id, column = iota((rows, sink_total), 0), iota((rows, sink_total), 1)
    slot = lax.rem(column, 2 * sinks)
    pair = lax.div(column, 2 * sinks)
    sink_valid = (
        (lax.rem(pair, heads) == lax.div(row_id, requests))
        & (lax.div(pair, heads) == lax.rem(row_id, requests))
        & (slot < sinks)
        & (slot < limit)
    )
    sink_scores = jnp.where(sink_valid, sink_scores, -1e30)

    mine = iota((requests, slots), 0)
    for copy in key_copies:
        copy.wait()
    scores = []
    for h in range(heads):
        keys = window[:, h, 0].reshape(requests * slots, size)
        found = lax.dot_general(query[h * requests : (h + 1) * requests], keys, across, preferred_element_type=F32)
        own = jnp.where(mine == 0, found[:, :slots], 0.0)
        for r in range(1, requests):
            own = jnp.where(mine == r, found[:, r * slots : (r + 1) * slots], own)
        scores.append(own)
    scores = jnp.concatenate(scores, axis=0) / root_size
    valid = iota((rows, slots), 1) >= sinks + slots - limit
    scores = jnp.where(valid, scores, -1e30)

    highest = jnp.maximum(
        jnp.maximum(jnp.max(scores, axis=-1, keepdims=True), jnp.max(sink_scores, axis=-1, keepdims=True)),
        self_scores,
    )
    window_exp = jnp.exp(scores - highest)
    sink_exp = jnp.where(sink_valid, jnp.exp(sink_scores - highest), 0.0)
    self_exp = jnp.exp(self_scores - highest)
    total = jnp.sum(window_exp, axis=-1, keepdims=True) + jnp.sum(sink_exp, axis=-1, keepdims=True) + self_exp
    window_weight = (window_exp / total).astype(BF16).astype(F32)
    sink_weight = pltpu.roll(sink_exp / total, sinks, 1).astype(BF16)
    self_weight = (self_exp / total).astype(BF16).astype(F32)
    mixture = dot(sink_weight, sink_rows) + self_weight * fresh_value
    for copy in value_copies:
        copy.wait()
    mixed = []
    for h in range(heads):
        own = window_weight[h * requests : (h + 1) * requests]
        wide = jnp.concatenate([jnp.where(mine == r, own, 0.0) for r in range(requests)], axis=1).astype(BF16)
        values = window[:, h, 1].reshape(requests * slots, size)
        mixed.append(mixture[h * requests : (h + 1) * requests] + dot(wide, values))
    out_copy.wait()
    result[...] = dot(jnp.concatenate(mixed, axis=1).astype(BF16), out_weight[...]).astype(result.dtype)


def attend_fast(hidden, own_lengths, sink_rows, window_rows, qkv_weight, out_weight):
    requests, width = hidden.shape
    heads, sinks, size = sink_rows.shape[1], sink_rows.shape[3], sink_rows.shape[4]
    qkv = qkv_weight.reshape(-1, size)
    out = out_weight.reshape(-1, width)
    return pl.pallas_call(
        lambda *refs: attend_kernel(heads, sinks, *refs),
        out_shape=jax.ShapeDtypeStruct((requests, width), BF16),
        in_specs=[HBM] * 6,
        out_specs=VMEM,
        scratch_shapes=[
            pltpu.VMEM(hidden.shape, BF16),
            pltpu.VMEM((1, requests), jnp.int32),
            pltpu.VMEM((sink_rows.size // size, size), BF16),
            pltpu.VMEM(qkv.shape, BF16),
            pltpu.VMEM(window_rows.shape, BF16),
            pltpu.VMEM(out.shape, BF16),
            pltpu.VMEM((3 * heads * requests, qkv.shape[0]), BF16),
            pltpu.SemaphoreType.DMA((3,)),
            pltpu.SemaphoreType.DMA((8,)),
            pltpu.SemaphoreType.DMA((2, requests)),
            pltpu.SemaphoreType.DMA,
        ],
        compiler_params=pltpu.CompilerParams(vmem_limit_bytes=60 * MEGA),
        name="attend",
    )(
        hidden,
        own_lengths[None, :],
        sink_rows.reshape(-1, size),
        qkv,
        window_rows,
        out,
    )


def expert_kernel(chunks, near, far, *refs):
    w_in, refs = refs[:chunks], refs[chunks:]
    ids_hbm, route_hbm, in_hbm, out_hbm, terms, act, w_near, own_columns, *refs = refs
    rows_scr, ids, route, w_last, w_far, small_sems, last_sems, out_sems = refs
    count, tokens, share = terms.shape
    group = 2 * count
    requests = tokens // group
    units = act.shape[1]
    own = lax.axis_index("guide") * count + lax.axis_index("dp")
    first_expert = (own * lax.axis_size("mp") + lax.axis_index("mp")) * (units // FFE)
    guide, place = lax.axis_index("guide"), lax.axis_index("dp")
    half_width = count * share
    runs = units // out_sems.shape[1]
    out_copies = [
        [
            pltpu.make_async_copy(
                out_hbm.at[pl.ds(i * runs, runs), pl.ds(pl.multiple_of(half * half_width, half_width), half_width)],
                target.at[pl.ds(i * runs, runs), :],
                out_sems.at[k, i],
            )
            for i in range(out_sems.shape[1])
        ]
        for k, (half, target) in enumerate(((1 - guide, w_far), (guide, w_near)))
    ]
    small_copies = [
        pltpu.make_async_copy(ids_hbm, ids, small_sems.at[0]),
        pltpu.make_async_copy(route_hbm, route, small_sems.at[1]),
    ]
    last = w_last.shape[2]
    last_copies = [
        pltpu.make_async_copy(in_hbm.at[k, :, pl.ds(units - last, last)], w_last.at[k], last_sems.at[k])
        for k in range(2)
    ]
    for copy in small_copies + last_copies + out_copies[0] + out_copies[1]:
        copy.start()
    for first, source in ((0, near), (count, far)):
        values = source[...].astype(F32)
        for i in range(count):
            start = pl.multiple_of((own ^ (first + i)) * requests, requests)
            rows_scr[pl.ds(start, requests), :] = values[i * requests : (i + 1) * requests]
    own_columns[...] = rows_scr[:, pl.ds(pl.multiple_of(own * share, share), share)]
    rows = rows_scr[...]
    moe_in = (rows * lax.rsqrt(jnp.mean(rows * rows, axis=-1, keepdims=True) + EPSILON)).astype(BF16)
    for copy in small_copies:
        copy.wait()
    per_stream = ids.shape[2]
    diagonal = iota((per_stream, per_stream), 0) == iota((per_stream, per_stream), 1)

    def factor_of(expert):
        columns = []
        for stream in range(2):
            row = jnp.sum(jnp.where(ids[stream] == expert, route[stream], 0.0), axis=0, keepdims=True)
            spread_out = jnp.broadcast_to(row, (per_stream, per_stream))
            columns.append(jnp.sum(jnp.where(diagonal, spread_out, 0.0), axis=-1, keepdims=True))
        return jnp.concatenate(columns, axis=0)

    start = 0
    for weight in (*w_in, w_last):
        if weight is w_last:
            for copy in last_copies:
                copy.wait()
        unit, start = start, start + weight.shape[2]
        factor = factor_of(first_expert + unit // FFE)
        gate = dot(moe_in, weight[0])
        upward = dot(moe_in, weight[1])
        act[:, unit:start] = (gate / (1.0 + jnp.exp(-gate)) * upward * factor).astype(BF16)
    for copy in out_copies[0]:
        copy.wait()
    for d in range(count):
        terms[place ^ d] = dot(act[...], w_far[:, d * share : (d + 1) * share]).astype(BF16)
    for copy in out_copies[1]:
        copy.wait()


def experts_fast(near, far, expert_ids, route_weight, w_in, expert_in, expert_out, share):
    width = near.shape[1]
    count = lax.axis_size("dp")
    tokens = 2 * near.shape[0]
    units = expert_out.shape[0]
    last = units - sum(weight.shape[2] for weight in w_in)
    top = expert_ids.shape[-1]
    return pl.pallas_call(
        lambda *refs: expert_kernel(len(w_in), *refs),
        out_shape=[
            jax.ShapeDtypeStruct((count, tokens, share), BF16),
            jax.ShapeDtypeStruct((tokens, units), BF16),
            jax.ShapeDtypeStruct((units, count * share), BF16),
            jax.ShapeDtypeStruct((tokens, share), F32),
        ],
        in_specs=[VMEM] * (2 + len(w_in)) + [HBM] * 4,
        out_specs=[VMEM] * 4,
        scratch_shapes=[
            pltpu.VMEM((tokens, width), F32),
            pltpu.VMEM((2, top, tokens // 2), jnp.int32),
            pltpu.VMEM((2, top, tokens // 2), F32),
            pltpu.VMEM((2, width, last), BF16),
            pltpu.VMEM((units, count * share), BF16),
            pltpu.SemaphoreType.DMA((2,)),
            pltpu.SemaphoreType.DMA((2,)),
            pltpu.SemaphoreType.DMA((2, 4)),
        ],
        compiler_params=pltpu.CompilerParams(vmem_limit_bytes=29 * MEGA),
        name="experts",
    )(near, far, *w_in, jnp.swapaxes(expert_ids, 1, 2), jnp.swapaxes(route_weight, 1, 2), expert_in, expert_out)


def down_kernel(act, weight, terms):
    count, _, share = terms.shape
    place = lax.axis_index("dp")
    for d in range(count):
        terms[place ^ d] = dot(act[...], weight[:, d * share : (d + 1) * share]).astype(BF16)


def down_fast(act, weight, share):
    tokens, units = act.shape
    count = weight.shape[1] // share
    return pl.pallas_call(
        down_kernel,
        out_shape=jax.ShapeDtypeStruct((count, tokens, share), BF16),
        in_specs=[VMEM] * 2,
        out_specs=VMEM,
        compiler_params=pltpu.CompilerParams(vmem_limit_bytes=8 * MEGA),
        cost_estimate=pl.CostEstimate(
            flops=2 * tokens * units * count * share, bytes_accessed=2 * units * count * share, transcendentals=0
        ),
        name="down",
    )(act, weight)


def add_up(blocks):
    total = blocks[0][...].astype(F32)
    for block in blocks[1:]:
        total = total + block[...].astype(F32)
    return total


def sum_kernel(*refs):
    refs[-1][...] = add_up(refs[:-1]).astype(BF16)


def sum_fast(blocks):
    return pl.pallas_call(
        sum_kernel,
        out_shape=jax.ShapeDtypeStruct(blocks[0].shape, BF16),
        in_specs=[VMEM] * len(blocks),
        out_specs=VMEM,
        compiler_params=pltpu.CompilerParams(vmem_limit_bytes=8 * MEGA),
        name="add_up",
    )(*blocks)


def head_kernel(chunk, other, own_columns, left, right, weight, early, target, scratch):
    tokens = own_columns.shape[0]
    rows = early.shape[0]
    count = tokens // rows
    requests = rows // 2
    half_width = weight.shape[1] // 2
    per_half = half_width // chunk
    guide, own = lax.axis_index("guide"), lax.axis_index("dp")
    summed = own_columns[...] + (left[...].astype(F32) + right[...].astype(F32))

    def hand_out(values, start):
        width = values.shape[1]
        scratch[:, :width] = values
        for k in range(count):
            first = pl.multiple_of((own ^ k) * requests, requests)
            second = pl.multiple_of(tokens // 2 + (own ^ k) * requests, requests)
            block = jnp.concatenate(
                [scratch[pl.ds(first, requests), :width], scratch[pl.ds(second, requests), :width]], axis=0
            ).astype(BF16)
            if k == count - 1:
                early[:, start : start + width] = block
            else:
                target[k, :, start : start + width] = block

    squares = jnp.broadcast_to(jnp.sum(summed * summed, axis=-1, keepdims=True), (tokens, NOTE))
    raw_in = summed.astype(BF16)
    half = 1 - guide if other else guide
    hand_out(squares, half_width)
    for c in range(per_half):
        first = pl.multiple_of(half * half_width + c * chunk, 128)
        hand_out(dot(raw_in, weight[:, pl.ds(first, chunk)]), c * chunk)


def head_fast(other, own_columns, left, right, weight):
    count = lax.axis_size("dp")
    tokens = own_columns.shape[0]
    half_width = weight.shape[1] // 2
    return pl.pallas_call(
        lambda *refs: head_kernel(256, other, *refs),
        out_shape=[
            jax.ShapeDtypeStruct((tokens // count, half_width + NOTE), BF16),
            jax.ShapeDtypeStruct((count - 1, tokens // count, half_width + NOTE), BF16),
        ],
        in_specs=[VMEM] * 4,
        out_specs=[VMEM] * 2,
        scratch_shapes=[pltpu.VMEM((tokens, 256), F32)],
        compiler_params=pltpu.CompilerParams(vmem_limit_bytes=12 * MEGA),
        cost_estimate=pl.CostEstimate(
            flops=tokens * weight.size, bytes_accessed=weight.size, transcendentals=0
        ),
        name="head",
    )(own_columns, left, right, weight)


def early_kernel(near, received, waiting, total, passed):
    total[...] = add_up([near, received]).astype(BF16)
    passed[...] = waiting[...]


def early_fast(near, received, waiting):
    return pl.pallas_call(
        early_kernel,
        out_shape=[jax.ShapeDtypeStruct(near.shape, BF16), jax.ShapeDtypeStruct(waiting.shape, BF16)],
        in_specs=[VMEM] * 3,
        out_specs=[VMEM] * 2,
        compiler_params=pltpu.CompilerParams(vmem_limit_bytes=8 * MEGA),
        name="early",
    )(near, received, waiting)


def pair_kernel(near, received, *results):
    for k, result in enumerate(results):
        result[...] = (near[k].astype(F32) + received[k].astype(F32)).astype(BF16)


def pair_fast(near, received):
    count = near.shape[0]
    return pl.pallas_call(
        pair_kernel,
        out_shape=[jax.ShapeDtypeStruct(near.shape[1:], BF16)] * count,
        in_specs=[VMEM, VMEM],
        out_specs=[VMEM] * count,
        compiler_params=pltpu.CompilerParams(vmem_limit_bytes=8 * MEGA),
        name="pair",
    )(near, received)


def guide_kernel(width, weight, *refs):
    result = refs[-1]
    requests, half_width = result.shape[0], result.shape[3]
    total = add_up(refs[:-1])
    scale = lax.rsqrt(total[:, half_width : half_width + 1] / width + EPSILON)
    diagonal = iota((requests, requests), 0) == iota((requests, requests), 1)
    guidance = jnp.broadcast_to(weight[...], (requests, requests))
    factor = jnp.sum(jnp.where(diagonal, guidance, 0.0), axis=-1, keepdims=True)
    guided = total[:requests, :half_width] * (scale[:requests] * factor) + total[requests:, :half_width] * (
        scale[requests:] * (1.0 - factor)
    )
    for r in range(requests):
        result[r, 0] = guided[r : r + 1]


def guide_fast(blocks, guidance, width):
    rows, columns = blocks[0].shape
    return pl.pallas_call(
        lambda *refs: guide_kernel(width, *refs),
        out_shape=jax.ShapeDtypeStruct((rows // 2, 1, 1, columns - NOTE), F32),
        in_specs=[VMEM] * (1 + len(blocks)),
        out_specs=VMEM,
        compiler_params=pltpu.CompilerParams(vmem_limit_bytes=12 * MEGA),
        name="guide",
    )(guidance[None, :], *blocks)


def fits(hidden, sink_rows, expert_in, vocab_weight):
    return (
        lax.axis_size(ROWS) == 8
        and lax.axis_size("mp") == 4
        and hidden.shape[0] == 8
        and sink_rows.shape[1] == 4
        and expert_in.shape[2] % (2 * FFE) == 0
        and vocab_weight.shape[0] % 128 == 0
        and vocab_weight.shape[1] % 512 == 0
    )


def fast_body(
    states,
    lengths,
    sink_cache,
    window_cache,
    qkv_weight,
    out_weight,
    expert_ids,
    route_weight,
    expert_in,
    expert_out,
    vocab_weight,
    guidance,
):
    hidden = states[0]
    partial_out = attend_fast(hidden, lengths[0], sink_cache[0], window_cache[0], qkv_weight, out_weight)
    chunk = expert_in.shape[2] // 4
    received = step(partial_out, "mp", 1)
    w0 = load_fast(expert_in, 0, chunk, 47, lengths)
    pair = join_fast(True, [partial_out, received], w0)
    received = step(pair, "mp", 2)
    w1 = load_fast(expert_in, chunk, chunk, 43, pair)
    residual = join_fast(True, [hidden, pair, received], w1)
    blocks = swap([residual] * lax.axis_size("dp"), "dp")
    w2 = load_fast(expert_in, 2 * chunk, chunk, 39, residual)
    near = join_fast(False, blocks, w2)
    far = step(near, "guide", 1)
    w3 = load_fast(expert_in, 3 * chunk, chunk // 2, 37, near)
    share = vocab_weight.shape[0]
    terms, act, w_near, own_columns = experts_fast(
        near, far, expert_ids, route_weight, [w0, w1, w2, w3], expert_in, expert_out, share
    )
    received = step(terms, "guide", 1)
    part = sum_fast(swap(pair_fast(down_fast(act, w_near, share), received), "dp"))
    received = step(part, "mp", 1)
    pair = (part.astype(F32) + received.astype(F32)).astype(BF16)
    received = step(pair, "mp", 2)
    far_early, far = head_fast(True, own_columns, pair, received, vocab_weight)
    far_early = step(far_early, "guide", 1)
    near_early, near = head_fast(False, own_columns, pair, received, vocab_weight)
    last = lax.axis_size("dp") - 1
    early, far = early_fast(near_early, far_early, far)
    blocks = pair_fast(near, step(far, "guide", 1))
    logits = [step(early, "dp", last)]
    logits += [blocks[0]] + [step(blocks[k], "dp", k) for k in range(1, last)]
    return guide_fast(logits, guidance, hidden.shape[1])


def rotate(vectors, positions):
    full_width = vectors.shape[-1]
    half_width = full_width // 2
    step_index = jnp.arange(half_width, dtype=jnp.float32)
    inverse = jnp.exp(step_index * (-2.0 * math.log(10000.0) / full_width))
    angles = positions.astype(jnp.float32)[:, None] * inverse[None, :]
    cosine = jnp.cos(angles)[:, None, :]
    sine_part = jnp.sin(angles)[:, None, :]
    first_half = vectors[..., :half_width]
    second = vectors[..., half_width:]
    return jnp.concatenate(
        [first_half * cosine - second * sine_part, second * cosine + first_half * sine_part],
        axis=-1,
    )


def rms_norm(values):
    return values * lax.rsqrt(jnp.mean(values * values, axis=-1, keepdims=True) + EPSILON)


def attend(hidden, own_lengths, sink_rows, window_rows, qkv_weight, out_weight):
    normed = rms_norm(hidden.astype(jnp.float32)).astype(jnp.bfloat16)
    projected = jnp.einsum("rd,dthe->rthe", normed, qkv_weight, preferred_element_type=jnp.float32)
    query_rot = rotate(projected[:, 0], own_lengths).astype(jnp.bfloat16)
    fresh_key = rotate(projected[:, 1], own_lengths).astype(jnp.bfloat16)
    fresh_value = projected[:, 2].astype(jnp.bfloat16)
    sink_count = sink_rows.shape[3]
    window_count = window_rows.shape[3]
    root_size = math.sqrt(query_rot.shape[-1])
    sink_scores = (
        jnp.einsum(
            "rhe,rhse->rhs", query_rot, sink_rows[:, :, 0], preferred_element_type=jnp.float32
        )
        / root_size
    )
    window_scores = (
        jnp.einsum(
            "rhe,rhwe->rhw", query_rot, window_rows[:, :, 0], preferred_element_type=jnp.float32
        )
        / root_size
    )
    self_scores = (
        jnp.einsum("rhe,rhe->rh", query_rot, fresh_key, preferred_element_type=jnp.float32)
        / root_size
    )
    length_limit = own_lengths[:, None, None]
    sink_valid = jnp.arange(sink_count, dtype=jnp.int32)[None, None, :] < length_limit
    window_valid = (
        jnp.arange(window_count, dtype=jnp.int32)[None, None, :]
        >= sink_count + window_count - length_limit
    )
    sink_scores = jnp.where(sink_valid, sink_scores, -1e30)
    window_scores = jnp.where(window_valid, window_scores, -1e30)
    highest = jnp.maximum(
        jnp.maximum(jnp.max(sink_scores, axis=-1), jnp.max(window_scores, axis=-1)), self_scores
    )
    sink_exp = jnp.exp(sink_scores - highest[..., None])
    window_exp = jnp.exp(window_scores - highest[..., None])
    self_exp = jnp.exp(self_scores - highest)
    totals = jnp.sum(sink_exp, axis=-1) + jnp.sum(window_exp, axis=-1) + self_exp
    sink_prob = (sink_exp / totals[..., None]).astype(jnp.bfloat16)
    window_prob = (window_exp / totals[..., None]).astype(jnp.bfloat16)
    self_prob = (self_exp / totals).astype(jnp.bfloat16)
    mixture = (
        jnp.einsum(
            "rhs,rhse->rhe", sink_prob, sink_rows[:, :, 1], preferred_element_type=jnp.float32
        )
        + jnp.einsum(
            "rhw,rhwe->rhe", window_prob, window_rows[:, :, 1], preferred_element_type=jnp.float32
        )
        + self_prob[..., None].astype(jnp.float32) * fresh_value.astype(jnp.float32)
    ).astype(jnp.bfloat16)
    return jnp.einsum("rhe,hed->rd", mixture, out_weight, preferred_element_type=jnp.float32)


def body(
    states,
    lengths,
    sink_cache,
    window_cache,
    qkv_weight,
    out_weight,
    expert_ids,
    route_weight,
    expert_in,
    expert_out,
    vocab_weight,
    guidance,
):
    hidden = states[0]
    if fits(hidden, sink_cache[0], expert_in, vocab_weight):
        return fast_body(
            states,
            lengths,
            sink_cache,
            window_cache,
            qkv_weight,
            out_weight,
            expert_ids,
            route_weight,
            expert_in,
            expert_out,
            vocab_weight,
            guidance,
        )
    request_count, width = hidden.shape
    group = lax.axis_size(ROWS)
    mp = lax.axis_size("mp")
    tokens = group * request_count

    partial_out = attend(hidden, lengths[0], sink_cache[0], window_cache[0], qkv_weight, out_weight)
    first = lax.axis_index("mp") == 0
    partial_out = partial_out + jnp.where(first, hidden.astype(jnp.float32), 0.0)
    partials = spread(partial_out.astype(jnp.bfloat16), ALL).reshape(group, mp, request_count, width)
    residual = jnp.sum(partials.astype(jnp.float32), axis=1).reshape(tokens, width).astype(jnp.bfloat16)
    moe_in = rms_norm(residual.astype(jnp.float32)).astype(jnp.bfloat16)

    unit_count = expert_in.shape[2]
    unit_start = lax.axis_index(ALL) * unit_count
    unit_expert = (unit_start + jnp.arange(unit_count, dtype=jnp.int32)) // FFE
    choice_rows = expert_ids.reshape(-1, expert_ids.shape[-1])
    route_rows = route_weight.reshape(-1, route_weight.shape[-1])
    coefficient = jnp.sum(
        jnp.where(
            choice_rows[:, :, None] == unit_expert[None, None, :], route_rows[:, :, None], 0.0
        ),
        axis=1,
    )
    gate = jnp.dot(moe_in, expert_in[0], preferred_element_type=jnp.float32)
    upward = jnp.dot(moe_in, expert_in[1], preferred_element_type=jnp.float32)
    activated = (jax.nn.silu(gate) * upward * coefficient).astype(jnp.bfloat16)
    expert_terms = jnp.dot(activated, expert_out, preferred_element_type=jnp.float32).astype(jnp.bfloat16)

    share = vocab_weight.shape[0]
    sent = jnp.swapaxes(expert_terms.reshape(tokens, group, share), 0, 1)
    expert_part = jnp.sum(trade(sent, ROWS).astype(jnp.float32), axis=0)
    expert_total = jnp.sum(spread(expert_part.astype(jnp.bfloat16), "mp").astype(jnp.float32), axis=0)
    own_columns = lax.dynamic_slice_in_dim(residual, lax.axis_index(ROWS) * share, share, 1)
    summed = own_columns.astype(jnp.float32) + expert_total

    squares = jnp.sum(summed * summed, axis=-1)
    notes = spread(jnp.concatenate([squares, guidance]), ROWS)
    scale = lax.rsqrt(jnp.sum(notes[:, :tokens], axis=0) / width + EPSILON).reshape(2, -1, 1)
    weight = notes[: group // 2, tokens:].reshape(-1, 1)

    raw = jnp.dot(summed.astype(jnp.bfloat16), vocab_weight, preferred_element_type=jnp.float32)
    raw = raw.reshape(2, tokens // 2, -1)
    mixed = raw[0] * (scale[0] * weight) + raw[1] * (scale[1] * (1.0 - weight))
    half_width = mixed.shape[1] // 2
    mixed = mixed.astype(jnp.bfloat16).reshape(group // 2, request_count, 2, half_width)
    sent = jnp.transpose(mixed, (2, 0, 1, 3)).reshape(group, request_count, half_width)
    guided = jnp.sum(trade(sent, ROWS).astype(jnp.float32), axis=0)
    return guided.reshape(request_count, 1, 1, half_width)


def solution(mesh):
    in_specs = (
        P("guide", "dp", None),
        P("guide", "dp"),
        P("guide", "dp", "mp", None, None, None),
        P("guide", "dp", "mp", None, None, None),
        P(None, None, "mp", None),
        P("mp", None, None),
        P(),
        P(),
        P(None, None, ("guide", "dp", "mp")),
        P(("guide", "dp", "mp"), None),
        P(("guide", "dp"), "mp"),
        P("dp"),
    )
    out_specs = P("dp", "mp", "guide", None)
    return jax.shard_map(body, mesh=mesh, in_specs=in_specs, out_specs=out_specs, check_vma=False)
```
